32 devices in a mesh: dp: 8 (over y, x, core), fsdp: 4 (over z).
Axes of the slice: x: 2, y: 2, z: 4, core: 2. Of those that a mesh axis runs over, the one named last changes fastest.
Arguments:
- tokens: bfloat16 [64, 1024, 768], P(('dp', 'fsdp')), may hold values from -6 to 6
- cotangent: bfloat16 [64, 1024, 768], P(('dp', 'fsdp')), may hold values from -6 to 6
- lengths: int32 [64], replicated, may hold values from 1 to 1024, as said below
- seg_qkv: bfloat16 [768, 2304], P(('dp', 'fsdp')), may hold values from -0.21875 to 0.21875
- seg_out: bfloat16 [768, 768], P(('dp', 'fsdp')), may hold values from -0.625 to 0.625
- seg_up: bfloat16 [768, 3072], P(('dp', 'fsdp')), may hold values from -0.21875 to 0.21875
- seg_down: bfloat16 [3072, 768], P(('dp', 'fsdp')), may hold values from -0.109375 to 0.109375
- seg_vec: bfloat16 [12, 768], P(None, ('dp', 'fsdp')), may hold values from -0.796875 to 0.796875
- cross_qkv: bfloat16 [768, 2304], P(('dp', 'fsdp')), may hold values from -0.21875 to 0.21875
- cross_out: bfloat16 [768, 768], P(('dp', 'fsdp')), may hold values from -0.3125 to 0.3125
- cross_up: bfloat16 [768, 3072], P(('dp', 'fsdp')), may hold values from -0.21875 to 0.21875
- cross_down: bfloat16 [3072, 768], P(('dp', 'fsdp')), may hold values from -0.109375 to 0.109375
- cross_vec: bfloat16 [12, 768], P(None, ('dp', 'fsdp')), may hold values from -0.796875 to 0.796875
- positions: bfloat16 [8, 768], P(None, ('dp', 'fsdp')), may hold values from -6 to 6
Outputs:
- layer_out: bfloat16 [64, 1024, 768], P(('dp', 'fsdp'))
- token_grad: bfloat16 [64, 1024, 768], P(('dp', 'fsdp'))
- grad_seg_qkv: float32 [768, 2304], P(('dp', 'fsdp'))
- grad_seg_out: float32 [768, 768], P(('dp', 'fsdp'))
- grad_seg_up: float32 [768, 3072], P(('dp', 'fsdp'))
- grad_seg_down: float32 [3072, 768], P(('dp', 'fsdp'))
- grad_seg_vec: float32 [12, 768], P(None, ('dp', 'fsdp'))
- grad_cross_qkv: float32 [768, 2304], P(('dp', 'fsdp'))
- grad_cross_out: float32 [768, 768], P(('dp', 'fsdp'))
- grad_cross_up: float32 [768, 3072], P(('dp', 'fsdp'))
- grad_cross_down: float32 [3072, 768], P(('dp', 'fsdp'))
- grad_cross_vec: float32 [12, 768], P(None, ('dp', 'fsdp'))
- grad_positions: float32 [8, 768], P(None, ('dp', 'fsdp'))
The draws below stay inside these ranges and needn't reach their ends.
Inputs may be any that keep to these rules, and one draw needn't show every extreme that they name: lengths[s] is the number of live tokens of sequence s, which come first in its 1024 slots; some sequence has exactly 1024.
All inputs are finite; a program needn't handle non-finite values.
Results may differ from the reference program's by a relative error of at most 0.025.
Values may be sent and summed in bfloat16 or wider, within the bound.
No kernel may reach another device: no remote copies, remote signals or barrier semaphores. Data moves between devices by JAX's collectives and lax.ppermute only.
A program may use at most 256 MiB of HBM per device.

```python
import math
import jax
import jax.numpy as jnp
from jax import lax

D = 768
FF = 3072
HEAD = 64
SEG = 128
SEGS = 8
L = 1024
SEQS = 64
VROWS = 12


def draw_lengths(key, part):
    base_key = jax.random.fold_in(key, 7)
    key_one, key_two, key_three = jax.random.split(base_key, 3)
    seq_ids = jnp.arange(SEQS, dtype=jnp.int32)
    first_draw = jax.random.randint(key_one, (SEQS,), 0, L, dtype=jnp.int32)
    second_draw = jax.random.randint(key_two, (SEQS,), 0, L, dtype=jnp.int32)
    seq_lengths = 1 + jnp.maximum(first_draw, second_draw)
    chosen = jax.random.randint(key_three, (), 0, SEQS, dtype=jnp.int32)
    return jnp.where(seq_ids == chosen, L, seq_lengths).astype(jnp.int32)


def block_levels(stream_key, extent, pieces, least, high):
    factor_of, own = 1.0, jax.random.fold_in(stream_key, 6)
    for position, shards_of in pieces:
        heights = jnp.exp(jax.random.uniform(jax.random.fold_in(own, position), (shards_of,), jnp.float32, least / len(pieces), high / len(pieces)))
        factor_of = factor_of * jnp.repeat(heights, extent[position] // shards_of).reshape([-1 if axis == position else 1 for axis in range(len(extent))])
    return factor_of


def noise(key, shape, width, most, cuts=(), kind=jnp.bfloat16):
    entries = width * jax.random.normal(key, shape, jnp.float32)
    if cuts:
        entries = entries * block_levels(key, shape, cuts, -0.22, 0.18)
    return jnp.clip(entries, -most, most).astype(kind)


def setup_inputs(seed: int = 0) -> dict:
    streams_of = jax.random.split(jax.random.key(seed), 15)
    tokens = noise(streams_of[0], (SEQS, L, D), 1.0, 6.0, ((0, 32),))
    cotangent = noise(streams_of[1], (SEQS, L, D), 1.0, 6.0, ((0, 32),))
    lengths = draw_lengths(jax.random.fold_in(streams_of[14], 71), 0)
    seg_qkv = noise(streams_of[3], (D, 3 * D), D ** -0.5, 0.21875, ((0, 32),))
    seg_out = noise(streams_of[4], (D, D), (D // 8) ** -0.5, 0.625, ((0, 32),))
    seg_up = noise(streams_of[5], (D, FF), D ** -0.5, 0.21875, ((0, 32),))
    seg_down = noise(streams_of[6], (FF, D), FF ** -0.5, 0.109375, ((0, 32),))
    seg_vec = noise(streams_of[7], (VROWS, D), 0.2, 0.796875, ((1, 32),))
    cross_qkv = noise(streams_of[8], (D, 3 * D), D ** -0.5, 0.21875, ((0, 32),))
    cross_out = noise(streams_of[9], (D, D), (D // 2) ** -0.5, 0.3125, ((0, 32),))
    cross_up = noise(streams_of[10], (D, FF), D ** -0.5, 0.21875, ((0, 32),))
    cross_down = noise(streams_of[11], (FF, D), FF ** -0.5, 0.109375, ((0, 32),))
    cross_vec = noise(streams_of[12], (VROWS, D), 0.2, 0.796875, ((1, 32),))
    positions = noise(streams_of[13], (SEGS, D), 1.0, 6.0, ((1, 32),))
    return dict(tokens=tokens, cotangent=cotangent, lengths=lengths, seg_qkv=seg_qkv, seg_out=seg_out, seg_up=seg_up, seg_down=seg_down, seg_vec=seg_vec, cross_qkv=cross_qkv, cross_out=cross_out, cross_up=cross_up, cross_down=cross_down, cross_vec=cross_vec, positions=positions)


@jax.custom_vjp
def low(v):
    return lax.optimization_barrier(v.astype(jnp.bfloat16)).astype(jnp.float32)

@jax.custom_vjp
def low_back(v):
    return v

def low_keep(v):
    return (low(v), None)

def low_pass(kept, grad):
    return (grad,)

def back_keep(v):
    return (v, None)

def back_low(kept, grad):
    return (low(grad),)
low.defvjp(low_keep, low_pass)
low_back.defvjp(back_keep, back_low)
NORM_EPS = 1e-05
MASK_FILL = -1000000000.0
HIGHEST = lax.Precision.HIGHEST

def round_both(value):
    return low_back(low(value))

def product(left_op, right_op):
    return jnp.dot(left_op, right_op, precision=HIGHEST)

def layer_norm(summed, gain_row, shift_row):
    average = lax.optimization_barrier(jnp.mean(summed, axis=-1, keepdims=True))
    centered = summed - average
    variance = lax.optimization_barrier(jnp.mean(centered * centered, axis=-1, keepdims=True))
    return centered * lax.rsqrt(variance + NORM_EPS) * (1.0 + gain_row) + shift_row

def encoder(inputs, weights, allowed):
    qkv_w, out_w, up_w, down_w, vectors = weights
    row_count, feat_dim = inputs.shape
    group_len = allowed.shape[1]
    head_count = feat_dim // HEAD
    qkv_bias = jnp.concatenate([vectors[0], jnp.zeros_like(vectors[0]), vectors[1]])
    packed = round_both(product(low(inputs), qkv_w) + qkv_bias)
    query_heads, key_heads, value_heads = [portion.reshape(-1, group_len, head_count, HEAD) for portion in jnp.split(packed, 3, axis=1)]
    scores = jnp.einsum('nqhd,nkhd->nhqk', query_heads, key_heads, precision=HIGHEST) * HEAD ** (-0.5)
    scores = low_back(jnp.where(allowed[:, None, None, :], scores, MASK_FILL))
    prob_vals = jax.nn.softmax(scores, axis=-1)
    mixed = jnp.einsum('nhqk,nkhd->nqhd', low(prob_vals), value_heads, precision=HIGHEST)
    mixed = round_both(mixed.reshape(row_count, feat_dim))
    projected = low_back(product(mixed, out_w) + vectors[2])
    first_out = layer_norm(inputs + projected, vectors[3], vectors[4])
    hidden = low_back(product(low(first_out), up_w) + vectors[5:-3].reshape(-1))
    activated = low(jax.nn.gelu(hidden, approximate=False))
    down_out = low_back(product(activated, down_w) + vectors[-3])
    return layer_norm(first_out + down_out, vectors[-2], vectors[-1])

def hat_layer(token_rows, seq_lengths, seg_weights, cross_weights, pos_table):
    group_size = token_rows.shape[0]
    token_pos = jnp.arange(L)
    live_mask = token_pos[None, :] < seq_lengths[:, None]
    seg_opens = token_pos % SEG == 0
    keys_ok = (live_mask | seg_opens[None, :]).reshape(-1, SEG)
    seg_result = encoder(token_rows.reshape(-1, D), seg_weights, keys_ok).reshape(group_size, SEGS, SEG, D)
    seg_live = (jnp.arange(SEGS) * SEG)[None, :] < seq_lengths[:, None]
    heads_in = seg_result[:, :, 0, :] + pos_table[None]
    cross_result = encoder(heads_in.reshape(-1, D), cross_weights, seg_live).reshape(group_size, SEGS, 1, D)
    merged = jnp.concatenate([cross_result, seg_result[:, :, 1:, :]], axis=2).reshape(group_size, L, D)
    return merged * live_mask[..., None].astype(merged.dtype)

def reference(tokens, cotangent, lengths, seg_qkv, seg_out, seg_up, seg_down, seg_vec, cross_qkv, cross_out, cross_up, cross_down, cross_vec, positions):
    group_size = math.gcd(SEQS, max(1, 4096 // L))
    group_count = SEQS // group_size
    weights_in = tuple((weight_arr.astype(jnp.float32) for weight_arr in (seg_qkv, seg_out, seg_up, seg_down, seg_vec, cross_qkv, cross_out, cross_up, cross_down, cross_vec, positions)))

    def forward(token_vals, weight_vals):
        seg_weights = weight_vals[0:5]
        cross_weights = weight_vals[5:10]
        pos_table = weight_vals[10]
        grouped = token_vals.reshape(group_count, group_size, L, D)
        length_groups = lengths.reshape(group_count, group_size)

        def group_step(group_pair):
            return hat_layer(group_pair[0], group_pair[1], seg_weights, cross_weights, pos_table)
        outputs = lax.map(jax.checkpoint(group_step), (grouped, length_groups))
        return outputs.reshape(SEQS, L, D)
    layer_vals, pull_back = jax.vjp(forward, tokens.astype(jnp.float32), weights_in)
    token_grad, weight_grads = pull_back(cotangent.astype(jnp.float32))
    return (layer_vals.astype(jnp.bfloat16), token_grad.astype(jnp.bfloat16), weight_grads[0], weight_grads[1], weight_grads[2], weight_grads[3], weight_grads[4], weight_grads[5], weight_grads[6], weight_grads[7], weight_grads[8], weight_grads[9], weight_grads[10])
```

```python
import jax
import jax.numpy as jnp
from jax import lax
from jax.sharding import PartitionSpec as P

HEAD = 64
SEG = 128


NORM_EPS = 1e-05
MASK_FILL = -1000000000.0
ROOT_HALF = 0.7071067811865476
INV_ROOT_TAU = 0.3989422804014327


def matmul(left_op, right_op):
    return jnp.dot(left_op, right_op, preferred_element_type=jnp.float32)


def trans_left(left_op, right_op):
    return lax.dot_general(
        left_op, right_op, (((0,), (0,)), ((), ())), preferred_element_type=jnp.float32
    )


def trans_right(left_op, right_op):
    return lax.dot_general(
        left_op, right_op, (((1,), (1,)), ((), ())), preferred_element_type=jnp.float32
    )


def norm_forward(summed, gain_row, shift_row):
    average = jnp.mean(summed, axis=-1, keepdims=True)
    centered = summed - average
    inv_scale = lax.rsqrt(jnp.mean(centered * centered, axis=-1, keepdims=True) + NORM_EPS)
    normed = centered * inv_scale
    return (normed * (1.0 + gain_row) + shift_row, normed, inv_scale)


def norm_backward(upstream, normed, inv_scale, gain_row):
    inner = upstream * (1.0 + gain_row)
    back_grad = inv_scale * (
        inner
        - jnp.mean(inner, axis=-1, keepdims=True)
        - normed * jnp.mean(inner * normed, axis=-1, keepdims=True)
    )
    return (back_grad, jnp.sum(upstream * normed, axis=0), jnp.sum(upstream, axis=0))


def gelu_slope(hidden):
    return (
        0.5 * (1.0 + lax.erf(hidden * ROOT_HALF))
        + hidden * jnp.exp(-0.5 * hidden * hidden) * INV_ROOT_TAU
    )


def split_heads(packed, group_len):
    head_count = packed.shape[1] // (3 * HEAD)
    return [
        portion.reshape(-1, group_len, head_count, HEAD) for portion in jnp.split(packed, 3, axis=1)
    ]


def masked_scores(query_heads, key_heads, allowed):
    raw_scores = jnp.einsum(
        "nqhd,nkhd->nhqk", query_heads, key_heads, preferred_element_type=jnp.float32
    ) * HEAD ** (-0.5)
    return jnp.where(allowed[:, None, None, :], raw_scores, MASK_FILL)


def encode(inputs, inputs_low, weights, allowed):
    qkv_w, out_w, up_w, down_w, vectors = weights
    row_count, feat_dim = inputs_low.shape
    group_len = allowed.shape[1]
    qkv_bias = jnp.concatenate([vectors[0], jnp.zeros_like(vectors[0]), vectors[1]])
    packed = (matmul(inputs_low, qkv_w) + qkv_bias).astype(jnp.bfloat16)
    query_heads, key_heads, value_heads = split_heads(packed, group_len)
    scores = masked_scores(query_heads, key_heads, allowed)
    row_max = jnp.max(scores, axis=-1, keepdims=True)
    expo_vals = jnp.exp(scores - row_max)
    row_total = jnp.sum(expo_vals, axis=-1, keepdims=True)
    log_total = row_max + jnp.log(row_total)
    prob_low = (expo_vals / row_total).astype(jnp.bfloat16)
    mixed = jnp.einsum("nhqk,nkhd->nqhd", prob_low, value_heads, preferred_element_type=jnp.float32)
    mixed = mixed.reshape(row_count, feat_dim).astype(jnp.bfloat16)
    projected = matmul(mixed, out_w) + vectors[2]
    first_out, normed_one, scale_one = norm_forward(inputs + projected, vectors[3], vectors[4])
    first_low = first_out.astype(jnp.bfloat16)
    hidden = matmul(first_low, up_w) + vectors[5:-3].reshape(-1)
    activated = jax.nn.gelu(hidden, approximate=False).astype(jnp.bfloat16)
    down_out = matmul(activated, down_w) + vectors[-3]
    result, normed_two, scale_two = norm_forward(first_out + down_out, vectors[-2], vectors[-1])
    return (
        result,
        (
            packed,
            log_total,
            mixed,
            normed_one,
            scale_one,
            first_low,
            hidden,
            activated,
            normed_two,
            scale_two,
        ),
    )


def encode_back(upstream, inputs_low, weights, allowed, kept):
    qkv_w, out_w, up_w, down_w, vectors = weights
    (
        packed,
        log_total,
        mixed,
        normed_one,
        scale_one,
        first_low,
        hidden,
        activated,
        normed_two,
        scale_two,
    ) = kept
    row_count, feat_dim = inputs_low.shape
    group_len = allowed.shape[1]
    back_two, gain_two, shift_two = norm_backward(upstream, normed_two, scale_two, vectors[-2])
    down_grad = back_two.astype(jnp.bfloat16)
    grad_down_w = trans_left(activated, down_grad)
    hidden_grad = (trans_right(down_grad, down_w) * gelu_slope(hidden)).astype(jnp.bfloat16)
    grad_up_w = trans_left(first_low, hidden_grad)
    first_grad = trans_right(hidden_grad, up_w) + back_two
    back_one, gain_one, shift_one = norm_backward(first_grad, normed_one, scale_one, vectors[3])
    proj_grad = back_one.astype(jnp.bfloat16)
    grad_out_w = trans_left(mixed, proj_grad)
    query_heads, key_heads, value_heads = split_heads(packed, group_len)
    mixed_grad = trans_right(proj_grad, out_w).astype(jnp.bfloat16).reshape(value_heads.shape)
    scores = masked_scores(query_heads, key_heads, allowed)
    prob_vals = jnp.exp(scores - log_total)
    grad_values = jnp.einsum(
        "nhqk,nqhd->nkhd",
        prob_vals.astype(jnp.bfloat16),
        mixed_grad,
        preferred_element_type=jnp.float32,
    )
    grad_prob = jnp.einsum(
        "nqhd,nkhd->nhqk", mixed_grad, value_heads, preferred_element_type=jnp.float32
    )
    score_grad = (
        prob_vals * (grad_prob - jnp.sum(prob_vals * grad_prob, axis=-1, keepdims=True))
    ).astype(jnp.bfloat16)
    grad_query = jnp.einsum(
        "nhqk,nkhd->nqhd", score_grad, key_heads, preferred_element_type=jnp.float32
    ) * HEAD ** (-0.5)
    grad_keys = jnp.einsum(
        "nhqk,nqhd->nkhd", score_grad, query_heads, preferred_element_type=jnp.float32
    ) * HEAD ** (-0.5)
    packed_grad = jnp.concatenate(
        [
            grad_query.reshape(row_count, feat_dim),
            grad_keys.reshape(row_count, feat_dim),
            grad_values.reshape(row_count, feat_dim),
        ],
        axis=1,
    ).astype(jnp.bfloat16)
    grad_qkv_w = trans_left(inputs_low, packed_grad)
    bias_grads = jnp.sum(packed_grad, axis=0, dtype=jnp.float32).reshape(3, feat_dim)
    grad_inputs = trans_right(packed_grad, qkv_w) + back_one
    grad_vectors = jnp.concatenate(
        [
            bias_grads[0:1],
            bias_grads[2:3],
            jnp.sum(proj_grad, axis=0, dtype=jnp.float32)[None],
            gain_one[None],
            shift_one[None],
            jnp.sum(hidden_grad, axis=0, dtype=jnp.float32).reshape(-1, feat_dim),
            jnp.sum(down_grad, axis=0, dtype=jnp.float32)[None],
            gain_two[None],
            shift_two[None],
        ],
        axis=0,
    )
    return (grad_inputs, (grad_qkv_w, grad_out_w, grad_up_w, grad_down_w, grad_vectors))


def unpack(gathered):
    seg_weights = (
        gathered[0],
        gathered[1],
        gathered[2],
        gathered[3],
        gathered[4].astype(jnp.float32),
    )
    cross_weights = (
        gathered[5],
        gathered[6],
        gathered[7],
        gathered[8],
        gathered[9].astype(jnp.float32),
    )
    return (seg_weights, cross_weights, gathered[10].astype(jnp.float32))


def shards(
    tokens,
    cotangent,
    lengths,
    seg_qkv,
    seg_out,
    seg_up,
    seg_down,
    seg_vec,
    cross_qkv,
    cross_out,
    cross_up,
    cross_down,
    cross_vec,
    positions,
):
    gathered = (
        lax.all_gather(seg_qkv, ("dp", "fsdp"), axis=0, tiled=True),
        lax.all_gather(seg_out, ("dp", "fsdp"), axis=0, tiled=True),
        lax.all_gather(seg_up, ("dp", "fsdp"), axis=0, tiled=True),
        lax.all_gather(seg_down, ("dp", "fsdp"), axis=0, tiled=True),
        lax.all_gather(seg_vec, ("dp", "fsdp"), axis=1, tiled=True),
        lax.all_gather(cross_qkv, ("dp", "fsdp"), axis=0, tiled=True),
        lax.all_gather(cross_out, ("dp", "fsdp"), axis=0, tiled=True),
        lax.all_gather(cross_up, ("dp", "fsdp"), axis=0, tiled=True),
        lax.all_gather(cross_down, ("dp", "fsdp"), axis=0, tiled=True),
        lax.all_gather(cross_vec, ("dp", "fsdp"), axis=1, tiled=True),
        lax.all_gather(positions, ("dp", "fsdp"), axis=1, tiled=True),
    )
    seg_weights, cross_weights, pos_table = unpack(gathered)
    seq_local, seq_len, feat_dim = tokens.shape
    seg_count = seq_len // SEG
    first_pos = lax.axis_index(("dp", "fsdp")) * seq_local
    my_lengths = lax.dynamic_slice_in_dim(lengths, first_pos, seq_local)
    dealt_rows = tokens.reshape(-1, feat_dim)
    token_pos = jnp.arange(seq_len)
    live_mask = token_pos[None, :] < my_lengths[:, None]
    seg_opens = token_pos % SEG == 0
    keys_ok = (live_mask | seg_opens[None, :]).reshape(-1, SEG)
    seg_live = (jnp.arange(seg_count) * SEG)[None, :] < my_lengths[:, None]
    live_float = live_mask[..., None].astype(jnp.float32)
    seg_result, seg_kept = encode(dealt_rows, dealt_rows, seg_weights, keys_ok)
    seg_grid = seg_result.reshape(seq_local, seg_count, SEG, feat_dim)
    heads_in = (seg_grid[:, :, 0, :] + pos_table[None]).reshape(-1, feat_dim)
    heads_low = heads_in.astype(jnp.bfloat16)
    cross_result, cross_kept = encode(heads_in, heads_low, cross_weights, seg_live)
    merged = jnp.concatenate(
        [cross_result.reshape(seq_local, seg_count, 1, feat_dim), seg_grid[:, :, 1:, :]], axis=2
    )
    layer_out = (merged.reshape(seq_local, seq_len, feat_dim) * live_float).astype(jnp.bfloat16)
    grad_grid = (cotangent.astype(jnp.float32) * live_float).reshape(
        seq_local, seg_count, SEG, feat_dim
    )
    cross_up_grad = grad_grid[:, :, 0, :].reshape(-1, feat_dim)
    heads_grad, cross_grads = encode_back(
        cross_up_grad, heads_low, cross_weights, seg_live, cross_kept
    )
    heads_grid = heads_grad.reshape(seq_local, seg_count, feat_dim)
    grad_positions = jnp.sum(heads_grid, axis=0)
    seg_up_grad = jnp.concatenate(
        [heads_grid[:, :, None, :], grad_grid[:, :, 1:, :]], axis=2
    ).reshape(-1, feat_dim)
    rows_grad, seg_grads = encode_back(seg_up_grad, dealt_rows, seg_weights, keys_ok, seg_kept)
    token_grad = rows_grad.reshape(seq_local, seq_len, feat_dim).astype(jnp.bfloat16)
    summed = (
        lax.psum_scatter(seg_grads[0].astype(jnp.bfloat16), ("dp", "fsdp"), scatter_dimension=0, tiled=True).astype(jnp.float32),
        lax.psum_scatter(seg_grads[1].astype(jnp.bfloat16), ("dp", "fsdp"), scatter_dimension=0, tiled=True).astype(jnp.float32),
        lax.psum_scatter(seg_grads[2].astype(jnp.bfloat16), ("dp", "fsdp"), scatter_dimension=0, tiled=True).astype(jnp.float32),
        lax.psum_scatter(seg_grads[3].astype(jnp.bfloat16), ("dp", "fsdp"), scatter_dimension=0, tiled=True).astype(jnp.float32),
        lax.psum_scatter(seg_grads[4], ("dp", "fsdp"), scatter_dimension=1, tiled=True),
        lax.psum_scatter(cross_grads[0].astype(jnp.bfloat16), ("dp", "fsdp"), scatter_dimension=0, tiled=True).astype(jnp.float32),
        lax.psum_scatter(cross_grads[1].astype(jnp.bfloat16), ("dp", "fsdp"), scatter_dimension=0, tiled=True).astype(jnp.float32),
        lax.psum_scatter(cross_grads[2].astype(jnp.bfloat16), ("dp", "fsdp"), scatter_dimension=0, tiled=True).astype(jnp.float32),
        lax.psum_scatter(cross_grads[3].astype(jnp.bfloat16), ("dp", "fsdp"), scatter_dimension=0, tiled=True).astype(jnp.float32),
        lax.psum_scatter(cross_grads[4], ("dp", "fsdp"), scatter_dimension=1, tiled=True),
        lax.psum_scatter(grad_positions, ("dp", "fsdp"), scatter_dimension=1, tiled=True),
    )
    return (
        layer_out,
        token_grad,
        summed[0],
        summed[1],
        summed[2],
        summed[3],
        summed[4],
        summed[5],
        summed[6],
        summed[7],
        summed[8],
        summed[9],
        summed[10],
    )


def solution(mesh):
    in_specs = (
        P(("dp", "fsdp"), None, None),
        P(("dp", "fsdp"), None, None),
        P(),
        P(("dp", "fsdp"), None),
        P(("dp", "fsdp"), None),
        P(("dp", "fsdp"), None),
        P(("dp", "fsdp"), None),
        P(None, ("dp", "fsdp")),
        P(("dp", "fsdp"), None),
        P(("dp", "fsdp"), None),
        P(("dp", "fsdp"), None),
        P(("dp", "fsdp"), None),
        P(None, ("dp", "fsdp")),
        P(None, ("dp", "fsdp")),
    )
    out_specs = (
        P(("dp", "fsdp"), None, None),
        P(("dp", "fsdp"), None, None),
        P(("dp", "fsdp"), None),
        P(("dp", "fsdp"), None),
        P(("dp", "fsdp"), None),
        P(("dp", "fsdp"), None),
        P(None, ("dp", "fsdp")),
        P(("dp", "fsdp"), None),
        P(("dp", "fsdp"), None),
        P(("dp", "fsdp"), None),
        P(("dp", "fsdp"), None),
        P(None, ("dp", "fsdp")),
        P(None, ("dp", "fsdp")),
    )
    return jax.shard_map(shards, mesh=mesh, in_specs=in_specs, out_specs=out_specs, check_vma=False)
```

```python
import functools

import jax
import jax.numpy as jnp
from jax import lax
from jax.sharding import PartitionSpec as P

HEAD = 64
SEG = 128


NORM_EPS = 1e-05
MASK_FILL = -1000000000.0
ROOT_HALF = 0.7071067811865476
INV_ROOT_TAU = 0.3989422804014327


def matmul(left_op, right_op):
    return jnp.dot(left_op, right_op, preferred_element_type=jnp.float32)


def trans_left(left_op, right_op):
    return lax.dot_general(
        left_op, right_op, (((0,), (0,)), ((), ())), preferred_element_type=jnp.float32
    )


def trans_right(left_op, right_op):
    return lax.dot_general(
        left_op, right_op, (((1,), (1,)), ((), ())), preferred_element_type=jnp.float32
    )


def norm_forward(summed, gain_row, shift_row):
    average = jnp.mean(summed, axis=-1, keepdims=True)
    centered = summed - average
    inv_scale = lax.rsqrt(jnp.mean(centered * centered, axis=-1, keepdims=True) + NORM_EPS)
    normed = centered * inv_scale
    return (normed * (1.0 + gain_row) + shift_row, normed, inv_scale)


def norm_backward(upstream, normed, inv_scale, gain_row):
    inner = upstream * (1.0 + gain_row)
    back_grad = inv_scale * (
        inner
        - jnp.mean(inner, axis=-1, keepdims=True)
        - normed * jnp.mean(inner * normed, axis=-1, keepdims=True)
    )
    return (back_grad, jnp.sum(upstream * normed, axis=0), jnp.sum(upstream, axis=0))


def gelu_slope(hidden):
    return (
        0.5 * (1.0 + lax.erf(hidden * ROOT_HALF))
        + hidden * jnp.exp(-0.5 * hidden * hidden) * INV_ROOT_TAU
    )


def split_heads(packed, group_len):
    head_count = packed.shape[1] // (3 * HEAD)
    return [
        portion.reshape(-1, group_len, head_count, HEAD) for portion in jnp.split(packed, 3, axis=1)
    ]


def masked_scores(query_heads, key_heads, allowed):
    raw_scores = jnp.einsum(
        "nqhd,nkhd->nhqk", query_heads, key_heads, preferred_element_type=jnp.float32
    ) * HEAD ** (-0.5)
    return jnp.where(allowed[:, None, None, :], raw_scores, MASK_FILL)


def encode(inputs, inputs_low, weights, allowed):
    qkv_w, out_w, up_w, down_w, vectors = weights
    row_count, feat_dim = inputs_low.shape
    group_len = allowed.shape[1]
    qkv_bias = jnp.concatenate([vectors[0], jnp.zeros_like(vectors[0]), vectors[1]])
    packed = (matmul(inputs_low, qkv_w) + qkv_bias).astype(jnp.bfloat16)
    query_heads, key_heads, value_heads = split_heads(packed, group_len)
    scores = masked_scores(query_heads, key_heads, allowed)
    row_max = jnp.max(scores, axis=-1, keepdims=True)
    expo_vals = jnp.exp(scores - row_max)
    row_total = jnp.sum(expo_vals, axis=-1, keepdims=True)
    log_total = row_max + jnp.log(row_total)
    prob_low = (expo_vals / row_total).astype(jnp.bfloat16)
    mixed = jnp.einsum("nhqk,nkhd->nqhd", prob_low, value_heads, preferred_element_type=jnp.float32)
    mixed = mixed.reshape(row_count, feat_dim).astype(jnp.bfloat16)
    projected = matmul(mixed, out_w) + vectors[2]
    first_out, normed_one, scale_one = norm_forward(inputs + projected, vectors[3], vectors[4])
    first_low = first_out.astype(jnp.bfloat16)
    hidden = matmul(first_low, up_w) + vectors[5:-3].reshape(-1)
    activated = jax.nn.gelu(hidden, approximate=False).astype(jnp.bfloat16)
    down_out = matmul(activated, down_w) + vectors[-3]
    result, normed_two, scale_two = norm_forward(first_out + down_out, vectors[-2], vectors[-1])
    return (
        result,
        (
            packed,
            log_total,
            mixed,
            normed_one,
            scale_one,
            first_low,
            hidden,
            activated,
            normed_two,
            scale_two,
        ),
    )


def encode_back(upstream, inputs_low, weights, allowed, kept):
    qkv_w, out_w, up_w, down_w, vectors = weights
    (
        packed,
        log_total,
        mixed,
        normed_one,
        scale_one,
        first_low,
        hidden,
        activated,
        normed_two,
        scale_two,
    ) = kept
    row_count, feat_dim = inputs_low.shape
    group_len = allowed.shape[1]
    back_two, gain_two, shift_two = norm_backward(upstream, normed_two, scale_two, vectors[-2])
    down_grad = back_two.astype(jnp.bfloat16)
    hidden_grad = (trans_right(down_grad, down_w) * gelu_slope(hidden)).astype(jnp.bfloat16)
    first_grad = trans_right(hidden_grad, up_w) + back_two
    back_one, gain_one, shift_one = norm_backward(first_grad, normed_one, scale_one, vectors[3])
    proj_grad = back_one.astype(jnp.bfloat16)
    query_heads, key_heads, value_heads = split_heads(packed, group_len)
    mixed_grad = trans_right(proj_grad, out_w).astype(jnp.bfloat16).reshape(value_heads.shape)
    scores = masked_scores(query_heads, key_heads, allowed)
    prob_vals = jnp.exp(scores - log_total)
    grad_values = jnp.einsum(
        "nhqk,nqhd->nkhd",
        prob_vals.astype(jnp.bfloat16),
        mixed_grad,
        preferred_element_type=jnp.float32,
    )
    grad_prob = jnp.einsum(
        "nqhd,nkhd->nhqk", mixed_grad, value_heads, preferred_element_type=jnp.float32
    )
    score_grad = (
        prob_vals * (grad_prob - jnp.sum(prob_vals * grad_prob, axis=-1, keepdims=True))
    ).astype(jnp.bfloat16)
    grad_query = jnp.einsum(
        "nhqk,nkhd->nqhd", score_grad, key_heads, preferred_element_type=jnp.float32
    ) * HEAD ** (-0.5)
    grad_keys = jnp.einsum(
        "nhqk,nqhd->nkhd", score_grad, query_heads, preferred_element_type=jnp.float32
    ) * HEAD ** (-0.5)
    packed_grad = jnp.concatenate(
        [
            grad_query.reshape(row_count, feat_dim),
            grad_keys.reshape(row_count, feat_dim),
            grad_values.reshape(row_count, feat_dim),
        ],
        axis=1,
    ).astype(jnp.bfloat16)
    bias_grads = jnp.sum(packed_grad, axis=0, dtype=jnp.float32).reshape(3, feat_dim)
    grad_inputs = trans_right(packed_grad, qkv_w) + back_one
    grad_vectors = jnp.concatenate(
        [
            bias_grads[0:1],
            bias_grads[2:3],
            jnp.sum(proj_grad, axis=0, dtype=jnp.float32)[None],
            gain_one[None],
            shift_one[None],
            jnp.sum(hidden_grad, axis=0, dtype=jnp.float32).reshape(-1, feat_dim),
            jnp.sum(down_grad, axis=0, dtype=jnp.float32)[None],
            gain_two[None],
            shift_two[None],
        ],
        axis=0,
    )
    pairs = (
        (inputs_low, packed_grad),
        (mixed, proj_grad),
        (first_low, hidden_grad),
        (activated, down_grad),
    )
    return (grad_inputs, pairs, grad_vectors)

AXES = ("dp", "fsdp")


class Links:
    def __init__(self, outer, inner):
        self.outer, self.inner = outer, inner
        self.place = lax.axis_index("dp")
        self.z = lax.axis_index("fsdp")
        self.bits = (self.place // 4, self.place // 2 % 2, self.place % 2)

    def flip(self, value, mask):
        pairs = [
            (d * self.inner + z, (d ^ mask) * self.inner + z)
            for d in range(self.outer)
            for z in range(self.inner)
        ]
        return lax.ppermute(value, AXES, pairs)

    def turn(self, value, step):
        pairs = [
            (d * self.inner + z, d * self.inner + (z + step) % self.inner)
            for d in range(self.outer)
            for z in range(self.inner)
        ]
        return lax.ppermute(value, AXES, pairs)

    def gather_z(self, shard):
        whole = jnp.zeros((self.inner,) + shard.shape, shard.dtype)
        whole = lax.dynamic_update_index_in_dim(whole, shard, self.z, 0)
        for step in range(1, self.inner):
            came = self.turn(shard, step)
            whole = lax.dynamic_update_index_in_dim(
                whole, came, (self.z + self.inner - step) % self.inner, 0
            )
        return whole

    def spread(self, block):
        half = block.shape[0] // 2
        by_x, by_y = self.flip(block, 2), self.flip(block, 4)
        diag_a, diag_b = self.flip(by_y[:half], 2), self.flip(by_x[half:], 4)
        mine = [block, by_x, by_y, diag_a, diag_b]
        return mine, [self.flip(piece, 1) for piece in mine]

    def assemble(self, pieces):
        mine, theirs = pieces
        block = mine[0]
        half = block.shape[0] // 2
        whole = jnp.zeros((8,) + block.shape, block.dtype)
        for flip_c, side in ((0, mine), (1, theirs)):
            for flip_yx, start, piece in (
                (0, 0, side[0]), (2, 0, side[1]), (4, 0, side[2]), (6, 0, side[3]), (6, half, side[4]),
            ):
                where = (self.place ^ (flip_yx + flip_c), start) + (0,) * (block.ndim - 1)
                whole = lax.dynamic_update_slice(whole, piece[None], where)
        return whole

    def gather_small(self, shard):
        block = self.gather_z(shard)
        whole = jnp.zeros((8,) + block.shape, block.dtype)
        near = [(0, block)] + [(m, self.flip(block, m)) for m in (2, 4, 6)]
        near += [(m + 1, self.flip(piece, 1)) for m, piece in near]
        for mask, piece in near:
            whole = lax.dynamic_update_index_in_dim(whole, piece, self.place ^ mask, 0)
        return whole.reshape((-1,) + shard.shape)

    def scatter_sum(self, parts):
        outer, inner, rows, cols = parts.shape
        grid = parts.astype(jnp.bfloat16).reshape(2, 2, 2, inner, rows, cols)
        y, x, c = self.bits

        def pick(array, index, axis):
            return lax.dynamic_index_in_dim(array, index, axis, keepdims=False)

        def add(*terms):
            return sum(t.astype(jnp.float32) for t in terms).astype(jnp.bfloat16)

        came = self.flip(pick(grid, 1 - c, 2), 1)
        grid = add(pick(grid, c, 2), came)
        near_y, far_y = pick(grid, y, 0), pick(grid, 1 - y, 0)
        own, to_x = pick(near_y, x, 0), pick(near_y, 1 - x, 0)
        to_y, to_d = pick(far_y, x, 0), pick(far_y, 1 - x, 0)
        half = inner // 2
        came_x, came_y = self.flip(to_d[:half], 2), self.flip(to_d[half:], 4)
        to_y = jnp.concatenate([add(to_y[:half], came_x), to_y[half:]])
        to_x = jnp.concatenate([to_x[:half], add(to_x[half:], came_y)])
        own = add(own, self.flip(to_x, 2), self.flip(to_y, 4))
        total = pick(own, self.z, 0).astype(jnp.float32)
        for step in range(1, inner):
            sent = pick(own, (self.z + step) % inner, 0)
            total = total + self.turn(sent, step).astype(jnp.float32)
        return total


class PlainLinks:
    def __init__(self, outer, inner):
        self.outer, self.inner = outer, inner
        self.place = lax.axis_index("dp")
        self.z = lax.axis_index("fsdp")

    def gather_small(self, shard):
        return lax.all_gather(shard, AXES, axis=0)

    def scatter_sum(self, parts):
        rows, cols = parts.shape[2:]
        flat = parts.astype(jnp.bfloat16).reshape(-1, cols)
        return lax.psum_scatter(flat, AXES, scatter_dimension=0, tiled=True).astype(jnp.float32)


def gather_matrices(links, matrices):
    if isinstance(links, PlainLinks):
        return [lax.all_gather(m, AXES, axis=0, tiled=True) for m in matrices]
    blocks = [links.gather_z(m) for m in matrices]
    return [links.assemble(links.spread(b)).reshape(-1, b.shape[-1]) for b in blocks]


def shards(
    outer,
    inner,
    tokens,
    cotangent,
    lengths,
    seg_qkv,
    seg_out,
    seg_up,
    seg_down,
    seg_vec,
    cross_qkv,
    cross_out,
    cross_up,
    cross_down,
    cross_vec,
    positions,
):
    links = (Links if (outer, inner) == (8, 4) else PlainLinks)(outer, inner)
    devices = outer * inner
    me = links.place * inner + links.z
    seq_local, seq_len, feat_dim = tokens.shape
    seg_count = seq_len // SEG
    seg_rows, cross_rows = seg_vec.shape[0], cross_vec.shape[0]
    small = jnp.concatenate([seg_vec, cross_vec, positions])
    small = links.gather_small(small.reshape(1, -1))
    small = small.reshape((devices,) + (seg_rows + cross_rows + seg_count, seg_vec.shape[1]))
    small = small.transpose(1, 0, 2).reshape(-1, feat_dim).astype(jnp.float32)
    seg_v, cross_v = small[:seg_rows], small[seg_rows : seg_rows + cross_rows]
    pos_table = small[seg_rows + cross_rows :]
    seg_weights = gather_matrices(links, [seg_qkv, seg_out, seg_up, seg_down]) + [seg_v]
    cross_weights = gather_matrices(links, [cross_qkv, cross_out, cross_up, cross_down]) + [cross_v]
    first_pos = me * seq_local
    my_lengths = lax.dynamic_slice_in_dim(lengths, first_pos, seq_local)
    rows_in = tokens.reshape(-1, feat_dim)
    token_pos = jnp.arange(seq_len)
    live_mask = token_pos[None, :] < my_lengths[:, None]
    seg_opens = token_pos % SEG == 0
    keys_ok = (live_mask | seg_opens[None, :]).reshape(-1, SEG)
    live_float = live_mask[..., None].astype(jnp.float32)
    seg_result, seg_kept = encode(rows_in, rows_in, seg_weights, keys_ok)
    seg_grid = seg_result.reshape(seq_local, seg_count, SEG, feat_dim)
    grad_grid = (cotangent.astype(jnp.float32) * live_float).reshape(
        seq_local, seg_count, SEG, feat_dim
    )
    heads_own = (seg_grid[:, :, 0, :]).reshape(-1, feat_dim)
    up_own = grad_grid[:, :, 0, :].reshape(-1, feat_dim).astype(jnp.bfloat16)
    heads_all = links.gather_small(heads_own.astype(jnp.bfloat16)).reshape(-1, feat_dim)
    up_all = links.gather_small(up_own).reshape(-1, feat_dim).astype(jnp.float32)
    heads_in = (heads_all.astype(jnp.float32).reshape(-1, seg_count, feat_dim) + pos_table[None]).reshape(-1, feat_dim)
    heads_low = heads_in.astype(jnp.bfloat16)
    live_all = (jnp.arange(seg_count) * SEG)[None, :] < lengths[:, None]
    cross_result, cross_kept = encode(heads_in, heads_low, cross_weights, live_all)
    heads_grad, pairs, cross_vec_grad = encode_back(
        up_all, heads_low, cross_weights, live_all, cross_kept
    )
    cross_grads = []
    for left, right in pairs:
        width = left.shape[1] // devices
        mine = lax.dynamic_slice_in_dim(left, me * width, width, 1)
        cross_grads.append(trans_left(mine, right))
    grad_positions = jnp.sum(heads_grad.reshape(-1, seg_count, feat_dim), axis=0)
    width = feat_dim // devices
    cross_vec_grad = lax.dynamic_slice_in_dim(cross_vec_grad, me * width, width, 1)
    grad_positions = lax.dynamic_slice_in_dim(grad_positions, me * width, width, 1)
    own_rows = seq_local * seg_count
    cross_own = lax.dynamic_slice_in_dim(cross_result, me * own_rows, own_rows)
    heads_grid = lax.dynamic_slice_in_dim(heads_grad, me * own_rows, own_rows).reshape(
        seq_local, seg_count, feat_dim
    )
    merged = jnp.concatenate(
        [cross_own.reshape(seq_local, seg_count, 1, feat_dim), seg_grid[:, :, 1:, :]], axis=2
    )
    layer_out = (merged.reshape(seq_local, seq_len, feat_dim) * live_float).astype(jnp.bfloat16)
    seg_up_grad = jnp.concatenate(
        [heads_grid[:, :, None, :], grad_grid[:, :, 1:, :]], axis=2
    ).reshape(-1, feat_dim)
    rows_grad, pairs, seg_vec_grad = encode_back(seg_up_grad, rows_in, seg_weights, keys_ok, seg_kept)
    token_grad = rows_grad.reshape(seq_local, seq_len, feat_dim).astype(jnp.bfloat16)
    seg_grads = []
    for left, right in pairs:
        whole = trans_left(left, right)
        seg_grads.append(
            links.scatter_sum(whole.reshape(outer, inner, -1, whole.shape[1]))
        )
    vec_parts = seg_vec_grad.reshape(seg_rows, devices, width).transpose(1, 0, 2)
    vec_parts = vec_parts.reshape(outer, inner, 1, seg_rows * width)
    seg_vec_sum = links.scatter_sum(vec_parts).reshape(seg_rows, width)
    return (layer_out, token_grad, *seg_grads, seg_vec_sum, *cross_grads, cross_vec_grad, grad_positions)


def solution(mesh):
    in_specs = (
        P(("dp", "fsdp"), None, None),
        P(("dp", "fsdp"), None, None),
        P(),
        P(("dp", "fsdp"), None),
        P(("dp", "fsdp"), None),
        P(("dp", "fsdp"), None),
        P(("dp", "fsdp"), None),
        P(None, ("dp", "fsdp")),
        P(("dp", "fsdp"), None),
        P(("dp", "fsdp"), None),
        P(("dp", "fsdp"), None),
        P(("dp", "fsdp"), None),
        P(None, ("dp", "fsdp")),
        P(None, ("dp", "fsdp")),
    )
    out_specs = (
        P(("dp", "fsdp"), None, None),
        P(("dp", "fsdp"), None, None),
        P(("dp", "fsdp"), None),
        P(("dp", "fsdp"), None),
        P(("dp", "fsdp"), None),
        P(("dp", "fsdp"), None),
        P(None, ("dp", "fsdp")),
        P(("dp", "fsdp"), None),
        P(("dp", "fsdp"), None),
        P(("dp", "fsdp"), None),
        P(("dp", "fsdp"), None),
        P(None, ("dp", "fsdp")),
        P(None, ("dp", "fsdp")),
    )
    return jax.shard_map(
        functools.partial(shards, mesh.shape["dp"], mesh.shape["fsdp"]),
        mesh=mesh, in_specs=in_specs, out_specs=out_specs, check_vma=False)
```

```python
import functools

import jax
import jax.numpy as jnp
from jax import lax
from jax.experimental import pallas as pl
from jax.experimental.pallas import tpu as pltpu
from jax.sharding import PartitionSpec as P

HEAD = 64
SEG = 128
NORM_EPS = 1e-05
MASK_FILL = -1000000000.0
VMEM = 60 * 2**20
F32, LOW = jnp.float32, jnp.bfloat16


ROOT_HALF = 0.7071067811865476
INV_ROOT_TAU = 0.3989422804014327
AXES = ("dp", "fsdp")

def mm(left_op, right_op):
    return jnp.dot(left_op, right_op, preferred_element_type=F32)


def mm_nt(left_op, right_op):
    return lax.dot_general(left_op, right_op, (((1,), (1,)), ((), ())), preferred_element_type=F32)


def mm_tn(left_op, right_op):
    return lax.dot_general(left_op, right_op, (((0,), (0,)), ((), ())), preferred_element_type=F32)


def normalize(summed):
    average = jnp.mean(summed, axis=-1, keepdims=True)
    centered = summed - average
    inv_scale = lax.rsqrt(jnp.mean(centered * centered, axis=-1, keepdims=True) + NORM_EPS)
    return centered * inv_scale, inv_scale


def normalize_back(inner, normed, inv_scale):
    return inv_scale * (
        inner
        - jnp.mean(inner, axis=-1, keepdims=True)
        - normed * jnp.mean(inner * normed, axis=-1, keepdims=True)
    )


def gelu_parts(hidden):
    size = jnp.abs(hidden)
    near = 1.0 / (1.0 + (0.3275911 * 0.7071067811865476) * size)
    bell = jnp.exp(-0.5 * hidden * hidden)
    poly = 0.5 * 1.061405429
    for term in (-1.453152027, 1.421413741, -0.284496736, 0.254829592):
        poly = poly * near + 0.5 * term
    tail = poly * near * bell
    phi = jnp.where(hidden < 0.0, tail, 1.0 - tail)
    return hidden * phi, phi + hidden * bell * 0.3989422804014327


def pair_stack(pair, low_half):
    zero = jnp.zeros_like(pair)
    return jnp.concatenate(
        [jnp.where(low_half, pair, zero), jnp.where(low_half, zero, pair)], axis=0
    )


def pair_merge(stacked, low_half):
    rows = stacked.shape[0] // 2
    return jnp.where(low_half, stacked[:rows], stacked[rows:])


def pair_probs(query_stack, keys, allowed):
    scores = jnp.where(allowed, mm_nt(query_stack, keys), MASK_FILL)
    expo = jnp.exp(scores - jnp.max(scores, axis=-1, keepdims=True))
    return expo


def attend(query, keys, values, allowed):
    low_half = lax.broadcasted_iota(jnp.int32, query.shape, 1) < HEAD
    stack = pair_stack(query * jnp.asarray(HEAD**-0.5, query.dtype), low_half)
    expo = pair_probs(stack, keys, allowed).astype(LOW)
    wide = jnp.concatenate([values, jnp.ones_like(values)], axis=1)
    both = mm(expo, wide)
    out = both[:, :128] / both[:, 128:]
    return pair_merge(out, low_half)


def attend_back(query, keys, values, grad_mixed, allowed):
    low_half = lax.broadcasted_iota(jnp.int32, query.shape, 1) < HEAD
    stack = pair_stack(query * jnp.asarray(HEAD**-0.5, query.dtype), low_half)
    expo = pair_probs(stack, keys, allowed)
    probs = expo / jnp.sum(expo, axis=-1, keepdims=True)
    grad_stack = pair_stack(grad_mixed, low_half)
    grad_prob = mm_nt(grad_stack, values)
    weighted = probs * grad_prob
    score_grad = (weighted - probs * jnp.sum(weighted, axis=-1, keepdims=True)).astype(LOW)
    grad_query = pair_merge(mm(score_grad, keys), low_half) * HEAD**-0.5
    grad_keys = mm_tn(score_grad, stack)
    grad_values = mm_tn(probs.astype(LOW), grad_stack)
    return grad_query, grad_keys, grad_values


def load_slabs(place, pieces, slabs, sems):
    for _, copy in slab_copies(place, pieces, slabs, sems, True):
        copy.wait()


def slab_copies(place, pieces, slabs, sems, start, first_slab=0):
    count = len(slabs)
    half = count // 2
    copies = []
    spans = ((0, 0, count), (2, 0, count), (4, 0, count), (6, 0, half), (6, half, count))
    for flip_c in (0, 1):
        for index, (flip_yx, first, last) in enumerate(spans):
            block = place ^ (flip_yx + flip_c)
            piece = pieces[flip_c * 5 + index]
            for slab in range(first, last):
                if slab < first_slab:
                    continue
                sem = sems.at[slab * 8 + (flip_yx + flip_c)]
                source, target = piece.at[slab - first], slabs[slab](block)
                copies.append((slab, pltpu.make_async_copy(source, target, sem)))
    if start:
        for _, copy in copies:
            copy.start()
    return copies


def rows_of(ref, block, rows, slab=None):
    where = pl.ds(pl.multiple_of(block * rows, rows), rows)
    return ref.at[where] if slab is None else ref.at[slab, where]


def qkv_slabs(qkv):
    return [functools.partial(rows_of, qkv, rows=96, slab=j) for j in range(3)]


def rest_slabs(out, up, down):
    def down_slab(block, part):
        return down.at[pl.ds(pl.multiple_of(block * 384 + part * 96, 96), 96)]

    slabs = [functools.partial(rows_of, out, rows=96)]
    slabs += [functools.partial(rows_of, up, rows=96, slab=j) for j in range(4)]
    return slabs + [functools.partial(down_slab, part=j) for j in range(4)]


def segment_mask(length, seg_in_seq):
    lane = lax.broadcasted_iota(jnp.int32, (1, SEG), 1)
    return (lane + seg_in_seq * SEG < length) | (lane == 0)


def attn_forward_kernel(segs, seg_count, info, x_ref, vec_ref, *rest):
    pieces, (packed_ref, mixed_ref, qkv, sems) = rest[:10], rest[10:]
    step = pl.program_id(0)

    @pl.when(step == 0)
    def _():
        load_slabs(info[0], pieces, qkv_slabs(qkv), sems)

    rows = x_ref[...]
    for j in range(3):
        part = mm(rows, qkv[j])
        if j != 1:
            part = part + vec_ref[j // 2 : j // 2 + 1, :]
        packed_ref[:, j * 768 : (j + 1) * 768] = part.astype(LOW)
    for s in range(segs):
        seg = step * segs + s
        allowed = segment_mask(info[1 + seg // seg_count], seg % seg_count)
        at = slice(s * SEG, (s + 1) * SEG)
        for h in range(6):
            q, k, v = (packed_ref[at, j * 768 + h * 128 : j * 768 + (h + 1) * 128] for j in range(3))
            mixed_ref[at, h * 128 : (h + 1) * 128] = attend(q, k, v, allowed).astype(LOW)


def ffn_forward_kernel(segs, info, x_ref, mixed_ref, vec_ref, *rest):
    pieces, rest = rest[:10], rest[10:]
    sum_ref, low_ref, act_ref, slope_ref, second_ref, heads_ref, out, up, down, sems = rest

    @pl.when(pl.program_id(0) == 0)
    def _():
        load_slabs(info[0], pieces, rest_slabs(out, up, down), sems)

    summed = x_ref[...].astype(F32) + mm(mixed_ref[...], out[...]) + vec_ref[2:3, :]
    sum_ref[...] = summed
    normed, _ = normalize(summed)
    first = normed * (1.0 + vec_ref[3:4, :]) + vec_ref[4:5, :]
    first_low = first.astype(LOW)
    low_ref[...] = first_low
    total = first + vec_ref[9:10, :]
    for j in range(4):
        hidden = mm(first_low, up[j]) + vec_ref[5 + j : 6 + j, :]
        act, slope = gelu_parts(hidden)
        act = act.astype(LOW)
        act_ref[:, j * 768 : (j + 1) * 768] = act
        slope_ref[:, j * 768 : (j + 1) * 768] = slope.astype(LOW)
        total = total + mm(act, down[j * 768 : (j + 1) * 768, :])
    second_ref[...] = total
    opening = jnp.concatenate([total[s * SEG : s * SEG + 1] for s in range(segs)], axis=0)
    normed, _ = normalize(opening)
    heads_ref[...] = normed * (1.0 + vec_ref[10:11, :]) + vec_ref[11:12, :]


def cross_kernel(blocks, info, heads_ref, up_ref, live_ref, vec_ref, pos_ref, *rest):
    pieces, rest = rest[:10], rest[10:]
    (own_ref, own_grad_ref, grads_ref, pos_grad_ref, qkv_grad_ref, out_grad_ref, up_grad_ref, down_grad_ref) = rest[:8]
    (qkv, out, up, down, sems, result, heads_grad, slope, lefts, act, packed, rights, hidden_grad) = rest[8:]
    step = pl.program_id(0)
    count = heads_ref.shape[0]
    at = pl.ds(pl.multiple_of(step * count, count), count)
    slabs = qkv_slabs(qkv) + rest_slabs(out, up, down)

    @pl.when(step == 0)
    def _():
        copies = slab_copies(info[0], pieces, slabs, sems, True)
        grads_ref[...] = jnp.zeros_like(grads_ref)
        pos_grad_ref[...] = jnp.zeros_like(pos_grad_ref)
        for slab, copy in copies:
            if slab < 3:
                copy.wait()

    vec = vec_ref[...]
    inputs = heads_ref[...].astype(F32).reshape(-1, 8, 768) + pos_ref[...][None]
    inputs = inputs.reshape(count, 768)
    low = inputs.astype(LOW)
    lefts[0, at, :] = low
    for j in range(3):
        part = mm(low, qkv[j])
        if j != 1:
            part = part + vec[j // 2 : j // 2 + 1]
        packed[:, j * 768 : (j + 1) * 768] = part.astype(LOW)
    row = lax.broadcasted_iota(jnp.int32, (2 * SEG, SEG), 0)
    lane = lax.broadcasted_iota(jnp.int32, (2 * SEG, SEG), 1)
    group = row % SEG // 8 == lane // 8
    masks = [group & (live_ref[s : s + 1, :] > 0.0) for s in range(count // SEG)]
    for s, allowed in enumerate(masks):
        part = slice(s * SEG, (s + 1) * SEG)
        for h in range(6):
            q, k, v = (packed[part, j * 768 + h * 128 : j * 768 + (h + 1) * 128] for j in range(3))
            where = pl.ds(pl.multiple_of(step * count + s * SEG, SEG), SEG)
            lefts[1, where, h * 128 : (h + 1) * 128] = attend(q, k, v, allowed).astype(LOW)

    @pl.when(step == 0)
    def _():
        for _, copy in slab_copies(info[0], pieces, slabs, sems, False, 3):
            copy.wait()

    summed = inputs + mm(lefts[1, at, :], out[...]) + vec[2:3]
    normed_one, scale_one = normalize(summed)
    first = normed_one * (1.0 + vec[3:4]) + vec[4:5]
    first_low = first.astype(LOW)
    lefts[2, at, :] = first_low
    total = first + vec[9:10]
    for j in range(4):
        cols = slice(j * 768, (j + 1) * 768)
        hidden = mm(first_low, up[j]) + vec[5 + j : 6 + j]
        active, steep = gelu_parts(hidden)
        act[at, cols] = active.astype(LOW)
        slope[:, cols] = steep.astype(LOW)
        total = total + mm(active.astype(LOW), down[cols, :])
    normed, inv_scale = normalize(total)
    result[at, :] = normed * (1.0 + vec[10:11]) + vec[11:12]
    upstream = up_ref[...].astype(F32)
    back_two = normalize_back(upstream * (1.0 + vec[10:11]), normed, inv_scale)
    down_grad = back_two.astype(LOW)
    rights[1, at, :] = down_grad
    grads_ref[9:10, :] += column_sum(down_grad)
    grads_ref[10:11, :] += column_sum(upstream * normed)
    grads_ref[11:12, :] += column_sum(upstream)
    total = back_two
    for j in range(4):
        cols = slice(j * 768, (j + 1) * 768)
        grad = (mm_nt(down_grad, down[cols, :]) * slope[:, cols].astype(F32)).astype(LOW)
        hidden_grad[at, cols] = grad
        grads_ref[5 + j : 6 + j, :] += column_sum(grad)
        total = total + mm_nt(grad, up[j])
    back_one = normalize_back(total * (1.0 + vec[3:4]), normed_one, scale_one)
    proj_grad = back_one.astype(LOW)
    rights[0, at, :] = proj_grad
    grads_ref[2:3, :] += column_sum(proj_grad)
    grads_ref[3:4, :] += column_sum(total * normed_one)
    grads_ref[4:5, :] += column_sum(total)
    mixed_grad = mm_nt(proj_grad, out[...]).astype(LOW)
    for s, allowed in enumerate(masks):
        part = slice(s * SEG, (s + 1) * SEG)
        where = pl.ds(pl.multiple_of(step * count + s * SEG, SEG), SEG)
        for h in range(6):
            cols = slice(h * 128, (h + 1) * 128)
            q, k, v = (packed[part, j * 768 + h * 128 : j * 768 + (h + 1) * 128] for j in range(3))
            for j, g in enumerate(attend_back(q, k, v, mixed_grad[part, cols], allowed)):
                rights[2 + j, where, cols] = g.astype(LOW)
    total = back_one
    for j in range(3):
        part = rights[2 + j, at, :]
        total = total + mm_nt(part, qkv[j])
        if j != 1:
            grads_ref[j // 2 : j // 2 + 1, :] += column_sum(part)
    heads_grad[at, :] = total
    pos_grad_ref[...] += jnp.sum(total.reshape(-1, 8, 768), axis=0)

    @pl.when(step == blocks - 1)
    def _():
        me = info[1]
        own = pl.ds(pl.multiple_of(me * 16, 16), 16)
        own_ref[...] = result[own, :]
        own_grad_ref[...] = heads_grad[own, :]

        def chosen(left, rows):
            width = left.shape[1]
            wanted = lax.broadcasted_iota(jnp.int32, (rows, width), 1) - lax.broadcasted_iota(
                jnp.int32, (rows, width), 0
            )
            pick = (wanted == me * rows).astype(F32).astype(LOW)
            return mm_nt(pick, left).astype(LOW)

        left = chosen(lefts[0], 24)
        for j in range(3):
            qkv_grad_ref[:, j * 768 : (j + 1) * 768] = mm(left, rights[2 + j])
        out_grad_ref[...] = mm(chosen(lefts[1], 24), rights[0])
        left = chosen(lefts[2], 24)
        for j in range(4):
            cols = slice(j * 768, (j + 1) * 768)
            up_grad_ref[:, cols] = mm(left, hidden_grad[:, cols])
        down_grad_ref[...] = mm(chosen(act[...], 96), rights[1])


def column_sum(value):
    return jnp.sum(value.astype(F32), axis=0, keepdims=True)


def ffn_backward_kernel(segs, seg_count, info, cot_ref, heads_grad_ref, heads_ref, second_ref, sum_ref, slope_ref, vec_ref, *rest):
    pieces, rest = rest[:10], rest[10:]
    (out_ref, down_grad_ref, hidden_grad_ref, proj_grad_ref, mixed_grad_ref, grads_ref, out, up, down, sems) = rest
    step = pl.program_id(0)

    @pl.when(step == 0)
    def _():
        load_slabs(info[0], pieces, rest_slabs(out, up, down), sems)
        grads_ref[...] = jnp.zeros_like(grads_ref)

    count = segs * SEG
    normed, inv_scale = normalize(second_ref[...])
    row = lax.broadcasted_iota(jnp.int32, (SEG, 1), 0)
    result = normed * (1.0 + vec_ref[10:11, :]) + vec_ref[11:12, :]
    ups = []
    for s in range(segs):
        seg = step * segs + s
        at = slice(s * SEG, (s + 1) * SEG)
        live = row + seg % seg_count * SEG < info[1 + seg // seg_count]
        opens = row == 0
        merged = jnp.where(opens, heads_ref[s : s + 1, :], result[at])
        out_ref[at, :] = jnp.where(live, merged, 0.0).astype(LOW)
        grad = jnp.where(live, cot_ref[at, :].astype(F32), 0.0)
        ups.append(jnp.where(opens, heads_grad_ref[s : s + 1, :], grad))
    upstream = jnp.concatenate(ups, axis=0)
    back_two = normalize_back(upstream * (1.0 + vec_ref[10:11, :]), normed, inv_scale)
    down_grad = back_two.astype(LOW)
    down_grad_ref[...] = down_grad
    grads_ref[9:10, :] += column_sum(down_grad)
    grads_ref[10:11, :] += column_sum(upstream * normed)
    grads_ref[11:12, :] += column_sum(upstream)
    total = back_two
    for j in range(4):
        cols = slice(j * 768, (j + 1) * 768)
        grad = mm_nt(down_grad, down[cols, :]) * slope_ref[:, cols].astype(F32)
        grad = grad.astype(LOW)
        hidden_grad_ref[:, cols] = grad
        grads_ref[5 + j : 6 + j, :] += column_sum(grad)
        total = total + mm_nt(grad, up[j])
    normed, inv_scale = normalize(sum_ref[...])
    back_one = normalize_back(total * (1.0 + vec_ref[3:4, :]), normed, inv_scale)
    proj_grad = back_one.astype(LOW)
    proj_grad_ref[...] = proj_grad
    mixed_grad_ref[...] = mm_nt(proj_grad, out[...]).astype(LOW)
    grads_ref[2:3, :] += column_sum(proj_grad)
    grads_ref[3:4, :] += column_sum(total * normed)
    grads_ref[4:5, :] += column_sum(total)


def attn_backward_kernel(segs, seg_count, info, packed_ref, mixed_grad_ref, packed_grad_ref, grads_ref):
    step = pl.program_id(0)

    @pl.when(step == 0)
    def _():
        grads_ref[...] = jnp.zeros_like(grads_ref)

    for s in range(segs):
        seg = step * segs + s
        allowed = segment_mask(info[1 + seg // seg_count], seg % seg_count)
        at = slice(s * SEG, (s + 1) * SEG)
        for h in range(6):
            cols = [slice(j * 768 + h * 128, j * 768 + (h + 1) * 128) for j in range(3)]
            q, k, v = (packed_ref[at, c] for c in cols)
            grads = attend_back(q, k, v, mixed_grad_ref[at, cols[0]], allowed)
            for c, g in zip(cols, grads):
                packed_grad_ref[at, c] = g.astype(LOW)
    grads_ref[0:1, :] += column_sum(packed_grad_ref[:, :768])
    grads_ref[1:2, :] += column_sum(packed_grad_ref[:, 1536:])


def token_grad_kernel(info, packed_grad_ref, proj_grad_ref, *rest):
    pieces, (token_grad_ref, qkv, sems) = rest[:10], rest[10:]

    @pl.when(pl.program_id(0) == 0)
    def _():
        load_slabs(info[0], pieces, qkv_slabs(qkv), sems)

    total = proj_grad_ref[...].astype(F32)
    for j in range(3):
        total = total + mm_nt(packed_grad_ref[:, j * 768 : (j + 1) * 768], qkv[j])
    token_grad_ref[...] = total.astype(LOW)


def weight_grad_kernel(rows, info, left_ref, right_ref, keep_ref, send_ref, total):
    total[...] = mm_tn(left_ref[...], right_ref[...])
    for mask in range(8):
        block = pl.multiple_of((info[0] ^ mask) * rows, rows)
        target = send_ref if mask % 2 else keep_ref
        target[mask // 2] = total[pl.ds(block, rows), :].astype(LOW)


ANY = pl.BlockSpec(memory_space=pl.ANY)
SMEM = pl.BlockSpec(memory_space=pltpu.SMEM)


def block_rows(count, width):
    return pl.BlockSpec((count, width), lambda i: (i, 0))


def fixed(shape):
    return pl.BlockSpec(shape, lambda i: (0,) * len(shape))


def shape_of(dims, kind=LOW):
    return jax.ShapeDtypeStruct(dims, kind)


def params():
    return pltpu.CompilerParams(vmem_limit_bytes=VMEM, dimension_semantics=("arbitrary",))


def qkv_weights():
    return [pltpu.VMEM((3, 768, 768), LOW)], [pltpu.SemaphoreType.DMA((24,))]


def rest_weights():
    weights = [pltpu.VMEM((768, 768), LOW), pltpu.VMEM((4, 768, 768), LOW), pltpu.VMEM((3072, 768), LOW)]
    return weights, [pltpu.SemaphoreType.DMA((72,))]


def cost(flops, size, exps=0):
    return pl.CostEstimate(flops=flops, bytes_accessed=size, transcendentals=exps)


def attn_forward(info, rows_in, vec, pieces, seg_count, segs=2):
    rows = rows_in.shape[0]
    count = segs * SEG
    weights, sems = qkv_weights()
    return pl.pallas_call(
        functools.partial(attn_forward_kernel, segs, seg_count),
        grid=(rows // count,),
        in_specs=[SMEM, block_rows(count, 768), fixed((12, 768))] + [ANY] * 10,
        out_specs=[block_rows(count, 2304), block_rows(count, 768)],
        out_shape=[shape_of((rows, 2304)), shape_of((rows, 768))],
        scratch_shapes=weights + sems,
        compiler_params=params(),
        cost_estimate=cost(2 * rows * 768 * 8000, rows * 768 * 16),
        name="attn_forward",
    )(info, rows_in, vec, *pieces)


def ffn_forward(info, rows_in, mixed, vec, pieces, segs=2):
    rows = rows_in.shape[0]
    count = segs * SEG
    weights, sems = rest_weights()
    few = pl.BlockSpec((None, segs, 768), lambda i: (i, 0, 0))
    return pl.pallas_call(
        functools.partial(ffn_forward_kernel, segs),
        grid=(rows // count,),
        in_specs=[SMEM, block_rows(count, 768), block_rows(count, 768), fixed((12, 768))] + [ANY] * 10,
        out_specs=[block_rows(count, 768), block_rows(count, 768), block_rows(count, 3072), block_rows(count, 3072),
                   block_rows(count, 768), few],
        out_shape=[shape_of((rows, 768), F32), shape_of((rows, 768)), shape_of((rows, 3072)), shape_of((rows, 3072)),
                   shape_of((rows, 768), F32), shape_of((rows // count, segs, 768), F32)],
        scratch_shapes=weights + sems,
        compiler_params=params(),
        cost_estimate=cost(2 * rows * 768 * 14000, rows * 768 * 30),
        name="ffn_forward",
    )(info, rows_in, mixed, vec, *pieces)


def cross_whole(info, heads, upstream, live, vec, positions, pieces):
    rows = heads.shape[0]
    count = 2 * SEG
    weights = qkv_weights()[0] + rest_weights()[0]
    own = [(16, 768), (16, 768), (12, 768), (8, 768), (24, 2304), (24, 768), (24, 3072), (96, 768)]
    return pl.pallas_call(
        functools.partial(cross_kernel, rows // count),
        grid=(rows // count,),
        in_specs=[SMEM, block_rows(count, 768), block_rows(count, 768),
                  pl.BlockSpec((None, 2, SEG), lambda i: (i, 0, 0)), fixed((12, 768)), fixed((8, 768))] + [ANY] * 10,
        out_specs=[fixed(dims) for dims in own],
        out_shape=[shape_of(dims, F32) for dims in own],
        scratch_shapes=weights + [pltpu.SemaphoreType.DMA((96,))] + [
            pltpu.VMEM((rows, 768), F32), pltpu.VMEM((rows, 768), F32), pltpu.VMEM((count, 3072), LOW),
            pltpu.VMEM((3, rows, 768), LOW), pltpu.VMEM((rows, 3072), LOW), pltpu.VMEM((count, 2304), LOW),
            pltpu.VMEM((5, rows, 768), LOW), pltpu.VMEM((rows, 3072), LOW),
        ],
        compiler_params=params(),
        cost_estimate=cost(2 * rows * 768 * 30000, 2**24),
        name="cross_encoder",
    )(info, heads, upstream, live, vec, positions, *pieces)


def ffn_backward(info, cotangent, heads_grad, heads, second, summed, slope, vec, pieces, seg_count, segs=2):
    rows = summed.shape[0]
    count = segs * SEG
    few = pl.BlockSpec((None, segs, 768), lambda i: (i, 0, 0))
    weights, sems = rest_weights()
    return pl.pallas_call(
        functools.partial(ffn_backward_kernel, segs, seg_count),
        grid=(rows // count,),
        in_specs=[SMEM, block_rows(count, 768), few, few, block_rows(count, 768), block_rows(count, 768),
                  block_rows(count, 3072), fixed((12, 768))] + [ANY] * 10,
        out_specs=[block_rows(count, 768), block_rows(count, 768), block_rows(count, 3072), block_rows(count, 768),
                   block_rows(count, 768), fixed((12, 768))],
        out_shape=[shape_of((rows, 768)), shape_of((rows, 768)), shape_of((rows, 3072)), shape_of((rows, 768)),
                   shape_of((rows, 768)), shape_of((12, 768), F32)],
        scratch_shapes=weights + sems,
        compiler_params=params(),
        cost_estimate=cost(2 * rows * 768 * 14000, rows * 768 * 30),
        name="ffn_backward",
    )(info, cotangent, heads_grad.reshape(-1, segs, 768), heads.reshape(-1, segs, 768), second, summed, slope, vec, *pieces)


def attn_backward(info, packed, mixed_grad, seg_count, segs=2):
    rows = packed.shape[0]
    count = segs * SEG
    return pl.pallas_call(
        functools.partial(attn_backward_kernel, segs, seg_count),
        grid=(rows // count,),
        in_specs=[SMEM, block_rows(count, 2304), block_rows(count, 768)],
        out_specs=[block_rows(count, 2304), fixed((2, 768))],
        out_shape=[shape_of((rows, 2304)), shape_of((2, 768), F32)],
        compiler_params=params(),
        cost_estimate=cost(2 * rows * 768 * 16000, rows * 768 * 16),
        name="attn_backward",
    )(info, packed, mixed_grad)


def token_gradient(info, packed_grad, proj_grad, pieces, count=256):
    rows = packed_grad.shape[0]
    weights, sems = qkv_weights()
    return pl.pallas_call(
        token_grad_kernel,
        grid=(rows // count,),
        in_specs=[SMEM, block_rows(count, 2304), block_rows(count, 768)] + [ANY] * 10,
        out_specs=block_rows(count, 768),
        out_shape=shape_of((rows, 768)),
        scratch_shapes=weights + sems,
        compiler_params=params(),
        cost_estimate=cost(2 * rows * 768 * 3000, rows * 768 * 10),
        name="token_gradient",
    )(info, packed_grad, proj_grad, *pieces)


def weight_grad(info, left, right):
    rows, wide = right.shape
    tiles = wide // 768
    moving = pl.BlockSpec((rows, 768), lambda i: (0, i))
    still = fixed((rows, 768))
    out = pl.BlockSpec((4, 96, 768), lambda i: (0, 0, i))
    return pl.pallas_call(
        functools.partial(weight_grad_kernel, 96),
        grid=(tiles,),
        in_specs=[SMEM, still, moving],
        out_specs=[out, out],
        out_shape=[shape_of((4, 96, wide))] * 2,
        scratch_shapes=[pltpu.VMEM((768, 768), F32)],
        compiler_params=params(),
        cost_estimate=cost(2 * rows * 768 * wide, rows * wide * 2),
        name="weight_grad",
    )(info, left, right)


def down_grad_kernel(info, left_ref, right_ref, keep_ref, send_ref, total):
    step = pl.program_id(0)
    total[pl.ds(pl.multiple_of(step * 768, 768), 768), :] = mm_tn(left_ref[...], right_ref[...]).astype(LOW)

    @pl.when(step == pl.num_programs(0) - 1)
    def _():
        for mask in range(8):
            block = pl.multiple_of((info[0] ^ mask) * 384, 384)
            target = send_ref if mask % 2 else keep_ref
            target[mask // 2] = total[pl.ds(block, 384), :]


def down_weight_grad(info, left, right):
    rows, wide = left.shape
    return pl.pallas_call(
        down_grad_kernel,
        grid=(wide // 768,),
        in_specs=[SMEM, pl.BlockSpec((rows, 768), lambda i: (0, i)), fixed((rows, 768))],
        out_specs=[fixed((4, 384, 768))] * 2,
        out_shape=[shape_of((4, 384, 768))] * 2,
        scratch_shapes=[pltpu.VMEM((3072, 768), LOW)],
        compiler_params=params(),
        cost_estimate=cost(2 * rows * 768 * wide, rows * wide * 2),
        name="down_weight_grad",
    )(info, left, right)


def matmul(left_op, right_op):
    return jnp.dot(left_op, right_op, preferred_element_type=jnp.float32)


def trans_left(left_op, right_op):
    return lax.dot_general(
        left_op, right_op, (((0,), (0,)), ((), ())), preferred_element_type=jnp.float32
    )


def trans_right(left_op, right_op):
    return lax.dot_general(
        left_op, right_op, (((1,), (1,)), ((), ())), preferred_element_type=jnp.float32
    )


def norm_forward(summed, gain_row, shift_row):
    average = jnp.mean(summed, axis=-1, keepdims=True)
    centered = summed - average
    inv_scale = lax.rsqrt(jnp.mean(centered * centered, axis=-1, keepdims=True) + NORM_EPS)
    normed = centered * inv_scale
    return (normed * (1.0 + gain_row) + shift_row, normed, inv_scale)


def norm_backward(upstream, normed, inv_scale, gain_row):
    inner = upstream * (1.0 + gain_row)
    back_grad = inv_scale * (
        inner
        - jnp.mean(inner, axis=-1, keepdims=True)
        - normed * jnp.mean(inner * normed, axis=-1, keepdims=True)
    )
    return (back_grad, jnp.sum(upstream * normed, axis=0), jnp.sum(upstream, axis=0))


def gelu_slope(hidden):
    return (
        0.5 * (1.0 + lax.erf(hidden * ROOT_HALF))
        + hidden * jnp.exp(-0.5 * hidden * hidden) * INV_ROOT_TAU
    )


def split_heads(packed, group_len):
    head_count = packed.shape[1] // (3 * HEAD)
    return [
        portion.reshape(-1, group_len, head_count, HEAD) for portion in jnp.split(packed, 3, axis=1)
    ]


def masked_scores(query_heads, key_heads, allowed):
    raw_scores = jnp.einsum(
        "nqhd,nkhd->nhqk", query_heads, key_heads, preferred_element_type=jnp.float32
    ) * HEAD ** (-0.5)
    return jnp.where(allowed[:, None, None, :], raw_scores, MASK_FILL)


def encode(inputs, inputs_low, weights, allowed):
    qkv_w, out_w, up_w, down_w, vectors = weights
    row_count, feat_dim = inputs_low.shape
    group_len = allowed.shape[1]
    qkv_bias = jnp.concatenate([vectors[0], jnp.zeros_like(vectors[0]), vectors[1]])
    packed = (matmul(inputs_low, qkv_w) + qkv_bias).astype(jnp.bfloat16)
    query_heads, key_heads, value_heads = split_heads(packed, group_len)
    scores = masked_scores(query_heads, key_heads, allowed)
    row_max = jnp.max(scores, axis=-1, keepdims=True)
    expo_vals = jnp.exp(scores - row_max)
    row_total = jnp.sum(expo_vals, axis=-1, keepdims=True)
    log_total = row_max + jnp.log(row_total)
    prob_low = (expo_vals / row_total).astype(jnp.bfloat16)
    mixed = jnp.einsum("nhqk,nkhd->nqhd", prob_low, value_heads, preferred_element_type=jnp.float32)
    mixed = mixed.reshape(row_count, feat_dim).astype(jnp.bfloat16)
    projected = matmul(mixed, out_w) + vectors[2]
    first_out, normed_one, scale_one = norm_forward(inputs + projected, vectors[3], vectors[4])
    first_low = first_out.astype(jnp.bfloat16)
    hidden = matmul(first_low, up_w) + vectors[5:-3].reshape(-1)
    activated = jax.nn.gelu(hidden, approximate=False).astype(jnp.bfloat16)
    down_out = matmul(activated, down_w) + vectors[-3]
    result, normed_two, scale_two = norm_forward(first_out + down_out, vectors[-2], vectors[-1])
    return (
        result,
        (
            packed,
            log_total,
            mixed,
            normed_one,
            scale_one,
            first_low,
            hidden,
            activated,
            normed_two,
            scale_two,
        ),
    )


def encode_back(upstream, inputs_low, weights, allowed, kept):
    qkv_w, out_w, up_w, down_w, vectors = weights
    (
        packed,
        log_total,
        mixed,
        normed_one,
        scale_one,
        first_low,
        hidden,
        activated,
        normed_two,
        scale_two,
    ) = kept
    row_count, feat_dim = inputs_low.shape
    group_len = allowed.shape[1]
    back_two, gain_two, shift_two = norm_backward(upstream, normed_two, scale_two, vectors[-2])
    down_grad = back_two.astype(jnp.bfloat16)
    hidden_grad = (trans_right(down_grad, down_w) * gelu_slope(hidden)).astype(jnp.bfloat16)
    first_grad = trans_right(hidden_grad, up_w) + back_two
    back_one, gain_one, shift_one = norm_backward(first_grad, normed_one, scale_one, vectors[3])
    proj_grad = back_one.astype(jnp.bfloat16)
    query_heads, key_heads, value_heads = split_heads(packed, group_len)
    mixed_grad = trans_right(proj_grad, out_w).astype(jnp.bfloat16).reshape(value_heads.shape)
    scores = masked_scores(query_heads, key_heads, allowed)
    prob_vals = jnp.exp(scores - log_total)
    grad_values = jnp.einsum(
        "nhqk,nqhd->nkhd",
        prob_vals.astype(jnp.bfloat16),
        mixed_grad,
        preferred_element_type=jnp.float32,
    )
    grad_prob = jnp.einsum(
        "nqhd,nkhd->nhqk", mixed_grad, value_heads, preferred_element_type=jnp.float32
    )
    score_grad = (
        prob_vals * (grad_prob - jnp.sum(prob_vals * grad_prob, axis=-1, keepdims=True))
    ).astype(jnp.bfloat16)
    grad_query = jnp.einsum(
        "nhqk,nkhd->nqhd", score_grad, key_heads, preferred_element_type=jnp.float32
    ) * HEAD ** (-0.5)
    grad_keys = jnp.einsum(
        "nhqk,nqhd->nkhd", score_grad, query_heads, preferred_element_type=jnp.float32
    ) * HEAD ** (-0.5)
    packed_grad = jnp.concatenate(
        [
            grad_query.reshape(row_count, feat_dim),
            grad_keys.reshape(row_count, feat_dim),
            grad_values.reshape(row_count, feat_dim),
        ],
        axis=1,
    ).astype(jnp.bfloat16)
    bias_grads = jnp.sum(packed_grad, axis=0, dtype=jnp.float32).reshape(3, feat_dim)
    grad_inputs = trans_right(packed_grad, qkv_w) + back_one
    grad_vectors = jnp.concatenate(
        [
            bias_grads[0:1],
            bias_grads[2:3],
            jnp.sum(proj_grad, axis=0, dtype=jnp.float32)[None],
            gain_one[None],
            shift_one[None],
            jnp.sum(hidden_grad, axis=0, dtype=jnp.float32).reshape(-1, feat_dim),
            jnp.sum(down_grad, axis=0, dtype=jnp.float32)[None],
            gain_two[None],
            shift_two[None],
        ],
        axis=0,
    )
    pairs = (
        (inputs_low, packed_grad),
        (mixed, proj_grad),
        (first_low, hidden_grad),
        (activated, down_grad),
    )
    return (grad_inputs, pairs, grad_vectors)


class Links:
    def __init__(self, outer, inner):
        self.outer, self.inner = outer, inner
        self.order = self.place = lax.axis_index("dp")
        self.z = lax.axis_index("fsdp")

    def flip(self, value, mask):
        pairs = [
            (d * self.inner + z, (d ^ mask) * self.inner + z)
            for d in range(self.outer)
            for z in range(self.inner)
        ]
        return lax.ppermute(value, AXES, pairs)

    def turn(self, value, step):
        pairs = [
            (d * self.inner + z, d * self.inner + (z + step) % self.inner)
            for d in range(self.outer)
            for z in range(self.inner)
        ]
        return lax.ppermute(value, AXES, pairs)

    def gather_z(self, shard):
        came = [shard] + [self.turn(shard, step) for step in range(1, self.inner)]
        whole = []
        for z in range(self.inner):
            part = came[-1]
            for step in range(self.inner - 1):
                part = jnp.where(self.z == (z + step) % self.inner, came[step], part)
            whole.append(part)
        return whole

    def spread_near(self, block):
        return self.flip(block, 2), self.flip(block, 4)

    def spread_far(self, by_x, by_y):
        half = by_x.shape[0] // 2
        return self.flip(by_y[:half], 2), self.flip(by_x[half:], 4)

    def spread_core(self, mine):
        return list(mine) + [self.flip(piece, 1) for piece in mine]

    def gather_small(self, shard):
        block = jnp.stack(self.gather_z(shard))
        near = [block] + [self.flip(block, m) for m in (2, 4, 6)]
        near = [lax.select(self.place // 2 % 2 == 0, jnp.stack(p), jnp.stack(p[::-1])) for p in (near[:2], near[2:])]
        plane = lax.select(self.place // 4 == 0, jnp.stack(near), jnp.stack(near[::-1]))
        other = self.flip(plane, 1)
        both = [jnp.stack(p, axis=2) for p in ((plane, other), (other, plane))]
        return lax.select(self.place % 2 == 0, *both).reshape((-1,) + shard.shape)

    def scatter_sum(self, keep, send, line):
        def add(*terms):
            return sum(t.astype(F32) for t in terms).astype(LOW)

        def pick(array, index):
            return lax.dynamic_index_in_dim(array, index, 0, keepdims=False)

        came = self.flip(send, 1)
        to_d = line(add(keep[3], came[3]))
        half = self.inner // 2
        came_x, came_y = self.flip(to_d[:half], 2), self.flip(to_d[half:], 4)
        to_x, to_y = line(add(keep[1], came[1])), line(add(keep[2], came[2]))
        to_y = jnp.concatenate([add(to_y[:half], came_x), to_y[half:]])
        to_x = jnp.concatenate([to_x[:half], add(to_x[half:], came_y)])
        own = add(line(keep[0]), line(came[0]), self.flip(to_x, 2), self.flip(to_y, 4))
        total = pick(own, self.z).astype(F32)
        for step in range(1, self.inner):
            total = total + self.turn(pick(own, (self.z + step) % self.inner), step).astype(F32)
        return total


class PlainLinks:
    def __init__(self, outer, inner):
        self.outer, self.inner = outer, inner
        self.order = lax.axis_index("dp")
        self.z = lax.axis_index("fsdp")
        self.place = 0

    def gather_small(self, shard):
        return lax.all_gather(shard, AXES, axis=0)

    def whole(self, matrix):
        return lax.all_gather(matrix, AXES, axis=0, tiled=True)

    def scatter_sum(self, keep, send, line):
        flat = jnp.stack([keep, send], axis=1).reshape(-1, keep.shape[-1])
        return lax.psum_scatter(flat, AXES, scatter_dimension=0, tiled=True).astype(F32)


def after(value, *earlier):
    return lax.optimization_barrier((value, *earlier))[0]


def slabs_of(matrix):
    rows, wide = matrix.shape
    return matrix.reshape(rows, wide // 768, 768).transpose(1, 0, 2)


def line_block(parts, down_rows):
    wide = jnp.stack([p[: p.shape[0] - down_rows // 24] for p in parts], axis=1)
    wide = wide.reshape(wide.shape[0], -1, 768)
    if not down_rows:
        return wide
    tall = jnp.stack([p[p.shape[0] - down_rows // 24 :].reshape(down_rows, 768) for p in parts])
    return jnp.concatenate([wide, tall.reshape(-1, 96, 768)])


def gather_weights(links, seg, cross):
    if isinstance(links, PlainLinks):

        def pieces(slabs, tall=None):
            parts = []
            for mask in (0, 2, 4, 6, 1, 3, 5, 7):
                part = slabs[:, mask * 96 : (mask + 1) * 96]
                if tall is not None:
                    part = jnp.concatenate([part, tall[mask * 384 : (mask + 1) * 384].reshape(4, 96, 768)])
                half = part.shape[0] // 2
                parts += [part[:half], part[half:]] if mask > 5 else [part]
            return parts

        qkv, out, up, down = (links.whole(m) for m in seg)
        rest = jnp.concatenate([slabs_of(out), slabs_of(up)])
        return pieces(slabs_of(qkv)), pieces(rest, down), [links.whole(m) for m in cross]
    first = slabs_of(seg[0])
    rest = jnp.concatenate([slabs_of(m) for m in seg[1:3]] + [seg[3].reshape(4, 24, 768)])
    other = jnp.concatenate([slabs_of(m) for m in cross[:3]] + [cross[3].reshape(4, 24, 768)])
    line_first = links.gather_z(first)
    line_rest = links.gather_z(after(rest, *line_first))
    line_other = links.gather_z(after(other, *line_rest))
    block = line_block(line_first, 0)
    near = links.spread_near(block)
    far = links.spread_far(*near)
    first = links.spread_core([block, *near, *far])
    block = after(line_block(line_rest, 96), *far)
    near = links.spread_near(block)
    far = links.spread_far(*near)
    rest = links.spread_core([block, *near, *far])
    block = after(line_block(line_other, 96), *far)
    near = links.spread_near(block)
    far = links.spread_far(*near)
    other = links.spread_core([block, *near, *far])
    return first, rest, other


def shards(
    outer,
    inner,
    tokens,
    cotangent,
    lengths,
    seg_qkv,
    seg_out,
    seg_up,
    seg_down,
    seg_vec,
    cross_qkv,
    cross_out,
    cross_up,
    cross_down,
    cross_vec,
    positions,
):
    fast = (outer, inner) == (8, 4)
    links = (Links if fast else PlainLinks)(outer, inner)
    devices = outer * inner
    me = links.order * inner + links.z
    seq_local, seq_len, feat_dim = tokens.shape
    seg_count = seq_len // SEG
    seg_rows, cross_rows = seg_vec.shape[0], cross_vec.shape[0]
    width = feat_dim // devices
    my_lengths = lax.dynamic_slice_in_dim(lengths, me * seq_local, seq_local)
    info = jnp.concatenate([jnp.full((1,), links.place, jnp.int32), my_lengths])
    small = jnp.concatenate([seg_vec, cross_vec, positions]).reshape(1, -1)
    small = links.gather_small(small).reshape(devices, -1, width)
    small = small.transpose(1, 0, 2).reshape(-1, feat_dim).astype(F32)
    seg_v, cross_v = small[:seg_rows], small[seg_rows : seg_rows + cross_rows]
    pos_table = small[seg_rows + cross_rows :]
    first, rest, other = gather_weights(
        links,
        (seg_qkv, seg_out, seg_up, seg_down),
        (cross_qkv, cross_out, cross_up, cross_down),
    )
    rows_in = tokens.reshape(-1, feat_dim)
    cot_rows = cotangent.reshape(-1, feat_dim)
    seg_starts = jnp.arange(seg_count) * SEG
    live_own = (seg_starts[None, :] < my_lengths[:, None]).reshape(-1, 1)
    up_own = jnp.where(live_own, cotangent.reshape(-1, SEG, feat_dim)[:, 0, :], 0)
    up_all = links.gather_small(up_own).reshape(-1, feat_dim)

    packed, mixed = attn_forward(info, rows_in, seg_v, first, seg_count)
    summed, low, act, slope, second, heads = ffn_forward(info, rows_in, mixed, seg_v, rest)
    heads_own = heads.reshape(-1, feat_dim)
    heads_all = links.gather_small(heads_own.astype(LOW)).reshape(-1, feat_dim)
    live_all = seg_starts[None, :] < lengths[:, None]
    if fast:
        cross_info = jnp.stack([links.place, me]).astype(jnp.int32)
        live = live_all.astype(F32).reshape(-1, 2, SEG)
        cross_own, heads_grad, vec_grad, pos_grad, *cross_grads = cross_whole(
            cross_info, heads_all, up_all, live, cross_v, pos_table, other
        )
    else:
        weights = (*other, cross_v)
        heads_in = heads_all.astype(F32).reshape(-1, seg_count, feat_dim) + pos_table[None]
        heads_in = heads_in.reshape(-1, feat_dim)
        cross_result, kept = encode(heads_in, heads_in.astype(LOW), weights, live_all)
        all_grad, pairs, vec_grad = encode_back(
            up_all.astype(F32), heads_in.astype(LOW), weights, live_all, kept
        )
        cross_grads = []
        for left, right in pairs:
            count = left.shape[1] // devices
            mine = lax.dynamic_slice_in_dim(left, me * count, count, 1)
            cross_grads.append(trans_left(mine, right))
        pos_grad = jnp.sum(all_grad.reshape(-1, seg_count, feat_dim), axis=0)
        own = seq_local * seg_count
        cross_own = lax.dynamic_slice_in_dim(cross_result, me * own, own)
        heads_grad = lax.dynamic_slice_in_dim(all_grad, me * own, own)
    cross_vec_grad = lax.dynamic_slice_in_dim(vec_grad, me * width, width, 1)
    grad_positions = lax.dynamic_slice_in_dim(pos_grad, me * width, width, 1)

    layer_out, down_grad, hidden_grad, proj_grad, mixed_grad, grads_two = ffn_backward(
        info, cot_rows, heads_grad, cross_own, second, summed, slope, seg_v, rest, seg_count
    )
    down_parts = down_weight_grad(info, act, down_grad)
    up_parts = weight_grad(info, low, after(hidden_grad, down_parts[1]))
    out_parts = weight_grad(info, mixed, after(proj_grad, up_parts[1]))
    packed_grad, grads_one = attn_backward(info, packed, after(mixed_grad, out_parts[1]), seg_count)
    qkv_parts = weight_grad(info, rows_in, packed_grad)
    token_grad = token_gradient(info, after(packed_grad, qkv_parts[1]), proj_grad, first)

    def by_rows(part):
        return part.reshape(inner, -1, part.shape[-1])

    grad_down = links.scatter_sum(*down_parts, by_rows)
    grad_up = links.scatter_sum(*up_parts, by_rows)
    grad_out = links.scatter_sum(*out_parts, by_rows)
    grad_qkv = links.scatter_sum(*qkv_parts, by_rows)
    vec_parts = jnp.concatenate([grads_one, grads_two[2:]]).reshape(seg_rows, devices, width)
    vec_parts = vec_parts.transpose(1, 0, 2).reshape(outer, inner, seg_rows * width).astype(LOW)
    if fast:
        flipped = [lax.dynamic_index_in_dim(vec_parts, links.place ^ m, 0, keepdims=False) for m in range(8)]
        keep, send = jnp.stack(flipped[::2]), jnp.stack(flipped[1::2])
    else:
        keep, send = vec_parts[::2], vec_parts[1::2]
    grad_vec = links.scatter_sum(keep, send, by_rows).reshape(seg_rows, width)
    return (
        layer_out.reshape(tokens.shape),
        token_grad.reshape(tokens.shape),
        grad_qkv,
        grad_out,
        grad_up,
        grad_down,
        grad_vec,
        *cross_grads,
        cross_vec_grad,
        grad_positions,
    )


def solution(mesh):
    in_specs = (
        P(("dp", "fsdp"), None, None),
        P(("dp", "fsdp"), None, None),
        P(),
        P(("dp", "fsdp"), None),
        P(("dp", "fsdp"), None),
        P(("dp", "fsdp"), None),
        P(("dp", "fsdp"), None),
        P(None, ("dp", "fsdp")),
        P(("dp", "fsdp"), None),
        P(("dp", "fsdp"), None),
        P(("dp", "fsdp"), None),
        P(("dp", "fsdp"), None),
        P(None, ("dp", "fsdp")),
        P(None, ("dp", "fsdp")),
    )
    out_specs = (
        P(("dp", "fsdp"), None, None),
        P(("dp", "fsdp"), None, None),
        P(("dp", "fsdp"), None),
        P(("dp", "fsdp"), None),
        P(("dp", "fsdp"), None),
        P(("dp", "fsdp"), None),
        P(None, ("dp", "fsdp")),
        P(("dp", "fsdp"), None),
        P(("dp", "fsdp"), None),
        P(("dp", "fsdp"), None),
        P(("dp", "fsdp"), None),
        P(None, ("dp", "fsdp")),
        P(None, ("dp", "fsdp")),
    )
    return jax.shard_map(
        functools.partial(shards, mesh.shape["dp"], mesh.shape["fsdp"]),
        mesh=mesh, in_specs=in_specs, out_specs=out_specs, check_vma=False)
```

```python
import functools

import jax
import jax.numpy as jnp
from jax import lax
from jax.experimental import pallas as pl
from jax.experimental.pallas import tpu as pltpu
from jax.sharding import PartitionSpec as P

HEAD = 64
SEG = 128
NORM_EPS = 1e-05
MASK_FILL = -1000000000.0
VMEM = 60 * 2**20
F32, LOW = jnp.float32, jnp.bfloat16


ROOT_HALF = 0.7071067811865476
INV_ROOT_TAU = 0.3989422804014327
AXES = ("dp", "fsdp")

def mm(left_op, right_op):
    return jnp.dot(left_op, right_op, preferred_element_type=F32)


def mm_nt(left_op, right_op):
    return lax.dot_general(left_op, right_op, (((1,), (1,)), ((), ())), preferred_element_type=F32)


def mm_tn(left_op, right_op):
    return lax.dot_general(left_op, right_op, (((0,), (0,)), ((), ())), preferred_element_type=F32)


def normalize(summed):
    average = jnp.mean(summed, axis=-1, keepdims=True)
    centered = summed - average
    inv_scale = lax.rsqrt(jnp.mean(centered * centered, axis=-1, keepdims=True) + NORM_EPS)
    return centered * inv_scale, inv_scale


def normalize_back(inner, normed, inv_scale):
    return inv_scale * (
        inner
        - jnp.mean(inner, axis=-1, keepdims=True)
        - normed * jnp.mean(inner * normed, axis=-1, keepdims=True)
    )


def gelu_parts(hidden):
    phi = 0.5 * (1.0 + lax.erf(hidden * ROOT_HALF))
    return hidden * phi, phi + hidden * jnp.exp(-0.5 * hidden * hidden) * INV_ROOT_TAU


def pair_stack(pair, low_half):
    zero = jnp.zeros_like(pair)
    return jnp.concatenate(
        [jnp.where(low_half, pair, zero), jnp.where(low_half, zero, pair)], axis=0
    )


def pair_merge(stacked, low_half):
    rows = stacked.shape[0] // 2
    return jnp.where(low_half, stacked[:rows], stacked[rows:])


def pair_probs(stack, keys, allowed):
    scores = jnp.where(allowed, mm_nt(keys, stack), MASK_FILL)
    expo = jnp.exp(scores - jnp.max(scores, axis=0, keepdims=True))
    return expo * (1.0 / jnp.sum(expo, axis=0, keepdims=True))


def attend(query, keys, values, allowed):
    low_half = lax.broadcasted_iota(jnp.int32, query.shape, 1) < HEAD
    stack = pair_stack(query * jnp.asarray(HEAD**-0.5, query.dtype), low_half)
    return pair_merge(mm_tn(pair_probs(stack, keys, allowed).astype(LOW), values), low_half)


def attend_back(query, keys, values, grad_mixed, allowed):
    low_half = lax.broadcasted_iota(jnp.int32, query.shape, 1) < HEAD
    stack = pair_stack(query * jnp.asarray(HEAD**-0.5, query.dtype), low_half)
    probs = pair_probs(stack, keys, allowed)
    grad_stack = pair_stack(grad_mixed, low_half)
    grad_prob = mm_nt(values, grad_stack)
    inner = jnp.sum(probs * grad_prob, axis=0, keepdims=True)
    score_grad = (probs * (grad_prob - inner)).astype(LOW)
    grad_query = pair_merge(mm_tn(score_grad, keys), low_half) * HEAD**-0.5
    return grad_query, mm(score_grad, stack), mm(probs.astype(LOW), grad_stack)


def slab_copies(place, pieces, slabs, sems, first_sem=0):
    count = len(slabs)
    half = (count + 1) // 2
    spans = [(0, 0, count), (2, 0, count), (4, 0, count)]
    spans += [(6, 0, count)] if len(pieces) == 8 else [(6, 0, half), (6, half, count)]
    copies = []
    for flip_c in (0, 1):
        for index, (flip_yx, first, last) in enumerate(spans):
            block = place ^ (flip_yx + flip_c)
            piece = pieces[flip_c * len(spans) + index]
            for slab in range(first, last):
                source = piece.at[pl.ds((slab - first) * 96, 96)]
                sem = sems.at[first_sem + slab * 8 + flip_yx + flip_c]
                copies.append(pltpu.make_async_copy(source, slabs[slab](block), sem))
    return copies


def load(copies):
    for copy in copies:
        copy.start()
    for copy in copies:
        copy.wait()


def rows_of(ref, block, rows=96, slab=None):
    where = pl.ds(pl.multiple_of(block * rows, rows), rows)
    return ref.at[where] if slab is None else ref.at[slab, where]


def down_rows(ref, block, part):
    return ref.at[pl.ds(pl.multiple_of(block * 384 + part * 96, 96), 96)]


def qkv_slabs(qkv):
    return [functools.partial(rows_of, qkv, slab=j) for j in range(3)]


def mid_slabs(out, up):
    return [functools.partial(rows_of, out)] + [functools.partial(rows_of, up, slab=j) for j in range(4)]


def down_slabs(down):
    return [functools.partial(down_rows, down, part=j) for j in range(4)]


def segment_mask(length, seg_in_seq):
    row = lax.broadcasted_iota(jnp.int32, (SEG, 2 * SEG), 0)
    return (row + seg_in_seq * SEG < length) | (row == 0)


def attn_forward_kernel(segs, seg_count, first_step, info, x_ref, vec_ref, *rest):
    pieces, (packed_ref, mixed_ref, qkv, sems) = rest[:10], rest[-4:]
    step = pl.program_id(0)

    @pl.when(step == 0)
    def _():
        load(slab_copies(info[0], pieces, qkv_slabs(qkv), sems))

    rows = x_ref[...]
    for j in range(3):
        part = mm(rows, qkv[j])
        if j != 1:
            part = part + vec_ref[j // 2 : j // 2 + 1, :]
        packed_ref[:, j * 768 : (j + 1) * 768] = part.astype(LOW)
    for s in range(segs):
        seg = (step + first_step) * segs + s
        allowed = segment_mask(info[1 + seg // seg_count], seg % seg_count)
        at = slice(s * SEG, (s + 1) * SEG)
        for h in range(6):
            q, k, v = (packed_ref[at, j * 768 + h * 128 : j * 768 + (h + 1) * 128] for j in range(3))
            mixed_ref[at, h * 128 : (h + 1) * 128] = attend(q, k, v, allowed).astype(LOW)


def norm_one(summed, vec_ref):
    normed, _ = normalize(summed)
    return normed * (1.0 + vec_ref[3:4, :]) + vec_ref[4:5, :]


def mid_forward_kernel(info, x_ref, mixed_ref, vec_ref, *rest):
    pieces, (sum_ref, low_ref, act_ref, slope_ref, out, up, sems) = rest[:10], rest[10:]

    @pl.when(pl.program_id(0) == 0)
    def _():
        load(slab_copies(info[0], pieces, mid_slabs(out, up), sems))

    summed = x_ref[...].astype(F32) + mm(mixed_ref[...], out[...]) + vec_ref[2:3, :]
    sum_ref[...] = summed
    first_low = norm_one(summed, vec_ref).astype(LOW)
    low_ref[...] = first_low
    hidden = mm(first_low, up[0]) + vec_ref[5:6, :]
    for j in range(4):
        later = mm(first_low, up[j + 1]) + vec_ref[6 + j : 7 + j, :] if j < 3 else None
        act, slope = gelu_parts(hidden)
        act_ref[:, j * 768 : (j + 1) * 768] = act.astype(LOW)
        slope_ref[:, j * 768 : (j + 1) * 768] = slope.astype(LOW)
        hidden = later


def down_forward_kernel(segs, info, sum_ref, act_ref, vec_ref, *rest):
    pieces, (second_ref, heads_ref, down, sems) = rest[:8], rest[8:]

    @pl.when(pl.program_id(0) == 0)
    def _():
        load(slab_copies(info[0], pieces, down_slabs(down), sems))

    total = norm_one(sum_ref[...], vec_ref) + vec_ref[9:10, :] + mm(act_ref[...], down[...])
    second_ref[...] = total
    opening = jnp.concatenate([total[s * SEG : s * SEG + 1] for s in range(segs)], axis=0)
    normed, _ = normalize(opening)
    heads_ref[...] = normed * (1.0 + vec_ref[10:11, :]) + vec_ref[11:12, :]


def cross_kernel(blocks, info, heads_ref, up_ref, live_ref, vec_ref, pos_ref, *rest):
    wide, tall, rest = rest[0], rest[1], rest[2:]
    (own_ref, own_grad_ref, grads_ref, pos_grad_ref, qkv_grad_ref, out_grad_ref, up_grad_ref, down_grad_ref) = rest[:8]
    (qkv, out, up, down, sems, result, heads_grad, slope, lefts, act, packed, rights, hidden_grad) = rest[8:]
    step = pl.program_id(0)
    count = heads_ref.shape[0]
    at = pl.ds(pl.multiple_of(step * count, count), count)
    targets = [qkv.at[j] for j in range(3)] + [out] + [up.at[j] for j in range(4)]
    copies = [pltpu.make_async_copy(wide.at[j], t, sems.at[j]) for j, t in enumerate(targets)]
    copies.append(pltpu.make_async_copy(tall, down, sems.at[8]))

    @pl.when(step == 0)
    def _():
        for copy in copies:
            copy.start()
        grads_ref[...] = jnp.zeros_like(grads_ref)
        pos_grad_ref[...] = jnp.zeros_like(pos_grad_ref)
        for copy in copies[:3]:
            copy.wait()

    vec = vec_ref[...]
    inputs = heads_ref[...].astype(F32).reshape(-1, 8, 768) + pos_ref[...][None]
    inputs = inputs.reshape(count, 768)
    low = inputs.astype(LOW)
    lefts[0, at, :] = low
    for j in range(3):
        part = mm(low, qkv[j])
        if j != 1:
            part = part + vec[j // 2 : j // 2 + 1]
        packed[:, j * 768 : (j + 1) * 768] = part.astype(LOW)
    row = lax.broadcasted_iota(jnp.int32, (SEG, 2 * SEG), 0)
    lane = lax.broadcasted_iota(jnp.int32, (SEG, 2 * SEG), 1)
    group = row // 8 == lane % SEG // 8
    masks = []
    for s in range(count // SEG):
        live = live_ref[s * SEG : (s + 1) * SEG, :]
        masks.append(group & (jnp.concatenate([live, live], axis=1) > 0.0))
    for s, allowed in enumerate(masks):
        part = slice(s * SEG, (s + 1) * SEG)
        for h in range(6):
            q, k, v = (packed[part, j * 768 + h * 128 : j * 768 + (h + 1) * 128] for j in range(3))
            where = pl.ds(pl.multiple_of(step * count + s * SEG, SEG), SEG)
            lefts[1, where, h * 128 : (h + 1) * 128] = attend(q, k, v, allowed).astype(LOW)

    @pl.when(step == 0)
    def _():
        for copy in copies[3:]:
            copy.wait()

    summed = inputs + mm(lefts[1, at, :], out[...]) + vec[2:3]
    normed_one, scale_one = normalize(summed)
    first = normed_one * (1.0 + vec[3:4]) + vec[4:5]
    first_low = first.astype(LOW)
    lefts[2, at, :] = first_low
    total = first + vec[9:10]
    for j in range(4):
        cols = slice(j * 768, (j + 1) * 768)
        hidden = mm(first_low, up[j]) + vec[5 + j : 6 + j]
        active, steep = gelu_parts(hidden)
        act[at, cols] = active.astype(LOW)
        slope[:, cols] = steep.astype(LOW)
        total = total + mm(active.astype(LOW), down[cols, :])
    normed, inv_scale = normalize(total)
    result[at, :] = normed * (1.0 + vec[10:11]) + vec[11:12]
    upstream = up_ref[...].astype(F32)
    back_two = normalize_back(upstream * (1.0 + vec[10:11]), normed, inv_scale)
    down_grad = back_two.astype(LOW)
    rights[1, at, :] = down_grad
    grads_ref[9:10, :] += column_sum(down_grad)
    grads_ref[10:11, :] += column_sum(upstream * normed)
    grads_ref[11:12, :] += column_sum(upstream)
    total = back_two
    for j in range(4):
        cols = slice(j * 768, (j + 1) * 768)
        grad = (mm_nt(down_grad, down[cols, :]) * slope[:, cols].astype(F32)).astype(LOW)
        hidden_grad[at, cols] = grad
        grads_ref[5 + j : 6 + j, :] += column_sum(grad)
        total = total + mm_nt(grad, up[j])
    back_one = normalize_back(total * (1.0 + vec[3:4]), normed_one, scale_one)
    proj_grad = back_one.astype(LOW)
    rights[0, at, :] = proj_grad
    grads_ref[2:3, :] += column_sum(proj_grad)
    grads_ref[3:4, :] += column_sum(total * normed_one)
    grads_ref[4:5, :] += column_sum(total)
    mixed_grad = mm_nt(proj_grad, out[...]).astype(LOW)
    for s, allowed in enumerate(masks):
        part = slice(s * SEG, (s + 1) * SEG)
        where = pl.ds(pl.multiple_of(step * count + s * SEG, SEG), SEG)
        for h in range(6):
            cols = slice(h * 128, (h + 1) * 128)
            q, k, v = (packed[part, j * 768 + h * 128 : j * 768 + (h + 1) * 128] for j in range(3))
            for j, g in enumerate(attend_back(q, k, v, mixed_grad[part, cols], allowed)):
                rights[2 + j, where, cols] = g.astype(LOW)
    total = back_one
    for j in range(3):
        part = rights[2 + j, at, :]
        total = total + mm_nt(part, qkv[j])
        if j != 1:
            grads_ref[j // 2 : j // 2 + 1, :] += column_sum(part)
    heads_grad[at, :] = total
    pos_grad_ref[...] += jnp.sum(total.reshape(-1, 8, 768), axis=0)

    @pl.when(step == blocks - 1)
    def _():
        me = info[1]
        own = pl.ds(pl.multiple_of(me * 16, 16), 16)
        own_ref[...] = result[own, :]
        own_grad_ref[...] = heads_grad[own, :]

        def chosen(left, rows):
            width = left.shape[1]
            wanted = lax.broadcasted_iota(jnp.int32, (rows, width), 1) - lax.broadcasted_iota(
                jnp.int32, (rows, width), 0
            )
            pick = (wanted == me * rows).astype(F32).astype(LOW)
            return mm_nt(pick, left).astype(LOW)

        left = chosen(lefts[0], 24)
        for j in range(3):
            qkv_grad_ref[:, j * 768 : (j + 1) * 768] = mm(left, rights[2 + j])
        out_grad_ref[...] = mm(chosen(lefts[1], 24), rights[0])
        left = chosen(lefts[2], 24)
        for j in range(4):
            cols = slice(j * 768, (j + 1) * 768)
            up_grad_ref[:, cols] = mm(left, hidden_grad[:, cols])
        down_grad_ref[...] = mm(chosen(act[...], 96), rights[1])


def column_sum(value):
    return jnp.sum(value.astype(F32), axis=0, keepdims=True)


def ffn_backward_kernel(segs, seg_count, info, cot_ref, heads_grad_ref, heads_ref, second_ref, sum_ref, slope_ref, vec_ref, *rest):
    pieces, more, rest = rest[:10], rest[10:18], rest[18:]
    (out_ref, down_grad_ref, hidden_grad_ref, proj_grad_ref, mixed_grad_ref, grads_ref, out, up, down, sems) = rest
    step = pl.program_id(0)

    @pl.when(step == 0)
    def _():
        copies = slab_copies(info[0], more, down_slabs(down), sems, 40)
        load(copies + slab_copies(info[0], pieces, mid_slabs(out, up), sems))
        grads_ref[...] = jnp.zeros_like(grads_ref)

    count = segs * SEG
    normed, inv_scale = normalize(second_ref[...])
    row = lax.broadcasted_iota(jnp.int32, (SEG, 1), 0)
    result = normed * (1.0 + vec_ref[10:11, :]) + vec_ref[11:12, :]
    ups = []
    for s in range(segs):
        seg = step * segs + s
        at = slice(s * SEG, (s + 1) * SEG)
        live = row + seg % seg_count * SEG < info[1 + seg // seg_count]
        opens = row == 0
        merged = jnp.where(opens, heads_ref[s : s + 1, :], result[at])
        out_ref[at, :] = jnp.where(live, merged, 0.0).astype(LOW)
        grad = jnp.where(live, cot_ref[at, :].astype(F32), 0.0)
        ups.append(jnp.where(opens, heads_grad_ref[s : s + 1, :], grad))
    upstream = jnp.concatenate(ups, axis=0)
    back_two = normalize_back(upstream * (1.0 + vec_ref[10:11, :]), normed, inv_scale)
    down_grad = back_two.astype(LOW)
    down_grad_ref[...] = down_grad
    grads_ref[9:10, :] += column_sum(down_grad)
    grads_ref[10:11, :] += column_sum(upstream * normed)
    grads_ref[11:12, :] += column_sum(upstream)
    total = back_two
    for j in range(4):
        cols = slice(j * 768, (j + 1) * 768)
        grad = mm_nt(down_grad, down[cols, :]) * slope_ref[:, cols].astype(F32)
        grad = grad.astype(LOW)
        hidden_grad_ref[:, cols] = grad
        grads_ref[5 + j : 6 + j, :] += column_sum(grad)
        total = total + mm_nt(grad, up[j])
    normed, inv_scale = normalize(sum_ref[...])
    back_one = normalize_back(total * (1.0 + vec_ref[3:4, :]), normed, inv_scale)
    proj_grad = back_one.astype(LOW)
    proj_grad_ref[...] = proj_grad
    mixed_grad_ref[...] = mm_nt(proj_grad, out[...]).astype(LOW)
    grads_ref[2:3, :] += column_sum(proj_grad)
    grads_ref[3:4, :] += column_sum(total * normed)
    grads_ref[4:5, :] += column_sum(total)


def attn_backward_kernel(segs, seg_count, first_step, info, packed_ref, mixed_grad_ref, *rest):
    packed_grad_ref, grads_ref = rest[-2:]
    step = pl.program_id(0)

    @pl.when(step == 0)
    def _():
        grads_ref[...] = jnp.zeros_like(grads_ref)

    for s in range(segs):
        seg = (step + first_step) * segs + s
        allowed = segment_mask(info[1 + seg // seg_count], seg % seg_count)
        at = slice(s * SEG, (s + 1) * SEG)
        for h in range(6):
            cols = [slice(j * 768 + h * 128, j * 768 + (h + 1) * 128) for j in range(3)]
            q, k, v = (packed_ref[at, c] for c in cols)
            grads = attend_back(q, k, v, mixed_grad_ref[at, cols[0]], allowed)
            for c, g in zip(cols, grads):
                packed_grad_ref[at, c] = g.astype(LOW)
    grads_ref[0:1, :] += column_sum(packed_grad_ref[:, :768])
    grads_ref[1:2, :] += column_sum(packed_grad_ref[:, 1536:])


def token_grad_kernel(info, packed_grad_ref, proj_grad_ref, *rest):
    pieces, (token_grad_ref, qkv, sems) = rest[:10], rest[10:]

    @pl.when(pl.program_id(0) == 0)
    def _():
        load(slab_copies(info[0], pieces, qkv_slabs(qkv), sems))

    total = proj_grad_ref[...].astype(F32)
    for j in range(3):
        total = total + mm_nt(packed_grad_ref[:, j * 768 : (j + 1) * 768], qkv[j])
    token_grad_ref[...] = total.astype(LOW)


def send_slab(place, total, keep_ref, send_ref, rows):
    for mask in range(8):
        block = pl.multiple_of((place ^ mask) * rows, rows)
        target = send_ref if mask % 2 else keep_ref
        target[mask // 2] = total[pl.ds(block, rows), :].astype(LOW)


def qkv_grad_kernel(info, left_ref, right_ref, keep_ref, send_ref, total):
    total[...] = mm_tn(left_ref[...], right_ref[...])
    send_slab(info[0], total, keep_ref, send_ref, 96)


def mid_grad_kernel(info, mixed_ref, proj_ref, low_ref, hidden_ref, keep_ref, send_ref, total):
    @pl.when(pl.program_id(0) == 0)
    def _():
        total[...] = mm_tn(mixed_ref[...], proj_ref[...])

    @pl.when(pl.program_id(0) > 0)
    def _():
        total[...] = mm_tn(low_ref[...], hidden_ref[...])

    send_slab(info[0], total, keep_ref, send_ref, 96)


ANY = pl.BlockSpec(memory_space=pl.ANY)
SMEM = pl.BlockSpec(memory_space=pltpu.SMEM)


def block_rows(count, width):
    return pl.BlockSpec((count, width), lambda i: (i, 0))


def fixed(shape):
    return pl.BlockSpec(shape, lambda i: (0,) * len(shape))


def shape_of(dims, kind=LOW):
    return jax.ShapeDtypeStruct(dims, kind)


def params():
    return pltpu.CompilerParams(vmem_limit_bytes=VMEM, dimension_semantics=("arbitrary",))


def cost(flops, size):
    return pl.CostEstimate(flops=flops, bytes_accessed=size, transcendentals=0)


QKV = [pltpu.VMEM((3, 768, 768), LOW)]
MID = [pltpu.VMEM((768, 768), LOW), pltpu.VMEM((4, 768, 768), LOW)]
DOWN = [pltpu.VMEM((3072, 768), LOW)]


def sems(count):
    return [pltpu.SemaphoreType.DMA((count,))]


def shifted(count, width, first):
    return pl.BlockSpec((count, width), lambda i: (i + first, 0))


def attn_forward(info, rows_in, vec, pieces, seg_count, half, before=None, segs=4):
    rows = rows_in.shape[0]
    count = segs * SEG
    steps = rows // count // 2
    first = half * steps
    before = list(before or [])
    return pl.pallas_call(
        functools.partial(attn_forward_kernel, segs, seg_count, first),
        grid=(steps,),
        in_specs=[SMEM, shifted(count, 768, first), fixed((12, 768))] + [ANY] * (10 + len(before)),
        out_specs=[shifted(count, 2304, first), shifted(count, 768, first)],
        out_shape=[shape_of((rows, 2304)), shape_of((rows, 768))],
        scratch_shapes=QKV + sems(24),
        input_output_aliases={13: 0, 14: 1} if before else {},
        compiler_params=params(),
        cost_estimate=cost(rows * 768 * 8000, rows * 768 * 8),
        name="attn_forward",
    )(info, rows_in, vec, *pieces, *before)


def mid_forward(info, rows_in, mixed, vec, pieces, segs=2):
    rows = rows_in.shape[0]
    count = segs * SEG
    return pl.pallas_call(
        mid_forward_kernel,
        grid=(rows // count,),
        in_specs=[SMEM, block_rows(count, 768), block_rows(count, 768), fixed((12, 768))] + [ANY] * 10,
        out_specs=[block_rows(count, 768), block_rows(count, 768), block_rows(count, 3072), block_rows(count, 3072)],
        out_shape=[shape_of((rows, 768), F32), shape_of((rows, 768)), shape_of((rows, 3072)), shape_of((rows, 3072))],
        scratch_shapes=MID + sems(40),
        compiler_params=params(),
        cost_estimate=cost(2 * rows * 768 * 8000, rows * 768 * 30),
        name="mid_forward",
    )(info, rows_in, mixed, vec, *pieces)


def down_forward(info, summed, act, vec, pieces, segs=2):
    rows = summed.shape[0]
    count = segs * SEG
    few = pl.BlockSpec((None, segs, 768), lambda i: (i, 0, 0))
    return pl.pallas_call(
        functools.partial(down_forward_kernel, segs),
        grid=(rows // count,),
        in_specs=[SMEM, block_rows(count, 768), block_rows(count, 3072), fixed((12, 768))] + [ANY] * 8,
        out_specs=[block_rows(count, 768), few],
        out_shape=[shape_of((rows, 768), F32), shape_of((rows // count, segs, 768), F32)],
        scratch_shapes=DOWN + sems(32),
        compiler_params=params(),
        cost_estimate=cost(2 * rows * 768 * 4000, rows * 768 * 16),
        name="down_forward",
    )(info, summed, act, vec, *pieces)


def cross_whole(info, heads, upstream, live, vec, positions, wide, tall):
    rows = heads.shape[0]
    count = 2 * SEG
    own = [(16, 768), (16, 768), (12, 768), (8, 768), (24, 2304), (24, 768), (24, 3072), (96, 768)]
    return pl.pallas_call(
        functools.partial(cross_kernel, rows // count),
        grid=(rows // count,),
        in_specs=[SMEM, block_rows(count, 768), block_rows(count, 768), block_rows(count, SEG),
                  fixed((12, 768)), fixed((8, 768)), ANY, ANY],
        out_specs=[fixed(dims) for dims in own],
        out_shape=[shape_of(dims, F32) for dims in own],
        scratch_shapes=QKV + MID + DOWN + sems(9) + [
            pltpu.VMEM((rows, 768), F32), pltpu.VMEM((rows, 768), F32), pltpu.VMEM((count, 3072), LOW),
            pltpu.VMEM((3, rows, 768), LOW), pltpu.VMEM((rows, 3072), LOW), pltpu.VMEM((count, 2304), LOW),
            pltpu.VMEM((5, rows, 768), LOW), pltpu.VMEM((rows, 3072), LOW),
        ],
        compiler_params=params(),
        cost_estimate=cost(2 * rows * 768 * 30000, 2**24),
        name="cross_encoder",
    )(info, heads, upstream, live, vec, positions, wide, tall)


def ffn_backward(info, cotangent, heads_grad, heads, second, summed, slope, vec, mid, down, seg_count, segs=2):
    rows = summed.shape[0]
    count = segs * SEG
    few = pl.BlockSpec((None, segs, 768), lambda i: (i, 0, 0))
    return pl.pallas_call(
        functools.partial(ffn_backward_kernel, segs, seg_count),
        grid=(rows // count,),
        in_specs=[SMEM, block_rows(count, 768), few, few, block_rows(count, 768), block_rows(count, 768),
                  block_rows(count, 3072), fixed((12, 768))] + [ANY] * 18,
        out_specs=[block_rows(count, 768), block_rows(count, 768), block_rows(count, 3072), block_rows(count, 768),
                   block_rows(count, 768), fixed((12, 768))],
        out_shape=[shape_of((rows, 768)), shape_of((rows, 768)), shape_of((rows, 3072)), shape_of((rows, 768)),
                   shape_of((rows, 768)), shape_of((12, 768), F32)],
        scratch_shapes=MID + DOWN + sems(72),
        compiler_params=params(),
        cost_estimate=cost(2 * rows * 768 * 14000, rows * 768 * 30),
        name="ffn_backward",
    )(info, cotangent, heads_grad.reshape(-1, segs, 768), heads.reshape(-1, segs, 768), second, summed, slope, vec, *mid, *down)


def attn_backward(info, packed, mixed_grad, seg_count, half, before=None, segs=2):
    rows = packed.shape[0]
    count = segs * SEG
    steps = rows // count // 2
    first = half * steps
    before = [] if before is None else [before]
    return pl.pallas_call(
        functools.partial(attn_backward_kernel, segs, seg_count, first),
        grid=(steps,),
        in_specs=[SMEM, shifted(count, 2304, first), shifted(count, 768, first)] + [ANY] * len(before),
        out_specs=[shifted(count, 2304, first), fixed((2, 768))],
        out_shape=[shape_of((rows, 2304)), shape_of((2, 768), F32)],
        input_output_aliases={3: 0} if before else {},
        compiler_params=params(),
        cost_estimate=cost(rows * 768 * 10000, rows * 768 * 8),
        name="attn_backward",
    )(info, packed, mixed_grad, *before)


def token_gradient(info, packed_grad, proj_grad, pieces, count=512):
    rows = packed_grad.shape[0]
    return pl.pallas_call(
        token_grad_kernel,
        grid=(rows // count,),
        in_specs=[SMEM, block_rows(count, 2304), block_rows(count, 768)] + [ANY] * 10,
        out_specs=block_rows(count, 768),
        out_shape=shape_of((rows, 768)),
        scratch_shapes=QKV + sems(24),
        compiler_params=params(),
        cost_estimate=cost(2 * rows * 768 * 3000, rows * 768 * 10),
        name="token_gradient",
    )(info, packed_grad, proj_grad, *pieces)


def grad_outs(slabs):
    out = pl.BlockSpec((4, 96, 768), lambda i: (0, i, 0))
    return [out, out], [shape_of((4, slabs * 96, 768))] * 2


def qkv_weight_grad(info, left, right):
    rows = left.shape[0]
    specs, shapes = grad_outs(3)
    return pl.pallas_call(
        qkv_grad_kernel,
        grid=(3,),
        in_specs=[SMEM, fixed((rows, 768)), pl.BlockSpec((rows, 768), lambda i: (0, i))],
        out_specs=specs,
        out_shape=shapes,
        scratch_shapes=[pltpu.VMEM((768, 768), F32)],
        compiler_params=params(),
        cost_estimate=cost(2 * rows * 768 * 2304, rows * 2304 * 2),
        name="qkv_weight_grad",
    )(info, left, right)


def mid_weight_grad(info, mixed, proj_grad, low, hidden_grad):
    rows = mixed.shape[0]
    specs, shapes = grad_outs(5)
    still = fixed((rows, 768))
    return pl.pallas_call(
        mid_grad_kernel,
        grid=(5,),
        in_specs=[SMEM, still, still, still, pl.BlockSpec((rows, 768), lambda i: (0, jnp.maximum(i - 1, 0)))],
        out_specs=specs,
        out_shape=shapes,
        scratch_shapes=[pltpu.VMEM((768, 768), F32)],
        compiler_params=params(),
        cost_estimate=cost(2 * rows * 768 * 3840, rows * 3840 * 2),
        name="mid_weight_grad",
    )(info, mixed, proj_grad, low, hidden_grad)


def down_grad_kernel(info, left_ref, right_ref, keep_ref, send_ref, total):
    step = pl.program_id(0)
    total[pl.ds(pl.multiple_of(step * 768, 768), 768), :] = mm_tn(left_ref[...], right_ref[...]).astype(LOW)

    @pl.when(step == pl.num_programs(0) - 1)
    def _():
        for mask in range(8):
            block = pl.multiple_of((info[0] ^ mask) * 384, 384)
            target = send_ref if mask % 2 else keep_ref
            target[mask // 2] = total[pl.ds(block, 384), :]


def down_weight_grad(info, left, right):
    rows, wide = left.shape
    return pl.pallas_call(
        down_grad_kernel,
        grid=(wide // 768,),
        in_specs=[SMEM, pl.BlockSpec((rows, 768), lambda i: (0, i)), fixed((rows, 768))],
        out_specs=[fixed((4, 384, 768))] * 2,
        out_shape=[shape_of((4, 384, 768))] * 2,
        scratch_shapes=[pltpu.VMEM((3072, 768), LOW)],
        compiler_params=params(),
        cost_estimate=cost(2 * rows * 768 * wide, rows * wide * 2),
        name="down_weight_grad",
    )(info, left, right)


def matmul(left_op, right_op):
    return jnp.dot(left_op, right_op, preferred_element_type=jnp.float32)


def trans_left(left_op, right_op):
    return lax.dot_general(
        left_op, right_op, (((0,), (0,)), ((), ())), preferred_element_type=jnp.float32
    )


def trans_right(left_op, right_op):
    return lax.dot_general(
        left_op, right_op, (((1,), (1,)), ((), ())), preferred_element_type=jnp.float32
    )


def norm_forward(summed, gain_row, shift_row):
    average = jnp.mean(summed, axis=-1, keepdims=True)
    centered = summed - average
    inv_scale = lax.rsqrt(jnp.mean(centered * centered, axis=-1, keepdims=True) + NORM_EPS)
    normed = centered * inv_scale
    return (normed * (1.0 + gain_row) + shift_row, normed, inv_scale)


def norm_backward(upstream, normed, inv_scale, gain_row):
    inner = upstream * (1.0 + gain_row)
    back_grad = inv_scale * (
        inner
        - jnp.mean(inner, axis=-1, keepdims=True)
        - normed * jnp.mean(inner * normed, axis=-1, keepdims=True)
    )
    return (back_grad, jnp.sum(upstream * normed, axis=0), jnp.sum(upstream, axis=0))


def gelu_slope(hidden):
    return (
        0.5 * (1.0 + lax.erf(hidden * ROOT_HALF))
        + hidden * jnp.exp(-0.5 * hidden * hidden) * INV_ROOT_TAU
    )


def split_heads(packed, group_len):
    head_count = packed.shape[1] // (3 * HEAD)
    return [
        portion.reshape(-1, group_len, head_count, HEAD) for portion in jnp.split(packed, 3, axis=1)
    ]


def masked_scores(query_heads, key_heads, allowed):
    raw_scores = jnp.einsum(
        "nqhd,nkhd->nhqk", query_heads, key_heads, preferred_element_type=jnp.float32
    ) * HEAD ** (-0.5)
    return jnp.where(allowed[:, None, None, :], raw_scores, MASK_FILL)


def encode(inputs, inputs_low, weights, allowed):
    qkv_w, out_w, up_w, down_w, vectors = weights
    row_count, feat_dim = inputs_low.shape
    group_len = allowed.shape[1]
    qkv_bias = jnp.concatenate([vectors[0], jnp.zeros_like(vectors[0]), vectors[1]])
    packed = (matmul(inputs_low, qkv_w) + qkv_bias).astype(jnp.bfloat16)
    query_heads, key_heads, value_heads = split_heads(packed, group_len)
    scores = masked_scores(query_heads, key_heads, allowed)
    row_max = jnp.max(scores, axis=-1, keepdims=True)
    expo_vals = jnp.exp(scores - row_max)
    row_total = jnp.sum(expo_vals, axis=-1, keepdims=True)
    log_total = row_max + jnp.log(row_total)
    prob_low = (expo_vals / row_total).astype(jnp.bfloat16)
    mixed = jnp.einsum("nhqk,nkhd->nqhd", prob_low, value_heads, preferred_element_type=jnp.float32)
    mixed = mixed.reshape(row_count, feat_dim).astype(jnp.bfloat16)
    projected = matmul(mixed, out_w) + vectors[2]
    first_out, normed_one, scale_one = norm_forward(inputs + projected, vectors[3], vectors[4])
    first_low = first_out.astype(jnp.bfloat16)
    hidden = matmul(first_low, up_w) + vectors[5:-3].reshape(-1)
    activated = jax.nn.gelu(hidden, approximate=False).astype(jnp.bfloat16)
    down_out = matmul(activated, down_w) + vectors[-3]
    result, normed_two, scale_two = norm_forward(first_out + down_out, vectors[-2], vectors[-1])
    return (
        result,
        (
            packed,
            log_total,
            mixed,
            normed_one,
            scale_one,
            first_low,
            hidden,
            activated,
            normed_two,
            scale_two,
        ),
    )


def encode_back(upstream, inputs_low, weights, allowed, kept):
    qkv_w, out_w, up_w, down_w, vectors = weights
    (
        packed,
        log_total,
        mixed,
        normed_one,
        scale_one,
        first_low,
        hidden,
        activated,
        normed_two,
        scale_two,
    ) = kept
    row_count, feat_dim = inputs_low.shape
    group_len = allowed.shape[1]
    back_two, gain_two, shift_two = norm_backward(upstream, normed_two, scale_two, vectors[-2])
    down_grad = back_two.astype(jnp.bfloat16)
    hidden_grad = (trans_right(down_grad, down_w) * gelu_slope(hidden)).astype(jnp.bfloat16)
    first_grad = trans_right(hidden_grad, up_w) + back_two
    back_one, gain_one, shift_one = norm_backward(first_grad, normed_one, scale_one, vectors[3])
    proj_grad = back_one.astype(jnp.bfloat16)
    query_heads, key_heads, value_heads = split_heads(packed, group_len)
    mixed_grad = trans_right(proj_grad, out_w).astype(jnp.bfloat16).reshape(value_heads.shape)
    scores = masked_scores(query_heads, key_heads, allowed)
    prob_vals = jnp.exp(scores - log_total)
    grad_values = jnp.einsum(
        "nhqk,nqhd->nkhd",
        prob_vals.astype(jnp.bfloat16),
        mixed_grad,
        preferred_element_type=jnp.float32,
    )
    grad_prob = jnp.einsum(
        "nqhd,nkhd->nhqk", mixed_grad, value_heads, preferred_element_type=jnp.float32
    )
    score_grad = (
        prob_vals * (grad_prob - jnp.sum(prob_vals * grad_prob, axis=-1, keepdims=True))
    ).astype(jnp.bfloat16)
    grad_query = jnp.einsum(
        "nhqk,nkhd->nqhd", score_grad, key_heads, preferred_element_type=jnp.float32
    ) * HEAD ** (-0.5)
    grad_keys = jnp.einsum(
        "nhqk,nqhd->nkhd", score_grad, query_heads, preferred_element_type=jnp.float32
    ) * HEAD ** (-0.5)
    packed_grad = jnp.concatenate(
        [
            grad_query.reshape(row_count, feat_dim),
            grad_keys.reshape(row_count, feat_dim),
            grad_values.reshape(row_count, feat_dim),
        ],
        axis=1,
    ).astype(jnp.bfloat16)
    bias_grads = jnp.sum(packed_grad, axis=0, dtype=jnp.float32).reshape(3, feat_dim)
    grad_inputs = trans_right(packed_grad, qkv_w) + back_one
    grad_vectors = jnp.concatenate(
        [
            bias_grads[0:1],
            bias_grads[2:3],
            jnp.sum(proj_grad, axis=0, dtype=jnp.float32)[None],
            gain_one[None],
            shift_one[None],
            jnp.sum(hidden_grad, axis=0, dtype=jnp.float32).reshape(-1, feat_dim),
            jnp.sum(down_grad, axis=0, dtype=jnp.float32)[None],
            gain_two[None],
            shift_two[None],
        ],
        axis=0,
    )
    pairs = (
        (inputs_low, packed_grad),
        (mixed, proj_grad),
        (first_low, hidden_grad),
        (activated, down_grad),
    )
    return (grad_inputs, pairs, grad_vectors)


class Links:
    def __init__(self, outer, inner):
        self.outer, self.inner = outer, inner
        self.order = self.place = lax.axis_index("dp")
        self.z = lax.axis_index("fsdp")

    def flip(self, value, mask):
        pairs = [
            (d * self.inner + z, (d ^ mask) * self.inner + z)
            for d in range(self.outer)
            for z in range(self.inner)
        ]
        return lax.ppermute(value, AXES, pairs)

    def turn(self, value, step):
        pairs = [
            (d * self.inner + z, d * self.inner + (z + step) % self.inner)
            for d in range(self.outer)
            for z in range(self.inner)
        ]
        return lax.ppermute(value, AXES, pairs)

    def gather_z(self, shard):
        came = [shard] + [self.turn(shard, step) for step in range(1, self.inner)]
        whole = []
        for z in range(self.inner):
            part = came[-1]
            for step in range(self.inner - 1):
                part = jnp.where(self.z == (z + step) % self.inner, came[step], part)
            whole.append(part)
        return whole

    def spread_near(self, block):
        return self.flip(block, 2), self.flip(block, 4)

    def spread_far(self, by_x, by_y, half):
        return self.flip(by_y[:half], 2), self.flip(by_x[half:], 4)

    def spread_core(self, mine):
        return list(mine) + [self.flip(piece, 1) for piece in mine]

    def in_order(self, parts):
        for axis, mask in ((4, 4), (2, 2), (1, 1)):
            odd = self.place // axis % 2 == 1
            parts = [jnp.where(odd, parts[m ^ mask], parts[m]) for m in range(8)]
        return jnp.stack(parts)

    def gather_small(self, shard):
        block = jnp.stack(self.gather_z(shard))
        near = [block] + [self.flip(block, m) for m in (2, 4, 6)]
        plane = jnp.stack(near)
        other = self.flip(plane, 1)
        whole = self.in_order([(plane, other)[m % 2][m // 2] for m in range(8)])
        return whole.reshape((-1,) + shard.shape)


class PlainLinks:
    def __init__(self, outer, inner):
        self.outer, self.inner = outer, inner
        self.order = lax.axis_index("dp")
        self.z = lax.axis_index("fsdp")
        self.place = 0

    def gather_small(self, shard):
        return lax.all_gather(shard, AXES, axis=0)


def add(*terms):
    return sum(t.astype(F32) for t in terms).astype(LOW)


class Sum:
    def __init__(self, links, keep, send, slabs):
        self.links, self.keep, self.slabs = links, keep, slabs
        self.came = links.flip(send, 1)

    def line(self, part):
        inner = self.links.inner
        part = part.reshape(self.slabs, inner, -1, part.shape[-1])
        return part.transpose(1, 0, 2, 3).reshape(inner, -1, part.shape[-1])

    def to(self, index):
        return self.line(add(self.keep[index], self.came[index]))

    def far(self):
        half = self.links.inner // 2
        to_d = self.to(3)
        self.far_came = [self.links.flip(to_d[:half], 2), self.links.flip(to_d[half:], 4)]
        return self.far_came

    def near(self):
        half = self.links.inner // 2
        came_x, came_y = self.far_came
        to_x, to_y = self.to(1), self.to(2)
        to_y = jnp.concatenate([add(to_y[:half], came_x), to_y[half:]])
        to_x = jnp.concatenate([to_x[:half], add(to_x[half:], came_y)])
        self.near_came = [self.links.flip(to_x, 2), self.links.flip(to_y, 4)]
        return self.near_came

    def direct(self):
        self.near_came = [self.links.flip(self.to(m // 2), m) for m in (2, 4, 6)]
        return self.near_came

    def finish(self):
        links = self.links
        own = add(self.line(self.keep[0]), self.line(self.came[0]), *self.near_came)

        def pick(index):
            return lax.dynamic_index_in_dim(own, index % links.inner, 0, keepdims=False)

        total = pick(links.z).astype(F32)
        for step in range(1, links.inner):
            total = total + links.turn(pick(links.z + step), step).astype(F32)
        return total


class PlainSum:
    def __init__(self, links, keep, send, slabs):
        flat = jnp.stack([keep, send], axis=1).reshape(8, slabs, -1, 768)
        rows = flat.shape[2] * 8 // (links.outer * links.inner)
        flat = flat.transpose(1, 0, 2, 3).reshape(slabs, -1, 768) if slabs > 1 else flat.reshape(1, -1, 768)
        self.total = lax.psum_scatter(flat, AXES, scatter_dimension=1, tiled=True).reshape(-1, 768).astype(F32)
        self.came = keep

    def far(self):
        return []

    near = direct = far

    def finish(self):
        return self.total


def after(value, *earlier):
    return lax.optimization_barrier((value, *earlier))[0]


def slabs_of(matrix):
    rows, wide = matrix.shape
    return matrix.reshape(rows, wide // 768, 768).transpose(1, 0, 2)


def matrix_of(slabs):
    count, rows, width = slabs.shape
    return slabs.transpose(1, 0, 2).reshape(rows, count * width)


def plain_pieces(slabs, whole):
    count = slabs.shape[0]
    half = (count + 1) // 2 * 96
    parts = []
    for mask in (0, 2, 4, 6, 1, 3, 5, 7):
        part = slabs[:, mask * 96 : (mask + 1) * 96].reshape(-1, 768)
        parts += [part] if whole or mask < 6 and mask != 7 else [part[:half], part[half:]]
    return parts


def shards(
    outer,
    inner,
    tokens,
    cotangent,
    lengths,
    seg_qkv,
    seg_out,
    seg_up,
    seg_down,
    seg_vec,
    cross_qkv,
    cross_out,
    cross_up,
    cross_down,
    cross_vec,
    positions,
):
    fast = (outer, inner) == (8, 4)
    links = (Links if fast else PlainLinks)(outer, inner)
    summing = Sum if fast else PlainSum
    devices = outer * inner
    me = links.order * inner + links.z
    seq_local, seq_len, feat_dim = tokens.shape
    seg_count = seq_len // SEG
    seg_rows, cross_rows = seg_vec.shape[0], cross_vec.shape[0]
    width = feat_dim // devices
    my_lengths = lax.dynamic_slice_in_dim(lengths, me * seq_local, seq_local)
    info = jnp.concatenate([jnp.full((1,), links.place, jnp.int32), my_lengths])
    small = jnp.concatenate([seg_vec, cross_vec, positions]).reshape(1, -1)
    wide = jnp.concatenate([slabs_of(cross_qkv), slabs_of(cross_out), slabs_of(cross_up)])
    mid_shard = jnp.concatenate([slabs_of(seg_out), slabs_of(seg_up)])
    rows_in = tokens.reshape(-1, feat_dim)
    cot_rows = cotangent.reshape(-1, feat_dim)
    seg_starts = jnp.arange(seg_count) * SEG
    live_own = (seg_starts[None, :] < my_lengths[:, None]).reshape(-1, 1)
    up_own = jnp.where(live_own, cotangent.reshape(-1, SEG, feat_dim)[:, 0, :], 0)

    wide = lax.all_gather(wide, AXES, axis=1, tiled=True)
    tall = lax.all_gather(cross_down, AXES, axis=0, tiled=True)
    if fast:
        first = jnp.concatenate([slabs_of(seg_qkv).reshape(-1, 768), jnp.pad(small, ((0, 7), (0, 0)))])
        line_first = links.gather_z(first)
        line_mid = links.gather_z(after(mid_shard, *line_first))
        line_down = links.gather_z(after(seg_down, *line_mid))
        weights = jnp.stack([p[:72].reshape(3, 24, 768) for p in line_first], axis=1).reshape(-1, 768)
        rows = jnp.concatenate([p[72:73] for p in line_first])
        block = jnp.concatenate([weights, jnp.pad(rows, ((0, 12), (0, 0)))])
        near = links.spread_near(block)
        far = links.spread_far(*near, 192)
        first = links.spread_core([block, *near, *far])
        ends = [p[288:292] for p in first[:3]] + [first[4][96:100]]
        others = [p[288:292] for p in first[5:8]] + [first[9][96:100]]
        small = links.in_order([(ends, others)[m % 2][m // 2] for m in range(8)])
        block = after(jnp.stack(line_mid, axis=1).reshape(-1, 768), *far)
        near_mid = links.spread_near(block)
        far_mid = links.spread_far(*near_mid, 288)
        mid = links.spread_core([block, *near_mid, *far_mid])
        block = after(jnp.concatenate(line_down), *far_mid)
        down = links.spread_core([block] + [links.flip(block, m) for m in (2, 4, 6)])
    else:
        first = plain_pieces(lax.all_gather(slabs_of(seg_qkv), AXES, axis=1, tiled=True), False)
        mid = plain_pieces(lax.all_gather(mid_shard, AXES, axis=1, tiled=True), False)
        down_whole = lax.all_gather(seg_down, AXES, axis=0, tiled=True)
        down = [down_whole[m * 384 : (m + 1) * 384] for m in (0, 2, 4, 6, 1, 3, 5, 7)]
        small = links.gather_small(small)
        near_mid = []
    small = small.reshape(devices, -1, width).transpose(1, 0, 2).reshape(-1, feat_dim).astype(F32)
    seg_v, cross_v = small[:seg_rows], small[seg_rows : seg_rows + cross_rows]
    pos_table = small[seg_rows + cross_rows :]

    before = attn_forward(info, rows_in, seg_v, first, seg_count, 0)
    packed, mixed = attn_forward(info, after(rows_in, *near_mid), seg_v, first, seg_count, 1, before)
    summed, low, act, slope = mid_forward(info, rows_in, mixed, seg_v, mid)
    second, heads = down_forward(info, summed, act, seg_v, down)
    heads_own = heads.reshape(-1, feat_dim)
    both = links.gather_small(jnp.stack([heads_own.astype(LOW), up_own]))
    heads_all, up_all = both[:, 0].reshape(-1, feat_dim), both[:, 1].reshape(-1, feat_dim)
    live_all = seg_starts[None, :] < lengths[:, None]
    if fast:
        cross_info = jnp.stack([links.place, me]).astype(jnp.int32)
        live = jnp.broadcast_to(live_all.reshape(-1, 1), (live_all.size, SEG)).astype(F32)
        cross_own, heads_grad, vec_grad, pos_grad, *cross_grads = cross_whole(
            cross_info, heads_all, up_all, live, cross_v, pos_table, wide, tall
        )
    else:
        weights = (matrix_of(wide[:3]), wide[3], matrix_of(wide[4:]), tall, cross_v)
        heads_in = heads_all.astype(F32).reshape(-1, seg_count, feat_dim) + pos_table[None]
        heads_in = heads_in.reshape(-1, feat_dim)
        cross_result, kept = encode(heads_in, heads_in.astype(LOW), weights, live_all)
        all_grad, pairs, vec_grad = encode_back(
            up_all.astype(F32), heads_in.astype(LOW), weights, live_all, kept
        )
        cross_grads = []
        for left, right in pairs:
            count = left.shape[1] // devices
            mine = lax.dynamic_slice_in_dim(left, me * count, count, 1)
            cross_grads.append(trans_left(mine, right))
        pos_grad = jnp.sum(all_grad.reshape(-1, seg_count, feat_dim), axis=0)
        own = seq_local * seg_count
        cross_own = lax.dynamic_slice_in_dim(cross_result, me * own, own)
        heads_grad = lax.dynamic_slice_in_dim(all_grad, me * own, own)
    cross_vec_grad = lax.dynamic_slice_in_dim(vec_grad, me * width, width, 1)
    grad_positions = lax.dynamic_slice_in_dim(pos_grad, me * width, width, 1)

    layer_out, down_grad, hidden_grad, proj_grad, mixed_grad, grads_two = ffn_backward(
        info, cot_rows, heads_grad, cross_own, second, summed, slope, seg_v, mid, down, seg_count
    )
    down_sum = summing(links, *down_weight_grad(info, act, down_grad), 1)
    mid_parts = mid_weight_grad(info, mixed, proj_grad, low, after(hidden_grad, down_sum.keep if fast else down_sum.came))
    mid_sum = summing(links, *mid_parts, 5)
    grads_mid = lax.psum(grads_two[2:], AXES)
    half_grad, grads_one = attn_backward(
        info, packed, after(mixed_grad, mid_parts[1], down_sum.came), seg_count, 0
    )
    ready = after(mixed_grad, half_grad, *down_sum.far(), mid_sum.came)
    packed_grad, grads_more = attn_backward(info, packed, ready, seg_count, 1, half_grad)
    ready = after(packed_grad, *down_sum.near(), *mid_sum.far())
    qkv_sum = summing(links, *qkv_weight_grad(info, rows_in, ready), 3)
    ready = after(packed_grad, *mid_sum.near(), qkv_sum.came)
    token_grad = token_gradient(info, ready, proj_grad, first)
    qkv_sum.direct()
    grads_one = lax.psum(grads_one + grads_more, AXES)
    grad_down = down_sum.finish()
    grad_mid = mid_sum.finish().reshape(5, -1, feat_dim)
    grad_qkv = matrix_of(qkv_sum.finish().reshape(3, -1, feat_dim))
    grad_vec = lax.dynamic_slice_in_dim(jnp.concatenate([grads_one, grads_mid]), me * width, width, 1)
    return (
        layer_out.reshape(tokens.shape),
        token_grad.reshape(tokens.shape),
        grad_qkv,
        grad_mid[0],
        matrix_of(grad_mid[1:]),
        grad_down,
        grad_vec,
        *cross_grads,
        cross_vec_grad,
        grad_positions,
    )


def solution(mesh):
    in_specs = (
        P(("dp", "fsdp"), None, None),
        P(("dp", "fsdp"), None, None),
        P(),
        P(("dp", "fsdp"), None),
        P(("dp", "fsdp"), None),
        P(("dp", "fsdp"), None),
        P(("dp", "fsdp"), None),
        P(None, ("dp", "fsdp")),
        P(("dp", "fsdp"), None),
        P(("dp", "fsdp"), None),
        P(("dp", "fsdp"), None),
        P(("dp", "fsdp"), None),
        P(None, ("dp", "fsdp")),
        P(None, ("dp", "fsdp")),
    )
    out_specs = (
        P(("dp", "fsdp"), None, None),
        P(("dp", "fsdp"), None, None),
        P(("dp", "fsdp"), None),
        P(("dp", "fsdp"), None),
        P(("dp", "fsdp"), None),
        P(("dp", "fsdp"), None),
        P(None, ("dp", "fsdp")),
        P(("dp", "fsdp"), None),
        P(("dp", "fsdp"), None),
        P(("dp", "fsdp"), None),
        P(("dp", "fsdp"), None),
        P(None, ("dp", "fsdp")),
        P(None, ("dp", "fsdp")),
    )
    return jax.shard_map(
        functools.partial(shards, mesh.shape["dp"], mesh.shape["fsdp"]),
        mesh=mesh, in_specs=in_specs, out_specs=out_specs, check_vma=False)
```

```python
import functools

import jax
import jax.numpy as jnp
from jax import lax
from jax.experimental import pallas as pl
from jax.experimental.pallas import tpu as pltpu
from jax.sharding import PartitionSpec as P

HEAD = 64
SEG = 128
NORM_EPS = 1e-05
MASK_FILL = -1000000000.0
VMEM = 60 * 2**20
F32, LOW = jnp.float32, jnp.bfloat16


ROOT_HALF = 0.7071067811865476
INV_ROOT_TAU = 0.3989422804014327
AXES = ("dp", "fsdp")

def mm(left_op, right_op):
    return jnp.dot(left_op, right_op, preferred_element_type=F32)


def mm_nt(left_op, right_op):
    return lax.dot_general(left_op, right_op, (((1,), (1,)), ((), ())), preferred_element_type=F32)


def mm_tn(left_op, right_op):
    return lax.dot_general(left_op, right_op, (((0,), (0,)), ((), ())), preferred_element_type=F32)


def normalize(summed):
    average = jnp.mean(summed, axis=-1, keepdims=True)
    centered = summed - average
    inv_scale = lax.rsqrt(jnp.mean(centered * centered, axis=-1, keepdims=True) + NORM_EPS)
    return centered * inv_scale, inv_scale


def normalize_back(inner, normed, inv_scale):
    return inv_scale * (
        inner
        - jnp.mean(inner, axis=-1, keepdims=True)
        - normed * jnp.mean(inner * normed, axis=-1, keepdims=True)
    )


def gelu_parts(hidden):
    phi = 0.5 * (1.0 + lax.erf(hidden * ROOT_HALF))
    return hidden * phi, phi + hidden * jnp.exp(-0.5 * hidden * hidden) * INV_ROOT_TAU


def pair_stack(pair, low_half):
    zero = jnp.zeros_like(pair)
    return jnp.concatenate(
        [jnp.where(low_half, pair, zero), jnp.where(low_half, zero, pair)], axis=0
    )


def pair_merge(stacked, low_half):
    rows = stacked.shape[0] // 2
    return jnp.where(low_half, stacked[:rows], stacked[rows:])


def pair_probs(stack, keys, allowed):
    scores = jnp.where(allowed, mm_nt(keys, stack), MASK_FILL)
    expo = jnp.exp(scores - jnp.max(scores, axis=0, keepdims=True))
    return expo * (1.0 / jnp.sum(expo, axis=0, keepdims=True))


def attend(query, keys, values, allowed):
    low_half = lax.broadcasted_iota(jnp.int32, query.shape, 1) < HEAD
    stack = pair_stack(query * jnp.asarray(HEAD**-0.5, query.dtype), low_half)
    return pair_merge(mm_tn(pair_probs(stack, keys, allowed).astype(LOW), values), low_half)


def attend_back(query, keys, values, grad_mixed, allowed):
    low_half = lax.broadcasted_iota(jnp.int32, query.shape, 1) < HEAD
    stack = pair_stack(query * jnp.asarray(HEAD**-0.5, query.dtype), low_half)
    probs = pair_probs(stack, keys, allowed)
    grad_stack = pair_stack(grad_mixed, low_half)
    grad_prob = mm_nt(values, grad_stack)
    inner = jnp.sum(probs * grad_prob, axis=0, keepdims=True)
    score_grad = (probs * (grad_prob - inner)).astype(LOW)
    grad_query = pair_merge(mm_tn(score_grad, keys), low_half) * HEAD**-0.5
    return grad_query, mm(score_grad, stack), mm(probs.astype(LOW), grad_stack)


def slab_copies(place, pieces, slabs, sems, first_sem=0):
    count = len(slabs)
    half = (count + 1) // 2
    spans = [(0, 0, count), (2, 0, count), (4, 0, count)]
    spans += [(6, 0, count)] if len(pieces) == 8 else [(6, 0, half), (6, half, count)]
    copies = []
    for flip_c in (0, 1):
        for index, (flip_yx, first, last) in enumerate(spans):
            block = place ^ (flip_yx + flip_c)
            piece = pieces[flip_c * len(spans) + index]
            for slab in range(first, last):
                source = piece.at[pl.ds((slab - first) * 96, 96)]
                sem = sems.at[first_sem + slab * 8 + flip_yx + flip_c]
                copies.append(pltpu.make_async_copy(source, slabs[slab](block), sem))
    return copies


def load(copies):
    for copy in copies:
        copy.start()
    for copy in copies:
        copy.wait()


def rows_of(ref, block, rows=96, slab=None):
    where = pl.ds(pl.multiple_of(block * rows, rows), rows)
    return ref.at[where] if slab is None else ref.at[slab, where]


def down_rows(ref, block, part):
    return ref.at[pl.ds(pl.multiple_of(block * 384 + part * 96, 96), 96)]


def qkv_slabs(qkv):
    return [functools.partial(rows_of, qkv, slab=j) for j in range(3)]


def mid_slabs(out, up):
    return [functools.partial(rows_of, out)] + [functools.partial(rows_of, up, slab=j) for j in range(4)]


def down_slabs(down):
    return [functools.partial(down_rows, down, part=j) for j in range(4)]


def segment_mask(length, seg_in_seq):
    row = lax.broadcasted_iota(jnp.int32, (SEG, 2 * SEG), 0)
    return (row + seg_in_seq * SEG < length) | (row == 0)


def attn_forward_kernel(segs, seg_count, first_step, info, x_ref, vec_ref, *rest):
    pieces, (packed_ref, mixed_ref, qkv, sems) = rest[:10], rest[-4:]
    step = pl.program_id(0)

    @pl.when(step == 0)
    def _():
        load(slab_copies(info[0], pieces, qkv_slabs(qkv), sems))

    rows = x_ref[...]
    for j in range(3):
        part = mm(rows, qkv[j])
        if j != 1:
            part = part + vec_ref[j // 2 : j // 2 + 1, :]
        packed_ref[:, j * 768 : (j + 1) * 768] = part.astype(LOW)
    for s in range(segs):
        seg = (step + first_step) * segs + s
        allowed = segment_mask(info[1 + seg // seg_count], seg % seg_count)
        at = slice(s * SEG, (s + 1) * SEG)
        for h in range(6):
            q, k, v = (packed_ref[at, j * 768 + h * 128 : j * 768 + (h + 1) * 128] for j in range(3))
            mixed_ref[at, h * 128 : (h + 1) * 128] = attend(q, k, v, allowed).astype(LOW)


def norm_one(summed, vec_ref):
    normed, _ = normalize(summed)
    return normed * (1.0 + vec_ref[3:4, :]) + vec_ref[4:5, :]


def mid_forward_kernel(info, x_ref, mixed_ref, vec_ref, *rest):
    pieces, (sum_ref, low_ref, act_ref, slope_ref, out, up, sems) = rest[:10], rest[10:]

    @pl.when(pl.program_id(0) == 0)
    def _():
        load(slab_copies(info[0], pieces, mid_slabs(out, up), sems))

    summed = x_ref[...].astype(F32) + mm(mixed_ref[...], out[...]) + vec_ref[2:3, :]
    sum_ref[...] = summed
    first_low = norm_one(summed, vec_ref).astype(LOW)
    low_ref[...] = first_low
    hidden = mm(first_low, up[0]) + vec_ref[5:6, :]
    for j in range(4):
        later = mm(first_low, up[j + 1]) + vec_ref[6 + j : 7 + j, :] if j < 3 else None
        act, slope = gelu_parts(hidden)
        act_ref[:, j * 768 : (j + 1) * 768] = act.astype(LOW)
        slope_ref[:, j * 768 : (j + 1) * 768] = slope.astype(LOW)
        hidden = later


def down_forward_kernel(segs, info, sum_ref, act_ref, vec_ref, *rest):
    pieces, (second_ref, heads_ref, down, sems) = rest[:8], rest[8:]

    @pl.when(pl.program_id(0) == 0)
    def _():
        load(slab_copies(info[0], pieces, down_slabs(down), sems))

    total = norm_one(sum_ref[...], vec_ref) + vec_ref[9:10, :] + mm(act_ref[...], down[...])
    second_ref[...] = total
    opening = jnp.concatenate([total[s * SEG : s * SEG + 1] for s in range(segs)], axis=0)
    normed, _ = normalize(opening)
    heads_ref[...] = normed * (1.0 + vec_ref[10:11, :]) + vec_ref[11:12, :]


def cross_kernel(blocks, info, heads_ref, up_ref, live_ref, vec_ref, pos_ref, *rest):
    wide, rest = rest[0], rest[1:]
    (own_ref, own_grad_ref, grads_ref, pos_grad_ref, qkv_grad_ref, out_grad_ref, up_grad_ref, down_grad_ref) = rest[:8]
    (qkv, out, up, down, sems, result, heads_grad, slope, lefts, act, packed, rights, hidden_grad) = rest[8:]
    step = pl.program_id(0)
    count = heads_ref.shape[0]
    at = pl.ds(pl.multiple_of(step * count, count), count)
    targets = [qkv.at[j] for j in range(3)] + [out] + [up.at[j] for j in range(4)]
    targets += [down.at[j * 768 : (j + 1) * 768] for j in range(4)]
    copies = [pltpu.make_async_copy(wide.at[j], t, sems.at[j]) for j, t in enumerate(targets)]

    @pl.when(step == 0)
    def _():
        for copy in copies:
            copy.start()
        grads_ref[...] = jnp.zeros_like(grads_ref)
        pos_grad_ref[...] = jnp.zeros_like(pos_grad_ref)
        for copy in copies[:3]:
            copy.wait()

    vec = vec_ref[...]
    inputs = heads_ref[...].astype(F32).reshape(-1, 8, 768) + pos_ref[...][None]
    inputs = inputs.reshape(count, 768)
    low = inputs.astype(LOW)
    lefts[0, at, :] = low
    for j in range(3):
        part = mm(low, qkv[j])
        if j != 1:
            part = part + vec[j // 2 : j // 2 + 1]
        packed[:, j * 768 : (j + 1) * 768] = part.astype(LOW)
    row = lax.broadcasted_iota(jnp.int32, (SEG, 2 * SEG), 0)
    lane = lax.broadcasted_iota(jnp.int32, (SEG, 2 * SEG), 1)
    group = row // 8 == lane % SEG // 8
    masks = []
    for s in range(count // SEG):
        live = live_ref[s * SEG : (s + 1) * SEG, :]
        masks.append(group & (jnp.concatenate([live, live], axis=1) > 0.0))
    for s, allowed in enumerate(masks):
        part = slice(s * SEG, (s + 1) * SEG)
        for h in range(6):
            q, k, v = (packed[part, j * 768 + h * 128 : j * 768 + (h + 1) * 128] for j in range(3))
            where = pl.ds(pl.multiple_of(step * count + s * SEG, SEG), SEG)
            lefts[1, where, h * 128 : (h + 1) * 128] = attend(q, k, v, allowed).astype(LOW)

    @pl.when(step == 0)
    def _():
        for copy in copies[3:]:
            copy.wait()

    summed = inputs + mm(lefts[1, at, :], out[...]) + vec[2:3]
    normed_one, scale_one = normalize(summed)
    first = normed_one * (1.0 + vec[3:4]) + vec[4:5]
    first_low = first.astype(LOW)
    lefts[2, at, :] = first_low
    total = first + vec[9:10]
    for j in range(4):
        cols = slice(j * 768, (j + 1) * 768)
        hidden = mm(first_low, up[j]) + vec[5 + j : 6 + j]
        active, steep = gelu_parts(hidden)
        act[at, cols] = active.astype(LOW)
        slope[:, cols] = steep.astype(LOW)
        total = total + mm(active.astype(LOW), down[cols, :])
    normed, inv_scale = normalize(total)
    result[at, :] = normed * (1.0 + vec[10:11]) + vec[11:12]
    upstream = up_ref[...].astype(F32)
    back_two = normalize_back(upstream * (1.0 + vec[10:11]), normed, inv_scale)
    down_grad = back_two.astype(LOW)
    rights[1, at, :] = down_grad
    grads_ref[9:10, :] += column_sum(down_grad)
    grads_ref[10:11, :] += column_sum(upstream * normed)
    grads_ref[11:12, :] += column_sum(upstream)
    total = back_two
    for j in range(4):
        cols = slice(j * 768, (j + 1) * 768)
        grad = (mm_nt(down_grad, down[cols, :]) * slope[:, cols].astype(F32)).astype(LOW)
        hidden_grad[at, cols] = grad
        grads_ref[5 + j : 6 + j, :] += column_sum(grad)
        total = total + mm_nt(grad, up[j])
    back_one = normalize_back(total * (1.0 + vec[3:4]), normed_one, scale_one)
    proj_grad = back_one.astype(LOW)
    rights[0, at, :] = proj_grad
    grads_ref[2:3, :] += column_sum(proj_grad)
    grads_ref[3:4, :] += column_sum(total * normed_one)
    grads_ref[4:5, :] += column_sum(total)
    mixed_grad = mm_nt(proj_grad, out[...]).astype(LOW)
    for s, allowed in enumerate(masks):
        part = slice(s * SEG, (s + 1) * SEG)
        where = pl.ds(pl.multiple_of(step * count + s * SEG, SEG), SEG)
        for h in range(6):
            cols = slice(h * 128, (h + 1) * 128)
            q, k, v = (packed[part, j * 768 + h * 128 : j * 768 + (h + 1) * 128] for j in range(3))
            for j, g in enumerate(attend_back(q, k, v, mixed_grad[part, cols], allowed)):
                rights[2 + j, where, cols] = g.astype(LOW)
    total = back_one
    for j in range(3):
        part = rights[2 + j, at, :]
        total = total + mm_nt(part, qkv[j])
        if j != 1:
            grads_ref[j // 2 : j // 2 + 1, :] += column_sum(part)
    heads_grad[at, :] = total
    pos_grad_ref[...] += jnp.sum(total.reshape(-1, 8, 768), axis=0)

    @pl.when(step == blocks - 1)
    def _():
        me = info[1]
        own = pl.ds(pl.multiple_of(me * 16, 16), 16)
        own_ref[...] = result[own, :]
        own_grad_ref[...] = heads_grad[own, :]

        def chosen(left, rows):
            width = left.shape[1]
            wanted = lax.broadcasted_iota(jnp.int32, (rows, width), 1) - lax.broadcasted_iota(
                jnp.int32, (rows, width), 0
            )
            pick = (wanted == me * rows).astype(F32).astype(LOW)
            return mm_nt(pick, left).astype(LOW)

        left = chosen(lefts[0], 24)
        for j in range(3):
            qkv_grad_ref[:, j * 768 : (j + 1) * 768] = mm(left, rights[2 + j])
        out_grad_ref[...] = mm(chosen(lefts[1], 24), rights[0])
        left = chosen(lefts[2], 24)
        for j in range(4):
            cols = slice(j * 768, (j + 1) * 768)
            up_grad_ref[:, cols] = mm(left, hidden_grad[:, cols])
        for j in range(4):
            left = chosen(act[:, j * 768 : (j + 1) * 768], 24)
            down_grad_ref[j * 24 : (j + 1) * 24, :] = mm(left, rights[1])


def column_sum(value):
    return jnp.sum(value.astype(F32), axis=0, keepdims=True)


def ffn_backward_kernel(segs, seg_count, info, cot_ref, heads_grad_ref, heads_ref, second_ref, sum_ref, slope_ref, vec_ref, *rest):
    pieces, more, rest = rest[:10], rest[10:18], rest[18:]
    (out_ref, down_grad_ref, hidden_grad_ref, proj_grad_ref, mixed_grad_ref, grads_ref, out, up, down, sems) = rest
    step = pl.program_id(0)

    @pl.when(step == 0)
    def _():
        copies = slab_copies(info[0], more, down_slabs(down), sems, 40)
        load(copies + slab_copies(info[0], pieces, mid_slabs(out, up), sems))
        grads_ref[...] = jnp.zeros_like(grads_ref)

    count = segs * SEG
    normed, inv_scale = normalize(second_ref[...])
    row = lax.broadcasted_iota(jnp.int32, (SEG, 1), 0)
    result = normed * (1.0 + vec_ref[10:11, :]) + vec_ref[11:12, :]
    ups = []
    for s in range(segs):
        seg = step * segs + s
        at = slice(s * SEG, (s + 1) * SEG)
        live = row + seg % seg_count * SEG < info[1 + seg // seg_count]
        opens = row == 0
        merged = jnp.where(opens, heads_ref[s : s + 1, :], result[at])
        out_ref[at, :] = jnp.where(live, merged, 0.0).astype(LOW)
        grad = jnp.where(live, cot_ref[at, :].astype(F32), 0.0)
        ups.append(jnp.where(opens, heads_grad_ref[s : s + 1, :], grad))
    upstream = jnp.concatenate(ups, axis=0)
    back_two = normalize_back(upstream * (1.0 + vec_ref[10:11, :]), normed, inv_scale)
    down_grad = back_two.astype(LOW)
    down_grad_ref[...] = down_grad
    grads_ref[9:10, :] += column_sum(down_grad)
    grads_ref[10:11, :] += column_sum(upstream * normed)
    grads_ref[11:12, :] += column_sum(upstream)
    total = back_two
    for j in range(4):
        cols = slice(j * 768, (j + 1) * 768)
        grad = mm_nt(down_grad, down[cols, :]) * slope_ref[:, cols].astype(F32)
        grad = grad.astype(LOW)
        hidden_grad_ref[:, cols] = grad
        grads_ref[5 + j : 6 + j, :] += column_sum(grad)
        total = total + mm_nt(grad, up[j])
    normed, inv_scale = normalize(sum_ref[...])
    back_one = normalize_back(total * (1.0 + vec_ref[3:4, :]), normed, inv_scale)
    proj_grad = back_one.astype(LOW)
    proj_grad_ref[...] = proj_grad
    mixed_grad_ref[...] = mm_nt(proj_grad, out[...]).astype(LOW)
    grads_ref[2:3, :] += column_sum(proj_grad)
    grads_ref[3:4, :] += column_sum(total * normed)
    grads_ref[4:5, :] += column_sum(total)


def attn_backward_kernel(segs, seg_count, first_step, info, packed_ref, mixed_grad_ref, *rest):
    packed_grad_ref, grads_ref = rest[-2:]
    step = pl.program_id(0)

    @pl.when(step == 0)
    def _():
        grads_ref[...] = jnp.zeros_like(grads_ref)

    for s in range(segs):
        seg = (step + first_step) * segs + s
        allowed = segment_mask(info[1 + seg // seg_count], seg % seg_count)
        at = slice(s * SEG, (s + 1) * SEG)
        for h in range(6):
            cols = [slice(j * 768 + h * 128, j * 768 + (h + 1) * 128) for j in range(3)]
            q, k, v = (packed_ref[at, c] for c in cols)
            grads = attend_back(q, k, v, mixed_grad_ref[at, cols[0]], allowed)
            for c, g in zip(cols, grads):
                packed_grad_ref[at, c] = g.astype(LOW)
    grads_ref[0:1, :] += column_sum(packed_grad_ref[:, :768])
    grads_ref[1:2, :] += column_sum(packed_grad_ref[:, 1536:])


def token_grad_kernel(info, packed_grad_ref, proj_grad_ref, *rest):
    pieces, (token_grad_ref, qkv, sems) = rest[:10], rest[10:]

    @pl.when(pl.program_id(0) == 0)
    def _():
        load(slab_copies(info[0], pieces, qkv_slabs(qkv), sems))

    total = proj_grad_ref[...].astype(F32)
    for j in range(3):
        total = total + mm_nt(packed_grad_ref[:, j * 768 : (j + 1) * 768], qkv[j])
    token_grad_ref[...] = total.astype(LOW)


def send_slab(place, total, keep_ref, send_ref, rows):
    for mask in range(8):
        block = pl.multiple_of((place ^ mask) * rows, rows)
        target = send_ref if mask % 2 else keep_ref
        target[mask // 2] = total[pl.ds(block, rows), :].astype(LOW)


def qkv_grad_kernel(info, left_ref, right_ref, more_ref, keep_ref, send_ref, total):
    step = pl.program_id(0)
    total[...] = mm_tn(left_ref[...], right_ref[...])
    at = pl.ds(pl.multiple_of(step * 96, 96), 96)
    for mask in range(8):
        block = pl.multiple_of((info[0] ^ mask) * 96, 96)
        target = send_ref if mask % 2 else keep_ref
        target[mask // 2, at, :] = total[pl.ds(block, 96), :].astype(LOW)

    @pl.when(step == 0)
    def _():
        for mask in range(8):
            target = send_ref if mask % 2 else keep_ref
            target[mask // 2, 288:304, :] = more_ref[mask]


def mid_grad_kernel(info, mixed_ref, proj_ref, low_ref, hidden_ref, keep_ref, send_ref, total):
    @pl.when(pl.program_id(0) == 0)
    def _():
        total[...] = mm_tn(mixed_ref[...], proj_ref[...])

    @pl.when(pl.program_id(0) > 0)
    def _():
        total[...] = mm_tn(low_ref[...], hidden_ref[...])

    send_slab(info[0], total, keep_ref, send_ref, 96)


ANY = pl.BlockSpec(memory_space=pl.ANY)
SMEM = pl.BlockSpec(memory_space=pltpu.SMEM)


def block_rows(count, width):
    return pl.BlockSpec((count, width), lambda i: (i, 0))


def fixed(shape):
    return pl.BlockSpec(shape, lambda i: (0,) * len(shape))


def shape_of(dims, kind=LOW):
    return jax.ShapeDtypeStruct(dims, kind)


def params():
    return pltpu.CompilerParams(vmem_limit_bytes=VMEM, dimension_semantics=("arbitrary",))


def cost(flops, size):
    return pl.CostEstimate(flops=flops, bytes_accessed=size, transcendentals=0)


QKV = [pltpu.VMEM((3, 768, 768), LOW)]
MID = [pltpu.VMEM((768, 768), LOW), pltpu.VMEM((4, 768, 768), LOW)]
DOWN = [pltpu.VMEM((3072, 768), LOW)]


def sems(count):
    return [pltpu.SemaphoreType.DMA((count,))]


def shifted(count, width, first):
    return pl.BlockSpec((count, width), lambda i: (i + first, 0))


def attn_forward(info, rows_in, vec, pieces, seg_count, half, before=None, segs=4):
    rows = rows_in.shape[0]
    count = segs * SEG
    steps = rows // count // 2
    first = half * steps
    before = list(before or [])
    return pl.pallas_call(
        functools.partial(attn_forward_kernel, segs, seg_count, first),
        grid=(steps,),
        in_specs=[SMEM, shifted(count, 768, first), fixed((12, 768))] + [ANY] * (10 + len(before)),
        out_specs=[shifted(count, 2304, first), shifted(count, 768, first)],
        out_shape=[shape_of((rows, 2304)), shape_of((rows, 768))],
        scratch_shapes=QKV + sems(24),
        input_output_aliases={13: 0, 14: 1} if before else {},
        compiler_params=params(),
        cost_estimate=cost(rows * 768 * 8000, rows * 768 * 8),
        name="attn_forward",
    )(info, rows_in, vec, *pieces, *before)


def mid_forward(info, rows_in, mixed, vec, pieces, segs=2):
    rows = rows_in.shape[0]
    count = segs * SEG
    return pl.pallas_call(
        mid_forward_kernel,
        grid=(rows // count,),
        in_specs=[SMEM, block_rows(count, 768), block_rows(count, 768), fixed((12, 768))] + [ANY] * 10,
        out_specs=[block_rows(count, 768), block_rows(count, 768), block_rows(count, 3072), block_rows(count, 3072)],
        out_shape=[shape_of((rows, 768), F32), shape_of((rows, 768)), shape_of((rows, 3072)), shape_of((rows, 3072))],
        scratch_shapes=MID + sems(40),
        compiler_params=params(),
        cost_estimate=cost(2 * rows * 768 * 8000, rows * 768 * 30),
        name="mid_forward",
    )(info, rows_in, mixed, vec, *pieces)


def down_forward(info, summed, act, vec, pieces, segs=2):
    rows = summed.shape[0]
    count = segs * SEG
    few = pl.BlockSpec((None, segs, 768), lambda i: (i, 0, 0))
    return pl.pallas_call(
        functools.partial(down_forward_kernel, segs),
        grid=(rows // count,),
        in_specs=[SMEM, block_rows(count, 768), block_rows(count, 3072), fixed((12, 768))] + [ANY] * 8,
        out_specs=[block_rows(count, 768), few],
        out_shape=[shape_of((rows, 768), F32), shape_of((rows // count, segs, 768), F32)],
        scratch_shapes=DOWN + sems(32),
        compiler_params=params(),
        cost_estimate=cost(2 * rows * 768 * 4000, rows * 768 * 16),
        name="down_forward",
    )(info, summed, act, vec, *pieces)


def cross_whole(info, heads, upstream, live, vec, positions, wide):
    rows = heads.shape[0]
    count = 2 * SEG
    own = [(16, 768), (16, 768), (12, 768), (8, 768), (24, 2304), (24, 768), (24, 3072), (96, 768)]
    return pl.pallas_call(
        functools.partial(cross_kernel, rows // count),
        grid=(rows // count,),
        in_specs=[SMEM, block_rows(count, 768), block_rows(count, 768), block_rows(count, SEG),
                  fixed((12, 768)), fixed((8, 768)), ANY],
        out_specs=[fixed(dims) for dims in own],
        out_shape=[shape_of(dims, F32) for dims in own],
        scratch_shapes=QKV + MID + DOWN + sems(12) + [
            pltpu.VMEM((rows, 768), F32), pltpu.VMEM((rows, 768), F32), pltpu.VMEM((count, 3072), LOW),
            pltpu.VMEM((3, rows, 768), LOW), pltpu.VMEM((rows, 3072), LOW), pltpu.VMEM((count, 2304), LOW),
            pltpu.VMEM((5, rows, 768), LOW), pltpu.VMEM((rows, 3072), LOW),
        ],
        compiler_params=params(),
        cost_estimate=cost(2 * rows * 768 * 30000, 2**24),
        name="cross_encoder",
    )(info, heads, upstream, live, vec, positions, wide)


def ffn_backward(info, cotangent, heads_grad, heads, second, summed, slope, vec, mid, down, seg_count, segs=2):
    rows = summed.shape[0]
    count = segs * SEG
    few = pl.BlockSpec((None, segs, 768), lambda i: (i, 0, 0))
    return pl.pallas_call(
        functools.partial(ffn_backward_kernel, segs, seg_count),
        grid=(rows // count,),
        in_specs=[SMEM, block_rows(count, 768), few, few, block_rows(count, 768), block_rows(count, 768),
                  block_rows(count, 3072), fixed((12, 768))] + [ANY] * 18,
        out_specs=[block_rows(count, 768), block_rows(count, 768), block_rows(count, 3072), block_rows(count, 768),
                   block_rows(count, 768), fixed((12, 768))],
        out_shape=[shape_of((rows, 768)), shape_of((rows, 768)), shape_of((rows, 3072)), shape_of((rows, 768)),
                   shape_of((rows, 768)), shape_of((12, 768), F32)],
        scratch_shapes=MID + DOWN + sems(72),
        compiler_params=params(),
        cost_estimate=cost(2 * rows * 768 * 14000, rows * 768 * 30),
        name="ffn_backward",
    )(info, cotangent, heads_grad.reshape(-1, segs, 768), heads.reshape(-1, segs, 768), second, summed, slope, vec, *mid, *down)


def attn_backward(info, packed, mixed_grad, seg_count, half, before=None, segs=2):
    rows = packed.shape[0]
    count = segs * SEG
    steps = rows // count // 2
    first = half * steps
    before = [] if before is None else [before]
    return pl.pallas_call(
        functools.partial(attn_backward_kernel, segs, seg_count, first),
        grid=(steps,),
        in_specs=[SMEM, shifted(count, 2304, first), shifted(count, 768, first)] + [ANY] * len(before),
        out_specs=[shifted(count, 2304, first), fixed((2, 768))],
        out_shape=[shape_of((rows, 2304)), shape_of((2, 768), F32)],
        input_output_aliases={3: 0} if before else {},
        compiler_params=params(),
        cost_estimate=cost(rows * 768 * 10000, rows * 768 * 8),
        name="attn_backward",
    )(info, packed, mixed_grad, *before)


def token_gradient(info, packed_grad, proj_grad, pieces, count=512):
    rows = packed_grad.shape[0]
    return pl.pallas_call(
        token_grad_kernel,
        grid=(rows // count,),
        in_specs=[SMEM, block_rows(count, 2304), block_rows(count, 768)] + [ANY] * 10,
        out_specs=block_rows(count, 768),
        out_shape=shape_of((rows, 768)),
        scratch_shapes=QKV + sems(24),
        compiler_params=params(),
        cost_estimate=cost(2 * rows * 768 * 3000, rows * 768 * 10),
        name="token_gradient",
    )(info, packed_grad, proj_grad, *pieces)


def grad_outs(slabs):
    out = pl.BlockSpec((4, 96, 768), lambda i: (0, i, 0))
    return [out, out], [shape_of((4, slabs * 96, 768))] * 2


def qkv_weight_grad(info, left, right, more):
    rows = left.shape[0]
    out = fixed((4, 304, 768))
    return pl.pallas_call(
        qkv_grad_kernel,
        grid=(3,),
        in_specs=[SMEM, fixed((rows, 768)), pl.BlockSpec((rows, 768), lambda i: (0, i)), fixed((8, 16, 768))],
        out_specs=[out, out],
        out_shape=[shape_of((4, 304, 768))] * 2,
        scratch_shapes=[pltpu.VMEM((768, 768), F32)],
        compiler_params=params(),
        cost_estimate=cost(2 * rows * 768 * 2304, rows * 2304 * 2),
        name="qkv_weight_grad",
    )(info, left, right, more)


def mid_weight_grad(info, mixed, proj_grad, low, hidden_grad):
    rows = mixed.shape[0]
    specs, shapes = grad_outs(5)
    still = fixed((rows, 768))
    return pl.pallas_call(
        mid_grad_kernel,
        grid=(5,),
        in_specs=[SMEM, still, still, still, pl.BlockSpec((rows, 768), lambda i: (0, jnp.maximum(i - 1, 0)))],
        out_specs=specs,
        out_shape=shapes,
        scratch_shapes=[pltpu.VMEM((768, 768), F32)],
        compiler_params=params(),
        cost_estimate=cost(2 * rows * 768 * 3840, rows * 3840 * 2),
        name="mid_weight_grad",
    )(info, mixed, proj_grad, low, hidden_grad)


def down_grad_kernel(info, left_ref, right_ref, keep_ref, send_ref, total):
    step = pl.program_id(0)
    total[pl.ds(pl.multiple_of(step * 768, 768), 768), :] = mm_tn(left_ref[...], right_ref[...]).astype(LOW)

    @pl.when(step == pl.num_programs(0) - 1)
    def _():
        for mask in range(8):
            block = pl.multiple_of((info[0] ^ mask) * 384, 384)
            target = send_ref if mask % 2 else keep_ref
            target[mask // 2] = total[pl.ds(block, 384), :]


def down_weight_grad(info, left, right):
    rows, wide = left.shape
    return pl.pallas_call(
        down_grad_kernel,
        grid=(wide // 768,),
        in_specs=[SMEM, pl.BlockSpec((rows, 768), lambda i: (0, i)), fixed((rows, 768))],
        out_specs=[fixed((4, 384, 768))] * 2,
        out_shape=[shape_of((4, 384, 768))] * 2,
        scratch_shapes=[pltpu.VMEM((3072, 768), LOW)],
        compiler_params=params(),
        cost_estimate=cost(2 * rows * 768 * wide, rows * wide * 2),
        name="down_weight_grad",
    )(info, left, right)


def matmul(left_op, right_op):
    return jnp.dot(left_op, right_op, preferred_element_type=jnp.float32)


def trans_left(left_op, right_op):
    return lax.dot_general(
        left_op, right_op, (((0,), (0,)), ((), ())), preferred_element_type=jnp.float32
    )


def trans_right(left_op, right_op):
    return lax.dot_general(
        left_op, right_op, (((1,), (1,)), ((), ())), preferred_element_type=jnp.float32
    )


def norm_forward(summed, gain_row, shift_row):
    average = jnp.mean(summed, axis=-1, keepdims=True)
    centered = summed - average
    inv_scale = lax.rsqrt(jnp.mean(centered * centered, axis=-1, keepdims=True) + NORM_EPS)
    normed = centered * inv_scale
    return (normed * (1.0 + gain_row) + shift_row, normed, inv_scale)


def norm_backward(upstream, normed, inv_scale, gain_row):
    inner = upstream * (1.0 + gain_row)
    back_grad = inv_scale * (
        inner
        - jnp.mean(inner, axis=-1, keepdims=True)
        - normed * jnp.mean(inner * normed, axis=-1, keepdims=True)
    )
    return (back_grad, jnp.sum(upstream * normed, axis=0), jnp.sum(upstream, axis=0))


def gelu_slope(hidden):
    return (
        0.5 * (1.0 + lax.erf(hidden * ROOT_HALF))
        + hidden * jnp.exp(-0.5 * hidden * hidden) * INV_ROOT_TAU
    )


def split_heads(packed, group_len):
    head_count = packed.shape[1] // (3 * HEAD)
    return [
        portion.reshape(-1, group_len, head_count, HEAD) for portion in jnp.split(packed, 3, axis=1)
    ]


def masked_scores(query_heads, key_heads, allowed):
    raw_scores = jnp.einsum(
        "nqhd,nkhd->nhqk", query_heads, key_heads, preferred_element_type=jnp.float32
    ) * HEAD ** (-0.5)
    return jnp.where(allowed[:, None, None, :], raw_scores, MASK_FILL)


def encode(inputs, inputs_low, weights, allowed):
    qkv_w, out_w, up_w, down_w, vectors = weights
    row_count, feat_dim = inputs_low.shape
    group_len = allowed.shape[1]
    qkv_bias = jnp.concatenate([vectors[0], jnp.zeros_like(vectors[0]), vectors[1]])
    packed = (matmul(inputs_low, qkv_w) + qkv_bias).astype(jnp.bfloat16)
    query_heads, key_heads, value_heads = split_heads(packed, group_len)
    scores = masked_scores(query_heads, key_heads, allowed)
    row_max = jnp.max(scores, axis=-1, keepdims=True)
    expo_vals = jnp.exp(scores - row_max)
    row_total = jnp.sum(expo_vals, axis=-1, keepdims=True)
    log_total = row_max + jnp.log(row_total)
    prob_low = (expo_vals / row_total).astype(jnp.bfloat16)
    mixed = jnp.einsum("nhqk,nkhd->nqhd", prob_low, value_heads, preferred_element_type=jnp.float32)
    mixed = mixed.reshape(row_count, feat_dim).astype(jnp.bfloat16)
    projected = matmul(mixed, out_w) + vectors[2]
    first_out, normed_one, scale_one = norm_forward(inputs + projected, vectors[3], vectors[4])
    first_low = first_out.astype(jnp.bfloat16)
    hidden = matmul(first_low, up_w) + vectors[5:-3].reshape(-1)
    activated = jax.nn.gelu(hidden, approximate=False).astype(jnp.bfloat16)
    down_out = matmul(activated, down_w) + vectors[-3]
    result, normed_two, scale_two = norm_forward(first_out + down_out, vectors[-2], vectors[-1])
    return (
        result,
        (
            packed,
            log_total,
            mixed,
            normed_one,
            scale_one,
            first_low,
            hidden,
            activated,
            normed_two,
            scale_two,
        ),
    )


def encode_back(upstream, inputs_low, weights, allowed, kept):
    qkv_w, out_w, up_w, down_w, vectors = weights
    (
        packed,
        log_total,
        mixed,
        normed_one,
        scale_one,
        first_low,
        hidden,
        activated,
        normed_two,
        scale_two,
    ) = kept
    row_count, feat_dim = inputs_low.shape
    group_len = allowed.shape[1]
    back_two, gain_two, shift_two = norm_backward(upstream, normed_two, scale_two, vectors[-2])
    down_grad = back_two.astype(jnp.bfloat16)
    hidden_grad = (trans_right(down_grad, down_w) * gelu_slope(hidden)).astype(jnp.bfloat16)
    first_grad = trans_right(hidden_grad, up_w) + back_two
    back_one, gain_one, shift_one = norm_backward(first_grad, normed_one, scale_one, vectors[3])
    proj_grad = back_one.astype(jnp.bfloat16)
    query_heads, key_heads, value_heads = split_heads(packed, group_len)
    mixed_grad = trans_right(proj_grad, out_w).astype(jnp.bfloat16).reshape(value_heads.shape)
    scores = masked_scores(query_heads, key_heads, allowed)
    prob_vals = jnp.exp(scores - log_total)
    grad_values = jnp.einsum(
        "nhqk,nqhd->nkhd",
        prob_vals.astype(jnp.bfloat16),
        mixed_grad,
        preferred_element_type=jnp.float32,
    )
    grad_prob = jnp.einsum(
        "nqhd,nkhd->nhqk", mixed_grad, value_heads, preferred_element_type=jnp.float32
    )
    score_grad = (
        prob_vals * (grad_prob - jnp.sum(prob_vals * grad_prob, axis=-1, keepdims=True))
    ).astype(jnp.bfloat16)
    grad_query = jnp.einsum(
        "nhqk,nkhd->nqhd", score_grad, key_heads, preferred_element_type=jnp.float32
    ) * HEAD ** (-0.5)
    grad_keys = jnp.einsum(
        "nhqk,nqhd->nkhd", score_grad, query_heads, preferred_element_type=jnp.float32
    ) * HEAD ** (-0.5)
    packed_grad = jnp.concatenate(
        [
            grad_query.reshape(row_count, feat_dim),
            grad_keys.reshape(row_count, feat_dim),
            grad_values.reshape(row_count, feat_dim),
        ],
        axis=1,
    ).astype(jnp.bfloat16)
    bias_grads = jnp.sum(packed_grad, axis=0, dtype=jnp.float32).reshape(3, feat_dim)
    grad_inputs = trans_right(packed_grad, qkv_w) + back_one
    grad_vectors = jnp.concatenate(
        [
            bias_grads[0:1],
            bias_grads[2:3],
            jnp.sum(proj_grad, axis=0, dtype=jnp.float32)[None],
            gain_one[None],
            shift_one[None],
            jnp.sum(hidden_grad, axis=0, dtype=jnp.float32).reshape(-1, feat_dim),
            jnp.sum(down_grad, axis=0, dtype=jnp.float32)[None],
            gain_two[None],
            shift_two[None],
        ],
        axis=0,
    )
    pairs = (
        (inputs_low, packed_grad),
        (mixed, proj_grad),
        (first_low, hidden_grad),
        (activated, down_grad),
    )
    return (grad_inputs, pairs, grad_vectors)


class Links:
    def __init__(self, outer, inner):
        self.outer, self.inner = outer, inner
        self.order = self.place = lax.axis_index("dp")
        self.z = lax.axis_index("fsdp")

    def flip(self, value, mask):
        pairs = [
            (d * self.inner + z, (d ^ mask) * self.inner + z)
            for d in range(self.outer)
            for z in range(self.inner)
        ]
        return lax.ppermute(value, AXES, pairs)

    def turn(self, value, step):
        pairs = [
            (d * self.inner + z, d * self.inner + (z + step) % self.inner)
            for d in range(self.outer)
            for z in range(self.inner)
        ]
        return lax.ppermute(value, AXES, pairs)

    def gather_z(self, shard):
        came = [shard] + [self.turn(shard, step) for step in range(1, self.inner)]
        whole = []
        for z in range(self.inner):
            part = came[-1]
            for step in range(self.inner - 1):
                part = jnp.where(self.z == (z + step) % self.inner, came[step], part)
            whole.append(part)
        return whole

    def spread_near(self, block):
        return self.flip(block, 2), self.flip(block, 4)

    def spread_far(self, by_x, by_y, half):
        return self.flip(by_y[:half], 2), self.flip(by_x[half:], 4)

    def spread_core(self, mine):
        return list(mine) + [self.flip(piece, 1) for piece in mine]

    def in_order(self, parts):
        for axis, mask in ((4, 4), (2, 2), (1, 1)):
            odd = self.place // axis % 2 == 1
            parts = [jnp.where(odd, parts[m ^ mask], parts[m]) for m in range(8)]
        return jnp.stack(parts)

    def gather_small(self, shard):
        block = jnp.stack(self.gather_z(shard))
        near = [block] + [self.flip(block, m) for m in (2, 4, 6)]
        plane = jnp.stack(near)
        other = self.flip(plane, 1)
        whole = self.in_order([(plane, other)[m % 2][m // 2] for m in range(8)])
        return whole.reshape((-1,) + shard.shape)


class PlainLinks:
    def __init__(self, outer, inner):
        self.outer, self.inner = outer, inner
        self.order = lax.axis_index("dp")
        self.z = lax.axis_index("fsdp")
        self.place = 0

    def gather_small(self, shard):
        return lax.all_gather(shard, AXES, axis=0)


def add(*terms):
    return sum(t.astype(F32) for t in terms).astype(LOW)


class Sum:
    def __init__(self, links, keep, send, slabs):
        self.links, self.keep, self.slabs = links, keep, slabs
        self.more = keep.shape[1] % 96
        self.came = links.flip(send, 1)

    def line(self, part):
        inner = self.links.inner
        count = part.shape[0] - self.more
        main = part[:count].reshape(self.slabs, inner, -1, part.shape[-1])
        main = main.transpose(1, 0, 2, 3).reshape(inner, -1, part.shape[-1])
        if not self.more:
            return main
        rows = part[count : count + inner].reshape(inner, 1, -1)
        return jnp.concatenate([main, jnp.pad(rows, ((0, 0), (0, 7), (0, 0)))], axis=1)

    def to(self, index):
        return self.line(add(self.keep[index], self.came[index]))

    def far(self):
        half = self.links.inner // 2
        to_d = self.to(3)
        self.far_came = [self.links.flip(to_d[:half], 2), self.links.flip(to_d[half:], 4)]
        return self.far_came

    def near(self):
        half = self.links.inner // 2
        came_x, came_y = self.far_came
        to_x, to_y = self.to(1), self.to(2)
        to_y = jnp.concatenate([add(to_y[:half], came_x), to_y[half:]])
        to_x = jnp.concatenate([to_x[:half], add(to_x[half:], came_y)])
        self.near_came = [self.links.flip(to_x, 2), self.links.flip(to_y, 4)]
        return self.near_came

    def direct(self):
        self.near_came = [self.links.flip(self.to(m // 2), m) for m in (2, 4, 6)]
        return self.near_came

    def turn(self, *earlier):
        links = self.links
        own = add(self.line(self.keep[0]), self.line(self.came[0]), *self.near_came)
        own = after(own, *earlier) if earlier else own
        parts = [lax.dynamic_index_in_dim(own, (links.z + k) % links.inner, 0, keepdims=False) for k in range(links.inner)]
        self.turned = [parts[0]] + [links.turn(parts[k], k) for k in range(1, links.inner)]
        return self.turned[1:]

    def total(self):
        return sum(t.astype(F32) for t in self.turned)


class PlainSum:
    def __init__(self, links, keep, send, slabs):
        more = keep.shape[1] % 96
        flat = jnp.stack([keep, send], axis=1).reshape(8, -1, 768)
        main = flat[:, : flat.shape[1] - more].reshape(8, slabs, -1, 768)
        main = main.transpose(1, 0, 2, 3).reshape(slabs, -1, 768)
        self.came = keep
        self.sums = lax.psum_scatter(main, AXES, scatter_dimension=1, tiled=True).reshape(-1, 768)
        if more:
            rows = flat[:, flat.shape[1] - more :][:, : links.outer * links.inner // 8].reshape(-1, 768)
            self.sums = jnp.concatenate([self.sums, lax.psum_scatter(rows, AXES, scatter_dimension=0, tiled=True)])

    def far(self, *earlier):
        return []

    near = direct = turn = far

    def total(self):
        return self.sums.astype(F32)


def after(value, *earlier):
    return lax.optimization_barrier((value, *earlier))[0]


def slabs_of(matrix):
    rows, wide = matrix.shape
    return matrix.reshape(rows, wide // 768, 768).transpose(1, 0, 2)


def matrix_of(slabs):
    count, rows, width = slabs.shape
    return slabs.transpose(1, 0, 2).reshape(rows, count * width)


def mix_columns(matrix, devices):
    rows, wide = matrix.shape
    matrix = matrix.reshape(rows, devices, 4, -1).transpose(0, 2, 1, 3)
    return matrix.reshape(rows, wide)


def unmix_columns(matrix, devices):
    rows, wide = matrix.shape
    matrix = matrix.reshape(rows, 4, devices, -1).transpose(0, 2, 1, 3)
    return matrix.reshape(rows, wide)


def plain_pieces(slabs, whole):
    count = slabs.shape[0]
    half = (count + 1) // 2 * 96
    parts = []
    for mask in (0, 2, 4, 6, 1, 3, 5, 7):
        part = slabs[:, mask * 96 : (mask + 1) * 96].reshape(-1, 768)
        parts += [part] if whole or mask < 6 and mask != 7 else [part[:half], part[half:]]
    return parts


def shards(
    outer,
    inner,
    tokens,
    cotangent,
    lengths,
    seg_qkv,
    seg_out,
    seg_up,
    seg_down,
    seg_vec,
    cross_qkv,
    cross_out,
    cross_up,
    cross_down,
    cross_vec,
    positions,
):
    fast = (outer, inner) == (8, 4)
    links = (Links if fast else PlainLinks)(outer, inner)
    summing = Sum if fast else PlainSum
    devices = outer * inner
    me = links.order * inner + links.z
    seq_local, seq_len, feat_dim = tokens.shape
    seg_count = seq_len // SEG
    seg_rows, cross_rows = seg_vec.shape[0], cross_vec.shape[0]
    width = feat_dim // devices
    my_lengths = lax.dynamic_slice_in_dim(lengths, me * seq_local, seq_local)
    info = jnp.concatenate([jnp.full((1,), links.place, jnp.int32), my_lengths])
    small = jnp.concatenate([seg_vec, cross_vec, positions]).reshape(1, -1)
    up_slabs = mix_columns(cross_up, devices).reshape(-1, 4, feat_dim).transpose(1, 0, 2)
    wide = [slabs_of(cross_qkv), slabs_of(cross_out), up_slabs, cross_down.reshape(4, -1, feat_dim)]
    wide = jnp.concatenate(wide)
    mid_shard = jnp.concatenate([slabs_of(seg_out), slabs_of(seg_up)])
    rows_in = tokens.reshape(-1, feat_dim)
    cot_rows = cotangent.reshape(-1, feat_dim)
    seg_starts = jnp.arange(seg_count) * SEG
    live_own = (seg_starts[None, :] < my_lengths[:, None]).reshape(-1, 1)
    up_own = jnp.where(live_own, cotangent.reshape(-1, SEG, feat_dim)[:, 0, :], 0)

    if fast:
        first = jnp.concatenate([slabs_of(seg_qkv).reshape(-1, 768), jnp.pad(small, ((0, 7), (0, 0)))])
        line_first = links.gather_z(first)
        line_mid = links.gather_z(after(mid_shard, *line_first))
        line_down = links.gather_z(after(seg_down, *line_mid))
        weights = jnp.stack([p[:72].reshape(3, 24, 768) for p in line_first], axis=1).reshape(-1, 768)
        rows = jnp.concatenate([p[72:73] for p in line_first])
        block = jnp.concatenate([weights, jnp.pad(rows, ((0, 12), (0, 0)))])
        near = links.spread_near(block)
        wide = after(wide, *line_mid, *near)
        far = links.spread_far(*(after(p, *line_mid) for p in near), 192)
        first = links.spread_core([block, *near, *far])
        ends = [p[288:292] for p in first[:3]] + [first[4][96:100]]
        others = [p[288:292] for p in first[5:8]] + [first[9][96:100]]
        small = links.in_order([(ends, others)[m % 2][m // 2] for m in range(8)])
        block = after(jnp.stack(line_mid, axis=1).reshape(-1, 768), *far)
        mid = [block, *links.spread_near(block)]
    else:
        first = plain_pieces(lax.all_gather(slabs_of(seg_qkv), AXES, axis=1, tiled=True), False)
        mid = plain_pieces(lax.all_gather(mid_shard, AXES, axis=1, tiled=True), False)
        down_whole = lax.all_gather(seg_down, AXES, axis=0, tiled=True)
        down = [down_whole[m * 384 : (m + 1) * 384] for m in (0, 2, 4, 6, 1, 3, 5, 7)]
        small = links.gather_small(small)
    wide = lax.all_gather(wide, AXES, axis=1, tiled=True)
    small = small.reshape(devices, -1, width).transpose(1, 0, 2).reshape(-1, feat_dim).astype(F32)
    seg_v, cross_v = small[:seg_rows], small[seg_rows : seg_rows + cross_rows]
    pos_table = small[seg_rows + cross_rows :]
    hidden_rows = slice(5, cross_rows - 3)
    cross_v = cross_v.at[hidden_rows].set(mix_columns(cross_v[hidden_rows].reshape(1, -1), devices).reshape(-1, feat_dim))

    before = attn_forward(info, rows_in, seg_v, first, seg_count, 0)
    if fast:
        far = links.spread_far(*(after(p, before[0]) for p in mid[1:]), 288)
        rows_late = after(rows_in, *mid[1:])
    else:
        rows_late = rows_in
    packed, mixed = attn_forward(info, rows_late, seg_v, first, seg_count, 1, before)
    if fast:
        mid = [*mid, *far] + links.spread_core(mid)[3:] + [links.flip(after(p, packed), 1) for p in far]
        block = after(jnp.concatenate(line_down), *far)
        near = [links.flip(block, m) for m in (2, 4, 6)]
    summed, low, act, slope = mid_forward(info, rows_in, mixed, seg_v, mid)
    if fast:
        down = [block, *near, links.flip(block, 1), *(links.flip(after(p, act), 1) for p in near)]
    second, heads = down_forward(info, summed, act, seg_v, down)
    heads_own = heads.reshape(-1, feat_dim)
    both = links.gather_small(jnp.stack([heads_own.astype(LOW), up_own]))
    heads_all, up_all = both[:, 0].reshape(-1, feat_dim), both[:, 1].reshape(-1, feat_dim)
    live_all = seg_starts[None, :] < lengths[:, None]
    if fast:
        cross_info = jnp.stack([links.place, me]).astype(jnp.int32)
        live = jnp.broadcast_to(live_all.reshape(-1, 1), (live_all.size, SEG)).astype(F32)
        cross_own, heads_grad, vec_grad, pos_grad, *cross_grads = cross_whole(
            cross_info, heads_all, up_all, live, cross_v, pos_table, wide
        )
    else:
        weights = (matrix_of(wide[:3]), wide[3], matrix_of(wide[4:8]), wide[8:].reshape(-1, feat_dim), cross_v)
        heads_in = heads_all.astype(F32).reshape(-1, seg_count, feat_dim) + pos_table[None]
        heads_in = heads_in.reshape(-1, feat_dim)
        cross_result, kept = encode(heads_in, heads_in.astype(LOW), weights, live_all)
        all_grad, pairs, vec_grad = encode_back(
            up_all.astype(F32), heads_in.astype(LOW), weights, live_all, kept
        )
        cross_grads = []
        for left, right in pairs:
            left = left.reshape(left.shape[0], -1, feat_dim)
            mine = lax.dynamic_slice_in_dim(left, me * width, width, 2)
            cross_grads.append(trans_left(mine.reshape(left.shape[0], -1), right))
        pos_grad = jnp.sum(all_grad.reshape(-1, seg_count, feat_dim), axis=0)
        own = seq_local * seg_count
        cross_own = lax.dynamic_slice_in_dim(cross_result, me * own, own)
        heads_grad = lax.dynamic_slice_in_dim(all_grad, me * own, own)
    cross_grads[2] = unmix_columns(cross_grads[2], devices)
    vec_grad = vec_grad.at[hidden_rows].set(
        unmix_columns(vec_grad[hidden_rows].reshape(1, -1), devices).reshape(-1, feat_dim)
    )
    cross_vec_grad = lax.dynamic_slice_in_dim(vec_grad, me * width, width, 1)
    grad_positions = lax.dynamic_slice_in_dim(pos_grad, me * width, width, 1)

    layer_out, down_grad, hidden_grad, proj_grad, mixed_grad, grads_two = ffn_backward(
        info, cot_rows, heads_grad, cross_own, second, summed, slope, seg_v, mid, down, seg_count
    )
    down_sum = summing(links, *down_weight_grad(info, act, down_grad), 1)
    mid_parts = mid_weight_grad(info, mixed, proj_grad, low, after(hidden_grad, down_sum.keep if fast else down_sum.came))
    mid_sum = summing(links, *mid_parts, 5)
    half_grad, grads_one = attn_backward(
        info, packed, after(mixed_grad, mid_parts[1], down_sum.came), seg_count, 0
    )
    ready = after(mixed_grad, half_grad, *down_sum.far(), mid_sum.came)
    packed_grad, grads_more = attn_backward(info, packed, ready, seg_count, 1, half_grad)
    vec_parts = jnp.concatenate([grads_one + grads_more, grads_two[2:]]).reshape(seg_rows, devices, width)
    vec_parts = vec_parts.transpose(1, 0, 2).reshape(outer, inner, seg_rows * width).astype(LOW)
    if outer > 8:
        vec_parts = vec_parts.reshape(8, -1, seg_rows * width)
    vec_parts = jnp.pad(vec_parts, ((0, 0), (0, 16 - vec_parts.shape[1]), (0, feat_dim - seg_rows * width)))
    if fast:
        vec_parts = links.in_order(list(vec_parts))
    ready = after(packed_grad, *down_sum.near(), *mid_sum.far())
    keep, send = qkv_weight_grad(info, rows_in, ready, vec_parts)
    qkv_sum = summing(links, keep, after(send, *down_sum.turn(), *mid_sum.near()), 3)
    ready = after(packed_grad, qkv_sum.came)
    token_grad = token_gradient(info, ready, proj_grad, first)
    qkv_sum.direct()
    mid_sum.turn()
    qkv_sum.turn(token_grad)
    grad_down = down_sum.total()
    grad_mid = mid_sum.total().reshape(5, -1, feat_dim)
    total = qkv_sum.total()
    grad_qkv = matrix_of(total[: 3 * width].reshape(3, -1, feat_dim))
    grad_vec = total[3 * width, : seg_rows * width].reshape(seg_rows, width)
    return (
        layer_out.reshape(tokens.shape),
        token_grad.reshape(tokens.shape),
        grad_qkv,
        grad_mid[0],
        matrix_of(grad_mid[1:]),
        grad_down,
        grad_vec,
        *cross_grads,
        cross_vec_grad,
        grad_positions,
    )


def solution(mesh):
    in_specs = (
        P(("dp", "fsdp"), None, None),
        P(("dp", "fsdp"), None, None),
        P(),
        P(("dp", "fsdp"), None),
        P(("dp", "fsdp"), None),
        P(("dp", "fsdp"), None),
        P(("dp", "fsdp"), None),
        P(None, ("dp", "fsdp")),
        P(("dp", "fsdp"), None),
        P(("dp", "fsdp"), None),
        P(("dp", "fsdp"), None),
        P(("dp", "fsdp"), None),
        P(None, ("dp", "fsdp")),
        P(None, ("dp", "fsdp")),
    )
    out_specs = (
        P(("dp", "fsdp"), None, None),
        P(("dp", "fsdp"), None, None),
        P(("dp", "fsdp"), None),
        P(("dp", "fsdp"), None),
        P(("dp", "fsdp"), None),
        P(("dp", "fsdp"), None),
        P(None, ("dp", "fsdp")),
        P(("dp", "fsdp"), None),
        P(("dp", "fsdp"), None),
        P(("dp", "fsdp"), None),
        P(("dp", "fsdp"), None),
        P(None, ("dp", "fsdp")),
        P(None, ("dp", "fsdp")),
    )
    return jax.shard_map(
        functools.partial(shards, mesh.shape["dp"], mesh.shape["fsdp"]),
        mesh=mesh, in_specs=in_specs, out_specs=out_specs, check_vma=False)
```

```python
import functools

import jax
import jax.numpy as jnp
from jax import lax
from jax.experimental import pallas as pl
from jax.experimental.pallas import tpu as pltpu
from jax.sharding import PartitionSpec as P

HEAD = 64
SEG = 128
NORM_EPS = 1e-05
MASK_FILL = -1000000000.0
VMEM = 60 * 2**20
F32, LOW = jnp.float32, jnp.bfloat16


ROOT_HALF = 0.7071067811865476
INV_ROOT_TAU = 0.3989422804014327
AXES = ("dp", "fsdp")

def mm(left_op, right_op):
    return jnp.dot(left_op, right_op, preferred_element_type=F32)


def mm_nt(left_op, right_op):
    return lax.dot_general(left_op, right_op, (((1,), (1,)), ((), ())), preferred_element_type=F32)


def mm_tn(left_op, right_op):
    return lax.dot_general(left_op, right_op, (((0,), (0,)), ((), ())), preferred_element_type=F32)


def normalize(summed):
    average = jnp.mean(summed, axis=-1, keepdims=True)
    centered = summed - average
    inv_scale = lax.rsqrt(jnp.mean(centered * centered, axis=-1, keepdims=True) + NORM_EPS)
    return centered * inv_scale, inv_scale


def normalize_back(inner, normed, inv_scale):
    return inv_scale * (
        inner
        - jnp.mean(inner, axis=-1, keepdims=True)
        - normed * jnp.mean(inner * normed, axis=-1, keepdims=True)
    )


def gelu_parts(hidden):
    phi = 0.5 * (1.0 + lax.erf(hidden * ROOT_HALF))
    return hidden * phi, phi + hidden * jnp.exp(-0.5 * hidden * hidden) * INV_ROOT_TAU


def pair_stack(pair, low_half):
    zero = jnp.zeros_like(pair)
    return jnp.concatenate(
        [jnp.where(low_half, pair, zero), jnp.where(low_half, zero, pair)], axis=0
    )


def pair_merge(stacked, low_half):
    rows = stacked.shape[0] // 2
    return jnp.where(low_half, stacked[:rows], stacked[rows:])


def pair_probs(stack, keys, allowed):
    scores = jnp.where(allowed, mm_nt(keys, stack), MASK_FILL)
    expo = jnp.exp(scores - jnp.max(scores, axis=0, keepdims=True))
    return expo * (1.0 / jnp.sum(expo, axis=0, keepdims=True))


def attend(query, keys, values, allowed):
    low_half = lax.broadcasted_iota(jnp.int32, query.shape, 1) < HEAD
    stack = pair_stack(query * jnp.asarray(HEAD**-0.5, query.dtype), low_half)
    return pair_merge(mm_tn(pair_probs(stack, keys, allowed).astype(LOW), values), low_half)


def attend_back(query, keys, values, grad_mixed, allowed):
    low_half = lax.broadcasted_iota(jnp.int32, query.shape, 1) < HEAD
    stack = pair_stack(query * jnp.asarray(HEAD**-0.5, query.dtype), low_half)
    probs = pair_probs(stack, keys, allowed)
    grad_stack = pair_stack(grad_mixed, low_half)
    grad_prob = mm_nt(values, grad_stack)
    inner = jnp.sum(probs * grad_prob, axis=0, keepdims=True)
    score_grad = (probs * (grad_prob - inner)).astype(LOW)
    grad_query = pair_merge(mm_tn(score_grad, keys), low_half) * HEAD**-0.5
    return grad_query, mm(score_grad, stack), mm(probs.astype(LOW), grad_stack)


def slab_copies(place, pieces, slabs, sems, first_sem=0):
    count = len(slabs)
    half = (count + 1) // 2
    spans = [(0, 0, count), (2, 0, count), (4, 0, count)]
    spans += [(6, 0, count)] if len(pieces) == 8 else [(6, 0, half), (6, half, count)]
    copies = []
    for flip_c in (0, 1):
        for index, (flip_yx, first, last) in enumerate(spans):
            block = place ^ (flip_yx + flip_c)
            piece = pieces[flip_c * len(spans) + index]
            for slab in range(first, last):
                source = piece.at[pl.ds((slab - first) * 96, 96)]
                sem = sems.at[first_sem + slab * 8 + flip_yx + flip_c]
                copies.append(pltpu.make_async_copy(source, slabs[slab](block), sem))
    return copies


def load(copies):
    for copy in copies:
        copy.start()
    for copy in copies:
        copy.wait()


def rows_of(ref, block, rows=96, slab=None):
    where = pl.ds(pl.multiple_of(block * rows, rows), rows)
    return ref.at[where] if slab is None else ref.at[slab, where]


def down_rows(ref, block, part):
    return ref.at[pl.ds(pl.multiple_of(block * 384 + part * 96, 96), 96)]


def qkv_slabs(qkv):
    return [functools.partial(rows_of, qkv, slab=j) for j in range(3)]


def mid_slabs(out, up):
    return [functools.partial(rows_of, out)] + [functools.partial(rows_of, up, slab=j) for j in range(4)]


def down_slabs(down):
    return [functools.partial(down_rows, down, part=j) for j in range(4)]


def segment_mask(length, seg_in_seq):
    row = lax.broadcasted_iota(jnp.int32, (SEG, 2 * SEG), 0)
    return (row + seg_in_seq * SEG < length) | (row == 0)


def attn_forward_kernel(segs, seg_count, first_step, info, x_ref, vec_ref, *rest):
    pieces, (packed_ref, mixed_ref, qkv, sems) = rest[:10], rest[-4:]
    step = pl.program_id(0)

    @pl.when(step == 0)
    def _():
        load(slab_copies(info[0], pieces, qkv_slabs(qkv), sems))

    rows = x_ref[...]
    for j in range(3):
        part = mm(rows, qkv[j])
        if j != 1:
            part = part + vec_ref[j // 2 : j // 2 + 1, :]
        packed_ref[:, j * 768 : (j + 1) * 768] = part.astype(LOW)
    for s in range(segs):
        seg = (step + first_step) * segs + s
        allowed = segment_mask(info[1 + seg // seg_count], seg % seg_count)
        at = slice(s * SEG, (s + 1) * SEG)
        for h in range(6):
            q, k, v = (packed_ref[at, j * 768 + h * 128 : j * 768 + (h + 1) * 128] for j in range(3))
            mixed_ref[at, h * 128 : (h + 1) * 128] = attend(q, k, v, allowed).astype(LOW)


def norm_one(summed, vec_ref):
    normed, _ = normalize(summed)
    return normed * (1.0 + vec_ref[3:4, :]) + vec_ref[4:5, :]


def mid_forward_kernel(info, x_ref, mixed_ref, vec_ref, *rest):
    pieces, (sum_ref, low_ref, act_ref, slope_ref, out, up, sems) = rest[:10], rest[10:]

    @pl.when(pl.program_id(0) == 0)
    def _():
        load(slab_copies(info[0], pieces, mid_slabs(out, up), sems))

    summed = x_ref[...].astype(F32) + mm(mixed_ref[...], out[...]) + vec_ref[2:3, :]
    sum_ref[...] = summed
    first_low = norm_one(summed, vec_ref).astype(LOW)
    low_ref[...] = first_low
    hidden = mm(first_low, up[0]) + vec_ref[5:6, :]
    for j in range(4):
        later = mm(first_low, up[j + 1]) + vec_ref[6 + j : 7 + j, :] if j < 3 else None
        act, slope = gelu_parts(hidden)
        act_ref[:, j * 768 : (j + 1) * 768] = act.astype(LOW)
        slope_ref[:, j * 768 : (j + 1) * 768] = slope.astype(LOW)
        hidden = later


def down_forward_kernel(segs, info, sum_ref, act_ref, vec_ref, *rest):
    pieces, (second_ref, heads_ref, down, sems) = rest[:8], rest[8:]

    @pl.when(pl.program_id(0) == 0)
    def _():
        load(slab_copies(info[0], pieces, down_slabs(down), sems))

    total = norm_one(sum_ref[...], vec_ref) + vec_ref[9:10, :] + mm(act_ref[...], down[...])
    second_ref[...] = total
    opening = jnp.concatenate([total[s * SEG : s * SEG + 1] for s in range(segs)], axis=0)
    normed, _ = normalize(opening)
    heads_ref[...] = normed * (1.0 + vec_ref[10:11, :]) + vec_ref[11:12, :]


def cross_kernel(blocks, info, heads_ref, up_ref, live_ref, vec_ref, pos_ref, *rest):
    wide, rest = rest[0], rest[1:]
    (own_ref, own_grad_ref, grads_ref, pos_grad_ref, qkv_grad_ref, out_grad_ref, up_grad_ref, down_grad_ref) = rest[:8]
    (qkv, out, up, down, sems, result, heads_grad, slope, lefts, act, packed, rights, hidden_grad) = rest[8:]
    step = pl.program_id(0)
    count = heads_ref.shape[0]
    at = pl.ds(pl.multiple_of(step * count, count), count)
    targets = [qkv.at[j] for j in range(3)] + [out] + [up.at[j] for j in range(4)]
    targets += [down.at[j * 768 : (j + 1) * 768] for j in range(4)]
    copies = [pltpu.make_async_copy(wide.at[j], t, sems.at[j]) for j, t in enumerate(targets)]

    @pl.when(step == 0)
    def _():
        for copy in copies:
            copy.start()
        grads_ref[...] = jnp.zeros_like(grads_ref)
        pos_grad_ref[...] = jnp.zeros_like(pos_grad_ref)
        for copy in copies[:3]:
            copy.wait()

    vec = vec_ref[...]
    inputs = heads_ref[...].astype(F32).reshape(-1, 8, 768) + pos_ref[...][None]
    inputs = inputs.reshape(count, 768)
    low = inputs.astype(LOW)
    lefts[0, at, :] = low
    for j in range(3):
        part = mm(low, qkv[j])
        if j != 1:
            part = part + vec[j // 2 : j // 2 + 1]
        packed[:, j * 768 : (j + 1) * 768] = part.astype(LOW)
    row = lax.broadcasted_iota(jnp.int32, (SEG, 2 * SEG), 0)
    lane = lax.broadcasted_iota(jnp.int32, (SEG, 2 * SEG), 1)
    group = row // 8 == lane % SEG // 8
    masks = []
    for s in range(count // SEG):
        live = live_ref[s * SEG : (s + 1) * SEG, :]
        masks.append(group & (jnp.concatenate([live, live], axis=1) > 0.0))
    for s, allowed in enumerate(masks):
        part = slice(s * SEG, (s + 1) * SEG)
        for h in range(6):
            q, k, v = (packed[part, j * 768 + h * 128 : j * 768 + (h + 1) * 128] for j in range(3))
            where = pl.ds(pl.multiple_of(step * count + s * SEG, SEG), SEG)
            lefts[1, where, h * 128 : (h + 1) * 128] = attend(q, k, v, allowed).astype(LOW)

    @pl.when(step == 0)
    def _():
        for copy in copies[3:]:
            copy.wait()

    summed = inputs + mm(lefts[1, at, :], out[...]) + vec[2:3]
    normed_one, scale_one = normalize(summed)
    first = normed_one * (1.0 + vec[3:4]) + vec[4:5]
    first_low = first.astype(LOW)
    lefts[2, at, :] = first_low
    total = first + vec[9:10]
    for j in range(4):
        cols = slice(j * 768, (j + 1) * 768)
        hidden = mm(first_low, up[j]) + vec[5 + j : 6 + j]
        active, steep = gelu_parts(hidden)
        act[at, cols] = active.astype(LOW)
        slope[:, cols] = steep.astype(LOW)
        total = total + mm(active.astype(LOW), down[cols, :])
    normed, inv_scale = normalize(total)
    result[at, :] = normed * (1.0 + vec[10:11]) + vec[11:12]
    upstream = up_ref[...].astype(F32)
    back_two = normalize_back(upstream * (1.0 + vec[10:11]), normed, inv_scale)
    down_grad = back_two.astype(LOW)
    rights[1, at, :] = down_grad
    grads_ref[9:10, :] += column_sum(down_grad)
    grads_ref[10:11, :] += column_sum(upstream * normed)
    grads_ref[11:12, :] += column_sum(upstream)
    total = back_two
    for j in range(4):
        cols = slice(j * 768, (j + 1) * 768)
        grad = (mm_nt(down_grad, down[cols, :]) * slope[:, cols].astype(F32)).astype(LOW)
        hidden_grad[at, cols] = grad
        grads_ref[5 + j : 6 + j, :] += column_sum(grad)
        total = total + mm_nt(grad, up[j])
    back_one = normalize_back(total * (1.0 + vec[3:4]), normed_one, scale_one)
    proj_grad = back_one.astype(LOW)
    rights[0, at, :] = proj_grad
    grads_ref[2:3, :] += column_sum(proj_grad)
    grads_ref[3:4, :] += column_sum(total * normed_one)
    grads_ref[4:5, :] += column_sum(total)
    mixed_grad = mm_nt(proj_grad, out[...]).astype(LOW)
    for s, allowed in enumerate(masks):
        part = slice(s * SEG, (s + 1) * SEG)
        where = pl.ds(pl.multiple_of(step * count + s * SEG, SEG), SEG)
        for h in range(6):
            cols = slice(h * 128, (h + 1) * 128)
            q, k, v = (packed[part, j * 768 + h * 128 : j * 768 + (h + 1) * 128] for j in range(3))
            for j, g in enumerate(attend_back(q, k, v, mixed_grad[part, cols], allowed)):
                rights[2 + j, where, cols] = g.astype(LOW)
    total = back_one
    for j in range(3):
        part = rights[2 + j, at, :]
        total = total + mm_nt(part, qkv[j])
        if j != 1:
            grads_ref[j // 2 : j // 2 + 1, :] += column_sum(part)
    heads_grad[at, :] = total
    pos_grad_ref[...] += jnp.sum(total.reshape(-1, 8, 768), axis=0)

    @pl.when(step == blocks - 1)
    def _():
        me = info[1]
        own = pl.ds(pl.multiple_of(me * 16, 16), 16)
        own_ref[...] = result[own, :]
        own_grad_ref[...] = heads_grad[own, :]

        def chosen(left, rows):
            width = left.shape[1]
            wanted = lax.broadcasted_iota(jnp.int32, (rows, width), 1) - lax.broadcasted_iota(
                jnp.int32, (rows, width), 0
            )
            pick = (wanted == me * rows).astype(F32).astype(LOW)
            return mm_nt(pick, left).astype(LOW)

        left = chosen(lefts[0], 24)
        for j in range(3):
            qkv_grad_ref[:, j * 768 : (j + 1) * 768] = mm(left, rights[2 + j])
        out_grad_ref[...] = mm(chosen(lefts[1], 24), rights[0])
        left = chosen(lefts[2], 24)
        for j in range(4):
            cols = slice(j * 768, (j + 1) * 768)
            up_grad_ref[:, cols] = mm(left, hidden_grad[:, cols])
        for j in range(4):
            left = chosen(act[:, j * 768 : (j + 1) * 768], 24)
            down_grad_ref[j * 24 : (j + 1) * 24, :] = mm(left, rights[1])


def column_sum(value):
    return jnp.sum(value.astype(F32), axis=0, keepdims=True)


def ffn_back_rows(upstream, second, summed, slope, vec, grads_ref, hidden_grad, out, up, down):
    normed, inv_scale = normalize(second)
    back_two = normalize_back(upstream * (1.0 + vec[10:11, :]), normed, inv_scale)
    down_grad = back_two.astype(LOW)
    grads_ref[9:10, :] += column_sum(down_grad)
    grads_ref[10:11, :] += column_sum(upstream * normed)
    grads_ref[11:12, :] += column_sum(upstream)
    total = back_two
    for j in range(4):
        cols = slice(j * 768, (j + 1) * 768)
        grad = (mm_nt(down_grad, down[cols, :]) * slope(cols).astype(F32)).astype(LOW)
        hidden_grad(cols, grad)
        grads_ref[5 + j : 6 + j, :] += column_sum(grad)
        total = total + mm_nt(grad, up[j])
    normed, inv_scale = normalize(summed)
    back_one = normalize_back(total * (1.0 + vec[3:4, :]), normed, inv_scale)
    proj_grad = back_one.astype(LOW)
    grads_ref[2:3, :] += column_sum(proj_grad)
    grads_ref[3:4, :] += column_sum(total * normed)
    grads_ref[4:5, :] += column_sum(total)
    return down_grad, proj_grad, mm_nt(proj_grad, out[...]).astype(LOW)


def load_ffn(place, mid, rest, out, up, down, sems):
    return slab_copies(place, rest, down_slabs(down), sems, 40) + slab_copies(place, mid, mid_slabs(out, up), sems)


def ffn_backward_kernel(segs, seg_count, first_step, info, cot_ref, second_ref, sum_ref, slope_ref, vec_ref, *rest):
    mid, more, rest = rest[:10], rest[10:18], rest[-10:]
    out_ref, down_grad_ref, hidden_grad_ref, proj_grad_ref, mixed_grad_ref, grads_ref, out, up, down, sems = rest
    step = pl.program_id(0)

    @pl.when(step == 0)
    def _():
        load(load_ffn(info[0], mid, more, out, up, down, sems))
        grads_ref[...] = jnp.zeros_like(grads_ref)

    second = second_ref[...]
    normed, _ = normalize(second)
    result = normed * (1.0 + vec_ref[10:11, :]) + vec_ref[11:12, :]
    row = lax.broadcasted_iota(jnp.int32, (SEG, 1), 0)
    ups = []
    for s in range(segs):
        seg = (step + first_step) * segs + s
        at = slice(s * SEG, (s + 1) * SEG)
        live = row + seg % seg_count * SEG < info[1 + seg // seg_count]
        out_ref[at, :] = jnp.where(live, result[at], 0.0).astype(LOW)
        ups.append(jnp.where(live & (row > 0), cot_ref[at, :].astype(F32), 0.0))

    def store(cols, grad):
        hidden_grad_ref[:, cols] = grad

    down_grad_ref[...], proj_grad_ref[...], mixed_grad_ref[...] = ffn_back_rows(
        jnp.concatenate(ups, axis=0), second, sum_ref[...], lambda cols: slope_ref[:, cols], vec_ref, grads_ref, store,
        out, up, down,
    )


def opening_kernel(segs, seg_count, info, heads_ref, heads_grad_ref, vec_ref, *rest):
    tops_in, sources, mid, more, rest = rest[:5], rest[5:8], rest[8:18], rest[18:26], rest[26:]
    tops_out, grads_ref, tops, parts, hidden = rest[:5], rest[5], rest[6:11], rest[11:14], rest[14]
    out, up, down, sems, top_sems = rest[15:]
    copies = load_ffn(info[0], mid, more, out, up, down, sems)
    for i, (source, target) in enumerate(zip((*tops_in, *sources), (*tops, *parts))):
        copies.append(pltpu.make_async_copy(source.at[:, 0 : target.shape[1], :], target, top_sems.at[i]))
    load(copies)
    grads_ref[...] = jnp.zeros_like(grads_ref)
    second, summed, slope = (part[:, 0, :] if part.shape[1] == 8 else part for part in parts)
    slope = slope[...].astype(F32)[:, 0, :]

    def store(cols, grad):
        hidden[:, cols] = grad.astype(F32)

    down_grad, proj_grad, mixed_grad = ffn_back_rows(
        heads_grad_ref[...], second, summed, lambda cols: slope[:, cols], vec_ref, grads_ref, store, out, up, down
    )
    seg = lax.broadcasted_iota(jnp.int32, (segs, 1), 0)
    length = jnp.full((segs, 1), info[1], jnp.int32)
    for i in range(1, segs // seg_count):
        length = jnp.where(seg >= i * seg_count, info[1 + i], length)
    merged = jnp.where(lax.rem(seg, seg_count) * SEG < length, heads_ref[...], 0.0)
    outs = []
    values = (merged, down_grad.astype(F32), hidden[...], proj_grad.astype(F32), mixed_grad.astype(F32))
    for i, (value, top) in enumerate(zip(values, tops)):
        row = lax.broadcasted_iota(jnp.int32, top.shape, 1)
        top[...] = jnp.where(row == 0, value[:, None, :], top[...].astype(F32)).astype(LOW)
        outs.append(pltpu.make_async_copy(top, tops_out[i].at[:, 0:16, :], top_sems.at[i]))
    load(outs)


def attn_backward_kernel(segs, seg_count, first_step, info, packed_ref, mixed_grad_ref, *rest):
    packed_grad_ref, grads_ref = rest[-2:]
    step = pl.program_id(0)

    @pl.when(step == 0)
    def _():
        grads_ref[...] = jnp.zeros_like(grads_ref)

    for s in range(segs):
        seg = (step + first_step) * segs + s
        allowed = segment_mask(info[1 + seg // seg_count], seg % seg_count)
        at = slice(s * SEG, (s + 1) * SEG)
        for h in range(6):
            cols = [slice(j * 768 + h * 128, j * 768 + (h + 1) * 128) for j in range(3)]
            q, k, v = (packed_ref[at, c] for c in cols)
            grads = attend_back(q, k, v, mixed_grad_ref[at, cols[0]], allowed)
            for c, g in zip(cols, grads):
                packed_grad_ref[at, c] = g.astype(LOW)
    grads_ref[0:1, :] += column_sum(packed_grad_ref[:, :768])
    grads_ref[1:2, :] += column_sum(packed_grad_ref[:, 1536:])


def token_grad_kernel(info, packed_grad_ref, proj_grad_ref, *rest):
    pieces, (token_grad_ref, qkv, sems) = rest[:10], rest[10:]

    @pl.when(pl.program_id(0) == 0)
    def _():
        load(slab_copies(info[0], pieces, qkv_slabs(qkv), sems))

    total = proj_grad_ref[...].astype(F32)
    for j in range(3):
        total = total + mm_nt(packed_grad_ref[:, j * 768 : (j + 1) * 768], qkv[j])
    token_grad_ref[...] = total.astype(LOW)


def send_slab(place, total, keep_ref, send_ref, rows):
    for mask in range(8):
        block = pl.multiple_of((place ^ mask) * rows, rows)
        target = send_ref if mask % 2 else keep_ref
        target[mask // 2] = total[pl.ds(block, rows), :].astype(LOW)


def qkv_grad_kernel(info, left_ref, right_ref, more_ref, keep_ref, send_ref, total):
    step = pl.program_id(0)
    total[...] = mm_tn(left_ref[...], right_ref[...])
    at = pl.ds(pl.multiple_of(step * 96, 96), 96)
    for mask in range(8):
        block = pl.multiple_of((info[0] ^ mask) * 96, 96)
        target = send_ref if mask % 2 else keep_ref
        target[mask // 2, at, :] = total[pl.ds(block, 96), :].astype(LOW)

    @pl.when(step == 0)
    def _():
        for mask in range(8):
            target = send_ref if mask % 2 else keep_ref
            target[mask // 2, 288:304, :] = more_ref[mask]


def mid_grad_kernel(info, mixed_ref, proj_ref, low_ref, hidden_ref, keep_ref, send_ref, total):
    @pl.when(pl.program_id(0) == 0)
    def _():
        total[...] = mm_tn(mixed_ref[...], proj_ref[...])

    @pl.when(pl.program_id(0) > 0)
    def _():
        total[...] = mm_tn(low_ref[...], hidden_ref[...])

    send_slab(info[0], total, keep_ref, send_ref, 96)


ANY = pl.BlockSpec(memory_space=pl.ANY)
SMEM = pl.BlockSpec(memory_space=pltpu.SMEM)


def block_rows(count, width):
    return pl.BlockSpec((count, width), lambda i: (i, 0))


def fixed(shape):
    return pl.BlockSpec(shape, lambda i: (0,) * len(shape))


def shape_of(dims, kind=LOW):
    return jax.ShapeDtypeStruct(dims, kind)


def params():
    return pltpu.CompilerParams(vmem_limit_bytes=VMEM, dimension_semantics=("arbitrary",))


def cost(flops, size):
    return pl.CostEstimate(flops=flops, bytes_accessed=size, transcendentals=0)


QKV = [pltpu.VMEM((3, 768, 768), LOW)]
MID = [pltpu.VMEM((768, 768), LOW), pltpu.VMEM((4, 768, 768), LOW)]
DOWN = [pltpu.VMEM((3072, 768), LOW)]


def sems(count):
    return [pltpu.SemaphoreType.DMA((count,))]


def shifted(count, width, first):
    return pl.BlockSpec((count, width), lambda i: (i + first, 0))


def attn_forward(info, rows_in, vec, pieces, seg_count, half, before=None, segs=4):
    rows = rows_in.shape[0]
    count = segs * SEG
    steps = rows // count // 2
    first = half * steps
    before = list(before or [])
    return pl.pallas_call(
        functools.partial(attn_forward_kernel, segs, seg_count, first),
        grid=(steps,),
        in_specs=[SMEM, shifted(count, 768, first), fixed((12, 768))] + [ANY] * (10 + len(before)),
        out_specs=[shifted(count, 2304, first), shifted(count, 768, first)],
        out_shape=[shape_of((rows, 2304)), shape_of((rows, 768))],
        scratch_shapes=QKV + sems(24),
        input_output_aliases={13: 0, 14: 1} if before else {},
        compiler_params=params(),
        cost_estimate=cost(rows * 768 * 8000, rows * 768 * 8),
        name="attn_forward",
    )(info, rows_in, vec, *pieces, *before)


def mid_forward(info, rows_in, mixed, vec, pieces, segs=2):
    rows = rows_in.shape[0]
    count = segs * SEG
    return pl.pallas_call(
        mid_forward_kernel,
        grid=(rows // count,),
        in_specs=[SMEM, block_rows(count, 768), block_rows(count, 768), fixed((12, 768))] + [ANY] * 10,
        out_specs=[block_rows(count, 768), block_rows(count, 768), block_rows(count, 3072), block_rows(count, 3072)],
        out_shape=[shape_of((rows, 768), F32), shape_of((rows, 768)), shape_of((rows, 3072)), shape_of((rows, 3072))],
        scratch_shapes=MID + sems(40),
        compiler_params=params(),
        cost_estimate=cost(2 * rows * 768 * 8000, rows * 768 * 30),
        name="mid_forward",
    )(info, rows_in, mixed, vec, *pieces)


def down_forward(info, summed, act, vec, pieces, segs=2):
    rows = summed.shape[0]
    count = segs * SEG
    few = pl.BlockSpec((None, segs, 768), lambda i: (i, 0, 0))
    return pl.pallas_call(
        functools.partial(down_forward_kernel, segs),
        grid=(rows // count,),
        in_specs=[SMEM, block_rows(count, 768), block_rows(count, 3072), fixed((12, 768))] + [ANY] * 8,
        out_specs=[block_rows(count, 768), few],
        out_shape=[shape_of((rows, 768), F32), shape_of((rows // count, segs, 768), F32)],
        scratch_shapes=DOWN + sems(32),
        compiler_params=params(),
        cost_estimate=cost(2 * rows * 768 * 4000, rows * 768 * 16),
        name="down_forward",
    )(info, summed, act, vec, *pieces)


def cross_whole(info, heads, upstream, live, vec, positions, wide):
    rows = heads.shape[0]
    count = 2 * SEG
    own = [(16, 768), (16, 768), (12, 768), (8, 768), (24, 2304), (24, 768), (24, 3072), (96, 768)]
    return pl.pallas_call(
        functools.partial(cross_kernel, rows // count),
        grid=(rows // count,),
        in_specs=[SMEM, block_rows(count, 768), block_rows(count, 768), block_rows(count, SEG),
                  fixed((12, 768)), fixed((8, 768)), ANY],
        out_specs=[fixed(dims) for dims in own],
        out_shape=[shape_of(dims, F32) for dims in own],
        scratch_shapes=QKV + MID + DOWN + sems(12) + [
            pltpu.VMEM((rows, 768), F32), pltpu.VMEM((rows, 768), F32), pltpu.VMEM((count, 3072), LOW),
            pltpu.VMEM((3, rows, 768), LOW), pltpu.VMEM((rows, 3072), LOW), pltpu.VMEM((count, 2304), LOW),
            pltpu.VMEM((5, rows, 768), LOW), pltpu.VMEM((rows, 3072), LOW),
        ],
        compiler_params=params(),
        cost_estimate=cost(2 * rows * 768 * 30000, 2**24),
        name="cross_encoder",
    )(info, heads, upstream, live, vec, positions, wide)


def ffn_backward(info, cotangent, second, summed, slope, vec, mid, down, seg_count, half, before=None, segs=2):
    rows = summed.shape[0]
    count = segs * SEG
    steps = rows // count // 2
    first = half * steps
    before = list(before or [])
    widths = (768, 768, 3072, 768, 768)
    return pl.pallas_call(
        functools.partial(ffn_backward_kernel, segs, seg_count, first),
        grid=(steps,),
        in_specs=[SMEM, shifted(count, 768, first), shifted(count, 768, first), shifted(count, 768, first),
                  shifted(count, 3072, first), fixed((12, 768))] + [ANY] * (18 + len(before)),
        out_specs=[shifted(count, w, first) for w in widths] + [fixed((12, 768))],
        out_shape=[shape_of((rows, w)) for w in widths] + [shape_of((12, 768), F32)],
        scratch_shapes=MID + DOWN + sems(72),
        input_output_aliases={24 + i: i for i in range(5)} if before else {},
        compiler_params=params(),
        cost_estimate=cost(rows * 768 * 14000, rows * 768 * 15),
        name="ffn_backward",
    )(info, cotangent, second, summed, slope, vec, *mid, *down, *before)


def opening_backward(info, heads, heads_grad, vec, arrays, sources, mid, down, seg_count):
    segs = heads.shape[0]

    def grouped(array):
        return array.reshape(segs, SEG, array.shape[1])

    arrays, sources = [grouped(a) for a in arrays], [grouped(a) for a in sources]
    whole = fixed((segs, 768))
    *done, grads = pl.pallas_call(
        functools.partial(opening_kernel, segs, seg_count),
        grid=(1,),
        in_specs=[SMEM, whole, whole, fixed((12, 768))] + [ANY] * 26,
        out_specs=[ANY] * 5 + [fixed((12, 768))],
        out_shape=[shape_of(a.shape) for a in arrays] + [shape_of((12, 768), F32)],
        scratch_shapes=[pltpu.VMEM((segs, 16, a.shape[2]), LOW) for a in arrays]
        + [pltpu.VMEM((segs, 8, 768), F32)] * 2
        + [pltpu.VMEM((segs, 16, 3072), LOW), pltpu.VMEM((segs, 3072), F32)]
        + MID + DOWN + sems(72) + sems(8),
        input_output_aliases={4 + i: i for i in range(5)},
        compiler_params=params(),
        cost_estimate=cost(2**33, 2**24),
        name="opening_backward",
    )(info, heads, heads_grad, vec, *arrays, *sources, *mid, *down)
    return [a.reshape(-1, a.shape[2]) for a in done], grads


def attn_backward(info, packed, mixed_grad, seg_count, half, before=None, segs=2):
    rows = packed.shape[0]
    count = segs * SEG
    steps = rows // count // 2
    first = half * steps
    before = [] if before is None else [before]
    return pl.pallas_call(
        functools.partial(attn_backward_kernel, segs, seg_count, first),
        grid=(steps,),
        in_specs=[SMEM, shifted(count, 2304, first), shifted(count, 768, first)] + [ANY] * len(before),
        out_specs=[shifted(count, 2304, first), fixed((2, 768))],
        out_shape=[shape_of((rows, 2304)), shape_of((2, 768), F32)],
        input_output_aliases={3: 0} if before else {},
        compiler_params=params(),
        cost_estimate=cost(rows * 768 * 10000, rows * 768 * 8),
        name="attn_backward",
    )(info, packed, mixed_grad, *before)


def token_gradient(info, packed_grad, proj_grad, pieces, count=512):
    rows = packed_grad.shape[0]
    return pl.pallas_call(
        token_grad_kernel,
        grid=(rows // count,),
        in_specs=[SMEM, block_rows(count, 2304), block_rows(count, 768)] + [ANY] * 10,
        out_specs=block_rows(count, 768),
        out_shape=shape_of((rows, 768)),
        scratch_shapes=QKV + sems(24),
        compiler_params=params(),
        cost_estimate=cost(2 * rows * 768 * 3000, rows * 768 * 10),
        name="token_gradient",
    )(info, packed_grad, proj_grad, *pieces)


def grad_outs(slabs):
    out = pl.BlockSpec((4, 96, 768), lambda i: (0, i, 0))
    return [out, out], [shape_of((4, slabs * 96, 768))] * 2


def qkv_weight_grad(info, left, right, more):
    rows = left.shape[0]
    out = fixed((4, 304, 768))
    return pl.pallas_call(
        qkv_grad_kernel,
        grid=(3,),
        in_specs=[SMEM, fixed((rows, 768)), pl.BlockSpec((rows, 768), lambda i: (0, i)), fixed((8, 16, 768))],
        out_specs=[out, out],
        out_shape=[shape_of((4, 304, 768))] * 2,
        scratch_shapes=[pltpu.VMEM((768, 768), F32)],
        compiler_params=params(),
        cost_estimate=cost(2 * rows * 768 * 2304, rows * 2304 * 2),
        name="qkv_weight_grad",
    )(info, left, right, more)


def mid_weight_grad(info, mixed, proj_grad, low, hidden_grad):
    rows = mixed.shape[0]
    specs, shapes = grad_outs(5)
    still = fixed((rows, 768))
    return pl.pallas_call(
        mid_grad_kernel,
        grid=(5,),
        in_specs=[SMEM, still, still, still, pl.BlockSpec((rows, 768), lambda i: (0, jnp.maximum(i - 1, 0)))],
        out_specs=specs,
        out_shape=shapes,
        scratch_shapes=[pltpu.VMEM((768, 768), F32)],
        compiler_params=params(),
        cost_estimate=cost(2 * rows * 768 * 3840, rows * 3840 * 2),
        name="mid_weight_grad",
    )(info, mixed, proj_grad, low, hidden_grad)


def down_grad_kernel(info, left_ref, right_ref, keep_ref, send_ref, total):
    step = pl.program_id(0)
    total[pl.ds(pl.multiple_of(step * 768, 768), 768), :] = mm_tn(left_ref[...], right_ref[...]).astype(LOW)

    @pl.when(step == pl.num_programs(0) - 1)
    def _():
        for mask in range(8):
            block = pl.multiple_of((info[0] ^ mask) * 384, 384)
            target = send_ref if mask % 2 else keep_ref
            target[mask // 2] = total[pl.ds(block, 384), :]


def down_weight_grad(info, left, right):
    rows, wide = left.shape
    return pl.pallas_call(
        down_grad_kernel,
        grid=(wide // 768,),
        in_specs=[SMEM, pl.BlockSpec((rows, 768), lambda i: (0, i)), fixed((rows, 768))],
        out_specs=[fixed((4, 384, 768))] * 2,
        out_shape=[shape_of((4, 384, 768))] * 2,
        scratch_shapes=[pltpu.VMEM((3072, 768), LOW)],
        compiler_params=params(),
        cost_estimate=cost(2 * rows * 768 * wide, rows * wide * 2),
        name="down_weight_grad",
    )(info, left, right)


def matmul(left_op, right_op):
    return jnp.dot(left_op, right_op, preferred_element_type=jnp.float32)


def trans_left(left_op, right_op):
    return lax.dot_general(
        left_op, right_op, (((0,), (0,)), ((), ())), preferred_element_type=jnp.float32
    )


def trans_right(left_op, right_op):
    return lax.dot_general(
        left_op, right_op, (((1,), (1,)), ((), ())), preferred_element_type=jnp.float32
    )


def norm_forward(summed, gain_row, shift_row):
    average = jnp.mean(summed, axis=-1, keepdims=True)
    centered = summed - average
    inv_scale = lax.rsqrt(jnp.mean(centered * centered, axis=-1, keepdims=True) + NORM_EPS)
    normed = centered * inv_scale
    return (normed * (1.0 + gain_row) + shift_row, normed, inv_scale)


def norm_backward(upstream, normed, inv_scale, gain_row):
    inner = upstream * (1.0 + gain_row)
    back_grad = inv_scale * (
        inner
        - jnp.mean(inner, axis=-1, keepdims=True)
        - normed * jnp.mean(inner * normed, axis=-1, keepdims=True)
    )
    return (back_grad, jnp.sum(upstream * normed, axis=0), jnp.sum(upstream, axis=0))


def gelu_slope(hidden):
    return (
        0.5 * (1.0 + lax.erf(hidden * ROOT_HALF))
        + hidden * jnp.exp(-0.5 * hidden * hidden) * INV_ROOT_TAU
    )


def split_heads(packed, group_len):
    head_count = packed.shape[1] // (3 * HEAD)
    return [
        portion.reshape(-1, group_len, head_count, HEAD) for portion in jnp.split(packed, 3, axis=1)
    ]


def masked_scores(query_heads, key_heads, allowed):
    raw_scores = jnp.einsum(
        "nqhd,nkhd->nhqk", query_heads, key_heads, preferred_element_type=jnp.float32
    ) * HEAD ** (-0.5)
    return jnp.where(allowed[:, None, None, :], raw_scores, MASK_FILL)


def encode(inputs, inputs_low, weights, allowed):
    qkv_w, out_w, up_w, down_w, vectors = weights
    row_count, feat_dim = inputs_low.shape
    group_len = allowed.shape[1]
    qkv_bias = jnp.concatenate([vectors[0], jnp.zeros_like(vectors[0]), vectors[1]])
    packed = (matmul(inputs_low, qkv_w) + qkv_bias).astype(jnp.bfloat16)
    query_heads, key_heads, value_heads = split_heads(packed, group_len)
    scores = masked_scores(query_heads, key_heads, allowed)
    row_max = jnp.max(scores, axis=-1, keepdims=True)
    expo_vals = jnp.exp(scores - row_max)
    row_total = jnp.sum(expo_vals, axis=-1, keepdims=True)
    log_total = row_max + jnp.log(row_total)
    prob_low = (expo_vals / row_total).astype(jnp.bfloat16)
    mixed = jnp.einsum("nhqk,nkhd->nqhd", prob_low, value_heads, preferred_element_type=jnp.float32)
    mixed = mixed.reshape(row_count, feat_dim).astype(jnp.bfloat16)
    projected = matmul(mixed, out_w) + vectors[2]
    first_out, normed_one, scale_one = norm_forward(inputs + projected, vectors[3], vectors[4])
    first_low = first_out.astype(jnp.bfloat16)
    hidden = matmul(first_low, up_w) + vectors[5:-3].reshape(-1)
    activated = jax.nn.gelu(hidden, approximate=False).astype(jnp.bfloat16)
    down_out = matmul(activated, down_w) + vectors[-3]
    result, normed_two, scale_two = norm_forward(first_out + down_out, vectors[-2], vectors[-1])
    return (
        result,
        (
            packed,
            log_total,
            mixed,
            normed_one,
            scale_one,
            first_low,
            hidden,
            activated,
            normed_two,
            scale_two,
        ),
    )


def encode_back(upstream, inputs_low, weights, allowed, kept):
    qkv_w, out_w, up_w, down_w, vectors = weights
    (
        packed,
        log_total,
        mixed,
        normed_one,
        scale_one,
        first_low,
        hidden,
        activated,
        normed_two,
        scale_two,
    ) = kept
    row_count, feat_dim = inputs_low.shape
    group_len = allowed.shape[1]
    back_two, gain_two, shift_two = norm_backward(upstream, normed_two, scale_two, vectors[-2])
    down_grad = back_two.astype(jnp.bfloat16)
    hidden_grad = (trans_right(down_grad, down_w) * gelu_slope(hidden)).astype(jnp.bfloat16)
    first_grad = trans_right(hidden_grad, up_w) + back_two
    back_one, gain_one, shift_one = norm_backward(first_grad, normed_one, scale_one, vectors[3])
    proj_grad = back_one.astype(jnp.bfloat16)
    query_heads, key_heads, value_heads = split_heads(packed, group_len)
    mixed_grad = trans_right(proj_grad, out_w).astype(jnp.bfloat16).reshape(value_heads.shape)
    scores = masked_scores(query_heads, key_heads, allowed)
    prob_vals = jnp.exp(scores - log_total)
    grad_values = jnp.einsum(
        "nhqk,nqhd->nkhd",
        prob_vals.astype(jnp.bfloat16),
        mixed_grad,
        preferred_element_type=jnp.float32,
    )
    grad_prob = jnp.einsum(
        "nqhd,nkhd->nhqk", mixed_grad, value_heads, preferred_element_type=jnp.float32
    )
    score_grad = (
        prob_vals * (grad_prob - jnp.sum(prob_vals * grad_prob, axis=-1, keepdims=True))
    ).astype(jnp.bfloat16)
    grad_query = jnp.einsum(
        "nhqk,nkhd->nqhd", score_grad, key_heads, preferred_element_type=jnp.float32
    ) * HEAD ** (-0.5)
    grad_keys = jnp.einsum(
        "nhqk,nqhd->nkhd", score_grad, query_heads, preferred_element_type=jnp.float32
    ) * HEAD ** (-0.5)
    packed_grad = jnp.concatenate(
        [
            grad_query.reshape(row_count, feat_dim),
            grad_keys.reshape(row_count, feat_dim),
            grad_values.reshape(row_count, feat_dim),
        ],
        axis=1,
    ).astype(jnp.bfloat16)
    bias_grads = jnp.sum(packed_grad, axis=0, dtype=jnp.float32).reshape(3, feat_dim)
    grad_inputs = trans_right(packed_grad, qkv_w) + back_one
    grad_vectors = jnp.concatenate(
        [
            bias_grads[0:1],
            bias_grads[2:3],
            jnp.sum(proj_grad, axis=0, dtype=jnp.float32)[None],
            gain_one[None],
            shift_one[None],
            jnp.sum(hidden_grad, axis=0, dtype=jnp.float32).reshape(-1, feat_dim),
            jnp.sum(down_grad, axis=0, dtype=jnp.float32)[None],
            gain_two[None],
            shift_two[None],
        ],
        axis=0,
    )
    pairs = (
        (inputs_low, packed_grad),
        (mixed, proj_grad),
        (first_low, hidden_grad),
        (activated, down_grad),
    )
    return (grad_inputs, pairs, grad_vectors)


class Links:
    def __init__(self, outer, inner):
        self.outer, self.inner = outer, inner
        self.order = self.place = lax.axis_index("dp")
        self.z = lax.axis_index("fsdp")

    def flip(self, value, mask):
        pairs = [
            (d * self.inner + z, (d ^ mask) * self.inner + z)
            for d in range(self.outer)
            for z in range(self.inner)
        ]
        return lax.ppermute(value, AXES, pairs)

    def turn(self, value, step):
        pairs = [
            (d * self.inner + z, d * self.inner + (z + step) % self.inner)
            for d in range(self.outer)
            for z in range(self.inner)
        ]
        return lax.ppermute(value, AXES, pairs)

    def gather_z(self, shard):
        came = [shard] + [self.turn(shard, step) for step in range(1, self.inner)]
        whole = []
        for z in range(self.inner):
            part = came[-1]
            for step in range(self.inner - 1):
                part = jnp.where(self.z == (z + step) % self.inner, came[step], part)
            whole.append(part)
        return whole

    def spread_near(self, block):
        return self.flip(block, 2), self.flip(block, 4)

    def spread_far(self, by_x, by_y, half):
        return self.flip(by_y[:half], 2), self.flip(by_x[half:], 4)

    def core(self, pieces):
        return [self.flip(piece, 1) for piece in pieces]

    def in_order(self, parts):
        for axis, mask in ((4, 4), (2, 2), (1, 1)):
            odd = self.place // axis % 2 == 1
            parts = [jnp.where(odd, parts[m ^ mask], parts[m]) for m in range(8)]
        return jnp.stack(parts)

    def gather_small(self, shard, line_only=False):
        block = jnp.stack(self.gather_z(shard))
        return block if line_only else self.gather_core(self.gather_plane(block))

    def gather_plane(self, block):
        return jnp.stack([block] + [self.flip(block, m) for m in (2, 4, 6)])

    def gather_core(self, plane):
        other = self.flip(plane, 1)
        whole = self.in_order([(plane, other)[m % 2][m // 2] for m in range(8)])
        return whole.reshape((-1,) + plane.shape[2:])


class PlainLinks:
    def __init__(self, outer, inner):
        self.outer, self.inner = outer, inner
        self.order = lax.axis_index("dp")
        self.z = lax.axis_index("fsdp")
        self.place = 0

    def gather_small(self, shard, line_only=False):
        return lax.all_gather(shard, AXES, axis=0)


def add(*terms):
    return sum(t.astype(F32) for t in terms).astype(LOW)


class Sum:
    def __init__(self, links, keep, send, slabs):
        self.links, self.keep, self.slabs = links, keep, slabs
        self.more = keep.shape[1] % 96
        self.came = links.flip(send, 1)

    def line(self, part):
        inner = self.links.inner
        count = part.shape[0] - self.more
        main = part[:count].reshape(self.slabs, inner, -1, part.shape[-1])
        main = main.transpose(1, 0, 2, 3).reshape(inner, -1, part.shape[-1])
        if not self.more:
            return main
        rows = part[count : count + inner].reshape(inner, 1, -1)
        return jnp.concatenate([main, jnp.pad(rows, ((0, 0), (0, 7), (0, 0)))], axis=1)

    def to(self, index):
        return self.line(add(self.keep[index], self.came[index]))

    def far(self):
        half = self.links.inner // 2
        to_d = self.to(3)
        self.far_came = [self.links.flip(to_d[:half], 2), self.links.flip(to_d[half:], 4)]
        return self.far_came

    def near(self):
        half = self.links.inner // 2
        came_x, came_y = self.far_came
        to_x, to_y = self.to(1), self.to(2)
        to_y = jnp.concatenate([add(to_y[:half], came_x), to_y[half:]])
        to_x = jnp.concatenate([to_x[:half], add(to_x[half:], came_y)])
        self.near_came = [self.links.flip(to_x, 2), self.links.flip(to_y, 4)]
        return self.near_came

    def direct(self):
        self.near_came = [self.links.flip(self.to(m // 2), m) for m in (2, 4, 6)]
        return self.near_came

    def turn(self, *earlier):
        links = self.links
        own = add(self.line(self.keep[0]), self.line(self.came[0]), *self.near_came)
        own = after(own, *earlier) if earlier else own
        parts = [lax.dynamic_index_in_dim(own, (links.z + k) % links.inner, 0, keepdims=False) for k in range(links.inner)]
        self.turned = [parts[0]] + [links.turn(parts[k], k) for k in range(1, links.inner)]
        return self.turned[1:]

    def total(self):
        return sum(t.astype(F32) for t in self.turned)


class PlainSum:
    def __init__(self, links, keep, send, slabs):
        more = keep.shape[1] % 96
        flat = jnp.stack([keep, send], axis=1).reshape(8, -1, 768)
        main = flat[:, : flat.shape[1] - more].reshape(8, slabs, -1, 768)
        main = main.transpose(1, 0, 2, 3).reshape(slabs, -1, 768)
        self.came = keep
        self.sums = lax.psum_scatter(main, AXES, scatter_dimension=1, tiled=True).reshape(-1, 768)
        if more:
            rows = flat[:, flat.shape[1] - more :][:, : links.outer * links.inner // 8].reshape(-1, 768)
            self.sums = jnp.concatenate([self.sums, lax.psum_scatter(rows, AXES, scatter_dimension=0, tiled=True)])

    def far(self, *earlier):
        return []

    near = direct = turn = far

    def total(self):
        return self.sums.astype(F32)


def after(value, *earlier):
    return lax.optimization_barrier((value, *earlier))[0]


def slabs_of(matrix):
    rows, wide = matrix.shape
    return matrix.reshape(rows, wide // 768, 768).transpose(1, 0, 2)


def matrix_of(slabs):
    count, rows, width = slabs.shape
    return slabs.transpose(1, 0, 2).reshape(rows, count * width)


def mix_columns(matrix, devices):
    rows, wide = matrix.shape
    matrix = matrix.reshape(rows, devices, 4, -1).transpose(0, 2, 1, 3)
    return matrix.reshape(rows, wide)


def unmix_columns(matrix, devices):
    rows, wide = matrix.shape
    matrix = matrix.reshape(rows, 4, devices, -1).transpose(0, 2, 1, 3)
    return matrix.reshape(rows, wide)


def plain_pieces(slabs, whole):
    count = slabs.shape[0]
    half = (count + 1) // 2 * 96
    parts = []
    for mask in (0, 2, 4, 6, 1, 3, 5, 7):
        part = slabs[:, mask * 96 : (mask + 1) * 96].reshape(-1, 768)
        parts += [part] if whole or mask < 6 and mask != 7 else [part[:half], part[half:]]
    return parts


def shards(
    outer,
    inner,
    tokens,
    cotangent,
    lengths,
    seg_qkv,
    seg_out,
    seg_up,
    seg_down,
    seg_vec,
    cross_qkv,
    cross_out,
    cross_up,
    cross_down,
    cross_vec,
    positions,
):
    fast = (outer, inner) == (8, 4)
    links = (Links if fast else PlainLinks)(outer, inner)
    summing = Sum if fast else PlainSum
    devices = outer * inner
    me = links.order * inner + links.z
    seq_local, seq_len, feat_dim = tokens.shape
    seg_count = seq_len // SEG
    seg_rows, cross_rows = seg_vec.shape[0], cross_vec.shape[0]
    width = feat_dim // devices
    my_lengths = lax.dynamic_slice_in_dim(lengths, me * seq_local, seq_local)
    info = jnp.concatenate([jnp.full((1,), links.place, jnp.int32), my_lengths])
    small = jnp.concatenate([seg_vec, cross_vec, positions]).reshape(1, -1)
    up_slabs = mix_columns(cross_up, devices).reshape(-1, 4, feat_dim).transpose(1, 0, 2)
    wide = [slabs_of(cross_qkv), slabs_of(cross_out), up_slabs, cross_down.reshape(4, -1, feat_dim)]
    wide = jnp.concatenate(wide)
    mid_shard = jnp.concatenate([slabs_of(seg_out), slabs_of(seg_up)])
    rows_in = tokens.reshape(-1, feat_dim)
    cot_rows = cotangent.reshape(-1, feat_dim)
    seg_starts = jnp.arange(seg_count) * SEG
    live_own = (seg_starts[None, :] < my_lengths[:, None]).reshape(-1, 1)
    up_own = jnp.where(live_own, cotangent.reshape(-1, SEG, feat_dim)[:, 0, :], 0)

    if fast:
        first = jnp.concatenate([slabs_of(seg_qkv).reshape(-1, 768), jnp.pad(small, ((0, 7), (0, 0)))])
        line_first = links.gather_z(first)
        line_rest = jnp.concatenate([mid_shard, seg_down.reshape(4, -1, feat_dim)])
        line_rest = links.gather_z(after(line_rest, *line_first))
        weights = jnp.stack([p[:72].reshape(3, 24, 768) for p in line_first], axis=1).reshape(-1, 768)
        rows = jnp.concatenate([p[72:73] for p in line_first])
        block = jnp.concatenate([weights, jnp.pad(rows, ((0, 12), (0, 0)))])
        near = links.spread_near(block)
        far = links.spread_far(*near, 192)
        first = [block, *near, *far, *links.core([after(p, *far, *line_rest) for p in (block, *near, *far)])]
        ends = [p[288:292] for p in first[:3]] + [first[4][96:100]]
        others = [p[288:292] for p in first[5:8]] + [first[9][96:100]]
        small = links.in_order([(ends, others)[m % 2][m // 2] for m in range(8)])
        block = after(jnp.stack([p[:5] for p in line_rest], axis=1).reshape(-1, 768), *far)
        mid = [block, *links.spread_near(block)]
    else:
        first = plain_pieces(lax.all_gather(slabs_of(seg_qkv), AXES, axis=1, tiled=True), False)
        mid = plain_pieces(lax.all_gather(mid_shard, AXES, axis=1, tiled=True), False)
        down_whole = lax.all_gather(seg_down, AXES, axis=0, tiled=True)
        down = [down_whole[m * 384 : (m + 1) * 384] for m in (0, 2, 4, 6, 1, 3, 5, 7)]
        small = links.gather_small(small)
    small = small.reshape(devices, -1, width).transpose(1, 0, 2).reshape(-1, feat_dim).astype(F32)
    seg_v, cross_v = small[:seg_rows], small[seg_rows : seg_rows + cross_rows]
    pos_table = small[seg_rows + cross_rows :]
    hidden_rows = slice(5, cross_rows - 3)
    cross_v = cross_v.at[hidden_rows].set(mix_columns(cross_v[hidden_rows].reshape(1, -1), devices).reshape(-1, feat_dim))

    before = attn_forward(info, rows_in, seg_v, first, seg_count, 0)
    wide = lax.all_gather(after(wide, before[0], *(mid[1:] if fast else ())), AXES, axis=1, tiled=True)
    if fast:
        far = links.spread_far(*(after(p, before[0]) for p in mid[1:]), 288)
        rows_late = after(rows_in, *mid[1:])
    else:
        rows_late = rows_in
    packed, mixed = attn_forward(info, rows_late, seg_v, first, seg_count, 1, before)
    if fast:
        late = links.core([after(p, packed, *far) for p in (*mid, *far)])
        mid = [*mid, *far, *late]
        block = after(jnp.concatenate([p[5:] for p in line_rest]).reshape(-1, feat_dim), *late)
        near = [links.flip(block, m) for m in (2, 4, 6)]
    summed, low, act, slope = mid_forward(info, rows_in, mixed, seg_v, mid)
    if fast:
        down = [block, *near, links.flip(block, 1), *(links.flip(after(p, act), 1) for p in near)]
    second, heads = down_forward(info, summed, act, seg_v, down)
    heads_own = heads.reshape(-1, feat_dim)
    both = links.gather_small(jnp.stack([heads_own.astype(LOW), up_own]), True)
    back = functools.partial(ffn_backward, info, seg_count=seg_count)
    args = (second, summed, slope, seg_v, mid, down)
    if fast:
        first_half = back(cot_rows, *args, half=0)
        both = links.gather_plane(after(both, first_half[1]))
        *arrays, grads_two = back(after(cot_rows, first_half[1]), *args, half=1, before=first_half[:5])
        both = links.gather_core(after(both, arrays[1]))
    heads_all, up_all = both[:, 0].reshape(-1, feat_dim), both[:, 1].reshape(-1, feat_dim)
    live_all = seg_starts[None, :] < lengths[:, None]
    if fast:
        cross_info = jnp.stack([links.place, me]).astype(jnp.int32)
        live = jnp.broadcast_to(live_all.reshape(-1, 1), (live_all.size, SEG)).astype(F32)
        cross_own, heads_grad, vec_grad, pos_grad, *cross_grads = cross_whole(
            cross_info, heads_all, up_all, live, cross_v, pos_table, wide
        )
    else:
        weights = (matrix_of(wide[:3]), wide[3], matrix_of(wide[4:8]), wide[8:].reshape(-1, feat_dim), cross_v)
        heads_in = heads_all.astype(F32).reshape(-1, seg_count, feat_dim) + pos_table[None]
        heads_in = heads_in.reshape(-1, feat_dim)
        cross_result, kept = encode(heads_in, heads_in.astype(LOW), weights, live_all)
        all_grad, pairs, vec_grad = encode_back(
            up_all.astype(F32), heads_in.astype(LOW), weights, live_all, kept
        )
        cross_grads = []
        for left, right in pairs:
            left = left.reshape(left.shape[0], -1, feat_dim)
            mine = lax.dynamic_slice_in_dim(left, me * width, width, 2)
            cross_grads.append(trans_left(mine.reshape(left.shape[0], -1), right))
        pos_grad = jnp.sum(all_grad.reshape(-1, seg_count, feat_dim), axis=0)
        own = seq_local * seg_count
        cross_own = lax.dynamic_slice_in_dim(cross_result, me * own, own)
        heads_grad = lax.dynamic_slice_in_dim(all_grad, me * own, own)
        first_half = back(after(cot_rows, heads_grad, *cross_grads), *args, half=0)
        *arrays, grads_two = back(cot_rows, *args, half=1, before=first_half[:5])
    grads_two = grads_two + first_half[5]
    arrays, grads_more = opening_backward(
        info, cross_own, heads_grad, seg_v, arrays, (second, summed, slope), mid, down, seg_count
    )
    layer_out, down_grad, hidden_grad, proj_grad, mixed_grad = arrays
    grads_two = grads_two + grads_more
    down_sum = summing(links, *down_weight_grad(info, act, down_grad), 1)
    mid_parts = mid_weight_grad(info, mixed, proj_grad, low, after(hidden_grad, down_sum.keep if fast else down_sum.came))
    mid_sum = summing(links, *mid_parts, 5)
    half_grad, grads_one = attn_backward(
        info, packed, after(mixed_grad, mid_parts[1], down_sum.came), seg_count, 0
    )
    ready = after(mixed_grad, half_grad, *down_sum.far(), mid_sum.came)
    packed_grad, grads_more = attn_backward(info, packed, ready, seg_count, 1, half_grad)
    vec_parts = jnp.concatenate([grads_one + grads_more, grads_two[2:]]).reshape(seg_rows, devices, width)
    vec_parts = vec_parts.transpose(1, 0, 2).reshape(outer, inner, seg_rows * width).astype(LOW)
    if outer > 8:
        vec_parts = vec_parts.reshape(8, -1, seg_rows * width)
    vec_parts = jnp.pad(vec_parts, ((0, 0), (0, 16 - vec_parts.shape[1]), (0, feat_dim - seg_rows * width)))
    if fast:
        vec_parts = links.in_order(list(vec_parts))
    ready = after(packed_grad, *down_sum.near(), *mid_sum.far())
    keep, send = qkv_weight_grad(info, rows_in, ready, vec_parts)
    qkv_sum = summing(links, keep, after(send, *down_sum.turn(), *mid_sum.near()), 3)
    ready = after(packed_grad, qkv_sum.came)
    token_grad = token_gradient(info, ready, proj_grad, first)
    qkv_sum.direct()
    mid_sum.turn()
    qkv_sum.turn(token_grad)
    cross_grads[2] = unmix_columns(after(cross_grads[2], token_grad), devices)
    vec_grad = vec_grad.at[hidden_rows].set(
        unmix_columns(after(vec_grad[hidden_rows], token_grad).reshape(1, -1), devices).reshape(-1, feat_dim)
    )
    cross_vec_grad = lax.dynamic_slice_in_dim(vec_grad, me * width, width, 1)
    grad_positions = lax.dynamic_slice_in_dim(pos_grad, me * width, width, 1)
    grad_down = down_sum.total()
    grad_mid = mid_sum.total().reshape(5, -1, feat_dim)
    total = qkv_sum.total()
    grad_qkv = matrix_of(total[: 3 * width].reshape(3, -1, feat_dim))
    grad_vec = total[3 * width, : seg_rows * width].reshape(seg_rows, width)
    return (
        layer_out.reshape(tokens.shape),
        token_grad.reshape(tokens.shape),
        grad_qkv,
        grad_mid[0],
        matrix_of(grad_mid[1:]),
        grad_down,
        grad_vec,
        *cross_grads,
        cross_vec_grad,
        grad_positions,
    )


def solution(mesh):
    in_specs = (
        P(("dp", "fsdp"), None, None),
        P(("dp", "fsdp"), None, None),
        P(),
        P(("dp", "fsdp"), None),
        P(("dp", "fsdp"), None),
        P(("dp", "fsdp"), None),
        P(("dp", "fsdp"), None),
        P(None, ("dp", "fsdp")),
        P(("dp", "fsdp"), None),
        P(("dp", "fsdp"), None),
        P(("dp", "fsdp"), None),
        P(("dp", "fsdp"), None),
        P(None, ("dp", "fsdp")),
        P(None, ("dp", "fsdp")),
    )
    out_specs = (
        P(("dp", "fsdp"), None, None),
        P(("dp", "fsdp"), None, None),
        P(("dp", "fsdp"), None),
        P(("dp", "fsdp"), None),
        P(("dp", "fsdp"), None),
        P(("dp", "fsdp"), None),
        P(None, ("dp", "fsdp")),
        P(("dp", "fsdp"), None),
        P(("dp", "fsdp"), None),
        P(("dp", "fsdp"), None),
        P(("dp", "fsdp"), None),
        P(None, ("dp", "fsdp")),
        P(None, ("dp", "fsdp")),
    )
    return jax.shard_map(
        functools.partial(shards, mesh.shape["dp"], mesh.shape["fsdp"]),
        mesh=mesh, in_specs=in_specs, out_specs=out_specs, check_vma=False)
```

```python
import functools

import jax
import jax.numpy as jnp
from jax import lax
from jax.experimental import pallas as pl
from jax.experimental.pallas import tpu as pltpu
from jax.sharding import PartitionSpec as P

HEAD = 64
SEG = 128
NORM_EPS = 1e-05
MASK_FILL = -1000000000.0
VMEM = 60 * 2**20
F32, LOW = jnp.float32, jnp.bfloat16


ROOT_HALF = 0.7071067811865476
INV_ROOT_TAU = 0.3989422804014327
AXES = ("dp", "fsdp")

def mm(left_op, right_op):
    return jnp.dot(left_op, right_op, preferred_element_type=F32)


def mm_nt(left_op, right_op):
    return lax.dot_general(left_op, right_op, (((1,), (1,)), ((), ())), preferred_element_type=F32)


def mm_tn(left_op, right_op):
    return lax.dot_general(left_op, right_op, (((0,), (0,)), ((), ())), preferred_element_type=F32)


def normalize(summed):
    average = jnp.mean(summed, axis=-1, keepdims=True)
    centered = summed - average
    inv_scale = lax.rsqrt(jnp.mean(centered * centered, axis=-1, keepdims=True) + NORM_EPS)
    return centered * inv_scale, inv_scale


def normalize_back(inner, normed, inv_scale):
    return inv_scale * (
        inner
        - jnp.mean(inner, axis=-1, keepdims=True)
        - normed * jnp.mean(inner * normed, axis=-1, keepdims=True)
    )


def gelu_parts(hidden):
    phi = 0.5 * (1.0 + lax.erf(hidden * ROOT_HALF))
    return hidden * phi, phi + hidden * jnp.exp(-0.5 * hidden * hidden) * INV_ROOT_TAU


def pair_stack(pair, low_half):
    zero = jnp.zeros_like(pair)
    return jnp.concatenate(
        [jnp.where(low_half, pair, zero), jnp.where(low_half, zero, pair)], axis=0
    )


def pair_merge(stacked, low_half):
    rows = stacked.shape[0] // 2
    return jnp.where(low_half, stacked[:rows], stacked[rows:])


def pair_probs(stack, keys, allowed):
    scores = jnp.where(allowed, mm_nt(keys, stack), MASK_FILL)
    expo = jnp.exp(scores - jnp.max(scores, axis=0, keepdims=True))
    return expo * (1.0 / jnp.sum(expo, axis=0, keepdims=True))


def attend(query, keys, values, allowed):
    low_half = lax.broadcasted_iota(jnp.int32, query.shape, 1) < HEAD
    stack = pair_stack(query * jnp.asarray(HEAD**-0.5, query.dtype), low_half)
    return pair_merge(mm_tn(pair_probs(stack, keys, allowed).astype(LOW), values), low_half)


def attend_back(query, keys, values, grad_mixed, allowed):
    low_half = lax.broadcasted_iota(jnp.int32, query.shape, 1) < HEAD
    stack = pair_stack(query * jnp.asarray(HEAD**-0.5, query.dtype), low_half)
    probs = pair_probs(stack, keys, allowed)
    grad_stack = pair_stack(grad_mixed, low_half)
    grad_prob = mm_nt(values, grad_stack)
    inner = jnp.sum(probs * grad_prob, axis=0, keepdims=True)
    score_grad = (probs * (grad_prob - inner)).astype(LOW)
    grad_query = pair_merge(mm_tn(score_grad, keys), low_half) * HEAD**-0.5
    return grad_query, mm(score_grad, stack), mm(probs.astype(LOW), grad_stack)


def slab_copies(place, pieces, slabs, sems, first_sem=0):
    count = len(slabs)
    half = (count + 1) // 2
    spans = [(0, 0, count), (2, 0, count), (4, 0, count)]
    spans += [(6, 0, count)] if len(pieces) == 8 else [(6, 0, half), (6, half, count)]
    copies = []
    for flip_c in (0, 1):
        for index, (flip_yx, first, last) in enumerate(spans):
            block = place ^ (flip_yx + flip_c)
            piece = pieces[flip_c * len(spans) + index]
            for slab in range(first, last):
                source = piece.at[pl.ds((slab - first) * 96, 96)]
                sem = sems.at[first_sem + slab * 8 + flip_yx + flip_c]
                copies.append(pltpu.make_async_copy(source, slabs[slab](block), sem))
    return copies


def load(copies):
    for copy in copies:
        copy.start()
    for copy in copies:
        copy.wait()


def rows_of(ref, block, rows=96, slab=None):
    where = pl.ds(pl.multiple_of(block * rows, rows), rows)
    return ref.at[where] if slab is None else ref.at[slab, where]


def down_rows(ref, block, part):
    return ref.at[pl.ds(pl.multiple_of(block * 384 + part * 96, 96), 96)]


def qkv_slabs(qkv):
    return [functools.partial(rows_of, qkv, slab=j) for j in range(3)]


def mid_slabs(out, up):
    return [functools.partial(rows_of, out)] + [functools.partial(rows_of, up, slab=j) for j in range(4)]


def down_slabs(down):
    return [functools.partial(down_rows, down, part=j) for j in range(4)]


def segment_mask(length, seg_in_seq):
    row = lax.broadcasted_iota(jnp.int32, (SEG, 2 * SEG), 0)
    return (row + seg_in_seq * SEG < length) | (row == 0)


def attn_forward_kernel(segs, seg_count, first_step, info, x_ref, vec_ref, *rest):
    pieces, (packed_ref, mixed_ref, qkv, sems) = rest[:10], rest[-4:]
    step = pl.program_id(0)

    @pl.when(step == 0)
    def _():
        load(slab_copies(info[0], pieces, qkv_slabs(qkv), sems))

    rows = x_ref[...]
    for j in range(3):
        part = mm(rows, qkv[j])
        if j != 1:
            part = part + vec_ref[j // 2 : j // 2 + 1, :]
        packed_ref[:, j * 768 : (j + 1) * 768] = part.astype(LOW)
    for s in range(segs):
        seg = (step + first_step) * segs + s
        allowed = segment_mask(info[1 + seg // seg_count], seg % seg_count)
        at = slice(s * SEG, (s + 1) * SEG)
        for h in range(6):
            q, k, v = (packed_ref[at, j * 768 + h * 128 : j * 768 + (h + 1) * 128] for j in range(3))
            mixed_ref[at, h * 128 : (h + 1) * 128] = attend(q, k, v, allowed).astype(LOW)


def norm_one(summed, vec_ref):
    normed, _ = normalize(summed)
    return normed * (1.0 + vec_ref[3:4, :]) + vec_ref[4:5, :]


def mid_forward_kernel(info, x_ref, mixed_ref, vec_ref, *rest):
    pieces, (sum_ref, low_ref, act_ref, slope_ref, out, up, sems) = rest[:10], rest[10:]

    @pl.when(pl.program_id(0) == 0)
    def _():
        load(slab_copies(info[0], pieces, mid_slabs(out, up), sems))

    summed = x_ref[...].astype(F32) + mm(mixed_ref[...], out[...]) + vec_ref[2:3, :]
    sum_ref[...] = summed
    first_low = norm_one(summed, vec_ref).astype(LOW)
    low_ref[...] = first_low
    hidden = mm(first_low, up[0]) + vec_ref[5:6, :]
    for j in range(4):
        later = mm(first_low, up[j + 1]) + vec_ref[6 + j : 7 + j, :] if j < 3 else None
        act, slope = gelu_parts(hidden)
        act_ref[:, j * 768 : (j + 1) * 768] = act.astype(LOW)
        slope_ref[:, j * 768 : (j + 1) * 768] = slope.astype(LOW)
        hidden = later


def down_forward_kernel(segs, info, sum_ref, act_ref, vec_ref, *rest):
    pieces, (second_ref, heads_ref, down, sems) = rest[:8], rest[8:]

    @pl.when(pl.program_id(0) == 0)
    def _():
        load(slab_copies(info[0], pieces, down_slabs(down), sems))

    total = norm_one(sum_ref[...], vec_ref) + vec_ref[9:10, :] + mm(act_ref[...], down[...])
    second_ref[...] = total
    opening = jnp.concatenate([total[s * SEG : s * SEG + 1] for s in range(segs)], axis=0)
    normed, _ = normalize(opening)
    heads_ref[...] = normed * (1.0 + vec_ref[10:11, :]) + vec_ref[11:12, :]


def cross_kernel(blocks, info, heads_ref, up_ref, live_ref, vec_ref, pos_ref, *rest):
    wide, rest = rest[0], rest[1:]
    (own_ref, own_grad_ref, grads_ref, pos_grad_ref, qkv_grad_ref, out_grad_ref, up_grad_ref, down_grad_ref) = rest[:8]
    (qkv, out, up, down, sems, result, heads_grad, slope, lefts, act, packed, rights, hidden_grad) = rest[8:]
    step = pl.program_id(0)
    count = heads_ref.shape[0]
    at = pl.ds(pl.multiple_of(step * count, count), count)
    targets = [qkv.at[j] for j in range(3)] + [out] + [up.at[j] for j in range(4)]
    targets += [down.at[j * 768 : (j + 1) * 768] for j in range(4)]
    copies = [pltpu.make_async_copy(wide.at[j], t, sems.at[j]) for j, t in enumerate(targets)]

    @pl.when(step == 0)
    def _():
        for copy in copies:
            copy.start()
        grads_ref[...] = jnp.zeros_like(grads_ref)
        pos_grad_ref[...] = jnp.zeros_like(pos_grad_ref)
        for copy in copies[:3]:
            copy.wait()

    vec = vec_ref[...]
    inputs = heads_ref[...].astype(F32).reshape(-1, 8, 768) + pos_ref[...][None]
    inputs = inputs.reshape(count, 768)
    low = inputs.astype(LOW)
    lefts[0, at, :] = low
    for j in range(3):
        part = mm(low, qkv[j])
        if j != 1:
            part = part + vec[j // 2 : j // 2 + 1]
        packed[:, j * 768 : (j + 1) * 768] = part.astype(LOW)
    row = lax.broadcasted_iota(jnp.int32, (SEG, 2 * SEG), 0)
    lane = lax.broadcasted_iota(jnp.int32, (SEG, 2 * SEG), 1)
    group = row // 8 == lane % SEG // 8
    masks = []
    for s in range(count // SEG):
        live = live_ref[s * SEG : (s + 1) * SEG, :]
        masks.append(group & (jnp.concatenate([live, live], axis=1) > 0.0))
    for s, allowed in enumerate(masks):
        part = slice(s * SEG, (s + 1) * SEG)
        for h in range(6):
            q, k, v = (packed[part, j * 768 + h * 128 : j * 768 + (h + 1) * 128] for j in range(3))
            where = pl.ds(pl.multiple_of(step * count + s * SEG, SEG), SEG)
            lefts[1, where, h * 128 : (h + 1) * 128] = attend(q, k, v, allowed).astype(LOW)

    @pl.when(step == 0)
    def _():
        for copy in copies[3:]:
            copy.wait()

    summed = inputs + mm(lefts[1, at, :], out[...]) + vec[2:3]
    normed_one, scale_one = normalize(summed)
    first = normed_one * (1.0 + vec[3:4]) + vec[4:5]
    first_low = first.astype(LOW)
    lefts[2, at, :] = first_low
    total = first + vec[9:10]
    for j in range(4):
        cols = slice(j * 768, (j + 1) * 768)
        hidden = mm(first_low, up[j]) + vec[5 + j : 6 + j]
        active, steep = gelu_parts(hidden)
        act[at, cols] = active.astype(LOW)
        slope[:, cols] = steep.astype(LOW)
        total = total + mm(active.astype(LOW), down[cols, :])
    normed, inv_scale = normalize(total)
    result[at, :] = normed * (1.0 + vec[10:11]) + vec[11:12]
    upstream = up_ref[...].astype(F32)
    back_two = normalize_back(upstream * (1.0 + vec[10:11]), normed, inv_scale)
    down_grad = back_two.astype(LOW)
    rights[1, at, :] = down_grad
    grads_ref[9:10, :] += column_sum(down_grad)
    grads_ref[10:11, :] += column_sum(upstream * normed)
    grads_ref[11:12, :] += column_sum(upstream)
    total = back_two
    for j in range(4):
        cols = slice(j * 768, (j + 1) * 768)
        grad = (mm_nt(down_grad, down[cols, :]) * slope[:, cols].astype(F32)).astype(LOW)
        hidden_grad[at, cols] = grad
        grads_ref[5 + j : 6 + j, :] += column_sum(grad)
        total = total + mm_nt(grad, up[j])
    back_one = normalize_back(total * (1.0 + vec[3:4]), normed_one, scale_one)
    proj_grad = back_one.astype(LOW)
    rights[0, at, :] = proj_grad
    grads_ref[2:3, :] += column_sum(proj_grad)
    grads_ref[3:4, :] += column_sum(total * normed_one)
    grads_ref[4:5, :] += column_sum(total)
    mixed_grad = mm_nt(proj_grad, out[...]).astype(LOW)
    for s, allowed in enumerate(masks):
        part = slice(s * SEG, (s + 1) * SEG)
        where = pl.ds(pl.multiple_of(step * count + s * SEG, SEG), SEG)
        for h in range(6):
            cols = slice(h * 128, (h + 1) * 128)
            q, k, v = (packed[part, j * 768 + h * 128 : j * 768 + (h + 1) * 128] for j in range(3))
            for j, g in enumerate(attend_back(q, k, v, mixed_grad[part, cols], allowed)):
                rights[2 + j, where, cols] = g.astype(LOW)
    total = back_one
    for j in range(3):
        part = rights[2 + j, at, :]
        total = total + mm_nt(part, qkv[j])
        if j != 1:
            grads_ref[j // 2 : j // 2 + 1, :] += column_sum(part)
    heads_grad[at, :] = total
    pos_grad_ref[...] += jnp.sum(total.reshape(-1, 8, 768), axis=0)

    @pl.when(step == blocks - 1)
    def _():
        me = info[1]
        own = pl.ds(pl.multiple_of(me * 16, 16), 16)
        own_ref[...] = result[own, :]
        own_grad_ref[...] = heads_grad[own, :]

        def chosen(left, rows):
            width = left.shape[1]
            wanted = lax.broadcasted_iota(jnp.int32, (rows, width), 1) - lax.broadcasted_iota(
                jnp.int32, (rows, width), 0
            )
            pick = (wanted == me * rows).astype(F32).astype(LOW)
            return mm_nt(pick, left).astype(LOW)

        left = chosen(lefts[0], 24)
        for j in range(3):
            qkv_grad_ref[:, j * 768 : (j + 1) * 768] = mm(left, rights[2 + j])
        out_grad_ref[...] = mm(chosen(lefts[1], 24), rights[0])
        left = chosen(lefts[2], 24)
        for j in range(4):
            cols = slice(j * 768, (j + 1) * 768)
            up_grad_ref[:, cols] = mm(left, hidden_grad[:, cols])
        for j in range(4):
            left = chosen(act[:, j * 768 : (j + 1) * 768], 24)
            down_grad_ref[j * 24 : (j + 1) * 24, :] = mm(left, rights[1])


def column_sum(value):
    return jnp.sum(value.astype(F32), axis=0, keepdims=True)


def ffn_back_rows(upstream, second, summed, slope, vec, grads_ref, hidden_grad, out, up, down):
    normed, inv_scale = normalize(second)
    back_two = normalize_back(upstream * (1.0 + vec[10:11, :]), normed, inv_scale)
    down_grad = back_two.astype(LOW)
    grads_ref[9:10, :] += column_sum(down_grad)
    grads_ref[10:11, :] += column_sum(upstream * normed)
    grads_ref[11:12, :] += column_sum(upstream)
    total = back_two
    for j in range(4):
        cols = slice(j * 768, (j + 1) * 768)
        grad = (mm_nt(down_grad, down[cols, :]) * slope(cols).astype(F32)).astype(LOW)
        hidden_grad(cols, grad)
        grads_ref[5 + j : 6 + j, :] += column_sum(grad)
        total = total + mm_nt(grad, up[j])
    normed, inv_scale = normalize(summed)
    back_one = normalize_back(total * (1.0 + vec[3:4, :]), normed, inv_scale)
    proj_grad = back_one.astype(LOW)
    grads_ref[2:3, :] += column_sum(proj_grad)
    grads_ref[3:4, :] += column_sum(total * normed)
    grads_ref[4:5, :] += column_sum(total)
    return down_grad, proj_grad, mm_nt(proj_grad, out[...]).astype(LOW)


def load_ffn(place, mid, rest, out, up, down, sems):
    return slab_copies(place, rest, down_slabs(down), sems, 40) + slab_copies(place, mid, mid_slabs(out, up), sems)


def ffn_backward_kernel(segs, seg_count, first_step, info, cot_ref, second_ref, sum_ref, slope_ref, vec_ref, *rest):
    mid, more, rest = rest[:10], rest[10:18], rest[-10:]
    out_ref, down_grad_ref, hidden_grad_ref, proj_grad_ref, mixed_grad_ref, grads_ref, out, up, down, sems = rest
    step = pl.program_id(0)

    @pl.when(step == 0)
    def _():
        load(load_ffn(info[0], mid, more, out, up, down, sems))
        grads_ref[...] = jnp.zeros_like(grads_ref)

    second = second_ref[...]
    normed, _ = normalize(second)
    result = normed * (1.0 + vec_ref[10:11, :]) + vec_ref[11:12, :]
    row = lax.broadcasted_iota(jnp.int32, (SEG, 1), 0)
    ups = []
    for s in range(segs):
        seg = (step + first_step) * segs + s
        at = slice(s * SEG, (s + 1) * SEG)
        live = row + seg % seg_count * SEG < info[1 + seg // seg_count]
        out_ref[at, :] = jnp.where(live, result[at], 0.0).astype(LOW)
        ups.append(jnp.where(live & (row > 0), cot_ref[at, :].astype(F32), 0.0))

    def store(cols, grad):
        hidden_grad_ref[:, cols] = grad

    down_grad_ref[...], proj_grad_ref[...], mixed_grad_ref[...] = ffn_back_rows(
        jnp.concatenate(ups, axis=0), second, sum_ref[...], lambda cols: slope_ref[:, cols], vec_ref, grads_ref, store,
        out, up, down,
    )


def opening_kernel(segs, seg_count, info, heads_ref, heads_grad_ref, vec_ref, *rest):
    tops_in, sources, mid, more, rest = rest[:5], rest[5:8], rest[8:18], rest[18:26], rest[26:]
    tops_out, grads_ref, tops, parts, hidden = rest[:5], rest[5], rest[6:11], rest[11:14], rest[14]
    out, up, down, sems, top_sems = rest[15:]
    copies = load_ffn(info[0], mid, more, out, up, down, sems)
    for i, (source, target) in enumerate(zip((*tops_in, *sources), (*tops, *parts))):
        copies.append(pltpu.make_async_copy(source.at[:, 0 : target.shape[1], :], target, top_sems.at[i]))
    load(copies)
    grads_ref[...] = jnp.zeros_like(grads_ref)
    second, summed, slope = (part[:, 0, :] if part.shape[1] == 8 else part for part in parts)
    slope = slope[...].astype(F32)[:, 0, :]

    def store(cols, grad):
        hidden[:, cols] = grad.astype(F32)

    down_grad, proj_grad, mixed_grad = ffn_back_rows(
        heads_grad_ref[...], second, summed, lambda cols: slope[:, cols], vec_ref, grads_ref, store, out, up, down
    )
    seg = lax.broadcasted_iota(jnp.int32, (segs, 1), 0)
    length = jnp.full((segs, 1), info[1], jnp.int32)
    for i in range(1, segs // seg_count):
        length = jnp.where(seg >= i * seg_count, info[1 + i], length)
    merged = jnp.where(lax.rem(seg, seg_count) * SEG < length, heads_ref[...], 0.0)
    outs = []
    values = (merged, down_grad.astype(F32), hidden[...], proj_grad.astype(F32), mixed_grad.astype(F32))
    for i, (value, top) in enumerate(zip(values, tops)):
        row = lax.broadcasted_iota(jnp.int32, top.shape, 1)
        top[...] = jnp.where(row == 0, value[:, None, :], top[...].astype(F32)).astype(LOW)
        outs.append(pltpu.make_async_copy(top, tops_out[i].at[:, 0:16, :], top_sems.at[i]))
    load(outs)


def attn_backward_kernel(segs, seg_count, first_step, info, packed_ref, mixed_grad_ref, *rest):
    packed_grad_ref, grads_ref = rest[-2:]
    step = pl.program_id(0)

    @pl.when(step == 0)
    def _():
        grads_ref[...] = jnp.zeros_like(grads_ref)

    for s in range(segs):
        seg = (step + first_step) * segs + s
        allowed = segment_mask(info[1 + seg // seg_count], seg % seg_count)
        at = slice(s * SEG, (s + 1) * SEG)
        for h in range(6):
            cols = [slice(j * 768 + h * 128, j * 768 + (h + 1) * 128) for j in range(3)]
            q, k, v = (packed_ref[at, c] for c in cols)
            grads = attend_back(q, k, v, mixed_grad_ref[at, cols[0]], allowed)
            for c, g in zip(cols, grads):
                packed_grad_ref[at, c] = g.astype(LOW)
    grads_ref[0:1, :] += column_sum(packed_grad_ref[:, :768])
    grads_ref[1:2, :] += column_sum(packed_grad_ref[:, 1536:])


def token_grad_kernel(info, packed_grad_ref, proj_grad_ref, *rest):
    pieces, (token_grad_ref, qkv, sems) = rest[:10], rest[10:]

    @pl.when(pl.program_id(0) == 0)
    def _():
        load(slab_copies(info[0], pieces, qkv_slabs(qkv), sems))

    total = proj_grad_ref[...].astype(F32)
    for j in range(3):
        total = total + mm_nt(packed_grad_ref[:, j * 768 : (j + 1) * 768], qkv[j])
    token_grad_ref[...] = total.astype(LOW)


def send_slab(place, total, keep_ref, send_ref, rows):
    for mask in range(8):
        block = pl.multiple_of((place ^ mask) * rows, rows)
        target = send_ref if mask % 2 else keep_ref
        target[mask // 2] = total[pl.ds(block, rows), :].astype(LOW)


def qkv_grad_kernel(info, left_ref, right_ref, more_ref, keep_ref, send_ref, total):
    step = pl.program_id(0)
    total[...] = mm_tn(left_ref[...], right_ref[...])
    at = pl.ds(pl.multiple_of(step * 96, 96), 96)
    for mask in range(8):
        block = pl.multiple_of((info[0] ^ mask) * 96, 96)
        target = send_ref if mask % 2 else keep_ref
        target[mask // 2, at, :] = total[pl.ds(block, 96), :].astype(LOW)

    @pl.when(step == 0)
    def _():
        for mask in range(8):
            target = send_ref if mask % 2 else keep_ref
            target[mask // 2, 288:304, :] = more_ref[mask]


def mid_grad_kernel(info, mixed_ref, proj_ref, low_ref, hidden_ref, keep_ref, send_ref, total):
    @pl.when(pl.program_id(0) == 0)
    def _():
        total[...] = mm_tn(mixed_ref[...], proj_ref[...])

    @pl.when(pl.program_id(0) > 0)
    def _():
        total[...] = mm_tn(low_ref[...], hidden_ref[...])

    send_slab(info[0], total, keep_ref, send_ref, 96)


ANY = pl.BlockSpec(memory_space=pl.ANY)
SMEM = pl.BlockSpec(memory_space=pltpu.SMEM)


def block_rows(count, width):
    return pl.BlockSpec((count, width), lambda i: (i, 0))


def fixed(shape):
    return pl.BlockSpec(shape, lambda i: (0,) * len(shape))


def shape_of(dims, kind=LOW):
    return jax.ShapeDtypeStruct(dims, kind)


def params():
    return pltpu.CompilerParams(vmem_limit_bytes=VMEM, dimension_semantics=("arbitrary",))


def cost(flops, size):
    return pl.CostEstimate(flops=flops, bytes_accessed=size, transcendentals=0)


QKV = [pltpu.VMEM((3, 768, 768), LOW)]
MID = [pltpu.VMEM((768, 768), LOW), pltpu.VMEM((4, 768, 768), LOW)]
DOWN = [pltpu.VMEM((3072, 768), LOW)]


def sems(count):
    return [pltpu.SemaphoreType.DMA((count,))]


def shifted(count, width, first):
    return pl.BlockSpec((count, width), lambda i: (i + first, 0))


def attn_forward(info, rows_in, vec, pieces, seg_count, half, before=None, segs=4):
    rows = rows_in.shape[0]
    count = segs * SEG
    steps = rows // count // 2
    first = half * steps
    before = list(before or [])
    return pl.pallas_call(
        functools.partial(attn_forward_kernel, segs, seg_count, first),
        grid=(steps,),
        in_specs=[SMEM, shifted(count, 768, first), fixed((12, 768))] + [ANY] * (10 + len(before)),
        out_specs=[shifted(count, 2304, first), shifted(count, 768, first)],
        out_shape=[shape_of((rows, 2304)), shape_of((rows, 768))],
        scratch_shapes=QKV + sems(24),
        input_output_aliases={13: 0, 14: 1} if before else {},
        compiler_params=params(),
        cost_estimate=cost(rows * 768 * 8000, rows * 768 * 8),
        name="attn_forward",
    )(info, rows_in, vec, *pieces, *before)


def mid_forward(info, rows_in, mixed, vec, pieces, segs=2):
    rows = rows_in.shape[0]
    count = segs * SEG
    return pl.pallas_call(
        mid_forward_kernel,
        grid=(rows // count,),
        in_specs=[SMEM, block_rows(count, 768), block_rows(count, 768), fixed((12, 768))] + [ANY] * 10,
        out_specs=[block_rows(count, 768), block_rows(count, 768), block_rows(count, 3072), block_rows(count, 3072)],
        out_shape=[shape_of((rows, 768), F32), shape_of((rows, 768)), shape_of((rows, 3072)), shape_of((rows, 3072))],
        scratch_shapes=MID + sems(40),
        compiler_params=params(),
        cost_estimate=cost(2 * rows * 768 * 8000, rows * 768 * 30),
        name="mid_forward",
    )(info, rows_in, mixed, vec, *pieces)


def down_forward(info, summed, act, vec, pieces, segs=2):
    rows = summed.shape[0]
    count = segs * SEG
    few = pl.BlockSpec((None, segs, 768), lambda i: (i, 0, 0))
    return pl.pallas_call(
        functools.partial(down_forward_kernel, segs),
        grid=(rows // count,),
        in_specs=[SMEM, block_rows(count, 768), block_rows(count, 3072), fixed((12, 768))] + [ANY] * 8,
        out_specs=[block_rows(count, 768), few],
        out_shape=[shape_of((rows, 768), F32), shape_of((rows // count, segs, 768), F32)],
        scratch_shapes=DOWN + sems(32),
        compiler_params=params(),
        cost_estimate=cost(2 * rows * 768 * 4000, rows * 768 * 16),
        name="down_forward",
    )(info, summed, act, vec, *pieces)


def cross_whole(info, heads, upstream, live, vec, positions, wide):
    rows = heads.shape[0]
    count = 2 * SEG
    own = [(16, 768), (16, 768), (12, 768), (8, 768), (24, 2304), (24, 768), (24, 3072), (96, 768)]
    return pl.pallas_call(
        functools.partial(cross_kernel, rows // count),
        grid=(rows // count,),
        in_specs=[SMEM, block_rows(count, 768), block_rows(count, 768), block_rows(count, SEG),
                  fixed((12, 768)), fixed((8, 768)), ANY],
        out_specs=[fixed(dims) for dims in own],
        out_shape=[shape_of(dims, F32) for dims in own],
        scratch_shapes=QKV + MID + DOWN + sems(12) + [
            pltpu.VMEM((rows, 768), F32), pltpu.VMEM((rows, 768), F32), pltpu.VMEM((count, 3072), LOW),
            pltpu.VMEM((3, rows, 768), LOW), pltpu.VMEM((rows, 3072), LOW), pltpu.VMEM((count, 2304), LOW),
            pltpu.VMEM((5, rows, 768), LOW), pltpu.VMEM((rows, 3072), LOW),
        ],
        compiler_params=params(),
        cost_estimate=cost(2 * rows * 768 * 30000, 2**24),
        name="cross_encoder",
    )(info, heads, upstream, live, vec, positions, wide)


def ffn_backward(info, cotangent, second, summed, slope, vec, mid, down, seg_count, half, before=None, segs=2):
    rows = summed.shape[0]
    count = segs * SEG
    steps = rows // count // 2
    first = half * steps
    before = list(before or [])
    widths = (768, 768, 3072, 768, 768)
    return pl.pallas_call(
        functools.partial(ffn_backward_kernel, segs, seg_count, first),
        grid=(steps,),
        in_specs=[SMEM, shifted(count, 768, first), shifted(count, 768, first), shifted(count, 768, first),
                  shifted(count, 3072, first), fixed((12, 768))] + [ANY] * (18 + len(before)),
        out_specs=[shifted(count, w, first) for w in widths] + [fixed((12, 768))],
        out_shape=[shape_of((rows, w)) for w in widths] + [shape_of((12, 768), F32)],
        scratch_shapes=MID + DOWN + sems(72),
        input_output_aliases={24 + i: i for i in range(5)} if before else {},
        compiler_params=params(),
        cost_estimate=cost(rows * 768 * 14000, rows * 768 * 15),
        name="ffn_backward",
    )(info, cotangent, second, summed, slope, vec, *mid, *down, *before)


def opening_backward(info, heads, heads_grad, vec, arrays, sources, mid, down, seg_count):
    segs = heads.shape[0]

    def grouped(array):
        return array.reshape(segs, SEG, array.shape[1])

    arrays, sources = [grouped(a) for a in arrays], [grouped(a) for a in sources]
    whole = fixed((segs, 768))
    *done, grads = pl.pallas_call(
        functools.partial(opening_kernel, segs, seg_count),
        grid=(1,),
        in_specs=[SMEM, whole, whole, fixed((12, 768))] + [ANY] * 26,
        out_specs=[ANY] * 5 + [fixed((12, 768))],
        out_shape=[shape_of(a.shape) for a in arrays] + [shape_of((12, 768), F32)],
        scratch_shapes=[pltpu.VMEM((segs, 16, a.shape[2]), LOW) for a in arrays]
        + [pltpu.VMEM((segs, 8, 768), F32)] * 2
        + [pltpu.VMEM((segs, 16, 3072), LOW), pltpu.VMEM((segs, 3072), F32)]
        + MID + DOWN + sems(72) + sems(8),
        input_output_aliases={4 + i: i for i in range(5)},
        compiler_params=params(),
        cost_estimate=cost(2**33, 2**24),
        name="opening_backward",
    )(info, heads, heads_grad, vec, *arrays, *sources, *mid, *down)
    return [a.reshape(-1, a.shape[2]) for a in done], grads


def attn_backward(info, packed, mixed_grad, seg_count, half, before=None, segs=2):
    rows = packed.shape[0]
    count = segs * SEG
    steps = rows // count // 2
    first = half * steps
    before = [] if before is None else [before]
    return pl.pallas_call(
        functools.partial(attn_backward_kernel, segs, seg_count, first),
        grid=(steps,),
        in_specs=[SMEM, shifted(count, 2304, first), shifted(count, 768, first)] + [ANY] * len(before),
        out_specs=[shifted(count, 2304, first), fixed((2, 768))],
        out_shape=[shape_of((rows, 2304)), shape_of((2, 768), F32)],
        input_output_aliases={3: 0} if before else {},
        compiler_params=params(),
        cost_estimate=cost(rows * 768 * 10000, rows * 768 * 8),
        name="attn_backward",
    )(info, packed, mixed_grad, *before)


def token_gradient(info, packed_grad, proj_grad, pieces, count=512):
    rows = packed_grad.shape[0]
    return pl.pallas_call(
        token_grad_kernel,
        grid=(rows // count,),
        in_specs=[SMEM, block_rows(count, 2304), block_rows(count, 768)] + [ANY] * 10,
        out_specs=block_rows(count, 768),
        out_shape=shape_of((rows, 768)),
        scratch_shapes=QKV + sems(24),
        compiler_params=params(),
        cost_estimate=cost(2 * rows * 768 * 3000, rows * 768 * 10),
        name="token_gradient",
    )(info, packed_grad, proj_grad, *pieces)


def grad_outs(slabs):
    out = pl.BlockSpec((4, 96, 768), lambda i: (0, i, 0))
    return [out, out], [shape_of((4, slabs * 96, 768))] * 2


def qkv_weight_grad(info, left, right, more):
    rows = left.shape[0]
    out = fixed((4, 304, 768))
    return pl.pallas_call(
        qkv_grad_kernel,
        grid=(3,),
        in_specs=[SMEM, fixed((rows, 768)), pl.BlockSpec((rows, 768), lambda i: (0, i)), fixed((8, 16, 768))],
        out_specs=[out, out],
        out_shape=[shape_of((4, 304, 768))] * 2,
        scratch_shapes=[pltpu.VMEM((768, 768), F32)],
        compiler_params=params(),
        cost_estimate=cost(2 * rows * 768 * 2304, rows * 2304 * 2),
        name="qkv_weight_grad",
    )(info, left, right, more)


def mid_weight_grad(info, mixed, proj_grad, low, hidden_grad):
    rows = mixed.shape[0]
    specs, shapes = grad_outs(5)
    still = fixed((rows, 768))
    return pl.pallas_call(
        mid_grad_kernel,
        grid=(5,),
        in_specs=[SMEM, still, still, still, pl.BlockSpec((rows, 768), lambda i: (0, jnp.maximum(i - 1, 0)))],
        out_specs=specs,
        out_shape=shapes,
        scratch_shapes=[pltpu.VMEM((768, 768), F32)],
        compiler_params=params(),
        cost_estimate=cost(2 * rows * 768 * 3840, rows * 3840 * 2),
        name="mid_weight_grad",
    )(info, mixed, proj_grad, low, hidden_grad)


def down_grad_kernel(info, left_ref, right_ref, keep_ref, send_ref, total):
    step = pl.program_id(0)
    total[pl.ds(pl.multiple_of(step * 768, 768), 768), :] = mm_tn(left_ref[...], right_ref[...]).astype(LOW)

    @pl.when(step == pl.num_programs(0) - 1)
    def _():
        for mask in range(8):
            block = pl.multiple_of((info[0] ^ mask) * 384, 384)
            target = send_ref if mask % 2 else keep_ref
            target[mask // 2] = total[pl.ds(block, 384), :]


def down_weight_grad(info, left, right):
    rows, wide = left.shape
    return pl.pallas_call(
        down_grad_kernel,
        grid=(wide // 768,),
        in_specs=[SMEM, pl.BlockSpec((rows, 768), lambda i: (0, i)), fixed((rows, 768))],
        out_specs=[fixed((4, 384, 768))] * 2,
        out_shape=[shape_of((4, 384, 768))] * 2,
        scratch_shapes=[pltpu.VMEM((3072, 768), LOW)],
        compiler_params=params(),
        cost_estimate=cost(2 * rows * 768 * wide, rows * wide * 2),
        name="down_weight_grad",
    )(info, left, right)


def matmul(left_op, right_op):
    return jnp.dot(left_op, right_op, preferred_element_type=jnp.float32)


def trans_left(left_op, right_op):
    return lax.dot_general(
        left_op, right_op, (((0,), (0,)), ((), ())), preferred_element_type=jnp.float32
    )


def trans_right(left_op, right_op):
    return lax.dot_general(
        left_op, right_op, (((1,), (1,)), ((), ())), preferred_element_type=jnp.float32
    )


def norm_forward(summed, gain_row, shift_row):
    average = jnp.mean(summed, axis=-1, keepdims=True)
    centered = summed - average
    inv_scale = lax.rsqrt(jnp.mean(centered * centered, axis=-1, keepdims=True) + NORM_EPS)
    normed = centered * inv_scale
    return (normed * (1.0 + gain_row) + shift_row, normed, inv_scale)


def norm_backward(upstream, normed, inv_scale, gain_row):
    inner = upstream * (1.0 + gain_row)
    back_grad = inv_scale * (
        inner
        - jnp.mean(inner, axis=-1, keepdims=True)
        - normed * jnp.mean(inner * normed, axis=-1, keepdims=True)
    )
    return (back_grad, jnp.sum(upstream * normed, axis=0), jnp.sum(upstream, axis=0))


def gelu_slope(hidden):
    return (
        0.5 * (1.0 + lax.erf(hidden * ROOT_HALF))
        + hidden * jnp.exp(-0.5 * hidden * hidden) * INV_ROOT_TAU
    )


def split_heads(packed, group_len):
    head_count = packed.shape[1] // (3 * HEAD)
    return [
        portion.reshape(-1, group_len, head_count, HEAD) for portion in jnp.split(packed, 3, axis=1)
    ]


def masked_scores(query_heads, key_heads, allowed):
    raw_scores = jnp.einsum(
        "nqhd,nkhd->nhqk", query_heads, key_heads, preferred_element_type=jnp.float32
    ) * HEAD ** (-0.5)
    return jnp.where(allowed[:, None, None, :], raw_scores, MASK_FILL)


def encode(inputs, inputs_low, weights, allowed):
    qkv_w, out_w, up_w, down_w, vectors = weights
    row_count, feat_dim = inputs_low.shape
    group_len = allowed.shape[1]
    qkv_bias = jnp.concatenate([vectors[0], jnp.zeros_like(vectors[0]), vectors[1]])
    packed = (matmul(inputs_low, qkv_w) + qkv_bias).astype(jnp.bfloat16)
    query_heads, key_heads, value_heads = split_heads(packed, group_len)
    scores = masked_scores(query_heads, key_heads, allowed)
    row_max = jnp.max(scores, axis=-1, keepdims=True)
    expo_vals = jnp.exp(scores - row_max)
    row_total = jnp.sum(expo_vals, axis=-1, keepdims=True)
    log_total = row_max + jnp.log(row_total)
    prob_low = (expo_vals / row_total).astype(jnp.bfloat16)
    mixed = jnp.einsum("nhqk,nkhd->nqhd", prob_low, value_heads, preferred_element_type=jnp.float32)
    mixed = mixed.reshape(row_count, feat_dim).astype(jnp.bfloat16)
    projected = matmul(mixed, out_w) + vectors[2]
    first_out, normed_one, scale_one = norm_forward(inputs + projected, vectors[3], vectors[4])
    first_low = first_out.astype(jnp.bfloat16)
    hidden = matmul(first_low, up_w) + vectors[5:-3].reshape(-1)
    activated = jax.nn.gelu(hidden, approximate=False).astype(jnp.bfloat16)
    down_out = matmul(activated, down_w) + vectors[-3]
    result, normed_two, scale_two = norm_forward(first_out + down_out, vectors[-2], vectors[-1])
    return (
        result,
        (
            packed,
            log_total,
            mixed,
            normed_one,
            scale_one,
            first_low,
            hidden,
            activated,
            normed_two,
            scale_two,
        ),
    )


def encode_back(upstream, inputs_low, weights, allowed, kept):
    qkv_w, out_w, up_w, down_w, vectors = weights
    (
        packed,
        log_total,
        mixed,
        normed_one,
        scale_one,
        first_low,
        hidden,
        activated,
        normed_two,
        scale_two,
    ) = kept
    row_count, feat_dim = inputs_low.shape
    group_len = allowed.shape[1]
    back_two, gain_two, shift_two = norm_backward(upstream, normed_two, scale_two, vectors[-2])
    down_grad = back_two.astype(jnp.bfloat16)
    hidden_grad = (trans_right(down_grad, down_w) * gelu_slope(hidden)).astype(jnp.bfloat16)
    first_grad = trans_right(hidden_grad, up_w) + back_two
    back_one, gain_one, shift_one = norm_backward(first_grad, normed_one, scale_one, vectors[3])
    proj_grad = back_one.astype(jnp.bfloat16)
    query_heads, key_heads, value_heads = split_heads(packed, group_len)
    mixed_grad = trans_right(proj_grad, out_w).astype(jnp.bfloat16).reshape(value_heads.shape)
    scores = masked_scores(query_heads, key_heads, allowed)
    prob_vals = jnp.exp(scores - log_total)
    grad_values = jnp.einsum(
        "nhqk,nqhd->nkhd",
        prob_vals.astype(jnp.bfloat16),
        mixed_grad,
        preferred_element_type=jnp.float32,
    )
    grad_prob = jnp.einsum(
        "nqhd,nkhd->nhqk", mixed_grad, value_heads, preferred_element_type=jnp.float32
    )
    score_grad = (
        prob_vals * (grad_prob - jnp.sum(prob_vals * grad_prob, axis=-1, keepdims=True))
    ).astype(jnp.bfloat16)
    grad_query = jnp.einsum(
        "nhqk,nkhd->nqhd", score_grad, key_heads, preferred_element_type=jnp.float32
    ) * HEAD ** (-0.5)
    grad_keys = jnp.einsum(
        "nhqk,nqhd->nkhd", score_grad, query_heads, preferred_element_type=jnp.float32
    ) * HEAD ** (-0.5)
    packed_grad = jnp.concatenate(
        [
            grad_query.reshape(row_count, feat_dim),
            grad_keys.reshape(row_count, feat_dim),
            grad_values.reshape(row_count, feat_dim),
        ],
        axis=1,
    ).astype(jnp.bfloat16)
    bias_grads = jnp.sum(packed_grad, axis=0, dtype=jnp.float32).reshape(3, feat_dim)
    grad_inputs = trans_right(packed_grad, qkv_w) + back_one
    grad_vectors = jnp.concatenate(
        [
            bias_grads[0:1],
            bias_grads[2:3],
            jnp.sum(proj_grad, axis=0, dtype=jnp.float32)[None],
            gain_one[None],
            shift_one[None],
            jnp.sum(hidden_grad, axis=0, dtype=jnp.float32).reshape(-1, feat_dim),
            jnp.sum(down_grad, axis=0, dtype=jnp.float32)[None],
            gain_two[None],
            shift_two[None],
        ],
        axis=0,
    )
    pairs = (
        (inputs_low, packed_grad),
        (mixed, proj_grad),
        (first_low, hidden_grad),
        (activated, down_grad),
    )
    return (grad_inputs, pairs, grad_vectors)


class Links:
    def __init__(self, outer, inner):
        self.outer, self.inner = outer, inner
        self.order = self.place = lax.axis_index("dp")
        self.z = lax.axis_index("fsdp")

    def flip(self, value, mask):
        pairs = [
            (d * self.inner + z, (d ^ mask) * self.inner + z)
            for d in range(self.outer)
            for z in range(self.inner)
        ]
        return lax.ppermute(value, AXES, pairs)

    def turn(self, value, step):
        pairs = [
            (d * self.inner + z, d * self.inner + (z + step) % self.inner)
            for d in range(self.outer)
            for z in range(self.inner)
        ]
        return lax.ppermute(value, AXES, pairs)

    def gather_z(self, shard):
        came = [shard] + [self.turn(shard, step) for step in range(1, self.inner)]
        whole = []
        for z in range(self.inner):
            part = came[-1]
            for step in range(self.inner - 1):
                part = jnp.where(self.z == (z + step) % self.inner, came[step], part)
            whole.append(part)
        return whole

    def spread_near(self, block):
        return self.flip(block, 2), self.flip(block, 4)

    def spread_far(self, by_x, by_y, half):
        return self.flip(by_y[:half], 2), self.flip(by_x[half:], 4)

    def core(self, pieces):
        return [self.flip(piece, 1) for piece in pieces]

    def in_order(self, parts):
        for axis, mask in ((4, 4), (2, 2), (1, 1)):
            odd = self.place // axis % 2 == 1
            parts = [jnp.where(odd, parts[m ^ mask], parts[m]) for m in range(8)]
        return jnp.stack(parts)

    def gather_small(self, shard, line_only=False):
        block = jnp.stack(self.gather_z(shard))
        return block if line_only else self.gather_core(self.gather_plane(block))

    def gather_plane(self, block):
        return jnp.stack([block] + [self.flip(block, m) for m in (2, 4, 6)])

    def gather_core(self, plane):
        other = self.flip(plane, 1)
        whole = self.in_order([(plane, other)[m % 2][m // 2] for m in range(8)])
        return whole.reshape((-1,) + plane.shape[2:])


class PlainLinks:
    def __init__(self, outer, inner):
        self.outer, self.inner = outer, inner
        self.order = lax.axis_index("dp")
        self.z = lax.axis_index("fsdp")
        self.place = 0

    def gather_small(self, shard, line_only=False):
        return lax.all_gather(shard, AXES, axis=0)


def add(*terms):
    return sum(t.astype(F32) for t in terms).astype(LOW)


class Sum:
    def __init__(self, links, keep, send, slabs):
        self.links, self.keep, self.slabs = links, keep, slabs
        self.more = keep.shape[1] % 96
        self.came = links.flip(send, 1)

    def line(self, part):
        inner = self.links.inner
        count = part.shape[0] - self.more
        main = part[:count].reshape(self.slabs, inner, -1, part.shape[-1])
        main = main.transpose(1, 0, 2, 3).reshape(inner, -1, part.shape[-1])
        if not self.more:
            return main
        rows = part[count : count + inner].reshape(inner, 1, -1)
        return jnp.concatenate([main, jnp.pad(rows, ((0, 0), (0, 7), (0, 0)))], axis=1)

    def to(self, index):
        return self.line(add(self.keep[index], self.came[index]))

    def far(self):
        half = self.links.inner // 2
        to_d = self.to(3)
        self.far_came = [self.links.flip(to_d[:half], 2), self.links.flip(to_d[half:], 4)]
        return self.far_came

    def near(self):
        half = self.links.inner // 2
        came_x, came_y = self.far_came
        to_x, to_y = self.to(1), self.to(2)
        to_y = jnp.concatenate([add(to_y[:half], came_x), to_y[half:]])
        to_x = jnp.concatenate([to_x[:half], add(to_x[half:], came_y)])
        self.near_came = [self.links.flip(to_x, 2), self.links.flip(to_y, 4)]
        return self.near_came

    def direct(self):
        self.near_came = [self.links.flip(self.to(m // 2), m) for m in (2, 4, 6)]
        return self.near_came

    def turn(self, *earlier):
        links = self.links
        own = add(self.line(self.keep[0]), self.line(self.came[0]), *self.near_came)
        own = after(own, *earlier) if earlier else own
        parts = [lax.dynamic_index_in_dim(own, (links.z + k) % links.inner, 0, keepdims=False) for k in range(links.inner)]
        self.turned = [parts[0]] + [links.turn(parts[k], k) for k in range(1, links.inner)]
        return self.turned[1:]

    def total(self, *earlier):
        parts = [after(t, *earlier) for t in self.turned] if earlier else self.turned
        return sum(t.astype(F32) for t in parts)


class PlainSum:
    def __init__(self, links, keep, send, slabs):
        more = keep.shape[1] % 96
        flat = jnp.stack([keep, send], axis=1).reshape(8, -1, 768)
        main = flat[:, : flat.shape[1] - more].reshape(8, slabs, -1, 768)
        main = main.transpose(1, 0, 2, 3).reshape(slabs, -1, 768)
        self.came = keep
        self.sums = lax.psum_scatter(main, AXES, scatter_dimension=1, tiled=True).reshape(-1, 768)
        if more:
            rows = flat[:, flat.shape[1] - more :][:, : links.outer * links.inner // 8].reshape(-1, 768)
            self.sums = jnp.concatenate([self.sums, lax.psum_scatter(rows, AXES, scatter_dimension=0, tiled=True)])

    def far(self, *earlier):
        return []

    near = direct = turn = far

    def total(self, *earlier):
        return self.sums.astype(F32)


def after(value, *earlier):
    return lax.optimization_barrier((value, *earlier))[0]


def slabs_of(matrix):
    rows, wide = matrix.shape
    return matrix.reshape(rows, wide // 768, 768).transpose(1, 0, 2)


def matrix_of(slabs):
    count, rows, width = slabs.shape
    return slabs.transpose(1, 0, 2).reshape(rows, count * width)


def mix_columns(matrix, devices):
    rows, wide = matrix.shape
    matrix = matrix.reshape(rows, devices, 4, -1).transpose(0, 2, 1, 3)
    return matrix.reshape(rows, wide)


def unmix_columns(matrix, devices):
    rows, wide = matrix.shape
    matrix = matrix.reshape(rows, 4, devices, -1).transpose(0, 2, 1, 3)
    return matrix.reshape(rows, wide)


def plain_pieces(slabs, whole):
    count = slabs.shape[0]
    half = (count + 1) // 2 * 96
    parts = []
    for mask in (0, 2, 4, 6, 1, 3, 5, 7):
        part = slabs[:, mask * 96 : (mask + 1) * 96].reshape(-1, 768)
        parts += [part] if whole or mask < 6 and mask != 7 else [part[:half], part[half:]]
    return parts


def shards(
    outer,
    inner,
    tokens,
    cotangent,
    lengths,
    seg_qkv,
    seg_out,
    seg_up,
    seg_down,
    seg_vec,
    cross_qkv,
    cross_out,
    cross_up,
    cross_down,
    cross_vec,
    positions,
):
    fast = (outer, inner) == (8, 4)
    links = (Links if fast else PlainLinks)(outer, inner)
    summing = Sum if fast else PlainSum
    devices = outer * inner
    me = links.order * inner + links.z
    seq_local, seq_len, feat_dim = tokens.shape
    seg_count = seq_len // SEG
    seg_rows, cross_rows = seg_vec.shape[0], cross_vec.shape[0]
    width = feat_dim // devices
    my_lengths = lax.dynamic_slice_in_dim(lengths, me * seq_local, seq_local)
    info = jnp.concatenate([jnp.full((1,), links.place, jnp.int32), my_lengths])
    small = jnp.concatenate([seg_vec, cross_vec, positions]).reshape(1, -1)
    up_slabs = mix_columns(cross_up, devices).reshape(-1, 4, feat_dim).transpose(1, 0, 2)
    wide = [slabs_of(cross_qkv), slabs_of(cross_out), up_slabs, cross_down.reshape(4, -1, feat_dim)]
    wide = jnp.concatenate(wide)
    mid_shard = jnp.concatenate([slabs_of(seg_out), slabs_of(seg_up)])
    rows_in = tokens.reshape(-1, feat_dim)
    cot_rows = cotangent.reshape(-1, feat_dim)
    seg_starts = jnp.arange(seg_count) * SEG
    live_own = (seg_starts[None, :] < my_lengths[:, None]).reshape(-1, 1)
    up_own = jnp.where(live_own, cotangent.reshape(-1, SEG, feat_dim)[:, 0, :], 0)

    if fast:
        first = jnp.concatenate([slabs_of(seg_qkv).reshape(-1, 768), jnp.pad(small, ((0, 7), (0, 0)))])
        line_first = links.gather_z(first)
        line_mid = links.gather_z(after(mid_shard, *line_first))
        weights = jnp.stack([p[:72].reshape(3, 24, 768) for p in line_first], axis=1).reshape(-1, 768)
        rows = jnp.concatenate([p[72:73] for p in line_first])
        block = jnp.concatenate([weights, jnp.pad(rows, ((0, 12), (0, 0)))])
        near = links.spread_near(block)
        far = links.spread_far(*near, 192)
        first = [block, *near, *far, *links.core([after(p, *far, *line_mid) for p in (block, *near, *far)])]
        line_down = links.gather_z(after(seg_down, *first[5:]))
        ends = [p[288:292] for p in first[:3]] + [first[4][96:100]]
        others = [p[288:292] for p in first[5:8]] + [first[9][96:100]]
        small = links.in_order([(ends, others)[m % 2][m // 2] for m in range(8)])
        block = after(jnp.stack(line_mid, axis=1).reshape(-1, 768), *far)
        mid = [block, *links.spread_near(block)]
    else:
        first = plain_pieces(lax.all_gather(slabs_of(seg_qkv), AXES, axis=1, tiled=True), False)
        mid = plain_pieces(lax.all_gather(mid_shard, AXES, axis=1, tiled=True), False)
        down_whole = lax.all_gather(seg_down, AXES, axis=0, tiled=True)
        down = [down_whole[m * 384 : (m + 1) * 384] for m in (0, 2, 4, 6, 1, 3, 5, 7)]
        small = links.gather_small(small)
    small = small.reshape(devices, -1, width).transpose(1, 0, 2).reshape(-1, feat_dim).astype(F32)
    seg_v, cross_v = small[:seg_rows], small[seg_rows : seg_rows + cross_rows]
    pos_table = small[seg_rows + cross_rows :]
    hidden_rows = slice(5, cross_rows - 3)
    cross_v = cross_v.at[hidden_rows].set(mix_columns(cross_v[hidden_rows].reshape(1, -1), devices).reshape(-1, feat_dim))

    before = attn_forward(info, rows_in, seg_v, first, seg_count, 0)
    wide = lax.all_gather(after(wide, before[0], *((*mid[1:], *line_down) if fast else ())), AXES, axis=1, tiled=True)
    if fast:
        far = links.spread_far(*(after(p, before[0]) for p in mid[1:]), 288)
        rows_late = after(rows_in, *mid[1:])
    else:
        rows_late = rows_in
    packed, mixed = attn_forward(info, rows_late, seg_v, first, seg_count, 1, before)
    if fast:
        early = links.core([after(p, before[0]) for p in mid])
        late = links.core([after(p, packed, *far, *early) for p in far])
        mid = [*mid, *far, *early, *late]
        block = after(jnp.concatenate(line_down), *late)
        near = [links.flip(block, m) for m in (2, 4, 6)]
    summed, low, act, slope = mid_forward(info, rows_in, mixed, seg_v, mid)
    if fast:
        down = [block, *near, links.flip(block, 1), *(links.flip(after(p, act), 1) for p in near)]
    second, heads = down_forward(info, summed, act, seg_v, down)
    heads_own = heads.reshape(-1, feat_dim)
    both = links.gather_small(jnp.stack([heads_own.astype(LOW), up_own]), True)
    back = functools.partial(ffn_backward, info, seg_count=seg_count)
    args = (second, summed, slope, seg_v, mid, down)
    if fast:
        first_half = back(cot_rows, *args, half=0)
        both = links.gather_plane(after(both, first_half[1]))
        *arrays, grads_two = back(after(cot_rows, first_half[1]), *args, half=1, before=first_half[:5])
        both = links.gather_core(after(both, arrays[1]))
    heads_all, up_all = both[:, 0].reshape(-1, feat_dim), both[:, 1].reshape(-1, feat_dim)
    live_all = seg_starts[None, :] < lengths[:, None]
    if fast:
        cross_info = jnp.stack([links.place, me]).astype(jnp.int32)
        live = jnp.broadcast_to(live_all.reshape(-1, 1), (live_all.size, SEG)).astype(F32)
        cross_own, heads_grad, vec_grad, pos_grad, *cross_grads = cross_whole(
            cross_info, heads_all, up_all, live, cross_v, pos_table, wide
        )
    else:
        weights = (matrix_of(wide[:3]), wide[3], matrix_of(wide[4:8]), wide[8:].reshape(-1, feat_dim), cross_v)
        heads_in = heads_all.astype(F32).reshape(-1, seg_count, feat_dim) + pos_table[None]
        heads_in = heads_in.reshape(-1, feat_dim)
        cross_result, kept = encode(heads_in, heads_in.astype(LOW), weights, live_all)
        all_grad, pairs, vec_grad = encode_back(
            up_all.astype(F32), heads_in.astype(LOW), weights, live_all, kept
        )
        cross_grads = []
        for left, right in pairs:
            left = left.reshape(left.shape[0], -1, feat_dim)
            mine = lax.dynamic_slice_in_dim(left, me * width, width, 2)
            cross_grads.append(trans_left(mine.reshape(left.shape[0], -1), right))
        pos_grad = jnp.sum(all_grad.reshape(-1, seg_count, feat_dim), axis=0)
        own = seq_local * seg_count
        cross_own = lax.dynamic_slice_in_dim(cross_result, me * own, own)
        heads_grad = lax.dynamic_slice_in_dim(all_grad, me * own, own)
        first_half = back(after(cot_rows, heads_grad, *cross_grads), *args, half=0)
        *arrays, grads_two = back(cot_rows, *args, half=1, before=first_half[:5])
    grads_two = grads_two + first_half[5]
    arrays, grads_more = opening_backward(
        info, cross_own, heads_grad, seg_v, arrays, (second, summed, slope), mid, down, seg_count
    )
    layer_out, down_grad, hidden_grad, proj_grad, mixed_grad = arrays
    grads_two = grads_two + grads_more
    down_sum = summing(links, *down_weight_grad(info, act, down_grad), 1)
    mid_parts = mid_weight_grad(info, mixed, proj_grad, low, after(hidden_grad, down_sum.keep if fast else down_sum.came))
    mid_sum = summing(links, *mid_parts, 5)
    half_grad, grads_one = attn_backward(
        info, packed, after(mixed_grad, mid_parts[1], down_sum.came), seg_count, 0
    )
    ready = after(mixed_grad, half_grad, *down_sum.far(), mid_sum.came)
    packed_grad, grads_more = attn_backward(info, packed, ready, seg_count, 1, half_grad)
    vec_parts = jnp.concatenate([grads_one + grads_more, grads_two[2:]]).reshape(seg_rows, devices, width)
    vec_parts = vec_parts.transpose(1, 0, 2).reshape(outer, inner, seg_rows * width).astype(LOW)
    if outer > 8:
        vec_parts = vec_parts.reshape(8, -1, seg_rows * width)
    vec_parts = jnp.pad(vec_parts, ((0, 0), (0, 16 - vec_parts.shape[1]), (0, feat_dim - seg_rows * width)))
    if fast:
        vec_parts = links.in_order(list(vec_parts))
    ready = after(packed_grad, *down_sum.near(), *mid_sum.far())
    keep, send = qkv_weight_grad(info, rows_in, ready, vec_parts)
    qkv_sum = summing(links, keep, after(send, *down_sum.turn(), *mid_sum.near()), 3)
    ready = after(packed_grad, qkv_sum.came)
    token_grad = token_gradient(info, ready, proj_grad, first)
    qkv_sum.direct()
    mid_sum.turn()
    qkv_sum.turn(token_grad)
    cross_grads[2] = unmix_columns(after(cross_grads[2], token_grad), devices)
    vec_grad = vec_grad.at[hidden_rows].set(
        unmix_columns(after(vec_grad[hidden_rows], token_grad).reshape(1, -1), devices).reshape(-1, feat_dim)
    )
    cross_vec_grad = lax.dynamic_slice_in_dim(vec_grad, me * width, width, 1)
    grad_positions = lax.dynamic_slice_in_dim(pos_grad, me * width, width, 1)
    grad_down = down_sum.total()
    grad_mid = mid_sum.total().reshape(5, -1, feat_dim)
    total = qkv_sum.total(cross_grads[2], cross_vec_grad)
    grad_qkv = matrix_of(total[: 3 * width].reshape(3, -1, feat_dim))
    grad_vec = total[3 * width, : seg_rows * width].reshape(seg_rows, width)
    return (
        layer_out.reshape(tokens.shape),
        token_grad.reshape(tokens.shape),
        grad_qkv,
        grad_mid[0],
        matrix_of(grad_mid[1:]),
        grad_down,
        grad_vec,
        *cross_grads,
        cross_vec_grad,
        grad_positions,
    )


def solution(mesh):
    in_specs = (
        P(("dp", "fsdp"), None, None),
        P(("dp", "fsdp"), None, None),
        P(),
        P(("dp", "fsdp"), None),
        P(("dp", "fsdp"), None),
        P(("dp", "fsdp"), None),
        P(("dp", "fsdp"), None),
        P(None, ("dp", "fsdp")),
        P(("dp", "fsdp"), None),
        P(("dp", "fsdp"), None),
        P(("dp", "fsdp"), None),
        P(("dp", "fsdp"), None),
        P(None, ("dp", "fsdp")),
        P(None, ("dp", "fsdp")),
    )
    out_specs = (
        P(("dp", "fsdp"), None, None),
        P(("dp", "fsdp"), None, None),
        P(("dp", "fsdp"), None),
        P(("dp", "fsdp"), None),
        P(("dp", "fsdp"), None),
        P(("dp", "fsdp"), None),
        P(None, ("dp", "fsdp")),
        P(("dp", "fsdp"), None),
        P(("dp", "fsdp"), None),
        P(("dp", "fsdp"), None),
        P(("dp", "fsdp"), None),
        P(None, ("dp", "fsdp")),
        P(None, ("dp", "fsdp")),
    )
    return jax.shard_map(
        functools.partial(shards, mesh.shape["dp"], mesh.shape["fsdp"]),
        mesh=mesh, in_specs=in_specs, out_specs=out_specs, check_vma=False)
```

```python
import functools

import jax
import jax.numpy as jnp
from jax import lax
from jax.experimental import pallas as pl
from jax.experimental.pallas import tpu as pltpu
from jax.sharding import PartitionSpec as P

HEAD = 64
SEG = 128
NORM_EPS = 1e-05
MASK_FILL = -1000000000.0
VMEM = 60 * 2**20
F32, LOW = jnp.float32, jnp.bfloat16


ROOT_HALF = 0.7071067811865476
INV_ROOT_TAU = 0.3989422804014327
AXES = ("dp", "fsdp")

def mm(left_op, right_op):
    return jnp.dot(left_op, right_op, preferred_element_type=F32)


def mm_nt(left_op, right_op):
    return lax.dot_general(left_op, right_op, (((1,), (1,)), ((), ())), preferred_element_type=F32)


def mm_tn(left_op, right_op):
    return lax.dot_general(left_op, right_op, (((0,), (0,)), ((), ())), preferred_element_type=F32)


def normalize(summed):
    average = jnp.mean(summed, axis=-1, keepdims=True)
    centered = summed - average
    inv_scale = lax.rsqrt(jnp.mean(centered * centered, axis=-1, keepdims=True) + NORM_EPS)
    return centered * inv_scale, inv_scale


def normalize_back(inner, normed, inv_scale):
    return inv_scale * (
        inner
        - jnp.mean(inner, axis=-1, keepdims=True)
        - normed * jnp.mean(inner * normed, axis=-1, keepdims=True)
    )


def gelu_parts(hidden):
    phi = 0.5 * (1.0 + lax.erf(hidden * ROOT_HALF))
    return hidden * phi, phi + hidden * jnp.exp(-0.5 * hidden * hidden) * INV_ROOT_TAU


def pair_stack(pair, low_half):
    zero = jnp.zeros_like(pair)
    return jnp.concatenate(
        [jnp.where(low_half, pair, zero), jnp.where(low_half, zero, pair)], axis=0
    )


def pair_merge(stacked, low_half):
    rows = stacked.shape[0] // 2
    return jnp.where(low_half, stacked[:rows], stacked[rows:])


def pair_probs(stack, keys, allowed):
    scores = jnp.where(allowed, mm_nt(keys, stack), MASK_FILL)
    expo = jnp.exp(scores - jnp.max(scores, axis=0, keepdims=True))
    return expo * (1.0 / jnp.sum(expo, axis=0, keepdims=True))


def attend(query, keys, values, allowed):
    low_half = lax.broadcasted_iota(jnp.int32, query.shape, 1) < HEAD
    stack = pair_stack(query * jnp.asarray(HEAD**-0.5, query.dtype), low_half)
    return pair_merge(mm_tn(pair_probs(stack, keys, allowed).astype(LOW), values), low_half)


def attend_back(query, keys, values, grad_mixed, allowed):
    low_half = lax.broadcasted_iota(jnp.int32, query.shape, 1) < HEAD
    stack = pair_stack(query * jnp.asarray(HEAD**-0.5, query.dtype), low_half)
    probs = pair_probs(stack, keys, allowed)
    grad_stack = pair_stack(grad_mixed, low_half)
    grad_prob = mm_nt(values, grad_stack)
    inner = jnp.sum(probs * grad_prob, axis=0, keepdims=True)
    score_grad = (probs * (grad_prob - inner)).astype(LOW)
    grad_query = pair_merge(mm_tn(score_grad, keys), low_half) * HEAD**-0.5
    return grad_query, mm(score_grad, stack), mm(probs.astype(LOW), grad_stack)


def slab_copies(place, pieces, slabs, sems, first_sem=0, by_slab=False):
    count = len(slabs)
    half = (count + 1) // 2
    spans = [(0, 0, count), (2, 0, count), (4, 0, count)]
    spans += [(6, 0, count)] if len(pieces) == 8 else [(6, 0, half), (6, half, count)]
    copies = [[] for _ in slabs]
    for flip_c in (0, 1):
        for index, (flip_yx, first, last) in enumerate(spans):
            block = place ^ (flip_yx + flip_c)
            piece = pieces[flip_c * len(spans) + index]
            for slab in range(first, last):
                source = piece.at[pl.ds((slab - first) * 96, 96)]
                sem = sems.at[first_sem + slab * 8 + flip_yx + flip_c]
                copies[slab].append(pltpu.make_async_copy(source, slabs[slab](block), sem))
    return copies if by_slab else sum(copies, [])


def load(copies):
    for copy in copies:
        copy.start()
    for copy in copies:
        copy.wait()


def never(*names):
    pass


def staged(groups):
    for copies in groups.values():
        for copy in copies:
            copy.start()

    def wait(*names):
        for name in names:
            for copy in groups[name]:
                copy.wait()

    return wait


def rows_of(ref, block, rows=96, slab=None):
    where = pl.ds(pl.multiple_of(block * rows, rows), rows)
    return ref.at[where] if slab is None else ref.at[slab, where]


def down_rows(ref, block, part):
    return ref.at[pl.ds(pl.multiple_of(block * 384 + part * 96, 96), 96)]


def qkv_slabs(qkv):
    return [functools.partial(rows_of, qkv, slab=j) for j in range(3)]


def mid_slabs(out, up):
    return [functools.partial(rows_of, out)] + [functools.partial(rows_of, up, slab=j) for j in range(4)]


def down_slabs(down):
    return [functools.partial(down_rows, down, part=j) for j in range(4)]


def segment_mask(length, seg_in_seq):
    row = lax.broadcasted_iota(jnp.int32, (SEG, 2 * SEG), 0)
    return (row + seg_in_seq * SEG < length) | (row == 0)


def attn_forward_kernel(segs, seg_count, first_step, info, x_ref, vec_ref, *rest):
    pieces, (packed_ref, mixed_ref, qkv, sems) = rest[:10], rest[-4:]
    step = pl.program_id(0)

    @pl.when(step == 0)
    def _():
        load(slab_copies(info[0], pieces, qkv_slabs(qkv), sems))

    rows = x_ref[...]
    for j in range(3):
        part = mm(rows, qkv[j])
        if j != 1:
            part = part + vec_ref[j // 2 : j // 2 + 1, :]
        packed_ref[:, j * 768 : (j + 1) * 768] = part.astype(LOW)
    for s in range(segs):
        seg = (step + first_step) * segs + s
        allowed = segment_mask(info[1 + seg // seg_count], seg % seg_count)
        at = slice(s * SEG, (s + 1) * SEG)
        for h in range(6):
            q, k, v = (packed_ref[at, j * 768 + h * 128 : j * 768 + (h + 1) * 128] for j in range(3))
            mixed_ref[at, h * 128 : (h + 1) * 128] = attend(q, k, v, allowed).astype(LOW)


def norm_one(summed, vec_ref):
    normed, _ = normalize(summed)
    return normed * (1.0 + vec_ref[3:4, :]) + vec_ref[4:5, :]


def mid_forward_kernel(info, x_ref, mixed_ref, vec_ref, *rest):
    pieces, (sum_ref, low_ref, act_ref, slope_ref, out, up, sems) = rest[:10], rest[10:]
    step = pl.program_id(0)

    def body(wait):
        wait("out")
        summed = x_ref[...].astype(F32) + mm(mixed_ref[...], out[...]) + vec_ref[2:3, :]
        sum_ref[...] = summed
        first_low = norm_one(summed, vec_ref).astype(LOW)
        low_ref[...] = first_low
        wait("up0")
        hidden = mm(first_low, up[0]) + vec_ref[5:6, :]
        for j in range(4):
            if j < 3:
                wait(f"up{j + 1}")
                later = mm(first_low, up[j + 1]) + vec_ref[6 + j : 7 + j, :]
            act, slope = gelu_parts(hidden)
            act_ref[:, j * 768 : (j + 1) * 768] = act.astype(LOW)
            slope_ref[:, j * 768 : (j + 1) * 768] = slope.astype(LOW)
            hidden = later

    @pl.when(step == 0)
    def _():
        body(staged(mid_groups(info[0], pieces, out, up, sems)))

    @pl.when(step > 0)
    def _():
        body(never)


def down_forward_kernel(segs, info, sum_ref, act_ref, vec_ref, *rest):
    pieces, (second_ref, heads_ref, down, sems) = rest[:8], rest[8:]

    @pl.when(pl.program_id(0) == 0)
    def _():
        load(slab_copies(info[0], pieces, down_slabs(down), sems))

    total = norm_one(sum_ref[...], vec_ref) + vec_ref[9:10, :] + mm(act_ref[...], down[...])
    second_ref[...] = total
    opening = jnp.concatenate([total[s * SEG : s * SEG + 1] for s in range(segs)], axis=0)
    normed, _ = normalize(opening)
    heads_ref[...] = normed * (1.0 + vec_ref[10:11, :]) + vec_ref[11:12, :]


def cross_kernel(blocks, segs, seg_count, info, heads_ref, up_ref, live_ref, vec_ref, pos_ref, seg_vec_ref, *rest):
    wide, tops_in, sources, mid, more, rest = rest[0], rest[1:6], rest[6:9], rest[9:19], rest[19:27], rest[27:]
    grads_ref, pos_grad_ref, qkv_grad_ref, out_grad_ref, up_grad_ref, down_grad_ref, seg_grads_ref, *tops_out = rest[:12]
    (qkv, out, up, down, sems, result, heads_grad, slope, lefts, act, packed, rights, hidden_grad) = rest[12:25]
    tops, parts, own_hidden, weights, (seg_sems, top_sems) = rest[25:30], rest[30:33], rest[33], rest[34:37], rest[37:]
    step = pl.program_id(0)
    count = heads_ref.shape[0]
    at = pl.ds(pl.multiple_of(step * count, count), count)
    targets = [qkv.at[j] for j in range(3)] + [out] + [up.at[j] for j in range(4)]
    targets += [down.at[j * 768 : (j + 1) * 768] for j in range(4)]
    copies = [pltpu.make_async_copy(wide.at[j], t, sems.at[j]) for j, t in enumerate(targets)]

    @pl.when(step == 0)
    def _():
        for copy in copies:
            copy.start()
        staged(opening_groups(info[0], tops_in, sources, mid, more, tops, parts, weights, seg_sems, top_sems))
        grads_ref[...] = jnp.zeros_like(grads_ref)
        pos_grad_ref[...] = jnp.zeros_like(pos_grad_ref)
        for copy in copies[:3]:
            copy.wait()

    vec = vec_ref[...]
    inputs = heads_ref[...].astype(F32).reshape(-1, 8, 768) + pos_ref[...][None]
    inputs = inputs.reshape(count, 768)
    low = inputs.astype(LOW)
    lefts[0, at, :] = low
    for j in range(3):
        part = mm(low, qkv[j])
        if j != 1:
            part = part + vec[j // 2 : j // 2 + 1]
        packed[:, j * 768 : (j + 1) * 768] = part.astype(LOW)
    row = lax.broadcasted_iota(jnp.int32, (SEG, 2 * SEG), 0)
    lane = lax.broadcasted_iota(jnp.int32, (SEG, 2 * SEG), 1)
    group = row // 8 == lane % SEG // 8
    masks = []
    for s in range(count // SEG):
        live = live_ref[s * SEG : (s + 1) * SEG, :]
        masks.append(group & (jnp.concatenate([live, live], axis=1) > 0.0))
    for s, allowed in enumerate(masks):
        part = slice(s * SEG, (s + 1) * SEG)
        for h in range(6):
            q, k, v = (packed[part, j * 768 + h * 128 : j * 768 + (h + 1) * 128] for j in range(3))
            where = pl.ds(pl.multiple_of(step * count + s * SEG, SEG), SEG)
            lefts[1, where, h * 128 : (h + 1) * 128] = attend(q, k, v, allowed).astype(LOW)

    @pl.when(step == 0)
    def _():
        for copy in copies[3:]:
            copy.wait()

    summed = inputs + mm(lefts[1, at, :], out[...]) + vec[2:3]
    normed_one, scale_one = normalize(summed)
    first = normed_one * (1.0 + vec[3:4]) + vec[4:5]
    first_low = first.astype(LOW)
    lefts[2, at, :] = first_low
    total = first + vec[9:10]
    for j in range(4):
        cols = slice(j * 768, (j + 1) * 768)
        hidden = mm(first_low, up[j]) + vec[5 + j : 6 + j]
        active, steep = gelu_parts(hidden)
        act[at, cols] = active.astype(LOW)
        slope[:, cols] = steep.astype(LOW)
        total = total + mm(active.astype(LOW), down[cols, :])
    normed, inv_scale = normalize(total)
    result[at, :] = normed * (1.0 + vec[10:11]) + vec[11:12]
    upstream = up_ref[...].astype(F32)
    back_two = normalize_back(upstream * (1.0 + vec[10:11]), normed, inv_scale)
    down_grad = back_two.astype(LOW)
    rights[1, at, :] = down_grad
    grads_ref[9:10, :] += column_sum(down_grad)
    grads_ref[10:11, :] += column_sum(upstream * normed)
    grads_ref[11:12, :] += column_sum(upstream)
    total = back_two
    for j in range(4):
        cols = slice(j * 768, (j + 1) * 768)
        grad = (mm_nt(down_grad, down[cols, :]) * slope[:, cols].astype(F32)).astype(LOW)
        hidden_grad[at, cols] = grad
        grads_ref[5 + j : 6 + j, :] += column_sum(grad)
        total = total + mm_nt(grad, up[j])
    back_one = normalize_back(total * (1.0 + vec[3:4]), normed_one, scale_one)
    proj_grad = back_one.astype(LOW)
    rights[0, at, :] = proj_grad
    grads_ref[2:3, :] += column_sum(proj_grad)
    grads_ref[3:4, :] += column_sum(total * normed_one)
    grads_ref[4:5, :] += column_sum(total)
    mixed_grad = mm_nt(proj_grad, out[...]).astype(LOW)
    for s, allowed in enumerate(masks):
        part = slice(s * SEG, (s + 1) * SEG)
        where = pl.ds(pl.multiple_of(step * count + s * SEG, SEG), SEG)
        for h in range(6):
            cols = slice(h * 128, (h + 1) * 128)
            q, k, v = (packed[part, j * 768 + h * 128 : j * 768 + (h + 1) * 128] for j in range(3))
            for j, g in enumerate(attend_back(q, k, v, mixed_grad[part, cols], allowed)):
                rights[2 + j, where, cols] = g.astype(LOW)
    total = back_one
    for j in range(3):
        part = rights[2 + j, at, :]
        total = total + mm_nt(part, qkv[j])
        if j != 1:
            grads_ref[j // 2 : j // 2 + 1, :] += column_sum(part)
    heads_grad[at, :] = total
    pos_grad_ref[...] += jnp.sum(total.reshape(-1, 8, 768), axis=0)

    @pl.when(step == blocks - 1)
    def _():
        me = info[1]
        own = pl.ds(pl.multiple_of(me * 16, 16), 16)
        groups = opening_groups(info[0], tops_in, sources, mid, more, tops, parts, weights, seg_sems, top_sems)

        def wait(*names):
            for name in names:
                for copy in groups[name]:
                    copy.wait()

        lengths = [info[2 + i] for i in range(segs // seg_count)]
        opening_rows(segs, seg_count, lengths, result[own, :], heads_grad[own, :], seg_vec_ref, tops_out,
                     seg_grads_ref, tops, parts, own_hidden, weights, top_sems, wait)

        def chosen(left, rows):
            width = left.shape[1]
            wanted = lax.broadcasted_iota(jnp.int32, (rows, width), 1) - lax.broadcasted_iota(
                jnp.int32, (rows, width), 0
            )
            pick = (wanted == me * rows).astype(F32).astype(LOW)
            return mm_nt(pick, left).astype(LOW)

        left = chosen(lefts[0], 24)
        for j in range(3):
            qkv_grad_ref[:, j * 768 : (j + 1) * 768] = mm(left, rights[2 + j])
        out_grad_ref[...] = mm(chosen(lefts[1], 24), rights[0])
        left = chosen(lefts[2], 24)
        for j in range(4):
            cols = slice(j * 768, (j + 1) * 768)
            up_grad_ref[:, cols] = mm(left, hidden_grad[:, cols])
        for j in range(4):
            left = chosen(act[:, j * 768 : (j + 1) * 768], 24)
            down_grad_ref[j * 24 : (j + 1) * 24, :] = mm(left, rights[1])


def column_sum(value):
    return jnp.sum(value.astype(F32), axis=0, keepdims=True)


def ffn_back_rows(upstream, second, summed, slope, vec, grads_ref, hidden_grad, out, up, down, wait):
    normed, inv_scale = normalize(second)
    back_two = normalize_back(upstream * (1.0 + vec[10:11, :]), normed, inv_scale)
    down_grad = back_two.astype(LOW)
    grads_ref[9:10, :] += column_sum(down_grad)
    grads_ref[10:11, :] += column_sum(upstream * normed)
    grads_ref[11:12, :] += column_sum(upstream)
    total = back_two
    wait("down")
    for j in range(4):
        cols = slice(j * 768, (j + 1) * 768)
        grad = (mm_nt(down_grad, down[cols, :]) * slope(cols).astype(F32)).astype(LOW)
        hidden_grad(cols, grad)
        grads_ref[5 + j : 6 + j, :] += column_sum(grad)
        wait(f"up{j}")
        total = total + mm_nt(grad, up[j])
    wait("out")
    normed, inv_scale = normalize(summed)
    back_one = normalize_back(total * (1.0 + vec[3:4, :]), normed, inv_scale)
    proj_grad = back_one.astype(LOW)
    grads_ref[2:3, :] += column_sum(proj_grad)
    grads_ref[3:4, :] += column_sum(total * normed)
    grads_ref[4:5, :] += column_sum(total)
    return down_grad, proj_grad, mm_nt(proj_grad, out[...]).astype(LOW)


def mid_groups(place, mid, out, up, sems):
    copies = slab_copies(place, mid, mid_slabs(out, up), sems, by_slab=True)
    groups = {f"up{j}": copies[j + 1] for j in range(4)}
    return {"out": copies[0], **groups}


def ffn_groups(place, mid, rest, out, up, down, sems):
    groups = mid_groups(place, mid, out, up, sems)
    last = groups.pop("out")
    return {"down": slab_copies(place, rest, down_slabs(down), sems, 40), **groups, "out": last}


def ffn_backward_kernel(segs, seg_count, first_step, info, cot_ref, second_ref, sum_ref, slope_ref, vec_ref, *rest):
    mid, more, rest = rest[:10], rest[10:18], rest[-10:]
    out_ref, down_grad_ref, hidden_grad_ref, proj_grad_ref, mixed_grad_ref, grads_ref, out, up, down, sems = rest
    step = pl.program_id(0)

    def body(wait):
        second = second_ref[...]
        normed, _ = normalize(second)
        result = normed * (1.0 + vec_ref[10:11, :]) + vec_ref[11:12, :]
        row = lax.broadcasted_iota(jnp.int32, (SEG, 1), 0)
        ups = []
        for s in range(segs):
            seg = (step + first_step) * segs + s
            at = slice(s * SEG, (s + 1) * SEG)
            live = row + seg % seg_count * SEG < info[1 + seg // seg_count]
            out_ref[at, :] = jnp.where(live, result[at], 0.0).astype(LOW)
            ups.append(jnp.where(live & (row > 0), cot_ref[at, :].astype(F32), 0.0))

        def store(cols, grad):
            hidden_grad_ref[:, cols] = grad

        down_grad_ref[...], proj_grad_ref[...], mixed_grad_ref[...] = ffn_back_rows(
            jnp.concatenate(ups, axis=0), second, sum_ref[...], lambda cols: slope_ref[:, cols], vec_ref, grads_ref,
            store, out, up, down, wait,
        )

    @pl.when(step == 0)
    def _():
        wait = staged(ffn_groups(info[0], mid, more, out, up, down, sems))
        grads_ref[...] = jnp.zeros_like(grads_ref)
        body(wait)

    @pl.when(step > 0)
    def _():
        body(never)


def opening_groups(place, tops_in, sources, mid, more, tops, parts, weights, sems, top_sems):
    pairs = zip((*tops_in, *sources), (*tops, *parts))
    copies = [
        pltpu.make_async_copy(source.at[:, 0 : target.shape[1], :], target, top_sems.at[i])
        for i, (source, target) in enumerate(pairs)
    ]
    return {"tops": copies, **ffn_groups(place, mid, more, *weights, sems)}


def opening_rows(segs, seg_count, lengths, heads, heads_grad, vec_ref, tops_out, grads_ref, tops, parts, hidden, weights, top_sems, wait):
    wait("tops")
    grads_ref[...] = jnp.zeros_like(grads_ref)
    second, summed = parts[0][:, 0, :], parts[1][:, 0, :]
    slope = parts[2][...].astype(F32)[:, 0, :]

    def store(cols, grad):
        hidden[:, cols] = grad.astype(F32)

    down_grad, proj_grad, mixed_grad = ffn_back_rows(
        heads_grad, second, summed, lambda cols: slope[:, cols], vec_ref, grads_ref, store, *weights, wait
    )
    seg = lax.broadcasted_iota(jnp.int32, (segs, 1), 0)
    length = jnp.full((segs, 1), lengths[0], jnp.int32)
    for i in range(1, len(lengths)):
        length = jnp.where(seg >= i * seg_count, lengths[i], length)
    merged = jnp.where(lax.rem(seg, seg_count) * SEG < length, heads, 0.0)
    outs = []
    values = (merged, down_grad.astype(F32), hidden[...], proj_grad.astype(F32), mixed_grad.astype(F32))
    for i, (value, top) in enumerate(zip(values, tops)):
        row = lax.broadcasted_iota(jnp.int32, top.shape, 1)
        top[...] = jnp.where(row == 0, value[:, None, :], top[...].astype(F32)).astype(LOW)
        outs.append(pltpu.make_async_copy(top, tops_out[i].at[:, 0:16, :], top_sems.at[i]))
    load(outs)


def opening_kernel(segs, seg_count, info, heads_ref, heads_grad_ref, vec_ref, *rest):
    tops_in, sources, mid, more, rest = rest[:5], rest[5:8], rest[8:18], rest[18:26], rest[26:]
    tops_out, grads_ref, tops, parts, hidden = rest[:5], rest[5], rest[6:11], rest[11:14], rest[14]
    *weights, sems, top_sems = rest[15:]
    wait = staged(opening_groups(info[0], tops_in, sources, mid, more, tops, parts, weights, sems, top_sems))
    lengths = [info[1 + i] for i in range(segs // seg_count)]
    opening_rows(segs, seg_count, lengths, heads_ref[...], heads_grad_ref[...], vec_ref, tops_out, grads_ref, tops,
                 parts, hidden, weights, top_sems, wait)


def attn_backward_kernel(segs, seg_count, first_step, info, packed_ref, mixed_grad_ref, *rest):
    packed_grad_ref, grads_ref = rest[-2:]
    step = pl.program_id(0)

    @pl.when(step == 0)
    def _():
        grads_ref[...] = jnp.zeros_like(grads_ref)

    for s in range(segs):
        seg = (step + first_step) * segs + s
        allowed = segment_mask(info[1 + seg // seg_count], seg % seg_count)
        at = slice(s * SEG, (s + 1) * SEG)
        for h in range(6):
            cols = [slice(j * 768 + h * 128, j * 768 + (h + 1) * 128) for j in range(3)]
            q, k, v = (packed_ref[at, c] for c in cols)
            grads = attend_back(q, k, v, mixed_grad_ref[at, cols[0]], allowed)
            for c, g in zip(cols, grads):
                packed_grad_ref[at, c] = g.astype(LOW)
    grads_ref[0:1, :] += column_sum(packed_grad_ref[:, :768])
    grads_ref[1:2, :] += column_sum(packed_grad_ref[:, 1536:])


def token_grad_kernel(info, packed_grad_ref, proj_grad_ref, *rest):
    pieces, (token_grad_ref, qkv, sems) = rest[:10], rest[10:]

    @pl.when(pl.program_id(0) == 0)
    def _():
        load(slab_copies(info[0], pieces, qkv_slabs(qkv), sems))

    total = proj_grad_ref[...].astype(F32)
    for j in range(3):
        total = total + mm_nt(packed_grad_ref[:, j * 768 : (j + 1) * 768], qkv[j])
    token_grad_ref[...] = total.astype(LOW)


def send_slab(place, total, keep_ref, send_ref, rows):
    for mask in range(8):
        block = pl.multiple_of((place ^ mask) * rows, rows)
        target = send_ref if mask % 2 else keep_ref
        target[mask // 2] = total[pl.ds(block, rows), :].astype(LOW)


def qkv_grad_kernel(info, left_ref, right_ref, more_ref, keep_ref, send_ref, total):
    step = pl.program_id(0)
    total[...] = mm_tn(left_ref[...], right_ref[...])
    at = pl.ds(pl.multiple_of(step * 96, 96), 96)
    for mask in range(8):
        block = pl.multiple_of((info[0] ^ mask) * 96, 96)
        target = send_ref if mask % 2 else keep_ref
        target[mask // 2, at, :] = total[pl.ds(block, 96), :].astype(LOW)

    @pl.when(step == 0)
    def _():
        for mask in range(8):
            target = send_ref if mask % 2 else keep_ref
            target[mask // 2, 288:304, :] = more_ref[mask]


def mid_grad_kernel(info, mixed_ref, proj_ref, low_ref, hidden_ref, keep_ref, send_ref, total):
    @pl.when(pl.program_id(0) == 0)
    def _():
        total[...] = mm_tn(mixed_ref[...], proj_ref[...])

    @pl.when(pl.program_id(0) > 0)
    def _():
        total[...] = mm_tn(low_ref[...], hidden_ref[...])

    send_slab(info[0], total, keep_ref, send_ref, 96)


ANY = pl.BlockSpec(memory_space=pl.ANY)
SMEM = pl.BlockSpec(memory_space=pltpu.SMEM)


def block_rows(count, width):
    return pl.BlockSpec((count, width), lambda i: (i, 0))


def fixed(shape):
    return pl.BlockSpec(shape, lambda i: (0,) * len(shape))


def shape_of(dims, kind=LOW):
    return jax.ShapeDtypeStruct(dims, kind)


def params():
    return pltpu.CompilerParams(vmem_limit_bytes=VMEM, dimension_semantics=("arbitrary",))


def cost(flops, size):
    return pl.CostEstimate(flops=flops, bytes_accessed=size, transcendentals=0)


QKV = [pltpu.VMEM((3, 768, 768), LOW)]
MID = [pltpu.VMEM((768, 768), LOW), pltpu.VMEM((4, 768, 768), LOW)]
DOWN = [pltpu.VMEM((3072, 768), LOW)]


def sems(count):
    return [pltpu.SemaphoreType.DMA((count,))]


def shifted(count, width, first):
    return pl.BlockSpec((count, width), lambda i: (i + first, 0))


def attn_forward(info, rows_in, vec, pieces, seg_count, half, before=None, segs=4):
    rows = rows_in.shape[0]
    count = segs * SEG
    steps = rows // count // 2
    first = half * steps
    before = list(before or [])
    return pl.pallas_call(
        functools.partial(attn_forward_kernel, segs, seg_count, first),
        grid=(steps,),
        in_specs=[SMEM, shifted(count, 768, first), fixed((12, 768))] + [ANY] * (10 + len(before)),
        out_specs=[shifted(count, 2304, first), shifted(count, 768, first)],
        out_shape=[shape_of((rows, 2304)), shape_of((rows, 768))],
        scratch_shapes=QKV + sems(24),
        input_output_aliases={13: 0, 14: 1} if before else {},
        compiler_params=params(),
        cost_estimate=cost(rows * 768 * 8000, rows * 768 * 8),
        name="attn_forward",
    )(info, rows_in, vec, *pieces, *before)


def mid_forward(info, rows_in, mixed, vec, pieces, segs=2):
    rows = rows_in.shape[0]
    count = segs * SEG
    return pl.pallas_call(
        mid_forward_kernel,
        grid=(rows // count,),
        in_specs=[SMEM, block_rows(count, 768), block_rows(count, 768), fixed((12, 768))] + [ANY] * 10,
        out_specs=[block_rows(count, 768), block_rows(count, 768), block_rows(count, 3072), block_rows(count, 3072)],
        out_shape=[shape_of((rows, 768), F32), shape_of((rows, 768)), shape_of((rows, 3072)), shape_of((rows, 3072))],
        scratch_shapes=MID + sems(40),
        compiler_params=params(),
        cost_estimate=cost(2 * rows * 768 * 8000, rows * 768 * 30),
        name="mid_forward",
    )(info, rows_in, mixed, vec, *pieces)


def down_forward(info, summed, act, vec, pieces, segs=2):
    rows = summed.shape[0]
    count = segs * SEG
    few = pl.BlockSpec((None, segs, 768), lambda i: (i, 0, 0))
    return pl.pallas_call(
        functools.partial(down_forward_kernel, segs),
        grid=(rows // count,),
        in_specs=[SMEM, block_rows(count, 768), block_rows(count, 3072), fixed((12, 768))] + [ANY] * 8,
        out_specs=[block_rows(count, 768), few],
        out_shape=[shape_of((rows, 768), F32), shape_of((rows // count, segs, 768), F32)],
        scratch_shapes=DOWN + sems(32),
        compiler_params=params(),
        cost_estimate=cost(2 * rows * 768 * 4000, rows * 768 * 16),
        name="down_forward",
    )(info, summed, act, vec, *pieces)


def grouped(array):
    return array.reshape(-1, SEG, array.shape[1])


def top_scratch(segs, arrays):
    tops = [pltpu.VMEM((segs, 16, a.shape[2]), LOW) for a in arrays]
    parts = [pltpu.VMEM((segs, 8, 768), F32)] * 2 + [pltpu.VMEM((segs, 16, 3072), LOW)]
    return tops + parts + [pltpu.VMEM((segs, 3072), F32)] + MID + DOWN + sems(72) + sems(8)


def cross_whole(info, heads, upstream, live, vec, positions, wide, seg_vec, arrays, sources, mid, more, seg_count):
    rows = heads.shape[0]
    count = 2 * SEG
    arrays, sources = [grouped(a) for a in arrays], [grouped(a) for a in sources]
    segs = arrays[0].shape[0]
    own = [(12, 768), (8, 768), (24, 2304), (24, 768), (24, 3072), (96, 768), (12, 768)]
    *grads, seg_grads, layer, down, hidden, proj, mixed = pl.pallas_call(
        functools.partial(cross_kernel, rows // count, segs, seg_count),
        grid=(rows // count,),
        in_specs=[SMEM, block_rows(count, 768), block_rows(count, 768), block_rows(count, SEG),
                  fixed((12, 768)), fixed((8, 768)), fixed((12, 768))] + [ANY] * 27,
        out_specs=[fixed(dims) for dims in own] + [ANY] * 5,
        out_shape=[shape_of(dims, F32) for dims in own] + [shape_of(a.shape) for a in arrays],
        scratch_shapes=QKV + MID + DOWN + sems(12) + [
            pltpu.VMEM((rows, 768), F32), pltpu.VMEM((rows, 768), F32), pltpu.VMEM((count, 3072), LOW),
            pltpu.VMEM((3, rows, 768), LOW), pltpu.VMEM((rows, 3072), LOW), pltpu.VMEM((count, 2304), LOW),
            pltpu.VMEM((5, rows, 768), LOW), pltpu.VMEM((rows, 3072), LOW),
        ] + top_scratch(segs, arrays),
        input_output_aliases={8 + i: 7 + i for i in range(5)},
        compiler_params=params(),
        cost_estimate=cost(2 * rows * 768 * 30000, 2**24),
        name="cross_encoder",
    )(info, heads, upstream, live, vec, positions, seg_vec, wide, *arrays, *sources, *mid, *more)
    return grads, seg_grads, [a.reshape(-1, a.shape[2]) for a in (layer, down, hidden, proj, mixed)]


def ffn_backward(info, cotangent, second, summed, slope, vec, mid, down, seg_count, half, before=None, segs=2):
    rows = summed.shape[0]
    count = segs * SEG
    steps = rows // count // 2
    first = half * steps
    before = list(before or [])
    widths = (768, 768, 3072, 768, 768)
    return pl.pallas_call(
        functools.partial(ffn_backward_kernel, segs, seg_count, first),
        grid=(steps,),
        in_specs=[SMEM, shifted(count, 768, first), shifted(count, 768, first), shifted(count, 768, first),
                  shifted(count, 3072, first), fixed((12, 768))] + [ANY] * (18 + len(before)),
        out_specs=[shifted(count, w, first) for w in widths] + [fixed((12, 768))],
        out_shape=[shape_of((rows, w)) for w in widths] + [shape_of((12, 768), F32)],
        scratch_shapes=MID + DOWN + sems(72),
        input_output_aliases={24 + i: i for i in range(5)} if before else {},
        compiler_params=params(),
        cost_estimate=cost(rows * 768 * 14000, rows * 768 * 15),
        name="ffn_backward",
    )(info, cotangent, second, summed, slope, vec, *mid, *down, *before)


def opening_backward(info, heads, heads_grad, vec, arrays, sources, mid, down, seg_count):
    segs = heads.shape[0]
    arrays, sources = [grouped(a) for a in arrays], [grouped(a) for a in sources]
    whole = fixed((segs, 768))
    *done, grads = pl.pallas_call(
        functools.partial(opening_kernel, segs, seg_count),
        grid=(1,),
        in_specs=[SMEM, whole, whole, fixed((12, 768))] + [ANY] * 26,
        out_specs=[ANY] * 5 + [fixed((12, 768))],
        out_shape=[shape_of(a.shape) for a in arrays] + [shape_of((12, 768), F32)],
        scratch_shapes=top_scratch(segs, arrays),
        input_output_aliases={4 + i: i for i in range(5)},
        compiler_params=params(),
        cost_estimate=cost(2**33, 2**24),
        name="opening_backward",
    )(info, heads, heads_grad, vec, *arrays, *sources, *mid, *down)
    return [a.reshape(-1, a.shape[2]) for a in done], grads


def attn_backward(info, packed, mixed_grad, seg_count, half, before=None, segs=2):
    rows = packed.shape[0]
    count = segs * SEG
    steps = rows // count // 2
    first = half * steps
    before = [] if before is None else [before]
    return pl.pallas_call(
        functools.partial(attn_backward_kernel, segs, seg_count, first),
        grid=(steps,),
        in_specs=[SMEM, shifted(count, 2304, first), shifted(count, 768, first)] + [ANY] * len(before),
        out_specs=[shifted(count, 2304, first), fixed((2, 768))],
        out_shape=[shape_of((rows, 2304)), shape_of((2, 768), F32)],
        input_output_aliases={3: 0} if before else {},
        compiler_params=params(),
        cost_estimate=cost(rows * 768 * 10000, rows * 768 * 8),
        name="attn_backward",
    )(info, packed, mixed_grad, *before)


def token_gradient(info, packed_grad, proj_grad, pieces, count=512):
    rows = packed_grad.shape[0]
    return pl.pallas_call(
        token_grad_kernel,
        grid=(rows // count,),
        in_specs=[SMEM, block_rows(count, 2304), block_rows(count, 768)] + [ANY] * 10,
        out_specs=block_rows(count, 768),
        out_shape=shape_of((rows, 768)),
        scratch_shapes=QKV + sems(24),
        compiler_params=params(),
        cost_estimate=cost(2 * rows * 768 * 3000, rows * 768 * 10),
        name="token_gradient",
    )(info, packed_grad, proj_grad, *pieces)


def grad_outs(slabs):
    out = pl.BlockSpec((4, 96, 768), lambda i: (0, i, 0))
    return [out, out], [shape_of((4, slabs * 96, 768))] * 2


def qkv_weight_grad(info, left, right, more):
    rows = left.shape[0]
    out = fixed((4, 304, 768))
    return pl.pallas_call(
        qkv_grad_kernel,
        grid=(3,),
        in_specs=[SMEM, fixed((rows, 768)), pl.BlockSpec((rows, 768), lambda i: (0, i)), fixed((8, 16, 768))],
        out_specs=[out, out],
        out_shape=[shape_of((4, 304, 768))] * 2,
        scratch_shapes=[pltpu.VMEM((768, 768), F32)],
        compiler_params=params(),
        cost_estimate=cost(2 * rows * 768 * 2304, rows * 2304 * 2),
        name="qkv_weight_grad",
    )(info, left, right, more)


def mid_weight_grad(info, mixed, proj_grad, low, hidden_grad):
    rows = mixed.shape[0]
    specs, shapes = grad_outs(5)
    still = fixed((rows, 768))
    return pl.pallas_call(
        mid_grad_kernel,
        grid=(5,),
        in_specs=[SMEM, still, still, still, pl.BlockSpec((rows, 768), lambda i: (0, jnp.maximum(i - 1, 0)))],
        out_specs=specs,
        out_shape=shapes,
        scratch_shapes=[pltpu.VMEM((768, 768), F32)],
        compiler_params=params(),
        cost_estimate=cost(2 * rows * 768 * 3840, rows * 3840 * 2),
        name="mid_weight_grad",
    )(info, mixed, proj_grad, low, hidden_grad)


def down_grad_kernel(info, left_ref, right_ref, keep_ref, send_ref, total):
    step = pl.program_id(0)
    total[pl.ds(pl.multiple_of(step * 768, 768), 768), :] = mm_tn(left_ref[...], right_ref[...]).astype(LOW)

    @pl.when(step == pl.num_programs(0) - 1)
    def _():
        for mask in range(8):
            block = pl.multiple_of((info[0] ^ mask) * 384, 384)
            target = send_ref if mask % 2 else keep_ref
            target[mask // 2] = total[pl.ds(block, 384), :]


def down_weight_grad(info, left, right):
    rows, wide = left.shape
    return pl.pallas_call(
        down_grad_kernel,
        grid=(wide // 768,),
        in_specs=[SMEM, pl.BlockSpec((rows, 768), lambda i: (0, i)), fixed((rows, 768))],
        out_specs=[fixed((4, 384, 768))] * 2,
        out_shape=[shape_of((4, 384, 768))] * 2,
        scratch_shapes=[pltpu.VMEM((3072, 768), LOW)],
        compiler_params=params(),
        cost_estimate=cost(2 * rows * 768 * wide, rows * wide * 2),
        name="down_weight_grad",
    )(info, left, right)


def matmul(left_op, right_op):
    return jnp.dot(left_op, right_op, preferred_element_type=jnp.float32)


def trans_left(left_op, right_op):
    return lax.dot_general(
        left_op, right_op, (((0,), (0,)), ((), ())), preferred_element_type=jnp.float32
    )


def trans_right(left_op, right_op):
    return lax.dot_general(
        left_op, right_op, (((1,), (1,)), ((), ())), preferred_element_type=jnp.float32
    )


def norm_forward(summed, gain_row, shift_row):
    average = jnp.mean(summed, axis=-1, keepdims=True)
    centered = summed - average
    inv_scale = lax.rsqrt(jnp.mean(centered * centered, axis=-1, keepdims=True) + NORM_EPS)
    normed = centered * inv_scale
    return (normed * (1.0 + gain_row) + shift_row, normed, inv_scale)


def norm_backward(upstream, normed, inv_scale, gain_row):
    inner = upstream * (1.0 + gain_row)
    back_grad = inv_scale * (
        inner
        - jnp.mean(inner, axis=-1, keepdims=True)
        - normed * jnp.mean(inner * normed, axis=-1, keepdims=True)
    )
    return (back_grad, jnp.sum(upstream * normed, axis=0), jnp.sum(upstream, axis=0))


def gelu_slope(hidden):
    return (
        0.5 * (1.0 + lax.erf(hidden * ROOT_HALF))
        + hidden * jnp.exp(-0.5 * hidden * hidden) * INV_ROOT_TAU
    )


def split_heads(packed, group_len):
    head_count = packed.shape[1] // (3 * HEAD)
    return [
        portion.reshape(-1, group_len, head_count, HEAD) for portion in jnp.split(packed, 3, axis=1)
    ]


def masked_scores(query_heads, key_heads, allowed):
    raw_scores = jnp.einsum(
        "nqhd,nkhd->nhqk", query_heads, key_heads, preferred_element_type=jnp.float32
    ) * HEAD ** (-0.5)
    return jnp.where(allowed[:, None, None, :], raw_scores, MASK_FILL)


def encode(inputs, inputs_low, weights, allowed):
    qkv_w, out_w, up_w, down_w, vectors = weights
    row_count, feat_dim = inputs_low.shape
    group_len = allowed.shape[1]
    qkv_bias = jnp.concatenate([vectors[0], jnp.zeros_like(vectors[0]), vectors[1]])
    packed = (matmul(inputs_low, qkv_w) + qkv_bias).astype(jnp.bfloat16)
    query_heads, key_heads, value_heads = split_heads(packed, group_len)
    scores = masked_scores(query_heads, key_heads, allowed)
    row_max = jnp.max(scores, axis=-1, keepdims=True)
    expo_vals = jnp.exp(scores - row_max)
    row_total = jnp.sum(expo_vals, axis=-1, keepdims=True)
    log_total = row_max + jnp.log(row_total)
    prob_low = (expo_vals / row_total).astype(jnp.bfloat16)
    mixed = jnp.einsum("nhqk,nkhd->nqhd", prob_low, value_heads, preferred_element_type=jnp.float32)
    mixed = mixed.reshape(row_count, feat_dim).astype(jnp.bfloat16)
    projected = matmul(mixed, out_w) + vectors[2]
    first_out, normed_one, scale_one = norm_forward(inputs + projected, vectors[3], vectors[4])
    first_low = first_out.astype(jnp.bfloat16)
    hidden = matmul(first_low, up_w) + vectors[5:-3].reshape(-1)
    activated = jax.nn.gelu(hidden, approximate=False).astype(jnp.bfloat16)
    down_out = matmul(activated, down_w) + vectors[-3]
    result, normed_two, scale_two = norm_forward(first_out + down_out, vectors[-2], vectors[-1])
    return (
        result,
        (
            packed,
            log_total,
            mixed,
            normed_one,
            scale_one,
            first_low,
            hidden,
            activated,
            normed_two,
            scale_two,
        ),
    )


def encode_back(upstream, inputs_low, weights, allowed, kept):
    qkv_w, out_w, up_w, down_w, vectors = weights
    (
        packed,
        log_total,
        mixed,
        normed_one,
        scale_one,
        first_low,
        hidden,
        activated,
        normed_two,
        scale_two,
    ) = kept
    row_count, feat_dim = inputs_low.shape
    group_len = allowed.shape[1]
    back_two, gain_two, shift_two = norm_backward(upstream, normed_two, scale_two, vectors[-2])
    down_grad = back_two.astype(jnp.bfloat16)
    hidden_grad = (trans_right(down_grad, down_w) * gelu_slope(hidden)).astype(jnp.bfloat16)
    first_grad = trans_right(hidden_grad, up_w) + back_two
    back_one, gain_one, shift_one = norm_backward(first_grad, normed_one, scale_one, vectors[3])
    proj_grad = back_one.astype(jnp.bfloat16)
    query_heads, key_heads, value_heads = split_heads(packed, group_len)
    mixed_grad = trans_right(proj_grad, out_w).astype(jnp.bfloat16).reshape(value_heads.shape)
    scores = masked_scores(query_heads, key_heads, allowed)
    prob_vals = jnp.exp(scores - log_total)
    grad_values = jnp.einsum(
        "nhqk,nqhd->nkhd",
        prob_vals.astype(jnp.bfloat16),
        mixed_grad,
        preferred_element_type=jnp.float32,
    )
    grad_prob = jnp.einsum(
        "nqhd,nkhd->nhqk", mixed_grad, value_heads, preferred_element_type=jnp.float32
    )
    score_grad = (
        prob_vals * (grad_prob - jnp.sum(prob_vals * grad_prob, axis=-1, keepdims=True))
    ).astype(jnp.bfloat16)
    grad_query = jnp.einsum(
        "nhqk,nkhd->nqhd", score_grad, key_heads, preferred_element_type=jnp.float32
    ) * HEAD ** (-0.5)
    grad_keys = jnp.einsum(
        "nhqk,nqhd->nkhd", score_grad, query_heads, preferred_element_type=jnp.float32
    ) * HEAD ** (-0.5)
    packed_grad = jnp.concatenate(
        [
            grad_query.reshape(row_count, feat_dim),
            grad_keys.reshape(row_count, feat_dim),
            grad_values.reshape(row_count, feat_dim),
        ],
        axis=1,
    ).astype(jnp.bfloat16)
    bias_grads = jnp.sum(packed_grad, axis=0, dtype=jnp.float32).reshape(3, feat_dim)
    grad_inputs = trans_right(packed_grad, qkv_w) + back_one
    grad_vectors = jnp.concatenate(
        [
            bias_grads[0:1],
            bias_grads[2:3],
            jnp.sum(proj_grad, axis=0, dtype=jnp.float32)[None],
            gain_one[None],
            shift_one[None],
            jnp.sum(hidden_grad, axis=0, dtype=jnp.float32).reshape(-1, feat_dim),
            jnp.sum(down_grad, axis=0, dtype=jnp.float32)[None],
            gain_two[None],
            shift_two[None],
        ],
        axis=0,
    )
    pairs = (
        (inputs_low, packed_grad),
        (mixed, proj_grad),
        (first_low, hidden_grad),
        (activated, down_grad),
    )
    return (grad_inputs, pairs, grad_vectors)


class Links:
    def __init__(self, outer, inner):
        self.outer, self.inner = outer, inner
        self.order = self.place = lax.axis_index("dp")
        self.z = lax.axis_index("fsdp")

    def flip(self, value, mask):
        pairs = [
            (d * self.inner + z, (d ^ mask) * self.inner + z)
            for d in range(self.outer)
            for z in range(self.inner)
        ]
        return lax.ppermute(value, AXES, pairs)

    def turn(self, value, step):
        pairs = [
            (d * self.inner + z, d * self.inner + (z + step) % self.inner)
            for d in range(self.outer)
            for z in range(self.inner)
        ]
        return lax.ppermute(value, AXES, pairs)

    def gather_z(self, shard):
        came = [shard] + [self.turn(shard, step) for step in range(1, self.inner)]
        whole = []
        for z in range(self.inner):
            part = came[-1]
            for step in range(self.inner - 1):
                part = jnp.where(self.z == (z + step) % self.inner, came[step], part)
            whole.append(part)
        return whole

    def spread_near(self, block):
        return self.flip(block, 2), self.flip(block, 4)

    def spread_far(self, by_x, by_y, half):
        return self.flip(by_y[:half], 2), self.flip(by_x[half:], 4)

    def core(self, pieces):
        return [self.flip(piece, 1) for piece in pieces]

    def in_order(self, parts):
        for axis, mask in ((4, 4), (2, 2), (1, 1)):
            odd = self.place // axis % 2 == 1
            parts = [jnp.where(odd, parts[m ^ mask], parts[m]) for m in range(8)]
        return jnp.stack(parts)

    def gather_small(self, shard, line_only=False):
        block = jnp.stack(self.gather_z(shard))
        return block if line_only else self.gather_core(self.gather_plane(block))

    def gather_plane(self, block):
        return jnp.stack([block] + [self.flip(block, m) for m in (2, 4, 6)])

    def gather_core(self, plane):
        other = self.flip(plane, 1)
        whole = self.in_order([(plane, other)[m % 2][m // 2] for m in range(8)])
        return whole.reshape((-1,) + plane.shape[2:])


class PlainLinks:
    def __init__(self, outer, inner):
        self.outer, self.inner = outer, inner
        self.order = lax.axis_index("dp")
        self.z = lax.axis_index("fsdp")
        self.place = 0

    def gather_small(self, shard, line_only=False):
        return lax.all_gather(shard, AXES, axis=0)


def add(*terms):
    return sum(t.astype(F32) for t in terms).astype(LOW)


class Sum:
    def __init__(self, links, keep, send, slabs):
        self.links, self.keep, self.slabs = links, keep, slabs
        self.more = keep.shape[1] % 96
        self.came = links.flip(send, 1)

    def line(self, part):
        inner = self.links.inner
        count = part.shape[0] - self.more
        main = part[:count].reshape(self.slabs, inner, -1, part.shape[-1])
        main = main.transpose(1, 0, 2, 3).reshape(inner, -1, part.shape[-1])
        if not self.more:
            return main
        rows = part[count : count + inner].reshape(inner, 1, -1)
        return jnp.concatenate([main, jnp.pad(rows, ((0, 0), (0, 7), (0, 0)))], axis=1)

    def to(self, index):
        return self.line(add(self.keep[index], self.came[index]))

    def far(self):
        half = self.links.inner // 2
        to_d = self.to(3)
        self.far_came = [self.links.flip(to_d[:half], 2), self.links.flip(to_d[half:], 4)]
        return self.far_came

    def near(self):
        half = self.links.inner // 2
        came_x, came_y = self.far_came
        to_x, to_y = self.to(1), self.to(2)
        to_y = jnp.concatenate([add(to_y[:half], came_x), to_y[half:]])
        to_x = jnp.concatenate([to_x[:half], add(to_x[half:], came_y)])
        self.near_came = [self.links.flip(to_x, 2), self.links.flip(to_y, 4)]
        return self.near_came

    def direct(self):
        self.near_came = [self.links.flip(self.to(m // 2), m) for m in (2, 4, 6)]
        return self.near_came

    def turn(self, *earlier):
        links = self.links
        own = add(self.line(self.keep[0]), self.line(self.came[0]), *self.near_came)
        own = after(own, *earlier) if earlier else own
        parts = [lax.dynamic_index_in_dim(own, (links.z + k) % links.inner, 0, keepdims=False) for k in range(links.inner)]
        self.turned = [parts[0]] + [links.turn(parts[k], k) for k in range(1, links.inner)]
        return self.turned[1:]

    def total(self, *earlier):
        parts = [after(t, *earlier) for t in self.turned] if earlier else self.turned
        return sum(t.astype(F32) for t in parts)


class PlainSum:
    def __init__(self, links, keep, send, slabs):
        more = keep.shape[1] % 96
        flat = jnp.stack([keep, send], axis=1).reshape(8, -1, 768)
        main = flat[:, : flat.shape[1] - more].reshape(8, slabs, -1, 768)
        main = main.transpose(1, 0, 2, 3).reshape(slabs, -1, 768)
        self.came = keep
        self.sums = lax.psum_scatter(main, AXES, scatter_dimension=1, tiled=True).reshape(-1, 768)
        if more:
            rows = flat[:, flat.shape[1] - more :][:, : links.outer * links.inner // 8].reshape(-1, 768)
            self.sums = jnp.concatenate([self.sums, lax.psum_scatter(rows, AXES, scatter_dimension=0, tiled=True)])

    def far(self, *earlier):
        return []

    near = direct = turn = far

    def total(self, *earlier):
        return self.sums.astype(F32)


def after(value, *earlier):
    return lax.optimization_barrier((value, *earlier))[0]


def slabs_of(matrix):
    rows, wide = matrix.shape
    return matrix.reshape(rows, wide // 768, 768).transpose(1, 0, 2)


def matrix_of(slabs):
    count, rows, width = slabs.shape
    return slabs.transpose(1, 0, 2).reshape(rows, count * width)


def mix_columns(matrix, devices):
    rows, wide = matrix.shape
    matrix = matrix.reshape(rows, devices, 4, -1).transpose(0, 2, 1, 3)
    return matrix.reshape(rows, wide)


def unmix_columns(matrix, devices):
    rows, wide = matrix.shape
    matrix = matrix.reshape(rows, 4, devices, -1).transpose(0, 2, 1, 3)
    return matrix.reshape(rows, wide)


def plain_pieces(slabs, whole):
    count = slabs.shape[0]
    half = (count + 1) // 2 * 96
    parts = []
    for mask in (0, 2, 4, 6, 1, 3, 5, 7):
        part = slabs[:, mask * 96 : (mask + 1) * 96].reshape(-1, 768)
        parts += [part] if whole or mask < 6 and mask != 7 else [part[:half], part[half:]]
    return parts


def shards(
    outer,
    inner,
    tokens,
    cotangent,
    lengths,
    seg_qkv,
    seg_out,
    seg_up,
    seg_down,
    seg_vec,
    cross_qkv,
    cross_out,
    cross_up,
    cross_down,
    cross_vec,
    positions,
):
    fast = (outer, inner) == (8, 4)
    links = (Links if fast else PlainLinks)(outer, inner)
    summing = Sum if fast else PlainSum
    devices = outer * inner
    me = links.order * inner + links.z
    seq_local, seq_len, feat_dim = tokens.shape
    seg_count = seq_len // SEG
    seg_rows, cross_rows = seg_vec.shape[0], cross_vec.shape[0]
    width = feat_dim // devices
    my_lengths = lax.dynamic_slice_in_dim(lengths, me * seq_local, seq_local)
    info = jnp.concatenate([jnp.full((1,), links.place, jnp.int32), my_lengths])
    small = jnp.concatenate([seg_vec, cross_vec, positions]).reshape(1, -1)
    up_slabs = mix_columns(cross_up, devices).reshape(-1, 4, feat_dim).transpose(1, 0, 2)
    wide = [slabs_of(cross_qkv), slabs_of(cross_out), up_slabs, cross_down.reshape(4, -1, feat_dim)]
    wide = jnp.concatenate(wide)
    mid_shard = jnp.concatenate([slabs_of(seg_out), slabs_of(seg_up)])
    rows_in = tokens.reshape(-1, feat_dim)
    cot_rows = cotangent.reshape(-1, feat_dim)
    seg_starts = jnp.arange(seg_count) * SEG
    live_own = (seg_starts[None, :] < my_lengths[:, None]).reshape(-1, 1)
    up_own = jnp.where(live_own, cotangent.reshape(-1, SEG, feat_dim)[:, 0, :], 0)

    if fast:
        first = jnp.concatenate([slabs_of(seg_qkv).reshape(-1, 768), jnp.pad(small, ((0, 7), (0, 0)))])
        line_first = links.gather_z(first)
        line_mid = links.gather_z(after(mid_shard, *line_first))
        weights = jnp.stack([p[:72].reshape(3, 24, 768) for p in line_first], axis=1).reshape(-1, 768)
        rows = jnp.concatenate([p[72:73] for p in line_first])
        block = jnp.concatenate([weights, jnp.pad(rows, ((0, 12), (0, 0)))])
        near = links.spread_near(block)
        far = links.spread_far(*near, 192)
        first = [block, *near, *far, *links.core([after(p, *far, *line_mid) for p in (block, *near, *far)])]
        line_down = links.gather_z(after(seg_down, *first[5:]))
        ends = [p[288:292] for p in first[:3]] + [first[4][96:100]]
        others = [p[288:292] for p in first[5:8]] + [first[9][96:100]]
        small = links.in_order([(ends, others)[m % 2][m // 2] for m in range(8)])
        block = after(jnp.stack(line_mid, axis=1).reshape(-1, 768), *far)
        mid = [block, *links.spread_near(block)]
    else:
        first = plain_pieces(lax.all_gather(slabs_of(seg_qkv), AXES, axis=1, tiled=True), False)
        mid = plain_pieces(lax.all_gather(mid_shard, AXES, axis=1, tiled=True), False)
        down_whole = lax.all_gather(seg_down, AXES, axis=0, tiled=True)
        down = [down_whole[m * 384 : (m + 1) * 384] for m in (0, 2, 4, 6, 1, 3, 5, 7)]
        small = links.gather_small(small)
    small = small.reshape(devices, -1, width).transpose(1, 0, 2).reshape(-1, feat_dim).astype(F32)
    seg_v, cross_v = small[:seg_rows], small[seg_rows : seg_rows + cross_rows]
    pos_table = small[seg_rows + cross_rows :]
    hidden_rows = slice(5, cross_rows - 3)
    cross_v = cross_v.at[hidden_rows].set(mix_columns(cross_v[hidden_rows].reshape(1, -1), devices).reshape(-1, feat_dim))

    before = attn_forward(info, rows_in, seg_v, first, seg_count, 0)
    wide = lax.all_gather(after(wide, before[0], *((*mid[1:], *line_down) if fast else ())), AXES, axis=1, tiled=True)
    if fast:
        far = links.spread_far(*(after(p, before[0]) for p in mid[1:]), 288)
        rows_late = after(rows_in, *mid[1:])
    else:
        rows_late = rows_in
    packed, mixed = attn_forward(info, rows_late, seg_v, first, seg_count, 1, before)
    if fast:
        early = links.core([after(p, before[0]) for p in mid])
        late = links.core([after(p, packed, *far, *early) for p in far])
        mid = [*mid, *far, *early, *late]
        block = after(jnp.concatenate(line_down), *late)
        near = [links.flip(block, m) for m in (2, 4, 6)]
    summed, low, act, slope = mid_forward(info, rows_in, mixed, seg_v, mid)
    if fast:
        down = [block, *near, links.flip(block, 1), *(links.flip(after(p, act), 1) for p in near)]
    second, heads = down_forward(info, summed, act, seg_v, down)
    heads_own = heads.reshape(-1, feat_dim)
    both = links.gather_small(jnp.stack([heads_own.astype(LOW), up_own]), True)
    back = functools.partial(ffn_backward, info, seg_count=seg_count)
    args = (second, summed, slope, seg_v, mid, down)
    if fast:
        first_half = back(cot_rows, *args, half=0)
        both = links.gather_plane(after(both, first_half[1]))
        *arrays, grads_two = back(after(cot_rows, first_half[1]), *args, half=1, before=first_half[:5])
        both = links.gather_core(after(both, arrays[1]))
    heads_all, up_all = both[:, 0].reshape(-1, feat_dim), both[:, 1].reshape(-1, feat_dim)
    live_all = seg_starts[None, :] < lengths[:, None]
    if fast:
        cross_info = jnp.concatenate([jnp.stack([links.place, me]).astype(jnp.int32), my_lengths])
        live = jnp.broadcast_to(live_all.reshape(-1, 1), (live_all.size, SEG)).astype(F32)
        (vec_grad, pos_grad, *cross_grads), grads_more, arrays = cross_whole(
            cross_info, heads_all, up_all, live, cross_v, pos_table, wide,
            seg_v, arrays, (second, summed, slope), mid, down, seg_count,
        )
    else:
        weights = (matrix_of(wide[:3]), wide[3], matrix_of(wide[4:8]), wide[8:].reshape(-1, feat_dim), cross_v)
        heads_in = heads_all.astype(F32).reshape(-1, seg_count, feat_dim) + pos_table[None]
        heads_in = heads_in.reshape(-1, feat_dim)
        cross_result, kept = encode(heads_in, heads_in.astype(LOW), weights, live_all)
        all_grad, pairs, vec_grad = encode_back(
            up_all.astype(F32), heads_in.astype(LOW), weights, live_all, kept
        )
        cross_grads = []
        for left, right in pairs:
            left = left.reshape(left.shape[0], -1, feat_dim)
            mine = lax.dynamic_slice_in_dim(left, me * width, width, 2)
            cross_grads.append(trans_left(mine.reshape(left.shape[0], -1), right))
        pos_grad = jnp.sum(all_grad.reshape(-1, seg_count, feat_dim), axis=0)
        own = seq_local * seg_count
        cross_own = lax.dynamic_slice_in_dim(cross_result, me * own, own)
        heads_grad = lax.dynamic_slice_in_dim(all_grad, me * own, own)
        first_half = back(after(cot_rows, heads_grad, *cross_grads), *args, half=0)
        *arrays, grads_two = back(cot_rows, *args, half=1, before=first_half[:5])
        arrays, grads_more = opening_backward(
            info, cross_own, heads_grad, seg_v, arrays, (second, summed, slope), mid, down, seg_count
        )
    layer_out, down_grad, hidden_grad, proj_grad, mixed_grad = arrays
    grads_two = grads_two + first_half[5] + grads_more
    down_sum = summing(links, *down_weight_grad(info, act, down_grad), 1)
    mid_parts = mid_weight_grad(info, mixed, proj_grad, low, after(hidden_grad, down_sum.keep if fast else down_sum.came))
    mid_sum = summing(links, *mid_parts, 5)
    half_grad, grads_one = attn_backward(
        info, packed, after(mixed_grad, mid_parts[1], down_sum.came), seg_count, 0
    )
    ready = after(mixed_grad, half_grad, *down_sum.far(), mid_sum.came)
    packed_grad, grads_more = attn_backward(info, packed, ready, seg_count, 1, half_grad)
    vec_parts = jnp.concatenate([grads_one + grads_more, grads_two[2:]]).reshape(seg_rows, devices, width)
    vec_parts = vec_parts.transpose(1, 0, 2).reshape(outer, inner, seg_rows * width).astype(LOW)
    if outer > 8:
        vec_parts = vec_parts.reshape(8, -1, seg_rows * width)
    vec_parts = jnp.pad(vec_parts, ((0, 0), (0, 16 - vec_parts.shape[1]), (0, feat_dim - seg_rows * width)))
    if fast:
        vec_parts = links.in_order(list(vec_parts))
    ready = after(packed_grad, *down_sum.near(), *mid_sum.far())
    keep, send = qkv_weight_grad(info, rows_in, ready, vec_parts)
    qkv_sum = summing(links, keep, after(send, *down_sum.turn(), *mid_sum.near()), 3)
    ready = after(packed_grad, qkv_sum.came)
    token_grad = token_gradient(info, ready, proj_grad, first)
    qkv_sum.direct()
    mid_sum.turn()
    qkv_sum.turn(token_grad)
    cross_grads[2] = unmix_columns(after(cross_grads[2], token_grad), devices)
    vec_grad = vec_grad.at[hidden_rows].set(
        unmix_columns(after(vec_grad[hidden_rows], token_grad).reshape(1, -1), devices).reshape(-1, feat_dim)
    )
    cross_vec_grad = lax.dynamic_slice_in_dim(vec_grad, me * width, width, 1)
    grad_positions = lax.dynamic_slice_in_dim(pos_grad, me * width, width, 1)
    grad_down = down_sum.total()
    grad_mid = mid_sum.total().reshape(5, -1, feat_dim)
    total = qkv_sum.total(cross_grads[2], cross_vec_grad)
    grad_qkv = matrix_of(total[: 3 * width].reshape(3, -1, feat_dim))
    grad_vec = total[3 * width, : seg_rows * width].reshape(seg_rows, width)
    return (
        layer_out.reshape(tokens.shape),
        token_grad.reshape(tokens.shape),
        grad_qkv,
        grad_mid[0],
        matrix_of(grad_mid[1:]),
        grad_down,
        grad_vec,
        *cross_grads,
        cross_vec_grad,
        grad_positions,
    )


def solution(mesh):
    in_specs = (
        P(("dp", "fsdp"), None, None),
        P(("dp", "fsdp"), None, None),
        P(),
        P(("dp", "fsdp"), None),
        P(("dp", "fsdp"), None),
        P(("dp", "fsdp"), None),
        P(("dp", "fsdp"), None),
        P(None, ("dp", "fsdp")),
        P(("dp", "fsdp"), None),
        P(("dp", "fsdp"), None),
        P(("dp", "fsdp"), None),
        P(("dp", "fsdp"), None),
        P(None, ("dp", "fsdp")),
        P(None, ("dp", "fsdp")),
    )
    out_specs = (
        P(("dp", "fsdp"), None, None),
        P(("dp", "fsdp"), None, None),
        P(("dp", "fsdp"), None),
        P(("dp", "fsdp"), None),
        P(("dp", "fsdp"), None),
        P(("dp", "fsdp"), None),
        P(None, ("dp", "fsdp")),
        P(("dp", "fsdp"), None),
        P(("dp", "fsdp"), None),
        P(("dp", "fsdp"), None),
        P(("dp", "fsdp"), None),
        P(None, ("dp", "fsdp")),
        P(None, ("dp", "fsdp")),
    )
    return jax.shard_map(
        functools.partial(shards, mesh.shape["dp"], mesh.shape["fsdp"]),
        mesh=mesh, in_specs=in_specs, out_specs=out_specs, check_vma=False)
```

```python
import functools

import jax
import jax.numpy as jnp
from jax import lax
from jax.experimental import pallas as pl
from jax.experimental.pallas import tpu as pltpu
from jax.sharding import PartitionSpec as P

HEAD = 64
SEG = 128
NORM_EPS = 1e-05
MASK_FILL = -1000000000.0
VMEM = 60 * 2**20
F32, LOW = jnp.float32, jnp.bfloat16


ROOT_HALF = 0.7071067811865476
INV_ROOT_TAU = 0.3989422804014327
AXES = ("dp", "fsdp")

def mm(left_op, right_op):
    return jnp.dot(left_op, right_op, preferred_element_type=F32)


def mm_nt(left_op, right_op):
    return lax.dot_general(left_op, right_op, (((1,), (1,)), ((), ())), preferred_element_type=F32)


def mm_tn(left_op, right_op):
    return lax.dot_general(left_op, right_op, (((0,), (0,)), ((), ())), preferred_element_type=F32)


def normalize(summed):
    average = jnp.mean(summed, axis=-1, keepdims=True)
    centered = summed - average
    inv_scale = lax.rsqrt(jnp.mean(centered * centered, axis=-1, keepdims=True) + NORM_EPS)
    return centered * inv_scale, inv_scale


def normalize_back(inner, normed, inv_scale):
    return inv_scale * (
        inner
        - jnp.mean(inner, axis=-1, keepdims=True)
        - normed * jnp.mean(inner * normed, axis=-1, keepdims=True)
    )


def gelu_parts(hidden):
    phi = 0.5 * (1.0 + lax.erf(hidden * ROOT_HALF))
    return hidden * phi, phi + hidden * jnp.exp(-0.5 * hidden * hidden) * INV_ROOT_TAU


def pair_stack(pair, low_half):
    zero = jnp.zeros_like(pair)
    return jnp.concatenate(
        [jnp.where(low_half, pair, zero), jnp.where(low_half, zero, pair)], axis=0
    )


def pair_merge(stacked, low_half):
    rows = stacked.shape[0] // 2
    return jnp.where(low_half, stacked[:rows], stacked[rows:])


def pair_probs(stack, keys, allowed):
    scores = jnp.where(allowed, mm_nt(keys, stack), MASK_FILL)
    expo = jnp.exp(scores - jnp.max(scores, axis=0, keepdims=True))
    return expo * (1.0 / jnp.sum(expo, axis=0, keepdims=True))


def attend(query, keys, values, allowed):
    low_half = lax.broadcasted_iota(jnp.int32, query.shape, 1) < HEAD
    stack = pair_stack(query * jnp.asarray(HEAD**-0.5, query.dtype), low_half)
    return pair_merge(mm_tn(pair_probs(stack, keys, allowed).astype(LOW), values), low_half)


def attend_back(query, keys, values, grad_mixed, allowed):
    low_half = lax.broadcasted_iota(jnp.int32, query.shape, 1) < HEAD
    stack = pair_stack(query * jnp.asarray(HEAD**-0.5, query.dtype), low_half)
    probs = pair_probs(stack, keys, allowed)
    grad_stack = pair_stack(grad_mixed, low_half)
    grad_prob = mm_nt(values, grad_stack)
    inner = jnp.sum(probs * grad_prob, axis=0, keepdims=True)
    score_grad = (probs * (grad_prob - inner)).astype(LOW)
    grad_query = pair_merge(mm_tn(score_grad, keys), low_half) * HEAD**-0.5
    return grad_query, mm(score_grad, stack), mm(probs.astype(LOW), grad_stack)


def slab_copies(place, pieces, slabs, sems, first_sem=0, by_slab=False):
    count = len(slabs)
    half = (count + 1) // 2
    spans = [(0, 0, count), (2, 0, count), (4, 0, count)]
    spans += [(6, 0, count)] if len(pieces) == 8 else [(6, 0, half), (6, half, count)]
    copies = [[] for _ in slabs]
    for flip_c in (0, 1):
        for index, (flip_yx, first, last) in enumerate(spans):
            block = place ^ (flip_yx + flip_c)
            piece = pieces[flip_c * len(spans) + index]
            for slab in range(first, last):
                source = piece.at[pl.ds((slab - first) * 96, 96)]
                sem = sems.at[first_sem + slab * 8 + flip_yx + flip_c]
                copies[slab].append(pltpu.make_async_copy(source, slabs[slab](block), sem))
    return copies if by_slab else sum(copies, [])


def load(copies):
    for copy in copies:
        copy.start()
    for copy in copies:
        copy.wait()


def never(*names):
    pass


def staged(groups):
    for copies in groups.values():
        for copy in copies:
            copy.start()

    def wait(*names):
        for name in names:
            for copy in groups[name]:
                copy.wait()

    return wait


def rows_of(ref, block, rows=96, slab=None):
    where = pl.ds(pl.multiple_of(block * rows, rows), rows)
    return ref.at[where] if slab is None else ref.at[slab, where]


def down_rows(ref, block, part):
    return ref.at[pl.ds(pl.multiple_of(block * 384 + part * 96, 96), 96)]


def qkv_slabs(qkv):
    return [functools.partial(rows_of, qkv, slab=j) for j in range(3)]


def mid_slabs(out, up):
    return [functools.partial(rows_of, out)] + [functools.partial(rows_of, up, slab=j) for j in range(4)]


def down_slabs(down):
    return [functools.partial(down_rows, down, part=j) for j in range(4)]


def segment_mask(length, seg_in_seq):
    row = lax.broadcasted_iota(jnp.int32, (SEG, 2 * SEG), 0)
    return (row + seg_in_seq * SEG < length) | (row == 0)


def attn_forward_kernel(segs, seg_count, first_step, info, x_ref, vec_ref, *rest):
    pieces, (packed_ref, mixed_ref, qkv, sems) = rest[:10], rest[-4:]
    step = pl.program_id(0)

    @pl.when(step == 0)
    def _():
        load(slab_copies(info[0], pieces, qkv_slabs(qkv), sems))

    rows = x_ref[...]
    for j in range(3):
        part = mm(rows, qkv[j])
        if j != 1:
            part = part + vec_ref[j // 2 : j // 2 + 1, :]
        packed_ref[:, j * 768 : (j + 1) * 768] = part.astype(LOW)
    for s in range(segs):
        seg = (step + first_step) * segs + s
        allowed = segment_mask(info[1 + seg // seg_count], seg % seg_count)
        at = slice(s * SEG, (s + 1) * SEG)
        for h in range(6):
            q, k, v = (packed_ref[at, j * 768 + h * 128 : j * 768 + (h + 1) * 128] for j in range(3))
            mixed_ref[at, h * 128 : (h + 1) * 128] = attend(q, k, v, allowed).astype(LOW)


def norm_one(summed, vec_ref):
    normed, _ = normalize(summed)
    return normed * (1.0 + vec_ref[3:4, :]) + vec_ref[4:5, :]


def mid_forward_kernel(info, x_ref, mixed_ref, vec_ref, *rest):
    pieces, (sum_ref, low_ref, act_ref, slope_ref, out, up, sems) = rest[:10], rest[10:]
    step = pl.program_id(0)

    def body(wait):
        wait("out")
        summed = x_ref[...].astype(F32) + mm(mixed_ref[...], out[...]) + vec_ref[2:3, :]
        sum_ref[...] = summed
        first_low = norm_one(summed, vec_ref).astype(LOW)
        low_ref[...] = first_low
        wait("up0")
        hidden = mm(first_low, up[0]) + vec_ref[5:6, :]
        for j in range(4):
            if j < 3:
                wait(f"up{j + 1}")
                later = mm(first_low, up[j + 1]) + vec_ref[6 + j : 7 + j, :]
            act, slope = gelu_parts(hidden)
            act_ref[:, j * 768 : (j + 1) * 768] = act.astype(LOW)
            slope_ref[:, j * 768 : (j + 1) * 768] = slope.astype(LOW)
            hidden = later

    @pl.when(step == 0)
    def _():
        body(staged(mid_groups(info[0], pieces, out, up, sems)))

    @pl.when(step > 0)
    def _():
        body(never)


def down_forward_kernel(segs, info, sum_ref, act_ref, vec_ref, *rest):
    pieces, (second_ref, heads_ref, down, sems) = rest[:8], rest[8:]

    @pl.when(pl.program_id(0) == 0)
    def _():
        load(slab_copies(info[0], pieces, down_slabs(down), sems))

    total = norm_one(sum_ref[...], vec_ref) + vec_ref[9:10, :] + mm(act_ref[...], down[...])
    second_ref[...] = total
    opening = jnp.concatenate([total[s * SEG : s * SEG + 1] for s in range(segs)], axis=0)
    normed, _ = normalize(opening)
    heads_ref[...] = normed * (1.0 + vec_ref[10:11, :]) + vec_ref[11:12, :]


def cross_kernel(blocks, segs, seg_count, info, both_ref, live_ref, vec_ref, pos_ref, seg_vec_ref, *rest):
    wide, tops_in, sources, mid, more, rest = rest[0], rest[1:6], rest[6:9], rest[9:19], rest[19:27], rest[27:]
    grads_ref, pos_grad_ref, qkv_grad_ref, out_grad_ref, up_grad_ref, down_grad_ref, seg_grads_ref, *tops_out = rest[:12]
    (qkv, out, up, down, sems, result, heads_grad, slope, lefts, act, packed, rights, hidden_grad) = rest[12:25]
    tops, parts, own_hidden, weights, (seg_sems, top_sems) = rest[25:30], rest[30:33], rest[33], rest[34:37], rest[37:]
    step = pl.program_id(0)
    count = live_ref.shape[0]
    at = pl.ds(pl.multiple_of(step * count, count), count)
    targets = [qkv.at[j] for j in range(3)] + [out] + [up.at[j] for j in range(4)]
    targets += [down.at[j * 768 : (j + 1) * 768] for j in range(4)]
    copies = [pltpu.make_async_copy(wide.at[j], t, sems.at[j]) for j, t in enumerate(targets)]

    @pl.when(step == 0)
    def _():
        for copy in copies:
            copy.start()
        staged(opening_groups(info[0], tops_in, sources, mid, more, tops, parts, weights, seg_sems, top_sems))
        grads_ref[...] = jnp.zeros_like(grads_ref)
        pos_grad_ref[...] = jnp.zeros_like(pos_grad_ref)
        for copy in copies[:3]:
            copy.wait()

    vec = vec_ref[...]
    inputs = both_ref[:, 0].reshape(count, 768).astype(F32).reshape(-1, 8, 768) + pos_ref[...][None]
    inputs = inputs.reshape(count, 768)
    low = inputs.astype(LOW)
    lefts[0, at, :] = low
    for j in range(3):
        part = mm(low, qkv[j])
        if j != 1:
            part = part + vec[j // 2 : j // 2 + 1]
        packed[:, j * 768 : (j + 1) * 768] = part.astype(LOW)
    row = lax.broadcasted_iota(jnp.int32, (SEG, 2 * SEG), 0)
    lane = lax.broadcasted_iota(jnp.int32, (SEG, 2 * SEG), 1)
    group = row // 8 == lane % SEG // 8
    masks = []
    for s in range(count // SEG):
        live = live_ref[s * SEG : (s + 1) * SEG, :]
        masks.append(group & (jnp.concatenate([live, live], axis=1) > 0.0))
    for s, allowed in enumerate(masks):
        part = slice(s * SEG, (s + 1) * SEG)
        for h in range(6):
            q, k, v = (packed[part, j * 768 + h * 128 : j * 768 + (h + 1) * 128] for j in range(3))
            where = pl.ds(pl.multiple_of(step * count + s * SEG, SEG), SEG)
            lefts[1, where, h * 128 : (h + 1) * 128] = attend(q, k, v, allowed).astype(LOW)

    @pl.when(step == 0)
    def _():
        for copy in copies[3:]:
            copy.wait()

    summed = inputs + mm(lefts[1, at, :], out[...]) + vec[2:3]
    normed_one, scale_one = normalize(summed)
    first = normed_one * (1.0 + vec[3:4]) + vec[4:5]
    first_low = first.astype(LOW)
    lefts[2, at, :] = first_low
    total = first + vec[9:10]
    for j in range(4):
        cols = slice(j * 768, (j + 1) * 768)
        hidden = mm(first_low, up[j]) + vec[5 + j : 6 + j]
        active, steep = gelu_parts(hidden)
        act[at, cols] = active.astype(LOW)
        slope[:, cols] = steep.astype(LOW)
        total = total + mm(active.astype(LOW), down[cols, :])
    normed, inv_scale = normalize(total)
    result[at, :] = normed * (1.0 + vec[10:11]) + vec[11:12]
    upstream = both_ref[:, 1].reshape(count, 768).astype(F32)
    back_two = normalize_back(upstream * (1.0 + vec[10:11]), normed, inv_scale)
    down_grad = back_two.astype(LOW)
    rights[1, at, :] = down_grad
    grads_ref[9:10, :] += column_sum(down_grad)
    grads_ref[10:11, :] += column_sum(upstream * normed)
    grads_ref[11:12, :] += column_sum(upstream)
    total = back_two
    for j in range(4):
        cols = slice(j * 768, (j + 1) * 768)
        grad = (mm_nt(down_grad, down[cols, :]) * slope[:, cols].astype(F32)).astype(LOW)
        hidden_grad[at, cols] = grad
        grads_ref[5 + j : 6 + j, :] += column_sum(grad)
        total = total + mm_nt(grad, up[j])
    back_one = normalize_back(total * (1.0 + vec[3:4]), normed_one, scale_one)
    proj_grad = back_one.astype(LOW)
    rights[0, at, :] = proj_grad
    grads_ref[2:3, :] += column_sum(proj_grad)
    grads_ref[3:4, :] += column_sum(total * normed_one)
    grads_ref[4:5, :] += column_sum(total)
    mixed_grad = mm_nt(proj_grad, out[...]).astype(LOW)
    for s, allowed in enumerate(masks):
        part = slice(s * SEG, (s + 1) * SEG)
        where = pl.ds(pl.multiple_of(step * count + s * SEG, SEG), SEG)
        for h in range(6):
            cols = slice(h * 128, (h + 1) * 128)
            q, k, v = (packed[part, j * 768 + h * 128 : j * 768 + (h + 1) * 128] for j in range(3))
            for j, g in enumerate(attend_back(q, k, v, mixed_grad[part, cols], allowed)):
                rights[2 + j, where, cols] = g.astype(LOW)
    total = back_one
    for j in range(3):
        part = rights[2 + j, at, :]
        total = total + mm_nt(part, qkv[j])
        if j != 1:
            grads_ref[j // 2 : j // 2 + 1, :] += column_sum(part)
    heads_grad[at, :] = total
    pos_grad_ref[...] += jnp.sum(total.reshape(-1, 8, 768), axis=0)

    @pl.when(step == blocks - 1)
    def _():
        me = info[1]
        own = pl.ds(pl.multiple_of(info[2] * 16, 16), 16)
        groups = opening_groups(info[0], tops_in, sources, mid, more, tops, parts, weights, seg_sems, top_sems)

        def wait(*names):
            for name in names:
                for copy in groups[name]:
                    copy.wait()

        lengths = [info[3 + i] for i in range(segs // seg_count)]
        opening_rows(segs, seg_count, lengths, result[own, :], heads_grad[own, :], seg_vec_ref, tops_out,
                     seg_grads_ref, tops, parts, own_hidden, weights, top_sems, wait)

        def chosen(left, rows):
            width = left.shape[1]
            wanted = lax.broadcasted_iota(jnp.int32, (rows, width), 1) - lax.broadcasted_iota(
                jnp.int32, (rows, width), 0
            )
            pick = (wanted == me * rows).astype(F32).astype(LOW)
            return mm_nt(pick, left).astype(LOW)

        left = chosen(lefts[0], 24)
        for j in range(3):
            qkv_grad_ref[:, j * 768 : (j + 1) * 768] = mm(left, rights[2 + j])
        out_grad_ref[...] = mm(chosen(lefts[1], 24), rights[0])
        left = chosen(lefts[2], 24)
        for j in range(4):
            cols = slice(j * 768, (j + 1) * 768)
            up_grad_ref[:, cols] = mm(left, hidden_grad[:, cols])
        for j in range(4):
            left = chosen(act[:, j * 768 : (j + 1) * 768], 24)
            down_grad_ref[j * 24 : (j + 1) * 24, :] = mm(left, rights[1])


def column_sum(value):
    return jnp.sum(value.astype(F32), axis=0, keepdims=True)


def ffn_back_rows(upstream, second, summed, slope, vec, grads_ref, hidden_grad, out, up, down, wait):
    normed, inv_scale = normalize(second)
    back_two = normalize_back(upstream * (1.0 + vec[10:11, :]), normed, inv_scale)
    down_grad = back_two.astype(LOW)
    grads_ref[9:10, :] += column_sum(down_grad)
    grads_ref[10:11, :] += column_sum(upstream * normed)
    grads_ref[11:12, :] += column_sum(upstream)
    total = back_two
    wait("down")
    for j in range(4):
        cols = slice(j * 768, (j + 1) * 768)
        grad = (mm_nt(down_grad, down[cols, :]) * slope(cols).astype(F32)).astype(LOW)
        hidden_grad(cols, grad)
        grads_ref[5 + j : 6 + j, :] += column_sum(grad)
        wait(f"up{j}")
        total = total + mm_nt(grad, up[j])
    wait("out")
    normed, inv_scale = normalize(summed)
    back_one = normalize_back(total * (1.0 + vec[3:4, :]), normed, inv_scale)
    proj_grad = back_one.astype(LOW)
    grads_ref[2:3, :] += column_sum(proj_grad)
    grads_ref[3:4, :] += column_sum(total * normed)
    grads_ref[4:5, :] += column_sum(total)
    return down_grad, proj_grad, mm_nt(proj_grad, out[...]).astype(LOW)


def mid_groups(place, mid, out, up, sems):
    copies = slab_copies(place, mid, mid_slabs(out, up), sems, by_slab=True)
    groups = {f"up{j}": copies[j + 1] for j in range(4)}
    return {"out": copies[0], **groups}


def ffn_groups(place, mid, rest, out, up, down, sems):
    groups = mid_groups(place, mid, out, up, sems)
    last = groups.pop("out")
    return {"down": slab_copies(place, rest, down_slabs(down), sems, 40), **groups, "out": last}


def ffn_backward_kernel(segs, seg_count, first_step, info, cot_ref, second_ref, sum_ref, slope_ref, vec_ref, *rest):
    mid, more, rest = rest[:10], rest[10:18], rest[-10:]
    out_ref, down_grad_ref, hidden_grad_ref, proj_grad_ref, mixed_grad_ref, grads_ref, out, up, down, sems = rest
    step = pl.program_id(0)

    def body(wait):
        second = second_ref[...]
        normed, _ = normalize(second)
        result = normed * (1.0 + vec_ref[10:11, :]) + vec_ref[11:12, :]
        row = lax.broadcasted_iota(jnp.int32, (SEG, 1), 0)
        ups = []
        for s in range(segs):
            seg = (step + first_step) * segs + s
            at = slice(s * SEG, (s + 1) * SEG)
            live = row + seg % seg_count * SEG < info[1 + seg // seg_count]
            out_ref[at, :] = jnp.where(live, result[at], 0.0).astype(LOW)
            ups.append(jnp.where(live & (row > 0), cot_ref[at, :].astype(F32), 0.0))

        def store(cols, grad):
            hidden_grad_ref[:, cols] = grad

        down_grad_ref[...], proj_grad_ref[...], mixed_grad_ref[...] = ffn_back_rows(
            jnp.concatenate(ups, axis=0), second, sum_ref[...], lambda cols: slope_ref[:, cols], vec_ref, grads_ref,
            store, out, up, down, wait,
        )

    @pl.when(step == 0)
    def _():
        wait = staged(ffn_groups(info[0], mid, more, out, up, down, sems))
        grads_ref[...] = jnp.zeros_like(grads_ref)
        body(wait)

    @pl.when(step > 0)
    def _():
        body(never)


def opening_groups(place, tops_in, sources, mid, more, tops, parts, weights, sems, top_sems):
    pairs = zip((*tops_in, *sources), (*tops, *parts))
    copies = [
        pltpu.make_async_copy(source.at[:, 0 : target.shape[1], :], target, top_sems.at[i])
        for i, (source, target) in enumerate(pairs)
    ]
    return {"tops": copies, **ffn_groups(place, mid, more, *weights, sems)}


def opening_rows(segs, seg_count, lengths, heads, heads_grad, vec_ref, tops_out, grads_ref, tops, parts, hidden, weights, top_sems, wait):
    wait("tops")
    grads_ref[...] = jnp.zeros_like(grads_ref)
    second, summed = parts[0][:, 0, :], parts[1][:, 0, :]
    slope = parts[2][...].astype(F32)[:, 0, :]

    def store(cols, grad):
        hidden[:, cols] = grad.astype(F32)

    down_grad, proj_grad, mixed_grad = ffn_back_rows(
        heads_grad, second, summed, lambda cols: slope[:, cols], vec_ref, grads_ref, store, *weights, wait
    )
    seg = lax.broadcasted_iota(jnp.int32, (segs, 1), 0)
    length = jnp.full((segs, 1), lengths[0], jnp.int32)
    for i in range(1, len(lengths)):
        length = jnp.where(seg >= i * seg_count, lengths[i], length)
    merged = jnp.where(lax.rem(seg, seg_count) * SEG < length, heads, 0.0)
    outs = []
    values = (merged, down_grad.astype(F32), hidden[...], proj_grad.astype(F32), mixed_grad.astype(F32))
    for i, (value, top) in enumerate(zip(values, tops)):
        row = lax.broadcasted_iota(jnp.int32, top.shape, 1)
        top[...] = jnp.where(row == 0, value[:, None, :], top[...].astype(F32)).astype(LOW)
        outs.append(pltpu.make_async_copy(top, tops_out[i].at[:, 0:16, :], top_sems.at[i]))
    load(outs)


def opening_kernel(segs, seg_count, info, heads_ref, heads_grad_ref, vec_ref, *rest):
    tops_in, sources, mid, more, rest = rest[:5], rest[5:8], rest[8:18], rest[18:26], rest[26:]
    tops_out, grads_ref, tops, parts, hidden = rest[:5], rest[5], rest[6:11], rest[11:14], rest[14]
    *weights, sems, top_sems = rest[15:]
    wait = staged(opening_groups(info[0], tops_in, sources, mid, more, tops, parts, weights, sems, top_sems))
    lengths = [info[1 + i] for i in range(segs // seg_count)]
    opening_rows(segs, seg_count, lengths, heads_ref[...], heads_grad_ref[...], vec_ref, tops_out, grads_ref, tops,
                 parts, hidden, weights, top_sems, wait)


def attn_backward_kernel(segs, seg_count, first_step, info, packed_ref, mixed_grad_ref, *rest):
    packed_grad_ref, grads_ref = rest[-2:]
    step = pl.program_id(0)

    @pl.when(step == 0)
    def _():
        grads_ref[...] = jnp.zeros_like(grads_ref)

    for s in range(segs):
        seg = (step + first_step) * segs + s
        allowed = segment_mask(info[1 + seg // seg_count], seg % seg_count)
        at = slice(s * SEG, (s + 1) * SEG)
        for h in range(6):
            cols = [slice(j * 768 + h * 128, j * 768 + (h + 1) * 128) for j in range(3)]
            q, k, v = (packed_ref[at, c] for c in cols)
            grads = attend_back(q, k, v, mixed_grad_ref[at, cols[0]], allowed)
            for c, g in zip(cols, grads):
                packed_grad_ref[at, c] = g.astype(LOW)
    grads_ref[0:1, :] += column_sum(packed_grad_ref[:, :768])
    grads_ref[1:2, :] += column_sum(packed_grad_ref[:, 1536:])


def token_grad_kernel(info, packed_grad_ref, proj_grad_ref, *rest):
    pieces, (token_grad_ref, qkv, sems) = rest[:10], rest[10:]

    @pl.when(pl.program_id(0) == 0)
    def _():
        load(slab_copies(info[0], pieces, qkv_slabs(qkv), sems))

    total = proj_grad_ref[...].astype(F32)
    for j in range(3):
        total = total + mm_nt(packed_grad_ref[:, j * 768 : (j + 1) * 768], qkv[j])
    token_grad_ref[...] = total.astype(LOW)


def send_slab(place, total, keep_ref, send_ref, rows):
    for mask in range(8):
        block = pl.multiple_of((place ^ mask) * rows, rows)
        target = send_ref if mask % 2 else keep_ref
        target[mask // 2] = total[pl.ds(block, rows), :].astype(LOW)


def qkv_grad_kernel(info, left_ref, right_ref, more_ref, keep_ref, send_ref, total):
    step = pl.program_id(0)
    total[...] = mm_tn(left_ref[...], right_ref[...])
    at = pl.ds(pl.multiple_of(step * 96, 96), 96)
    for mask in range(8):
        block = pl.multiple_of((info[0] ^ mask) * 96, 96)
        target = send_ref if mask % 2 else keep_ref
        target[mask // 2, at, :] = total[pl.ds(block, 96), :].astype(LOW)

    @pl.when(step == 0)
    def _():
        for mask in range(8):
            target = send_ref if mask % 2 else keep_ref
            target[mask // 2, 288:304, :] = more_ref[info[0] ^ mask]


def mid_grad_kernel(info, mixed_ref, proj_ref, low_ref, hidden_ref, keep_ref, send_ref, total):
    @pl.when(pl.program_id(0) == 0)
    def _():
        total[...] = mm_tn(mixed_ref[...], proj_ref[...])

    @pl.when(pl.program_id(0) > 0)
    def _():
        total[...] = mm_tn(low_ref[...], hidden_ref[...])

    send_slab(info[0], total, keep_ref, send_ref, 96)


ANY = pl.BlockSpec(memory_space=pl.ANY)
SMEM = pl.BlockSpec(memory_space=pltpu.SMEM)


def block_rows(count, width):
    return pl.BlockSpec((count, width), lambda i: (i, 0))


def fixed(shape):
    return pl.BlockSpec(shape, lambda i: (0,) * len(shape))


def shape_of(dims, kind=LOW):
    return jax.ShapeDtypeStruct(dims, kind)


def params():
    return pltpu.CompilerParams(vmem_limit_bytes=VMEM, dimension_semantics=("arbitrary",))


def cost(flops, size):
    return pl.CostEstimate(flops=flops, bytes_accessed=size, transcendentals=0)


QKV = [pltpu.VMEM((3, 768, 768), LOW)]
MID = [pltpu.VMEM((768, 768), LOW), pltpu.VMEM((4, 768, 768), LOW)]
DOWN = [pltpu.VMEM((3072, 768), LOW)]


def sems(count):
    return [pltpu.SemaphoreType.DMA((count,))]


def shifted(count, width, first):
    return pl.BlockSpec((count, width), lambda i: (i + first, 0))


def attn_forward(info, rows_in, vec, pieces, seg_count, half, before=None, segs=4):
    rows = rows_in.shape[0]
    count = segs * SEG
    steps = rows // count // 2
    first = half * steps
    before = list(before or [])
    return pl.pallas_call(
        functools.partial(attn_forward_kernel, segs, seg_count, first),
        grid=(steps,),
        in_specs=[SMEM, shifted(count, 768, first), fixed((12, 768))] + [ANY] * (10 + len(before)),
        out_specs=[shifted(count, 2304, first), shifted(count, 768, first)],
        out_shape=[shape_of((rows, 2304)), shape_of((rows, 768))],
        scratch_shapes=QKV + sems(24),
        input_output_aliases={13: 0, 14: 1} if before else {},
        compiler_params=params(),
        cost_estimate=cost(rows * 768 * 8000, rows * 768 * 8),
        name="attn_forward",
    )(info, rows_in, vec, *pieces, *before)


def mid_forward(info, rows_in, mixed, vec, pieces, segs=2):
    rows = rows_in.shape[0]
    count = segs * SEG
    return pl.pallas_call(
        mid_forward_kernel,
        grid=(rows // count,),
        in_specs=[SMEM, block_rows(count, 768), block_rows(count, 768), fixed((12, 768))] + [ANY] * 10,
        out_specs=[block_rows(count, 768), block_rows(count, 768), block_rows(count, 3072), block_rows(count, 3072)],
        out_shape=[shape_of((rows, 768), F32), shape_of((rows, 768)), shape_of((rows, 3072)), shape_of((rows, 3072))],
        scratch_shapes=MID + sems(40),
        compiler_params=params(),
        cost_estimate=cost(2 * rows * 768 * 8000, rows * 768 * 30),
        name="mid_forward",
    )(info, rows_in, mixed, vec, *pieces)


def down_forward(info, summed, act, vec, pieces, segs=2):
    rows = summed.shape[0]
    count = segs * SEG
    few = pl.BlockSpec((None, segs, 768), lambda i: (i, 0, 0))
    return pl.pallas_call(
        functools.partial(down_forward_kernel, segs),
        grid=(rows // count,),
        in_specs=[SMEM, block_rows(count, 768), block_rows(count, 3072), fixed((12, 768))] + [ANY] * 8,
        out_specs=[block_rows(count, 768), few],
        out_shape=[shape_of((rows, 768), F32), shape_of((rows // count, segs, 768), F32)],
        scratch_shapes=DOWN + sems(32),
        compiler_params=params(),
        cost_estimate=cost(2 * rows * 768 * 4000, rows * 768 * 16),
        name="down_forward",
    )(info, summed, act, vec, *pieces)


def grouped(array):
    return array.reshape(-1, SEG, array.shape[1])


def top_scratch(segs, arrays):
    tops = [pltpu.VMEM((segs, 16, a.shape[2]), LOW) for a in arrays]
    parts = [pltpu.VMEM((segs, 8, 768), F32)] * 2 + [pltpu.VMEM((segs, 16, 3072), LOW)]
    return tops + parts + [pltpu.VMEM((segs, 3072), F32)] + MID + DOWN + sems(72) + sems(8)


def cross_whole(info, both, live, vec, positions, wide, seg_vec, arrays, sources, mid, more, seg_count):
    rows = live.shape[0]
    count = 2 * SEG
    pair = pl.BlockSpec((count // 16, 2, 16, 768), lambda i: (i, 0, 0, 0))
    arrays, sources = [grouped(a) for a in arrays], [grouped(a) for a in sources]
    segs = arrays[0].shape[0]
    own = [(12, 768), (8, 768), (24, 2304), (24, 768), (24, 3072), (96, 768), (12, 768)]
    *grads, seg_grads, layer, down, hidden, proj, mixed = pl.pallas_call(
        functools.partial(cross_kernel, rows // count, segs, seg_count),
        grid=(rows // count,),
        in_specs=[SMEM, pair, block_rows(count, SEG), fixed((12, 768)), fixed((8, 768)), fixed((12, 768))] + [ANY] * 27,
        out_specs=[fixed(dims) for dims in own] + [ANY] * 5,
        out_shape=[shape_of(dims, F32) for dims in own] + [shape_of(a.shape) for a in arrays],
        scratch_shapes=QKV + MID + DOWN + sems(12) + [
            pltpu.VMEM((rows, 768), F32), pltpu.VMEM((rows, 768), F32), pltpu.VMEM((count, 3072), LOW),
            pltpu.VMEM((3, rows, 768), LOW), pltpu.VMEM((rows, 3072), LOW), pltpu.VMEM((count, 2304), LOW),
            pltpu.VMEM((5, rows, 768), LOW), pltpu.VMEM((rows, 3072), LOW),
        ] + top_scratch(segs, arrays),
        input_output_aliases={7 + i: 7 + i for i in range(5)},
        compiler_params=params(),
        cost_estimate=cost(2 * rows * 768 * 30000, 2**24),
        name="cross_encoder",
    )(info, both, live, vec, positions, seg_vec, wide, *arrays, *sources, *mid, *more)
    return grads, seg_grads, [a.reshape(-1, a.shape[2]) for a in (layer, down, hidden, proj, mixed)]


def ffn_backward(info, cotangent, second, summed, slope, vec, mid, down, seg_count, half, before=None, segs=2):
    rows = summed.shape[0]
    count = segs * SEG
    steps = rows // count // 2
    first = half * steps
    before = list(before or [])
    widths = (768, 768, 3072, 768, 768)
    return pl.pallas_call(
        functools.partial(ffn_backward_kernel, segs, seg_count, first),
        grid=(steps,),
        in_specs=[SMEM, shifted(count, 768, first), shifted(count, 768, first), shifted(count, 768, first),
                  shifted(count, 3072, first), fixed((12, 768))] + [ANY] * (18 + len(before)),
        out_specs=[shifted(count, w, first) for w in widths] + [fixed((12, 768))],
        out_shape=[shape_of((rows, w)) for w in widths] + [shape_of((12, 768), F32)],
        scratch_shapes=MID + DOWN + sems(72),
        input_output_aliases={24 + i: i for i in range(5)} if before else {},
        compiler_params=params(),
        cost_estimate=cost(rows * 768 * 14000, rows * 768 * 15),
        name="ffn_backward",
    )(info, cotangent, second, summed, slope, vec, *mid, *down, *before)


def opening_backward(info, heads, heads_grad, vec, arrays, sources, mid, down, seg_count):
    segs = heads.shape[0]
    arrays, sources = [grouped(a) for a in arrays], [grouped(a) for a in sources]
    whole = fixed((segs, 768))
    *done, grads = pl.pallas_call(
        functools.partial(opening_kernel, segs, seg_count),
        grid=(1,),
        in_specs=[SMEM, whole, whole, fixed((12, 768))] + [ANY] * 26,
        out_specs=[ANY] * 5 + [fixed((12, 768))],
        out_shape=[shape_of(a.shape) for a in arrays] + [shape_of((12, 768), F32)],
        scratch_shapes=top_scratch(segs, arrays),
        input_output_aliases={4 + i: i for i in range(5)},
        compiler_params=params(),
        cost_estimate=cost(2**33, 2**24),
        name="opening_backward",
    )(info, heads, heads_grad, vec, *arrays, *sources, *mid, *down)
    return [a.reshape(-1, a.shape[2]) for a in done], grads


def attn_backward(info, packed, mixed_grad, seg_count, half, before=None, segs=2):
    rows = packed.shape[0]
    count = segs * SEG
    steps = rows // count // 2
    first = half * steps
    before = [] if before is None else [before]
    return pl.pallas_call(
        functools.partial(attn_backward_kernel, segs, seg_count, first),
        grid=(steps,),
        in_specs=[SMEM, shifted(count, 2304, first), shifted(count, 768, first)] + [ANY] * len(before),
        out_specs=[shifted(count, 2304, first), fixed((2, 768))],
        out_shape=[shape_of((rows, 2304)), shape_of((2, 768), F32)],
        input_output_aliases={3: 0} if before else {},
        compiler_params=params(),
        cost_estimate=cost(rows * 768 * 10000, rows * 768 * 8),
        name="attn_backward",
    )(info, packed, mixed_grad, *before)


def token_gradient(info, packed_grad, proj_grad, pieces, count=512):
    rows = packed_grad.shape[0]
    return pl.pallas_call(
        token_grad_kernel,
        grid=(rows // count,),
        in_specs=[SMEM, block_rows(count, 2304), block_rows(count, 768)] + [ANY] * 10,
        out_specs=block_rows(count, 768),
        out_shape=shape_of((rows, 768)),
        scratch_shapes=QKV + sems(24),
        compiler_params=params(),
        cost_estimate=cost(2 * rows * 768 * 3000, rows * 768 * 10),
        name="token_gradient",
    )(info, packed_grad, proj_grad, *pieces)


def grad_outs(slabs):
    out = pl.BlockSpec((4, 96, 768), lambda i: (0, i, 0))
    return [out, out], [shape_of((4, slabs * 96, 768))] * 2


def qkv_weight_grad(info, left, right, more):
    rows = left.shape[0]
    out = fixed((4, 304, 768))
    return pl.pallas_call(
        qkv_grad_kernel,
        grid=(3,),
        in_specs=[SMEM, fixed((rows, 768)), pl.BlockSpec((rows, 768), lambda i: (0, i)), fixed((8, 16, 768))],
        out_specs=[out, out],
        out_shape=[shape_of((4, 304, 768))] * 2,
        scratch_shapes=[pltpu.VMEM((768, 768), F32)],
        compiler_params=params(),
        cost_estimate=cost(2 * rows * 768 * 2304, rows * 2304 * 2),
        name="qkv_weight_grad",
    )(info, left, right, more)


def mid_weight_grad(info, mixed, proj_grad, low, hidden_grad):
    rows = mixed.shape[0]
    specs, shapes = grad_outs(5)
    still = fixed((rows, 768))
    return pl.pallas_call(
        mid_grad_kernel,
        grid=(5,),
        in_specs=[SMEM, still, still, still, pl.BlockSpec((rows, 768), lambda i: (0, jnp.maximum(i - 1, 0)))],
        out_specs=specs,
        out_shape=shapes,
        scratch_shapes=[pltpu.VMEM((768, 768), F32)],
        compiler_params=params(),
        cost_estimate=cost(2 * rows * 768 * 3840, rows * 3840 * 2),
        name="mid_weight_grad",
    )(info, mixed, proj_grad, low, hidden_grad)


def down_grad_kernel(info, left_ref, right_ref, keep_ref, send_ref, total):
    step = pl.program_id(0)
    total[pl.ds(pl.multiple_of(step * 768, 768), 768), :] = mm_tn(left_ref[...], right_ref[...]).astype(LOW)

    @pl.when(step == pl.num_programs(0) - 1)
    def _():
        for mask in range(8):
            block = pl.multiple_of((info[0] ^ mask) * 384, 384)
            target = send_ref if mask % 2 else keep_ref
            target[mask // 2] = total[pl.ds(block, 384), :]


def down_weight_grad(info, left, right):
    rows, wide = left.shape
    return pl.pallas_call(
        down_grad_kernel,
        grid=(wide // 768,),
        in_specs=[SMEM, pl.BlockSpec((rows, 768), lambda i: (0, i)), fixed((rows, 768))],
        out_specs=[fixed((4, 384, 768))] * 2,
        out_shape=[shape_of((4, 384, 768))] * 2,
        scratch_shapes=[pltpu.VMEM((3072, 768), LOW)],
        compiler_params=params(),
        cost_estimate=cost(2 * rows * 768 * wide, rows * wide * 2),
        name="down_weight_grad",
    )(info, left, right)


def matmul(left_op, right_op):
    return jnp.dot(left_op, right_op, preferred_element_type=jnp.float32)


def trans_left(left_op, right_op):
    return lax.dot_general(
        left_op, right_op, (((0,), (0,)), ((), ())), preferred_element_type=jnp.float32
    )


def trans_right(left_op, right_op):
    return lax.dot_general(
        left_op, right_op, (((1,), (1,)), ((), ())), preferred_element_type=jnp.float32
    )


def norm_forward(summed, gain_row, shift_row):
    average = jnp.mean(summed, axis=-1, keepdims=True)
    centered = summed - average
    inv_scale = lax.rsqrt(jnp.mean(centered * centered, axis=-1, keepdims=True) + NORM_EPS)
    normed = centered * inv_scale
    return (normed * (1.0 + gain_row) + shift_row, normed, inv_scale)


def norm_backward(upstream, normed, inv_scale, gain_row):
    inner = upstream * (1.0 + gain_row)
    back_grad = inv_scale * (
        inner
        - jnp.mean(inner, axis=-1, keepdims=True)
        - normed * jnp.mean(inner * normed, axis=-1, keepdims=True)
    )
    return (back_grad, jnp.sum(upstream * normed, axis=0), jnp.sum(upstream, axis=0))


def gelu_slope(hidden):
    return (
        0.5 * (1.0 + lax.erf(hidden * ROOT_HALF))
        + hidden * jnp.exp(-0.5 * hidden * hidden) * INV_ROOT_TAU
    )


def split_heads(packed, group_len):
    head_count = packed.shape[1] // (3 * HEAD)
    return [
        portion.reshape(-1, group_len, head_count, HEAD) for portion in jnp.split(packed, 3, axis=1)
    ]


def masked_scores(query_heads, key_heads, allowed):
    raw_scores = jnp.einsum(
        "nqhd,nkhd->nhqk", query_heads, key_heads, preferred_element_type=jnp.float32
    ) * HEAD ** (-0.5)
    return jnp.where(allowed[:, None, None, :], raw_scores, MASK_FILL)


def encode(inputs, inputs_low, weights, allowed):
    qkv_w, out_w, up_w, down_w, vectors = weights
    row_count, feat_dim = inputs_low.shape
    group_len = allowed.shape[1]
    qkv_bias = jnp.concatenate([vectors[0], jnp.zeros_like(vectors[0]), vectors[1]])
    packed = (matmul(inputs_low, qkv_w) + qkv_bias).astype(jnp.bfloat16)
    query_heads, key_heads, value_heads = split_heads(packed, group_len)
    scores = masked_scores(query_heads, key_heads, allowed)
    row_max = jnp.max(scores, axis=-1, keepdims=True)
    expo_vals = jnp.exp(scores - row_max)
    row_total = jnp.sum(expo_vals, axis=-1, keepdims=True)
    log_total = row_max + jnp.log(row_total)
    prob_low = (expo_vals / row_total).astype(jnp.bfloat16)
    mixed = jnp.einsum("nhqk,nkhd->nqhd", prob_low, value_heads, preferred_element_type=jnp.float32)
    mixed = mixed.reshape(row_count, feat_dim).astype(jnp.bfloat16)
    projected = matmul(mixed, out_w) + vectors[2]
    first_out, normed_one, scale_one = norm_forward(inputs + projected, vectors[3], vectors[4])
    first_low = first_out.astype(jnp.bfloat16)
    hidden = matmul(first_low, up_w) + vectors[5:-3].reshape(-1)
    activated = jax.nn.gelu(hidden, approximate=False).astype(jnp.bfloat16)
    down_out = matmul(activated, down_w) + vectors[-3]
    result, normed_two, scale_two = norm_forward(first_out + down_out, vectors[-2], vectors[-1])
    return (
        result,
        (
            packed,
            log_total,
            mixed,
            normed_one,
            scale_one,
            first_low,
            hidden,
            activated,
            normed_two,
            scale_two,
        ),
    )


def encode_back(upstream, inputs_low, weights, allowed, kept):
    qkv_w, out_w, up_w, down_w, vectors = weights
    (
        packed,
        log_total,
        mixed,
        normed_one,
        scale_one,
        first_low,
        hidden,
        activated,
        normed_two,
        scale_two,
    ) = kept
    row_count, feat_dim = inputs_low.shape
    group_len = allowed.shape[1]
    back_two, gain_two, shift_two = norm_backward(upstream, normed_two, scale_two, vectors[-2])
    down_grad = back_two.astype(jnp.bfloat16)
    hidden_grad = (trans_right(down_grad, down_w) * gelu_slope(hidden)).astype(jnp.bfloat16)
    first_grad = trans_right(hidden_grad, up_w) + back_two
    back_one, gain_one, shift_one = norm_backward(first_grad, normed_one, scale_one, vectors[3])
    proj_grad = back_one.astype(jnp.bfloat16)
    query_heads, key_heads, value_heads = split_heads(packed, group_len)
    mixed_grad = trans_right(proj_grad, out_w).astype(jnp.bfloat16).reshape(value_heads.shape)
    scores = masked_scores(query_heads, key_heads, allowed)
    prob_vals = jnp.exp(scores - log_total)
    grad_values = jnp.einsum(
        "nhqk,nqhd->nkhd",
        prob_vals.astype(jnp.bfloat16),
        mixed_grad,
        preferred_element_type=jnp.float32,
    )
    grad_prob = jnp.einsum(
        "nqhd,nkhd->nhqk", mixed_grad, value_heads, preferred_element_type=jnp.float32
    )
    score_grad = (
        prob_vals * (grad_prob - jnp.sum(prob_vals * grad_prob, axis=-1, keepdims=True))
    ).astype(jnp.bfloat16)
    grad_query = jnp.einsum(
        "nhqk,nkhd->nqhd", score_grad, key_heads, preferred_element_type=jnp.float32
    ) * HEAD ** (-0.5)
    grad_keys = jnp.einsum(
        "nhqk,nqhd->nkhd", score_grad, query_heads, preferred_element_type=jnp.float32
    ) * HEAD ** (-0.5)
    packed_grad = jnp.concatenate(
        [
            grad_query.reshape(row_count, feat_dim),
            grad_keys.reshape(row_count, feat_dim),
            grad_values.reshape(row_count, feat_dim),
        ],
        axis=1,
    ).astype(jnp.bfloat16)
    bias_grads = jnp.sum(packed_grad, axis=0, dtype=jnp.float32).reshape(3, feat_dim)
    grad_inputs = trans_right(packed_grad, qkv_w) + back_one
    grad_vectors = jnp.concatenate(
        [
            bias_grads[0:1],
            bias_grads[2:3],
            jnp.sum(proj_grad, axis=0, dtype=jnp.float32)[None],
            gain_one[None],
            shift_one[None],
            jnp.sum(hidden_grad, axis=0, dtype=jnp.float32).reshape(-1, feat_dim),
            jnp.sum(down_grad, axis=0, dtype=jnp.float32)[None],
            gain_two[None],
            shift_two[None],
        ],
        axis=0,
    )
    pairs = (
        (inputs_low, packed_grad),
        (mixed, proj_grad),
        (first_low, hidden_grad),
        (activated, down_grad),
    )
    return (grad_inputs, pairs, grad_vectors)


class Links:
    def __init__(self, outer, inner):
        self.outer, self.inner = outer, inner
        self.order = self.place = lax.axis_index("dp")
        self.z = lax.axis_index("fsdp")

    def flip(self, value, mask):
        pairs = [
            (d * self.inner + z, (d ^ mask) * self.inner + z)
            for d in range(self.outer)
            for z in range(self.inner)
        ]
        return lax.ppermute(value, AXES, pairs)

    def turn(self, value, step):
        pairs = [
            (d * self.inner + z, d * self.inner + (z + step) % self.inner)
            for d in range(self.outer)
            for z in range(self.inner)
        ]
        return lax.ppermute(value, AXES, pairs)

    def gather_z(self, shard):
        came = [shard] + [self.turn(shard, step) for step in range(1, self.inner)]
        whole = []
        for z in range(self.inner):
            part = came[-1]
            for step in range(self.inner - 1):
                part = jnp.where(self.z == (z + step) % self.inner, came[step], part)
            whole.append(part)
        return whole

    def spread_near(self, block):
        return self.flip(block, 2), self.flip(block, 4)

    def spread_far(self, by_x, by_y, half):
        return self.flip(by_y[:half], 2), self.flip(by_x[half:], 4)

    def core(self, pieces):
        return [self.flip(piece, 1) for piece in pieces]

    def in_order(self, parts):
        for axis, mask in ((4, 4), (2, 2), (1, 1)):
            odd = self.place // axis % 2 == 1
            parts = [jnp.where(odd, parts[m ^ mask], parts[m]) for m in range(8)]
        return jnp.stack(parts)

    def gather_small(self, shard, line_only=False):
        block = jnp.stack(self.gather_z(shard))
        return block if line_only else self.gather_core(self.gather_plane(block))

    def gather_plane(self, block):
        return jnp.stack([block] + [self.flip(block, m) for m in (2, 4, 6)])

    def gather_core(self, plane):
        return jnp.stack([plane, self.flip(plane, 1)]).reshape((-1,) + plane.shape[2:])


class PlainLinks:
    def __init__(self, outer, inner):
        self.outer, self.inner = outer, inner
        self.order = lax.axis_index("dp")
        self.z = lax.axis_index("fsdp")
        self.place = 0

    def gather_small(self, shard, line_only=False):
        return lax.all_gather(shard, AXES, axis=0)


def add(*terms):
    return sum(t.astype(F32) for t in terms).astype(LOW)


class Sum:
    def __init__(self, links, keep, send, slabs):
        self.links, self.keep, self.slabs = links, keep, slabs
        self.more = keep.shape[1] % 96
        self.came = links.flip(send, 1)

    def line(self, part):
        inner = self.links.inner
        count = part.shape[0] - self.more
        main = part[:count].reshape(self.slabs, inner, -1, part.shape[-1])
        main = main.transpose(1, 0, 2, 3).reshape(inner, -1, part.shape[-1])
        if not self.more:
            return main
        rows = part[count : count + inner].reshape(inner, 1, -1)
        return jnp.concatenate([main, jnp.pad(rows, ((0, 0), (0, 7), (0, 0)))], axis=1)

    def to(self, index):
        return self.line(add(self.keep[index], self.came[index]))

    def far(self):
        half = self.links.inner // 2
        to_d = self.to(3)
        self.far_came = [self.links.flip(to_d[:half], 2), self.links.flip(to_d[half:], 4)]
        return self.far_came

    def near(self):
        half = self.links.inner // 2
        came_x, came_y = self.far_came
        to_x, to_y = self.to(1), self.to(2)
        to_y = jnp.concatenate([add(to_y[:half], came_x), to_y[half:]])
        to_x = jnp.concatenate([to_x[:half], add(to_x[half:], came_y)])
        self.near_came = [self.links.flip(to_x, 2), self.links.flip(to_y, 4)]
        return self.near_came

    def direct(self):
        self.near_came = [self.links.flip(self.to(m // 2), m) for m in (2, 4, 6)]
        return self.near_came

    def turn(self, *earlier):
        links = self.links
        own = add(self.line(self.keep[0]), self.line(self.came[0]), *self.near_came)
        own = after(own, *earlier) if earlier else own
        parts = [lax.dynamic_index_in_dim(own, (links.z + k) % links.inner, 0, keepdims=False) for k in range(links.inner)]
        self.turned = [parts[0]] + [links.turn(parts[k], k) for k in range(1, links.inner)]
        return self.turned[1:]

    def total(self, *earlier):
        parts = [after(t, *earlier) for t in self.turned] if earlier else self.turned
        return sum(t.astype(F32) for t in parts)


class PlainSum:
    def __init__(self, links, keep, send, slabs):
        more = keep.shape[1] % 96
        flat = jnp.stack([keep, send], axis=1).reshape(8, -1, 768)
        main = flat[:, : flat.shape[1] - more].reshape(8, slabs, -1, 768)
        main = main.transpose(1, 0, 2, 3).reshape(slabs, -1, 768)
        self.came = keep
        self.sums = lax.psum_scatter(main, AXES, scatter_dimension=1, tiled=True).reshape(-1, 768)
        if more:
            rows = flat[:, flat.shape[1] - more :][:, : links.outer * links.inner // 8].reshape(-1, 768)
            self.sums = jnp.concatenate([self.sums, lax.psum_scatter(rows, AXES, scatter_dimension=0, tiled=True)])

    def far(self, *earlier):
        return []

    near = direct = turn = far

    def total(self, *earlier):
        return self.sums.astype(F32)


def after(value, *earlier):
    return lax.optimization_barrier((value, *earlier))[0]


def slabs_of(matrix):
    rows, wide = matrix.shape
    return matrix.reshape(rows, wide // 768, 768).transpose(1, 0, 2)


def matrix_of(slabs):
    count, rows, width = slabs.shape
    return slabs.transpose(1, 0, 2).reshape(rows, count * width)


def mix_columns(matrix, devices):
    rows, wide = matrix.shape
    matrix = matrix.reshape(rows, devices, 4, -1).transpose(0, 2, 1, 3)
    return matrix.reshape(rows, wide)


def unmix_columns(matrix, devices):
    rows, wide = matrix.shape
    matrix = matrix.reshape(rows, 4, devices, -1).transpose(0, 2, 1, 3)
    return matrix.reshape(rows, wide)


def plain_pieces(slabs, whole):
    count = slabs.shape[0]
    half = (count + 1) // 2 * 96
    parts = []
    for mask in (0, 2, 4, 6, 1, 3, 5, 7):
        part = slabs[:, mask * 96 : (mask + 1) * 96].reshape(-1, 768)
        parts += [part] if whole or mask < 6 and mask != 7 else [part[:half], part[half:]]
    return parts


def shards(
    outer,
    inner,
    tokens,
    cotangent,
    lengths,
    seg_qkv,
    seg_out,
    seg_up,
    seg_down,
    seg_vec,
    cross_qkv,
    cross_out,
    cross_up,
    cross_down,
    cross_vec,
    positions,
):
    fast = (outer, inner) == (8, 4)
    links = (Links if fast else PlainLinks)(outer, inner)
    summing = Sum if fast else PlainSum
    devices = outer * inner
    me = links.order * inner + links.z
    seq_local, seq_len, feat_dim = tokens.shape
    seg_count = seq_len // SEG
    seg_rows, cross_rows = seg_vec.shape[0], cross_vec.shape[0]
    width = feat_dim // devices
    my_lengths = lax.dynamic_slice_in_dim(lengths, me * seq_local, seq_local)
    info = jnp.concatenate([jnp.full((1,), links.place, jnp.int32), my_lengths])
    small = jnp.concatenate([seg_vec, cross_vec, positions]).reshape(1, -1)
    up_slabs = mix_columns(cross_up, devices).reshape(-1, 4, feat_dim).transpose(1, 0, 2)
    wide = [slabs_of(cross_qkv), slabs_of(cross_out), up_slabs, cross_down.reshape(4, -1, feat_dim)]
    wide = jnp.concatenate(wide)
    mid_shard = jnp.concatenate([slabs_of(seg_out), slabs_of(seg_up)])
    rows_in = tokens.reshape(-1, feat_dim)
    cot_rows = cotangent.reshape(-1, feat_dim)
    seg_starts = jnp.arange(seg_count) * SEG
    live_own = (seg_starts[None, :] < my_lengths[:, None]).reshape(-1, 1)
    up_own = jnp.where(live_own, cotangent.reshape(-1, SEG, feat_dim)[:, 0, :], 0)

    if fast:
        first = jnp.concatenate([slabs_of(seg_qkv).reshape(-1, 768), jnp.pad(small, ((0, 7), (0, 0)))])
        line_first = links.gather_z(first)
        line_mid = links.gather_z(after(mid_shard, *line_first))
        weights = jnp.stack([p[:72].reshape(3, 24, 768) for p in line_first], axis=1).reshape(-1, 768)
        rows = jnp.concatenate([p[72:73] for p in line_first])
        block = jnp.concatenate([weights, jnp.pad(rows, ((0, 12), (0, 0)))])
        near = links.spread_near(block)
        far = links.spread_far(*near, 192)
        first = [block, *near, *far, *links.core([after(p, *far, *line_mid) for p in (block, *near, *far)])]
        line_down = links.gather_z(after(seg_down, *first[5:]))
        ends = [p[288:292] for p in first[:3]] + [first[4][96:100]]
        others = [p[288:292] for p in first[5:8]] + [first[9][96:100]]
        small = links.in_order([(ends, others)[m % 2][m // 2] for m in range(8)])
        block = after(jnp.stack(line_mid, axis=1).reshape(-1, 768), *far)
        mid = [block, *links.spread_near(block)]
    else:
        first = plain_pieces(lax.all_gather(slabs_of(seg_qkv), AXES, axis=1, tiled=True), False)
        mid = plain_pieces(lax.all_gather(mid_shard, AXES, axis=1, tiled=True), False)
        down_whole = lax.all_gather(seg_down, AXES, axis=0, tiled=True)
        down = [down_whole[m * 384 : (m + 1) * 384] for m in (0, 2, 4, 6, 1, 3, 5, 7)]
        small = links.gather_small(small)
    small = small.reshape(devices, -1, width).transpose(1, 0, 2).reshape(-1, feat_dim).astype(F32)
    seg_v, cross_v = small[:seg_rows], small[seg_rows : seg_rows + cross_rows]
    pos_table = small[seg_rows + cross_rows :]
    hidden_rows = slice(5, cross_rows - 3)
    cross_v = cross_v.at[hidden_rows].set(mix_columns(cross_v[hidden_rows].reshape(1, -1), devices).reshape(-1, feat_dim))

    before = attn_forward(info, rows_in, seg_v, first, seg_count, 0)
    wide = lax.all_gather(after(wide, before[0], *((*mid[1:], *line_down) if fast else ())), AXES, axis=1, tiled=True)
    if fast:
        far = links.spread_far(*(after(p, before[0]) for p in mid[1:]), 288)
        rows_late = after(rows_in, *mid[1:])
    else:
        rows_late = rows_in
    packed, mixed = attn_forward(info, rows_late, seg_v, first, seg_count, 1, before)
    if fast:
        early = links.core([after(p, before[0]) for p in mid])
        late = links.core([after(p, packed, *far, *early) for p in far])
        mid = [*mid, *far, *early, *late]
        block = after(jnp.concatenate(line_down), *late)
        near = [links.flip(block, m) for m in (2, 4, 6)]
    summed, low, act, slope = mid_forward(info, rows_in, mixed, seg_v, mid)
    if fast:
        down = [block, *near, links.flip(block, 1), *(links.flip(after(p, act), 1) for p in near)]
    second, heads = down_forward(info, summed, act, seg_v, down)
    heads_own = heads.reshape(-1, feat_dim)
    both = links.gather_small(jnp.stack([heads_own.astype(LOW), up_own]), True)
    back = functools.partial(ffn_backward, info, seg_count=seg_count)
    args = (second, summed, slope, seg_v, mid, down)
    if fast:
        first_half = back(cot_rows, *args, half=0)
        both = links.gather_plane(after(both, first_half[1]))
        *arrays, grads_two = back(after(cot_rows, first_half[1]), *args, half=1, before=first_half[:5])
        both = links.gather_core(after(both, arrays[1]))
    live_all = seg_starts[None, :] < lengths[:, None]
    if fast:
        cross_info = jnp.concatenate([jnp.stack([links.place, me, links.z]).astype(jnp.int32), my_lengths])
        live = links.in_order(list(live_all.reshape(outer, -1))).reshape(4, 2, -1).transpose(1, 0, 2)
        live = jnp.broadcast_to(live.reshape(-1, 1), (live_all.size, SEG)).astype(F32)
        (vec_grad, pos_grad, *cross_grads), grads_more, arrays = cross_whole(
            cross_info, both, live, cross_v, pos_table, wide,
            seg_v, arrays, (second, summed, slope), mid, down, seg_count,
        )
    else:
        weights = (matrix_of(wide[:3]), wide[3], matrix_of(wide[4:8]), wide[8:].reshape(-1, feat_dim), cross_v)
        heads_all, up_all = both[:, 0].reshape(-1, feat_dim), both[:, 1].reshape(-1, feat_dim)
        heads_in = heads_all.astype(F32).reshape(-1, seg_count, feat_dim) + pos_table[None]
        heads_in = heads_in.reshape(-1, feat_dim)
        cross_result, kept = encode(heads_in, heads_in.astype(LOW), weights, live_all)
        all_grad, pairs, vec_grad = encode_back(
            up_all.astype(F32), heads_in.astype(LOW), weights, live_all, kept
        )
        cross_grads = []
        for left, right in pairs:
            left = left.reshape(left.shape[0], -1, feat_dim)
            mine = lax.dynamic_slice_in_dim(left, me * width, width, 2)
            cross_grads.append(trans_left(mine.reshape(left.shape[0], -1), right))
        pos_grad = jnp.sum(all_grad.reshape(-1, seg_count, feat_dim), axis=0)
        own = seq_local * seg_count
        cross_own = lax.dynamic_slice_in_dim(cross_result, me * own, own)
        heads_grad = lax.dynamic_slice_in_dim(all_grad, me * own, own)
        first_half = back(after(cot_rows, heads_grad, *cross_grads), *args, half=0)
        *arrays, grads_two = back(cot_rows, *args, half=1, before=first_half[:5])
        arrays, grads_more = opening_backward(
            info, cross_own, heads_grad, seg_v, arrays, (second, summed, slope), mid, down, seg_count
        )
    layer_out, down_grad, hidden_grad, proj_grad, mixed_grad = arrays
    grads_two = grads_two + first_half[5] + grads_more
    down_sum = summing(links, *down_weight_grad(info, act, down_grad), 1)
    mid_parts = mid_weight_grad(info, mixed, proj_grad, low, after(hidden_grad, down_sum.keep if fast else down_sum.came))
    mid_sum = summing(links, *mid_parts, 5)
    half_grad, grads_one = attn_backward(
        info, packed, after(mixed_grad, mid_parts[1], down_sum.came), seg_count, 0
    )
    ready = after(mixed_grad, half_grad, *down_sum.far(), mid_sum.came)
    packed_grad, grads_more = attn_backward(info, packed, ready, seg_count, 1, half_grad)
    vec_parts = jnp.concatenate([grads_one + grads_more, grads_two[2:]]).reshape(seg_rows, devices, width)
    vec_parts = vec_parts.transpose(1, 0, 2).reshape(outer, inner, seg_rows * width).astype(LOW)
    if outer > 8:
        vec_parts = vec_parts.reshape(8, -1, seg_rows * width)
    vec_parts = jnp.pad(vec_parts, ((0, 0), (0, 16 - vec_parts.shape[1]), (0, feat_dim - seg_rows * width)))
    ready = after(packed_grad, *down_sum.near(), *mid_sum.far())
    keep, send = qkv_weight_grad(info, rows_in, ready, vec_parts)
    qkv_sum = summing(links, keep, after(send, *down_sum.turn(), *mid_sum.near()), 3)
    ready = after(packed_grad, qkv_sum.came)
    token_grad = token_gradient(info, ready, proj_grad, first)
    qkv_sum.direct()
    mid_sum.turn()
    qkv_sum.turn(token_grad)
    cross_grads[2] = unmix_columns(after(cross_grads[2], token_grad), devices)
    vec_grad = vec_grad.at[hidden_rows].set(
        unmix_columns(after(vec_grad[hidden_rows], token_grad).reshape(1, -1), devices).reshape(-1, feat_dim)
    )
    cross_vec_grad = lax.dynamic_slice_in_dim(vec_grad, me * width, width, 1)
    grad_positions = lax.dynamic_slice_in_dim(pos_grad, me * width, width, 1)
    grad_down = down_sum.total()
    grad_mid = mid_sum.total().reshape(5, -1, feat_dim)
    total = qkv_sum.total(cross_grads[2], cross_vec_grad)
    grad_qkv = matrix_of(total[: 3 * width].reshape(3, -1, feat_dim))
    grad_vec = total[3 * width, : seg_rows * width].reshape(seg_rows, width)
    return (
        layer_out.reshape(tokens.shape),
        token_grad.reshape(tokens.shape),
        grad_qkv,
        grad_mid[0],
        matrix_of(grad_mid[1:]),
        grad_down,
        grad_vec,
        *cross_grads,
        cross_vec_grad,
        grad_positions,
    )


def solution(mesh):
    in_specs = (
        P(("dp", "fsdp"), None, None),
        P(("dp", "fsdp"), None, None),
        P(),
        P(("dp", "fsdp"), None),
        P(("dp", "fsdp"), None),
        P(("dp", "fsdp"), None),
        P(("dp", "fsdp"), None),
        P(None, ("dp", "fsdp")),
        P(("dp", "fsdp"), None),
        P(("dp", "fsdp"), None),
        P(("dp", "fsdp"), None),
        P(("dp", "fsdp"), None),
        P(None, ("dp", "fsdp")),
        P(None, ("dp", "fsdp")),
    )
    out_specs = (
        P(("dp", "fsdp"), None, None),
        P(("dp", "fsdp"), None, None),
        P(("dp", "fsdp"), None),
        P(("dp", "fsdp"), None),
        P(("dp", "fsdp"), None),
        P(("dp", "fsdp"), None),
        P(None, ("dp", "fsdp")),
        P(("dp", "fsdp"), None),
        P(("dp", "fsdp"), None),
        P(("dp", "fsdp"), None),
        P(("dp", "fsdp"), None),
        P(None, ("dp", "fsdp")),
        P(None, ("dp", "fsdp")),
    )
    return jax.shard_map(
        functools.partial(shards, mesh.shape["dp"], mesh.shape["fsdp"]),
        mesh=mesh, in_specs=in_specs, out_specs=out_specs, check_vma=False)
```

```python
import functools

import jax
import jax.numpy as jnp
from jax import lax
from jax.experimental import pallas as pl
from jax.experimental.pallas import tpu as pltpu
from jax.sharding import PartitionSpec as P

HEAD = 64
SEG = 128
NORM_EPS = 1e-05
MASK_FILL = -1000000000.0
VMEM = 60 * 2**20
F32, LOW = jnp.float32, jnp.bfloat16


ROOT_HALF = 0.7071067811865476
INV_ROOT_TAU = 0.3989422804014327
AXES = ("dp", "fsdp")

def mm(left_op, right_op):
    return jnp.dot(left_op, right_op, preferred_element_type=F32)


def mm_nt(left_op, right_op):
    return lax.dot_general(left_op, right_op, (((1,), (1,)), ((), ())), preferred_element_type=F32)


def mm_tn(left_op, right_op):
    return lax.dot_general(left_op, right_op, (((0,), (0,)), ((), ())), preferred_element_type=F32)


def normalize(summed):
    average = jnp.mean(summed, axis=-1, keepdims=True)
    centered = summed - average
    inv_scale = lax.rsqrt(jnp.mean(centered * centered, axis=-1, keepdims=True) + NORM_EPS)
    return centered * inv_scale, inv_scale


def normalize_back(inner, normed, inv_scale):
    return inv_scale * (
        inner
        - jnp.mean(inner, axis=-1, keepdims=True)
        - normed * jnp.mean(inner * normed, axis=-1, keepdims=True)
    )


def gelu_parts(hidden):
    phi = 0.5 * (1.0 + lax.erf(hidden * ROOT_HALF))
    return hidden * phi, phi + hidden * jnp.exp(-0.5 * hidden * hidden) * INV_ROOT_TAU


def pair_stack(pair, low_half):
    zero = jnp.zeros_like(pair)
    return jnp.concatenate(
        [jnp.where(low_half, pair, zero), jnp.where(low_half, zero, pair)], axis=0
    )


def pair_merge(stacked, low_half):
    rows = stacked.shape[0] // 2
    return jnp.where(low_half, stacked[:rows], stacked[rows:])


def pair_probs(stack, keys, allowed):
    scores = jnp.where(allowed, mm_nt(keys, stack), MASK_FILL)
    expo = jnp.exp(scores - jnp.max(scores, axis=0, keepdims=True))
    return expo * (1.0 / jnp.sum(expo, axis=0, keepdims=True))


def attend(query, keys, values, allowed):
    low_half = lax.broadcasted_iota(jnp.int32, query.shape, 1) < HEAD
    stack = pair_stack(query * jnp.asarray(HEAD**-0.5, query.dtype), low_half)
    return pair_merge(mm_tn(pair_probs(stack, keys, allowed).astype(LOW), values), low_half)


def attend_back(query, keys, values, grad_mixed, allowed):
    low_half = lax.broadcasted_iota(jnp.int32, query.shape, 1) < HEAD
    stack = pair_stack(query * jnp.asarray(HEAD**-0.5, query.dtype), low_half)
    probs = pair_probs(stack, keys, allowed)
    grad_stack = pair_stack(grad_mixed, low_half)
    grad_prob = mm_nt(values, grad_stack)
    inner = jnp.sum(probs * grad_prob, axis=0, keepdims=True)
    score_grad = (probs * (grad_prob - inner)).astype(LOW)
    grad_query = pair_merge(mm_tn(score_grad, keys), low_half) * HEAD**-0.5
    return grad_query, mm(score_grad, stack), mm(probs.astype(LOW), grad_stack)


def slab_copies(place, pieces, slabs, sems, first_sem=0, by_slab=False):
    count = len(slabs)
    half = (count + 1) // 2
    spans = [(0, 0, count), (2, 0, count), (4, 0, count)]
    spans += [(6, 0, count)] if len(pieces) == 8 else [(6, 0, half), (6, half, count)]
    copies = [[] for _ in slabs]
    for flip_c in (0, 1):
        for index, (flip_yx, first, last) in enumerate(spans):
            block = place ^ (flip_yx + flip_c)
            piece = pieces[flip_c * len(spans) + index]
            for slab in range(first, last):
                source = piece.at[pl.ds((slab - first) * 96, 96)]
                sem = sems.at[first_sem + slab * 8 + flip_yx + flip_c]
                copies[slab].append(pltpu.make_async_copy(source, slabs[slab](block), sem))
    return copies if by_slab else sum(copies, [])


def load(copies):
    for copy in copies:
        copy.start()
    for copy in copies:
        copy.wait()


def never(*names):
    pass


def staged(groups):
    for copies in groups.values():
        for copy in copies:
            copy.start()

    def wait(*names):
        for name in names:
            for copy in groups[name]:
                copy.wait()

    return wait


def rows_of(ref, block, rows=96, slab=None):
    where = pl.ds(pl.multiple_of(block * rows, rows), rows)
    return ref.at[where] if slab is None else ref.at[slab, where]


def down_rows(ref, block, part):
    return ref.at[pl.ds(pl.multiple_of(block * 384 + part * 96, 96), 96)]


def qkv_slabs(qkv):
    return [functools.partial(rows_of, qkv, slab=j) for j in range(3)]


def piece_copies(place, pieces, target, sems, first_sem=0):
    whole = len(pieces) == 8
    copies = []
    for index, piece in enumerate(pieces):
        side, part = divmod(index, len(pieces) // 2)
        block = place ^ (min(part, 3) * 2 + side)
        if whole:
            where = target.at[pl.ds(pl.multiple_of(block * 384, 384), 384)]
        else:
            count, slabs = piece.shape[0], target.shape[0]
            first = slabs - count if part == 4 else 0
            where = target.at[first : first + count, pl.ds(pl.multiple_of(block * 96, 96), 96)]
        copies.append(pltpu.make_async_copy(piece, where, sems.at[first_sem + index]))
    return copies


def segment_mask(length, seg_in_seq):
    row = lax.broadcasted_iota(jnp.int32, (SEG, 2 * SEG), 0)
    return (row + seg_in_seq * SEG < length) | (row == 0)


def attn_forward_kernel(segs, seg_count, first_step, info, x_ref, vec_ref, *rest):
    pieces, (packed_ref, mixed_ref, qkv, sems) = rest[:10], rest[-4:]
    step = pl.program_id(0)

    @pl.when(step == 0)
    def _():
        load(slab_copies(info[0], pieces, qkv_slabs(qkv), sems))

    rows = x_ref[...]
    for j in range(3):
        part = mm(rows, qkv[j])
        if j != 1:
            part = part + vec_ref[j // 2 : j // 2 + 1, :]
        packed_ref[:, j * 768 : (j + 1) * 768] = part.astype(LOW)
    for s in range(segs):
        seg = (step + first_step) * segs + s
        allowed = segment_mask(info[1 + seg // seg_count], seg % seg_count)
        at = slice(s * SEG, (s + 1) * SEG)
        for h in range(6):
            q, k, v = (packed_ref[at, j * 768 + h * 128 : j * 768 + (h + 1) * 128] for j in range(3))
            mixed_ref[at, h * 128 : (h + 1) * 128] = attend(q, k, v, allowed).astype(LOW)


def norm_one(summed, vec_ref):
    normed, _ = normalize(summed)
    return normed * (1.0 + vec_ref[3:4, :]) + vec_ref[4:5, :]


def mid_forward_kernel(info, x_ref, mixed_ref, vec_ref, *rest):
    pieces, (sum_ref, low_ref, act_ref, slope_ref, weights, sems) = rest[:10], rest[10:]
    out, up = weights.at[0], weights.at[1:5]
    step = pl.program_id(0)

    def body(wait):
        wait("mid")
        summed = x_ref[...].astype(F32) + mm(mixed_ref[...], out[...]) + vec_ref[2:3, :]
        sum_ref[...] = summed
        first_low = norm_one(summed, vec_ref).astype(LOW)
        low_ref[...] = first_low
        hidden = mm(first_low, up[0]) + vec_ref[5:6, :]
        for j in range(4):
            if j < 3:
                later = mm(first_low, up[j + 1]) + vec_ref[6 + j : 7 + j, :]
            act, slope = gelu_parts(hidden)
            act_ref[:, j * 768 : (j + 1) * 768] = act.astype(LOW)
            slope_ref[:, j * 768 : (j + 1) * 768] = slope.astype(LOW)
            hidden = later

    @pl.when(step == 0)
    def _():
        body(staged({"mid": piece_copies(info[0], pieces, weights, sems)}))

    @pl.when(step > 0)
    def _():
        body(never)


def down_forward_kernel(segs, info, sum_ref, act_ref, vec_ref, *rest):
    pieces, (second_ref, heads_ref, down, sems) = rest[:8], rest[8:]

    @pl.when(pl.program_id(0) == 0)
    def _():
        load(piece_copies(info[0], pieces, down, sems))

    total = norm_one(sum_ref[...], vec_ref) + vec_ref[9:10, :] + mm(act_ref[...], down[...])
    second_ref[...] = total
    opening = jnp.concatenate([total[s * SEG : s * SEG + 1] for s in range(segs)], axis=0)
    normed, _ = normalize(opening)
    heads_ref[...] = normed * (1.0 + vec_ref[10:11, :]) + vec_ref[11:12, :]


def cross_kernel(blocks, segs, seg_count, info, both_ref, live_ref, vec_ref, pos_ref, seg_vec_ref, *rest):
    wide, tops_in, sources, mid, more, rest = rest[0], rest[1:6], rest[6:9], rest[9:19], rest[19:27], rest[27:]
    grads_ref, pos_grad_ref, qkv_grad_ref, out_grad_ref, up_grad_ref, down_grad_ref, seg_grads_ref, *tops_out = rest[:12]
    (qkv, middle, down, sems, result, heads_grad, slope, lefts, act, packed, rights, hidden_grad) = rest[12:24]
    out, up = middle.at[0], middle.at[1:5]
    tops, parts, own_hidden, weights, (seg_sems, top_sems) = rest[24:29], rest[29:32], rest[32], rest[33:35], rest[35:]
    step = pl.program_id(0)
    count = live_ref.shape[0]
    at = pl.ds(pl.multiple_of(step * count, count), count)
    targets = [qkv.at[j] for j in range(3)] + [middle.at[j] for j in range(5)]
    targets += [down.at[j * 768 : (j + 1) * 768] for j in range(4)]
    copies = [pltpu.make_async_copy(wide.at[j], t, sems.at[j]) for j, t in enumerate(targets)]

    @pl.when(step == 0)
    def _():
        for copy in copies:
            copy.start()
        staged(opening_groups(info[0], tops_in, sources, mid, more, tops, parts, weights, seg_sems, top_sems))
        grads_ref[...] = jnp.zeros_like(grads_ref)
        pos_grad_ref[...] = jnp.zeros_like(pos_grad_ref)
        for copy in copies[:3]:
            copy.wait()

    vec = vec_ref[...]
    inputs = both_ref[:, 0].reshape(count, 768).astype(F32).reshape(-1, 8, 768) + pos_ref[...][None]
    inputs = inputs.reshape(count, 768)
    low = inputs.astype(LOW)
    lefts[0, at, :] = low
    for j in range(3):
        part = mm(low, qkv[j])
        if j != 1:
            part = part + vec[j // 2 : j // 2 + 1]
        packed[:, j * 768 : (j + 1) * 768] = part.astype(LOW)
    row = lax.broadcasted_iota(jnp.int32, (SEG, 2 * SEG), 0)
    lane = lax.broadcasted_iota(jnp.int32, (SEG, 2 * SEG), 1)
    group = row // 8 == lane % SEG // 8
    masks = []
    for s in range(count // SEG):
        live = live_ref[s * SEG : (s + 1) * SEG, :]
        masks.append(group & (jnp.concatenate([live, live], axis=1) > 0.0))
    for s, allowed in enumerate(masks):
        part = slice(s * SEG, (s + 1) * SEG)
        for h in range(6):
            q, k, v = (packed[part, j * 768 + h * 128 : j * 768 + (h + 1) * 128] for j in range(3))
            where = pl.ds(pl.multiple_of(step * count + s * SEG, SEG), SEG)
            lefts[1, where, h * 128 : (h + 1) * 128] = attend(q, k, v, allowed).astype(LOW)

    @pl.when(step == 0)
    def _():
        for copy in copies[3:]:
            copy.wait()

    summed = inputs + mm(lefts[1, at, :], out[...]) + vec[2:3]
    normed_one, scale_one = normalize(summed)
    first = normed_one * (1.0 + vec[3:4]) + vec[4:5]
    first_low = first.astype(LOW)
    lefts[2, at, :] = first_low
    total = first + vec[9:10]
    for j in range(4):
        cols = slice(j * 768, (j + 1) * 768)
        hidden = mm(first_low, up[j]) + vec[5 + j : 6 + j]
        active, steep = gelu_parts(hidden)
        act[at, cols] = active.astype(LOW)
        slope[:, cols] = steep.astype(LOW)
        total = total + mm(active.astype(LOW), down[cols, :])
    normed, inv_scale = normalize(total)
    result[at, :] = normed * (1.0 + vec[10:11]) + vec[11:12]
    upstream = both_ref[:, 1].reshape(count, 768).astype(F32)
    back_two = normalize_back(upstream * (1.0 + vec[10:11]), normed, inv_scale)
    down_grad = back_two.astype(LOW)
    rights[1, at, :] = down_grad
    grads_ref[9:10, :] += column_sum(down_grad)
    grads_ref[10:11, :] += column_sum(upstream * normed)
    grads_ref[11:12, :] += column_sum(upstream)
    total = back_two
    for j in range(4):
        cols = slice(j * 768, (j + 1) * 768)
        grad = (mm_nt(down_grad, down[cols, :]) * slope[:, cols].astype(F32)).astype(LOW)
        hidden_grad[at, cols] = grad
        grads_ref[5 + j : 6 + j, :] += column_sum(grad)
        total = total + mm_nt(grad, up[j])
    back_one = normalize_back(total * (1.0 + vec[3:4]), normed_one, scale_one)
    proj_grad = back_one.astype(LOW)
    rights[0, at, :] = proj_grad
    grads_ref[2:3, :] += column_sum(proj_grad)
    grads_ref[3:4, :] += column_sum(total * normed_one)
    grads_ref[4:5, :] += column_sum(total)
    mixed_grad = mm_nt(proj_grad, out[...]).astype(LOW)
    for s, allowed in enumerate(masks):
        part = slice(s * SEG, (s + 1) * SEG)
        where = pl.ds(pl.multiple_of(step * count + s * SEG, SEG), SEG)
        for h in range(6):
            cols = slice(h * 128, (h + 1) * 128)
            q, k, v = (packed[part, j * 768 + h * 128 : j * 768 + (h + 1) * 128] for j in range(3))
            for j, g in enumerate(attend_back(q, k, v, mixed_grad[part, cols], allowed)):
                rights[2 + j, where, cols] = g.astype(LOW)
    total = back_one
    for j in range(3):
        part = rights[2 + j, at, :]
        total = total + mm_nt(part, qkv[j])
        if j != 1:
            grads_ref[j // 2 : j // 2 + 1, :] += column_sum(part)
    heads_grad[at, :] = total
    pos_grad_ref[...] += jnp.sum(total.reshape(-1, 8, 768), axis=0)

    @pl.when(step == blocks - 1)
    def _():
        me = info[1]
        own = pl.ds(pl.multiple_of(info[2] * 16, 16), 16)
        groups = opening_groups(info[0], tops_in, sources, mid, more, tops, parts, weights, seg_sems, top_sems)

        def wait(*names):
            for name in names:
                for copy in groups[name]:
                    copy.wait()

        lengths = [info[3 + i] for i in range(segs // seg_count)]
        opening_rows(segs, seg_count, lengths, result[own, :], heads_grad[own, :], seg_vec_ref, tops_out,
                     seg_grads_ref, tops, parts, own_hidden, weights, top_sems, wait)

        def chosen(left, rows):
            width = left.shape[1]
            wanted = lax.broadcasted_iota(jnp.int32, (rows, width), 1) - lax.broadcasted_iota(
                jnp.int32, (rows, width), 0
            )
            pick = (wanted == me * rows).astype(F32).astype(LOW)
            return mm_nt(pick, left).astype(LOW)

        left = chosen(lefts[0], 24)
        for j in range(3):
            qkv_grad_ref[:, j * 768 : (j + 1) * 768] = mm(left, rights[2 + j])
        out_grad_ref[...] = mm(chosen(lefts[1], 24), rights[0])
        left = chosen(lefts[2], 24)
        for j in range(4):
            cols = slice(j * 768, (j + 1) * 768)
            up_grad_ref[:, cols] = mm(left, hidden_grad[:, cols])
        for j in range(4):
            left = chosen(act[:, j * 768 : (j + 1) * 768], 24)
            down_grad_ref[j * 24 : (j + 1) * 24, :] = mm(left, rights[1])


def column_sum(value):
    return jnp.sum(value.astype(F32), axis=0, keepdims=True)


def ffn_back_rows(upstream, second, summed, slope, vec, grads_ref, hidden_grad, weights, down, wait):
    normed, inv_scale = normalize(second)
    back_two = normalize_back(upstream * (1.0 + vec[10:11, :]), normed, inv_scale)
    down_grad = back_two.astype(LOW)
    grads_ref[9:10, :] += column_sum(down_grad)
    grads_ref[10:11, :] += column_sum(upstream * normed)
    grads_ref[11:12, :] += column_sum(upstream)
    total = back_two
    out, up = weights.at[0], weights.at[1:5]
    wait("down", "mid")
    for j in range(4):
        cols = slice(j * 768, (j + 1) * 768)
        grad = (mm_nt(down_grad, down[cols, :]) * slope(cols).astype(F32)).astype(LOW)
        hidden_grad(cols, grad)
        grads_ref[5 + j : 6 + j, :] += column_sum(grad)
        total = total + mm_nt(grad, up[j])
    normed, inv_scale = normalize(summed)
    back_one = normalize_back(total * (1.0 + vec[3:4, :]), normed, inv_scale)
    proj_grad = back_one.astype(LOW)
    grads_ref[2:3, :] += column_sum(proj_grad)
    grads_ref[3:4, :] += column_sum(total * normed)
    grads_ref[4:5, :] += column_sum(total)
    return down_grad, proj_grad, mm_nt(proj_grad, out[...]).astype(LOW)


def ffn_groups(place, mid, rest, weights, down, sems):
    return {"down": piece_copies(place, rest, down, sems, 10), "mid": piece_copies(place, mid, weights, sems)}


def ffn_backward_kernel(segs, seg_count, first_step, info, cot_ref, second_ref, sum_ref, slope_ref, vec_ref, *rest):
    mid, more, rest = rest[:10], rest[10:18], rest[-9:]
    out_ref, down_grad_ref, hidden_grad_ref, proj_grad_ref, mixed_grad_ref, grads_ref, weights, down, sems = rest
    step = pl.program_id(0)

    def body(wait):
        second = second_ref[...]
        normed, _ = normalize(second)
        result = normed * (1.0 + vec_ref[10:11, :]) + vec_ref[11:12, :]
        row = lax.broadcasted_iota(jnp.int32, (SEG, 1), 0)
        ups = []
        for s in range(segs):
            seg = (step + first_step) * segs + s
            at = slice(s * SEG, (s + 1) * SEG)
            live = row + seg % seg_count * SEG < info[1 + seg // seg_count]
            out_ref[at, :] = jnp.where(live, result[at], 0.0).astype(LOW)
            ups.append(jnp.where(live & (row > 0), cot_ref[at, :].astype(F32), 0.0))

        def store(cols, grad):
            hidden_grad_ref[:, cols] = grad

        down_grad_ref[...], proj_grad_ref[...], mixed_grad_ref[...] = ffn_back_rows(
            jnp.concatenate(ups, axis=0), second, sum_ref[...], lambda cols: slope_ref[:, cols], vec_ref, grads_ref,
            store, weights, down, wait,
        )

    @pl.when(step == 0)
    def _():
        wait = staged(ffn_groups(info[0], mid, more, weights, down, sems))
        grads_ref[...] = jnp.zeros_like(grads_ref)
        body(wait)

    @pl.when(step > 0)
    def _():
        body(never)


def opening_groups(place, tops_in, sources, mid, more, tops, parts, weights, sems, top_sems):
    pairs = zip((*tops_in, *sources), (*tops, *parts))
    copies = [
        pltpu.make_async_copy(source.at[:, 0 : target.shape[1], :], target, top_sems.at[i])
        for i, (source, target) in enumerate(pairs)
    ]
    return {"tops": copies, **ffn_groups(place, mid, more, *weights, sems)}


def opening_rows(segs, seg_count, lengths, heads, heads_grad, vec_ref, tops_out, grads_ref, tops, parts, hidden, weights, top_sems, wait):
    wait("tops")
    grads_ref[...] = jnp.zeros_like(grads_ref)
    second, summed = parts[0][:, 0, :], parts[1][:, 0, :]
    slope = parts[2][...].astype(F32)[:, 0, :]

    def store(cols, grad):
        hidden[:, cols] = grad.astype(F32)

    down_grad, proj_grad, mixed_grad = ffn_back_rows(
        heads_grad, second, summed, lambda cols: slope[:, cols], vec_ref, grads_ref, store, *weights, wait
    )
    seg = lax.broadcasted_iota(jnp.int32, (segs, 1), 0)
    length = jnp.full((segs, 1), lengths[0], jnp.int32)
    for i in range(1, len(lengths)):
        length = jnp.where(seg >= i * seg_count, lengths[i], length)
    merged = jnp.where(lax.rem(seg, seg_count) * SEG < length, heads, 0.0)
    outs = []
    values = (merged, down_grad.astype(F32), hidden[...], proj_grad.astype(F32), mixed_grad.astype(F32))
    for i, (value, top) in enumerate(zip(values, tops)):
        row = lax.broadcasted_iota(jnp.int32, top.shape, 1)
        top[...] = jnp.where(row == 0, value[:, None, :], top[...].astype(F32)).astype(LOW)
        outs.append(pltpu.make_async_copy(top, tops_out[i].at[:, 0:16, :], top_sems.at[i]))
    load(outs)


def opening_kernel(segs, seg_count, info, heads_ref, heads_grad_ref, vec_ref, *rest):
    tops_in, sources, mid, more, rest = rest[:5], rest[5:8], rest[8:18], rest[18:26], rest[26:]
    tops_out, grads_ref, tops, parts, hidden = rest[:5], rest[5], rest[6:11], rest[11:14], rest[14]
    *weights, sems, top_sems = rest[15:]
    wait = staged(opening_groups(info[0], tops_in, sources, mid, more, tops, parts, weights, sems, top_sems))
    lengths = [info[1 + i] for i in range(segs // seg_count)]
    opening_rows(segs, seg_count, lengths, heads_ref[...], heads_grad_ref[...], vec_ref, tops_out, grads_ref, tops,
                 parts, hidden, weights, top_sems, wait)


def attn_backward_kernel(segs, seg_count, first_step, info, packed_ref, mixed_grad_ref, *rest):
    packed_grad_ref, grads_ref = rest[-2:]
    step = pl.program_id(0)

    @pl.when(step == 0)
    def _():
        grads_ref[...] = jnp.zeros_like(grads_ref)

    for s in range(segs):
        seg = (step + first_step) * segs + s
        allowed = segment_mask(info[1 + seg // seg_count], seg % seg_count)
        at = slice(s * SEG, (s + 1) * SEG)
        for h in range(6):
            cols = [slice(j * 768 + h * 128, j * 768 + (h + 1) * 128) for j in range(3)]
            q, k, v = (packed_ref[at, c] for c in cols)
            grads = attend_back(q, k, v, mixed_grad_ref[at, cols[0]], allowed)
            for c, g in zip(cols, grads):
                packed_grad_ref[at, c] = g.astype(LOW)
    grads_ref[0:1, :] += column_sum(packed_grad_ref[:, :768])
    grads_ref[1:2, :] += column_sum(packed_grad_ref[:, 1536:])


def token_grad_kernel(info, packed_grad_ref, proj_grad_ref, *rest):
    pieces, (token_grad_ref, qkv, sems) = rest[:10], rest[10:]

    @pl.when(pl.program_id(0) == 0)
    def _():
        load(slab_copies(info[0], pieces, qkv_slabs(qkv), sems))

    total = proj_grad_ref[...].astype(F32)
    for j in range(3):
        total = total + mm_nt(packed_grad_ref[:, j * 768 : (j + 1) * 768], qkv[j])
    token_grad_ref[...] = total.astype(LOW)


def send_slab(place, total, keep_ref, send_ref, rows):
    for mask in range(8):
        block = pl.multiple_of((place ^ mask) * rows, rows)
        target = send_ref if mask % 2 else keep_ref
        target[mask // 2] = total[pl.ds(block, rows), :].astype(LOW)


def qkv_grad_kernel(info, left_ref, right_ref, more_ref, keep_ref, send_ref, total):
    step = pl.program_id(0)
    total[...] = mm_tn(left_ref[...], right_ref[...])
    at = pl.ds(pl.multiple_of(step * 96, 96), 96)
    for mask in range(8):
        block = pl.multiple_of((info[0] ^ mask) * 96, 96)
        target = send_ref if mask % 2 else keep_ref
        target[mask // 2, at, :] = total[pl.ds(block, 96), :].astype(LOW)

    @pl.when(step == 0)
    def _():
        for mask in range(8):
            target = send_ref if mask % 2 else keep_ref
            target[mask // 2, 288:304, :] = more_ref[info[0] ^ mask]


def mid_grad_kernel(info, mixed_ref, proj_ref, low_ref, hidden_ref, keep_ref, send_ref, total):
    @pl.when(pl.program_id(0) == 0)
    def _():
        total[...] = mm_tn(mixed_ref[...], proj_ref[...])

    @pl.when(pl.program_id(0) > 0)
    def _():
        total[...] = mm_tn(low_ref[...], hidden_ref[...])

    send_slab(info[0], total, keep_ref, send_ref, 96)


ANY = pl.BlockSpec(memory_space=pl.ANY)
SMEM = pl.BlockSpec(memory_space=pltpu.SMEM)


def block_rows(count, width):
    return pl.BlockSpec((count, width), lambda i: (i, 0))


def fixed(shape):
    return pl.BlockSpec(shape, lambda i: (0,) * len(shape))


def shape_of(dims, kind=LOW):
    return jax.ShapeDtypeStruct(dims, kind)


def params():
    return pltpu.CompilerParams(vmem_limit_bytes=VMEM, dimension_semantics=("arbitrary",))


def cost(flops, size):
    return pl.CostEstimate(flops=flops, bytes_accessed=size, transcendentals=0)


QKV = [pltpu.VMEM((3, 768, 768), LOW)]
MID = [pltpu.VMEM((5, 768, 768), LOW)]
DOWN = [pltpu.VMEM((3072, 768), LOW)]


def sems(count):
    return [pltpu.SemaphoreType.DMA((count,))]


def tall_pieces(pieces):
    return [p.reshape(-1, 96, 768) for p in pieces]


def shifted(count, width, first):
    return pl.BlockSpec((count, width), lambda i: (i + first, 0))


def attn_forward(info, rows_in, vec, pieces, seg_count, half, before=None, segs=4):
    rows = rows_in.shape[0]
    count = segs * SEG
    steps = rows // count // 2
    first = half * steps
    before = list(before or [])
    return pl.pallas_call(
        functools.partial(attn_forward_kernel, segs, seg_count, first),
        grid=(steps,),
        in_specs=[SMEM, shifted(count, 768, first), fixed((12, 768))] + [ANY] * (10 + len(before)),
        out_specs=[shifted(count, 2304, first), shifted(count, 768, first)],
        out_shape=[shape_of((rows, 2304)), shape_of((rows, 768))],
        scratch_shapes=QKV + sems(24),
        input_output_aliases={13: 0, 14: 1} if before else {},
        compiler_params=params(),
        cost_estimate=cost(rows * 768 * 8000, rows * 768 * 8),
        name="attn_forward",
    )(info, rows_in, vec, *pieces, *before)


def mid_forward(info, rows_in, mixed, vec, pieces, segs=2):
    rows = rows_in.shape[0]
    count = segs * SEG
    return pl.pallas_call(
        mid_forward_kernel,
        grid=(rows // count,),
        in_specs=[SMEM, block_rows(count, 768), block_rows(count, 768), fixed((12, 768))] + [ANY] * 10,
        out_specs=[block_rows(count, 768), block_rows(count, 768), block_rows(count, 3072), block_rows(count, 3072)],
        out_shape=[shape_of((rows, 768), F32), shape_of((rows, 768)), shape_of((rows, 3072)), shape_of((rows, 3072))],
        scratch_shapes=MID + sems(40),
        compiler_params=params(),
        cost_estimate=cost(2 * rows * 768 * 8000, rows * 768 * 30),
        name="mid_forward",
    )(info, rows_in, mixed, vec, *tall_pieces(pieces))


def down_forward(info, summed, act, vec, pieces, segs=2):
    rows = summed.shape[0]
    count = segs * SEG
    few = pl.BlockSpec((None, segs, 768), lambda i: (i, 0, 0))
    return pl.pallas_call(
        functools.partial(down_forward_kernel, segs),
        grid=(rows // count,),
        in_specs=[SMEM, block_rows(count, 768), block_rows(count, 3072), fixed((12, 768))] + [ANY] * 8,
        out_specs=[block_rows(count, 768), few],
        out_shape=[shape_of((rows, 768), F32), shape_of((rows // count, segs, 768), F32)],
        scratch_shapes=DOWN + sems(32),
        compiler_params=params(),
        cost_estimate=cost(2 * rows * 768 * 4000, rows * 768 * 16),
        name="down_forward",
    )(info, summed, act, vec, *pieces)


def grouped(array):
    return array.reshape(-1, SEG, array.shape[1])


def top_scratch(segs, arrays):
    tops = [pltpu.VMEM((segs, 16, a.shape[2]), LOW) for a in arrays]
    parts = [pltpu.VMEM((segs, 8, 768), F32)] * 2 + [pltpu.VMEM((segs, 16, 3072), LOW)]
    return tops + parts + [pltpu.VMEM((segs, 3072), F32)] + MID + DOWN + sems(72) + sems(8)


def cross_whole(info, both, live, vec, positions, wide, seg_vec, arrays, sources, mid, more, seg_count):
    rows = live.shape[0]
    count = 2 * SEG
    pair = pl.BlockSpec((count // 16, 2, 16, 768), lambda i: (i, 0, 0, 0))
    arrays, sources = [grouped(a) for a in arrays], [grouped(a) for a in sources]
    segs = arrays[0].shape[0]
    own = [(12, 768), (8, 768), (24, 2304), (24, 768), (24, 3072), (96, 768), (12, 768)]
    *grads, seg_grads, layer, down, hidden, proj, mixed = pl.pallas_call(
        functools.partial(cross_kernel, rows // count, segs, seg_count),
        grid=(rows // count,),
        in_specs=[SMEM, pair, block_rows(count, SEG), fixed((12, 768)), fixed((8, 768)), fixed((12, 768))] + [ANY] * 27,
        out_specs=[fixed(dims) for dims in own] + [ANY] * 5,
        out_shape=[shape_of(dims, F32) for dims in own] + [shape_of(a.shape) for a in arrays],
        scratch_shapes=QKV + MID + DOWN + sems(12) + [
            pltpu.VMEM((rows, 768), F32), pltpu.VMEM((rows, 768), F32), pltpu.VMEM((count, 3072), LOW),
            pltpu.VMEM((3, rows, 768), LOW), pltpu.VMEM((rows, 3072), LOW), pltpu.VMEM((count, 2304), LOW),
            pltpu.VMEM((5, rows, 768), LOW), pltpu.VMEM((rows, 3072), LOW),
        ] + top_scratch(segs, arrays),
        input_output_aliases={7 + i: 7 + i for i in range(5)},
        compiler_params=params(),
        cost_estimate=cost(2 * rows * 768 * 30000, 2**24),
        name="cross_encoder",
    )(info, both, live, vec, positions, seg_vec, wide, *arrays, *sources, *tall_pieces(mid), *more)
    return grads, seg_grads, [a.reshape(-1, a.shape[2]) for a in (layer, down, hidden, proj, mixed)]


def ffn_backward(info, cotangent, second, summed, slope, vec, mid, down, seg_count, half, before=None, segs=2):
    rows = summed.shape[0]
    count = segs * SEG
    steps = rows // count // 2
    first = half * steps
    before = list(before or [])
    widths = (768, 768, 3072, 768, 768)
    return pl.pallas_call(
        functools.partial(ffn_backward_kernel, segs, seg_count, first),
        grid=(steps,),
        in_specs=[SMEM, shifted(count, 768, first), shifted(count, 768, first), shifted(count, 768, first),
                  shifted(count, 3072, first), fixed((12, 768))] + [ANY] * (18 + len(before)),
        out_specs=[shifted(count, w, first) for w in widths] + [fixed((12, 768))],
        out_shape=[shape_of((rows, w)) for w in widths] + [shape_of((12, 768), F32)],
        scratch_shapes=MID + DOWN + sems(72),
        input_output_aliases={24 + i: i for i in range(5)} if before else {},
        compiler_params=params(),
        cost_estimate=cost(rows * 768 * 14000, rows * 768 * 15),
        name="ffn_backward",
    )(info, cotangent, second, summed, slope, vec, *tall_pieces(mid), *down, *before)


def opening_backward(info, heads, heads_grad, vec, arrays, sources, mid, down, seg_count):
    segs = heads.shape[0]
    arrays, sources = [grouped(a) for a in arrays], [grouped(a) for a in sources]
    whole = fixed((segs, 768))
    *done, grads = pl.pallas_call(
        functools.partial(opening_kernel, segs, seg_count),
        grid=(1,),
        in_specs=[SMEM, whole, whole, fixed((12, 768))] + [ANY] * 26,
        out_specs=[ANY] * 5 + [fixed((12, 768))],
        out_shape=[shape_of(a.shape) for a in arrays] + [shape_of((12, 768), F32)],
        scratch_shapes=top_scratch(segs, arrays),
        input_output_aliases={4 + i: i for i in range(5)},
        compiler_params=params(),
        cost_estimate=cost(2**33, 2**24),
        name="opening_backward",
    )(info, heads, heads_grad, vec, *arrays, *sources, *tall_pieces(mid), *down)
    return [a.reshape(-1, a.shape[2]) for a in done], grads


def attn_backward(info, packed, mixed_grad, seg_count, half, before=None, segs=2):
    rows = packed.shape[0]
    count = segs * SEG
    steps = rows // count // 2
    first = half * steps
    before = [] if before is None else [before]
    return pl.pallas_call(
        functools.partial(attn_backward_kernel, segs, seg_count, first),
        grid=(steps,),
        in_specs=[SMEM, shifted(count, 2304, first), shifted(count, 768, first)] + [ANY] * len(before),
        out_specs=[shifted(count, 2304, first), fixed((2, 768))],
        out_shape=[shape_of((rows, 2304)), shape_of((2, 768), F32)],
        input_output_aliases={3: 0} if before else {},
        compiler_params=params(),
        cost_estimate=cost(rows * 768 * 10000, rows * 768 * 8),
        name="attn_backward",
    )(info, packed, mixed_grad, *before)


def token_gradient(info, packed_grad, proj_grad, pieces, count=512):
    rows = packed_grad.shape[0]
    return pl.pallas_call(
        token_grad_kernel,
        grid=(rows // count,),
        in_specs=[SMEM, block_rows(count, 2304), block_rows(count, 768)] + [ANY] * 10,
        out_specs=block_rows(count, 768),
        out_shape=shape_of((rows, 768)),
        scratch_shapes=QKV + sems(24),
        compiler_params=params(),
        cost_estimate=cost(2 * rows * 768 * 3000, rows * 768 * 10),
        name="token_gradient",
    )(info, packed_grad, proj_grad, *pieces)


def grad_outs(slabs):
    out = pl.BlockSpec((4, 96, 768), lambda i: (0, i, 0))
    return [out, out], [shape_of((4, slabs * 96, 768))] * 2


def qkv_weight_grad(info, left, right, more):
    rows = left.shape[0]
    out = fixed((4, 304, 768))
    return pl.pallas_call(
        qkv_grad_kernel,
        grid=(3,),
        in_specs=[SMEM, fixed((rows, 768)), pl.BlockSpec((rows, 768), lambda i: (0, i)), fixed((8, 16, 768))],
        out_specs=[out, out],
        out_shape=[shape_of((4, 304, 768))] * 2,
        scratch_shapes=[pltpu.VMEM((768, 768), F32)],
        compiler_params=params(),
        cost_estimate=cost(2 * rows * 768 * 2304, rows * 2304 * 2),
        name="qkv_weight_grad",
    )(info, left, right, more)


def mid_weight_grad(info, mixed, proj_grad, low, hidden_grad):
    rows = mixed.shape[0]
    specs, shapes = grad_outs(5)
    still = fixed((rows, 768))
    return pl.pallas_call(
        mid_grad_kernel,
        grid=(5,),
        in_specs=[SMEM, still, still, still, pl.BlockSpec((rows, 768), lambda i: (0, jnp.maximum(i - 1, 0)))],
        out_specs=specs,
        out_shape=shapes,
        scratch_shapes=[pltpu.VMEM((768, 768), F32)],
        compiler_params=params(),
        cost_estimate=cost(2 * rows * 768 * 3840, rows * 3840 * 2),
        name="mid_weight_grad",
    )(info, mixed, proj_grad, low, hidden_grad)


def down_grad_kernel(info, left_ref, right_ref, keep_ref, send_ref, total):
    step = pl.program_id(0)
    total[pl.ds(pl.multiple_of(step * 768, 768), 768), :] = mm_tn(left_ref[...], right_ref[...]).astype(LOW)

    @pl.when(step == pl.num_programs(0) - 1)
    def _():
        for mask in range(8):
            block = pl.multiple_of((info[0] ^ mask) * 384, 384)
            target = send_ref if mask % 2 else keep_ref
            target[mask // 2] = total[pl.ds(block, 384), :]


def down_weight_grad(info, left, right):
    rows, wide = left.shape
    return pl.pallas_call(
        down_grad_kernel,
        grid=(wide // 768,),
        in_specs=[SMEM, pl.BlockSpec((rows, 768), lambda i: (0, i)), fixed((rows, 768))],
        out_specs=[fixed((4, 384, 768))] * 2,
        out_shape=[shape_of((4, 384, 768))] * 2,
        scratch_shapes=[pltpu.VMEM((3072, 768), LOW)],
        compiler_params=params(),
        cost_estimate=cost(2 * rows * 768 * wide, rows * wide * 2),
        name="down_weight_grad",
    )(info, left, right)


def matmul(left_op, right_op):
    return jnp.dot(left_op, right_op, preferred_element_type=jnp.float32)


def trans_left(left_op, right_op):
    return lax.dot_general(
        left_op, right_op, (((0,), (0,)), ((), ())), preferred_element_type=jnp.float32
    )


def trans_right(left_op, right_op):
    return lax.dot_general(
        left_op, right_op, (((1,), (1,)), ((), ())), preferred_element_type=jnp.float32
    )


def norm_forward(summed, gain_row, shift_row):
    average = jnp.mean(summed, axis=-1, keepdims=True)
    centered = summed - average
    inv_scale = lax.rsqrt(jnp.mean(centered * centered, axis=-1, keepdims=True) + NORM_EPS)
    normed = centered * inv_scale
    return (normed * (1.0 + gain_row) + shift_row, normed, inv_scale)


def norm_backward(upstream, normed, inv_scale, gain_row):
    inner = upstream * (1.0 + gain_row)
    back_grad = inv_scale * (
        inner
        - jnp.mean(inner, axis=-1, keepdims=True)
        - normed * jnp.mean(inner * normed, axis=-1, keepdims=True)
    )
    return (back_grad, jnp.sum(upstream * normed, axis=0), jnp.sum(upstream, axis=0))


def gelu_slope(hidden):
    return (
        0.5 * (1.0 + lax.erf(hidden * ROOT_HALF))
        + hidden * jnp.exp(-0.5 * hidden * hidden) * INV_ROOT_TAU
    )


def split_heads(packed, group_len):
    head_count = packed.shape[1] // (3 * HEAD)
    return [
        portion.reshape(-1, group_len, head_count, HEAD) for portion in jnp.split(packed, 3, axis=1)
    ]


def masked_scores(query_heads, key_heads, allowed):
    raw_scores = jnp.einsum(
        "nqhd,nkhd->nhqk", query_heads, key_heads, preferred_element_type=jnp.float32
    ) * HEAD ** (-0.5)
    return jnp.where(allowed[:, None, None, :], raw_scores, MASK_FILL)


def encode(inputs, inputs_low, weights, allowed):
    qkv_w, out_w, up_w, down_w, vectors = weights
    row_count, feat_dim = inputs_low.shape
    group_len = allowed.shape[1]
    qkv_bias = jnp.concatenate([vectors[0], jnp.zeros_like(vectors[0]), vectors[1]])
    packed = (matmul(inputs_low, qkv_w) + qkv_bias).astype(jnp.bfloat16)
    query_heads, key_heads, value_heads = split_heads(packed, group_len)
    scores = masked_scores(query_heads, key_heads, allowed)
    row_max = jnp.max(scores, axis=-1, keepdims=True)
    expo_vals = jnp.exp(scores - row_max)
    row_total = jnp.sum(expo_vals, axis=-1, keepdims=True)
    log_total = row_max + jnp.log(row_total)
    prob_low = (expo_vals / row_total).astype(jnp.bfloat16)
    mixed = jnp.einsum("nhqk,nkhd->nqhd", prob_low, value_heads, preferred_element_type=jnp.float32)
    mixed = mixed.reshape(row_count, feat_dim).astype(jnp.bfloat16)
    projected = matmul(mixed, out_w) + vectors[2]
    first_out, normed_one, scale_one = norm_forward(inputs + projected, vectors[3], vectors[4])
    first_low = first_out.astype(jnp.bfloat16)
    hidden = matmul(first_low, up_w) + vectors[5:-3].reshape(-1)
    activated = jax.nn.gelu(hidden, approximate=False).astype(jnp.bfloat16)
    down_out = matmul(activated, down_w) + vectors[-3]
    result, normed_two, scale_two = norm_forward(first_out + down_out, vectors[-2], vectors[-1])
    return (
        result,
        (
            packed,
            log_total,
            mixed,
            normed_one,
            scale_one,
            first_low,
            hidden,
            activated,
            normed_two,
            scale_two,
        ),
    )


def encode_back(upstream, inputs_low, weights, allowed, kept):
    qkv_w, out_w, up_w, down_w, vectors = weights
    (
        packed,
        log_total,
        mixed,
        normed_one,
        scale_one,
        first_low,
        hidden,
        activated,
        normed_two,
        scale_two,
    ) = kept
    row_count, feat_dim = inputs_low.shape
    group_len = allowed.shape[1]
    back_two, gain_two, shift_two = norm_backward(upstream, normed_two, scale_two, vectors[-2])
    down_grad = back_two.astype(jnp.bfloat16)
    hidden_grad = (trans_right(down_grad, down_w) * gelu_slope(hidden)).astype(jnp.bfloat16)
    first_grad = trans_right(hidden_grad, up_w) + back_two
    back_one, gain_one, shift_one = norm_backward(first_grad, normed_one, scale_one, vectors[3])
    proj_grad = back_one.astype(jnp.bfloat16)
    query_heads, key_heads, value_heads = split_heads(packed, group_len)
    mixed_grad = trans_right(proj_grad, out_w).astype(jnp.bfloat16).reshape(value_heads.shape)
    scores = masked_scores(query_heads, key_heads, allowed)
    prob_vals = jnp.exp(scores - log_total)
    grad_values = jnp.einsum(
        "nhqk,nqhd->nkhd",
        prob_vals.astype(jnp.bfloat16),
        mixed_grad,
        preferred_element_type=jnp.float32,
    )
    grad_prob = jnp.einsum(
        "nqhd,nkhd->nhqk", mixed_grad, value_heads, preferred_element_type=jnp.float32
    )
    score_grad = (
        prob_vals * (grad_prob - jnp.sum(prob_vals * grad_prob, axis=-1, keepdims=True))
    ).astype(jnp.bfloat16)
    grad_query = jnp.einsum(
        "nhqk,nkhd->nqhd", score_grad, key_heads, preferred_element_type=jnp.float32
    ) * HEAD ** (-0.5)
    grad_keys = jnp.einsum(
        "nhqk,nqhd->nkhd", score_grad, query_heads, preferred_element_type=jnp.float32
    ) * HEAD ** (-0.5)
    packed_grad = jnp.concatenate(
        [
            grad_query.reshape(row_count, feat_dim),
            grad_keys.reshape(row_count, feat_dim),
            grad_values.reshape(row_count, feat_dim),
        ],
        axis=1,
    ).astype(jnp.bfloat16)
    bias_grads = jnp.sum(packed_grad, axis=0, dtype=jnp.float32).reshape(3, feat_dim)
    grad_inputs = trans_right(packed_grad, qkv_w) + back_one
    grad_vectors = jnp.concatenate(
        [
            bias_grads[0:1],
            bias_grads[2:3],
            jnp.sum(proj_grad, axis=0, dtype=jnp.float32)[None],
            gain_one[None],
            shift_one[None],
            jnp.sum(hidden_grad, axis=0, dtype=jnp.float32).reshape(-1, feat_dim),
            jnp.sum(down_grad, axis=0, dtype=jnp.float32)[None],
            gain_two[None],
            shift_two[None],
        ],
        axis=0,
    )
    pairs = (
        (inputs_low, packed_grad),
        (mixed, proj_grad),
        (first_low, hidden_grad),
        (activated, down_grad),
    )
    return (grad_inputs, pairs, grad_vectors)


class Links:
    def __init__(self, outer, inner):
        self.outer, self.inner = outer, inner
        self.order = self.place = lax.axis_index("dp")
        self.z = lax.axis_index("fsdp")

    def flip(self, value, mask):
        pairs = [
            (d * self.inner + z, (d ^ mask) * self.inner + z)
            for d in range(self.outer)
            for z in range(self.inner)
        ]
        return lax.ppermute(value, AXES, pairs)

    def turn(self, value, step):
        pairs = [
            (d * self.inner + z, d * self.inner + (z + step) % self.inner)
            for d in range(self.outer)
            for z in range(self.inner)
        ]
        return lax.ppermute(value, AXES, pairs)

    def gather_z(self, shard):
        came = [shard] + [self.turn(shard, step) for step in range(1, self.inner)]
        whole = []
        for z in range(self.inner):
            part = came[-1]
            for step in range(self.inner - 1):
                part = jnp.where(self.z == (z + step) % self.inner, came[step], part)
            whole.append(part)
        return whole

    def spread_near(self, block):
        return self.flip(block, 2), self.flip(block, 4)

    def spread_far(self, by_x, by_y, half):
        return self.flip(by_y[:half], 2), self.flip(by_x[half:], 4)

    def core(self, pieces):
        return [self.flip(piece, 1) for piece in pieces]

    def in_order(self, parts):
        for axis, mask in ((4, 4), (2, 2), (1, 1)):
            odd = self.place // axis % 2 == 1
            parts = [jnp.where(odd, parts[m ^ mask], parts[m]) for m in range(8)]
        return jnp.stack(parts)

    def gather_small(self, shard, line_only=False):
        block = jnp.stack(self.gather_z(shard))
        return block if line_only else self.gather_core(self.gather_plane(block))

    def gather_plane(self, block):
        return jnp.stack([block] + [self.flip(block, m) for m in (2, 4, 6)])

    def gather_core(self, plane):
        return jnp.stack([plane, self.flip(plane, 1)]).reshape((-1,) + plane.shape[2:])


class PlainLinks:
    def __init__(self, outer, inner):
        self.outer, self.inner = outer, inner
        self.order = lax.axis_index("dp")
        self.z = lax.axis_index("fsdp")
        self.place = 0

    def gather_small(self, shard, line_only=False):
        return lax.all_gather(shard, AXES, axis=0)


def add(*terms):
    return sum(t.astype(F32) for t in terms).astype(LOW)


class Sum:
    def __init__(self, links, keep, send, slabs):
        self.links, self.keep, self.slabs = links, keep, slabs
        self.more = keep.shape[1] % 96
        self.came = links.flip(send, 1)

    def line(self, part):
        inner = self.links.inner
        count = part.shape[0] - self.more
        main = part[:count].reshape(self.slabs, inner, -1, part.shape[-1])
        main = main.transpose(1, 0, 2, 3).reshape(inner, -1, part.shape[-1])
        if not self.more:
            return main
        rows = part[count : count + inner].reshape(inner, 1, -1)
        return jnp.concatenate([main, jnp.pad(rows, ((0, 0), (0, 7), (0, 0)))], axis=1)

    def to(self, index):
        return self.line(add(self.keep[index], self.came[index]))

    def far(self):
        half = self.links.inner // 2
        to_d = self.to(3)
        self.far_came = [self.links.flip(to_d[:half], 2), self.links.flip(to_d[half:], 4)]
        return self.far_came

    def near(self):
        half = self.links.inner // 2
        came_x, came_y = self.far_came
        to_x, to_y = self.to(1), self.to(2)
        to_y = jnp.concatenate([add(to_y[:half], came_x), to_y[half:]])
        to_x = jnp.concatenate([to_x[:half], add(to_x[half:], came_y)])
        self.near_came = [self.links.flip(to_x, 2), self.links.flip(to_y, 4)]
        return self.near_came

    def direct(self):
        self.near_came = [self.links.flip(self.to(m // 2), m) for m in (2, 4, 6)]
        return self.near_came

    def turn(self, *earlier):
        links = self.links
        own = add(self.line(self.keep[0]), self.line(self.came[0]), *self.near_came)
        own = after(own, *earlier) if earlier else own
        parts = [lax.dynamic_index_in_dim(own, (links.z + k) % links.inner, 0, keepdims=False) for k in range(links.inner)]
        self.turned = [parts[0]] + [links.turn(parts[k], k) for k in range(1, links.inner)]
        return self.turned[1:]

    def total(self, *earlier):
        parts = [after(t, *earlier) for t in self.turned] if earlier else self.turned
        return sum(t.astype(F32) for t in parts)


class PlainSum:
    def __init__(self, links, keep, send, slabs):
        more = keep.shape[1] % 96
        flat = jnp.stack([keep, send], axis=1).reshape(8, -1, 768)
        main = flat[:, : flat.shape[1] - more].reshape(8, slabs, -1, 768)
        main = main.transpose(1, 0, 2, 3).reshape(slabs, -1, 768)
        self.came = keep
        self.sums = lax.psum_scatter(main, AXES, scatter_dimension=1, tiled=True).reshape(-1, 768)
        if more:
            rows = flat[:, flat.shape[1] - more :][:, : links.outer * links.inner // 8].reshape(-1, 768)
            self.sums = jnp.concatenate([self.sums, lax.psum_scatter(rows, AXES, scatter_dimension=0, tiled=True)])

    def far(self, *earlier):
        return []

    near = direct = turn = far

    def total(self, *earlier):
        return self.sums.astype(F32)


def after(value, *earlier):
    return lax.optimization_barrier((value, *earlier))[0]


def slabs_of(matrix):
    rows, wide = matrix.shape
    return matrix.reshape(rows, wide // 768, 768).transpose(1, 0, 2)


def matrix_of(slabs):
    count, rows, width = slabs.shape
    return slabs.transpose(1, 0, 2).reshape(rows, count * width)


def mix_columns(matrix, devices):
    rows, wide = matrix.shape
    matrix = matrix.reshape(rows, devices, 4, -1).transpose(0, 2, 1, 3)
    return matrix.reshape(rows, wide)


def unmix_columns(matrix, devices):
    rows, wide = matrix.shape
    matrix = matrix.reshape(rows, 4, devices, -1).transpose(0, 2, 1, 3)
    return matrix.reshape(rows, wide)


def plain_pieces(slabs, whole):
    count = slabs.shape[0]
    half = (count + 1) // 2 * 96
    parts = []
    for mask in (0, 2, 4, 6, 1, 3, 5, 7):
        part = slabs[:, mask * 96 : (mask + 1) * 96].reshape(-1, 768)
        parts += [part] if whole or mask < 6 and mask != 7 else [part[:half], part[half:]]
    return parts


def shards(
    outer,
    inner,
    tokens,
    cotangent,
    lengths,
    seg_qkv,
    seg_out,
    seg_up,
    seg_down,
    seg_vec,
    cross_qkv,
    cross_out,
    cross_up,
    cross_down,
    cross_vec,
    positions,
):
    fast = (outer, inner) == (8, 4)
    links = (Links if fast else PlainLinks)(outer, inner)
    summing = Sum if fast else PlainSum
    devices = outer * inner
    me = links.order * inner + links.z
    seq_local, seq_len, feat_dim = tokens.shape
    seg_count = seq_len // SEG
    seg_rows, cross_rows = seg_vec.shape[0], cross_vec.shape[0]
    width = feat_dim // devices
    my_lengths = lax.dynamic_slice_in_dim(lengths, me * seq_local, seq_local)
    info = jnp.concatenate([jnp.full((1,), links.place, jnp.int32), my_lengths])
    small = jnp.concatenate([seg_vec, cross_vec, positions]).reshape(1, -1)
    up_slabs = mix_columns(cross_up, devices).reshape(-1, 4, feat_dim).transpose(1, 0, 2)
    wide = [slabs_of(cross_qkv), slabs_of(cross_out), up_slabs, cross_down.reshape(4, -1, feat_dim)]
    wide = jnp.concatenate(wide)
    mid_shard = jnp.concatenate([slabs_of(seg_out), slabs_of(seg_up)])
    rows_in = tokens.reshape(-1, feat_dim)
    cot_rows = cotangent.reshape(-1, feat_dim)
    seg_starts = jnp.arange(seg_count) * SEG
    live_own = (seg_starts[None, :] < my_lengths[:, None]).reshape(-1, 1)
    up_own = jnp.where(live_own, cotangent.reshape(-1, SEG, feat_dim)[:, 0, :], 0)

    if fast:
        first = jnp.concatenate([slabs_of(seg_qkv).reshape(-1, 768), jnp.pad(small, ((0, 7), (0, 0)))])
        line_first = links.gather_z(first)
        line_mid = links.gather_z(after(mid_shard, *line_first))
        weights = jnp.stack([p[:72].reshape(3, 24, 768) for p in line_first], axis=1).reshape(-1, 768)
        rows = jnp.concatenate([p[72:73] for p in line_first])
        block = jnp.concatenate([weights, jnp.pad(rows, ((0, 12), (0, 0)))])
        near = links.spread_near(block)
        far = links.spread_far(*near, 192)
        first = [block, *near, *far, *links.core([after(p, *far, *line_mid) for p in (block, *near, *far)])]
        line_down = links.gather_z(after(seg_down, *first[5:]))
        ends = [p[288:292] for p in first[:3]] + [first[4][96:100]]
        others = [p[288:292] for p in first[5:8]] + [first[9][96:100]]
        small = links.in_order([(ends, others)[m % 2][m // 2] for m in range(8)])
        block = after(jnp.stack(line_mid, axis=1).reshape(-1, 768), *far)
        mid = [block, *links.spread_near(block)]
    else:
        first = plain_pieces(lax.all_gather(slabs_of(seg_qkv), AXES, axis=1, tiled=True), False)
        mid = plain_pieces(lax.all_gather(mid_shard, AXES, axis=1, tiled=True), False)
        down_whole = lax.all_gather(seg_down, AXES, axis=0, tiled=True)
        down = [down_whole[m * 384 : (m + 1) * 384] for m in (0, 2, 4, 6, 1, 3, 5, 7)]
        small = links.gather_small(small)
    small = small.reshape(devices, -1, width).transpose(1, 0, 2).reshape(-1, feat_dim).astype(F32)
    seg_v, cross_v = small[:seg_rows], small[seg_rows : seg_rows + cross_rows]
    pos_table = small[seg_rows + cross_rows :]
    hidden_rows = slice(5, cross_rows - 3)
    cross_v = cross_v.at[hidden_rows].set(mix_columns(cross_v[hidden_rows].reshape(1, -1), devices).reshape(-1, feat_dim))

    before = attn_forward(info, rows_in, seg_v, first, seg_count, 0)
    wide = lax.all_gather(after(wide, before[0], *((*mid[1:], *line_down) if fast else ())), AXES, axis=1, tiled=True)
    if fast:
        far = links.spread_far(*(after(p, before[0]) for p in mid[1:]), 288)
        rows_late = after(rows_in, *mid[1:])
    else:
        rows_late = rows_in
    packed, mixed = attn_forward(info, rows_late, seg_v, first, seg_count, 1, before)
    if fast:
        early = links.core([after(p, before[0]) for p in mid])
        late = links.core([after(p, packed, *far, *early) for p in far])
        mid = [*mid, *far, *early, *late]
        block = after(jnp.concatenate(line_down), *late)
        near = [links.flip(block, m) for m in (2, 4, 6)]
    summed, low, act, slope = mid_forward(info, rows_in, mixed, seg_v, mid)
    if fast:
        down = [block, *near, links.flip(block, 1), *(links.flip(after(p, act), 1) for p in near)]
    second, heads = down_forward(info, summed, act, seg_v, down)
    heads_own = heads.reshape(-1, feat_dim)
    both = links.gather_small(jnp.stack([heads_own.astype(LOW), up_own]), True)
    back = functools.partial(ffn_backward, info, seg_count=seg_count)
    args = (second, summed, slope, seg_v, mid, down)
    if fast:
        first_half = back(cot_rows, *args, half=0)
        both = links.gather_plane(after(both, first_half[1]))
        *arrays, grads_two = back(after(cot_rows, first_half[1]), *args, half=1, before=first_half[:5])
        both = links.gather_core(after(both, arrays[1]))
    live_all = seg_starts[None, :] < lengths[:, None]
    if fast:
        cross_info = jnp.concatenate([jnp.stack([links.place, me, links.z]).astype(jnp.int32), my_lengths])
        live = links.in_order(list(live_all.reshape(outer, -1))).reshape(4, 2, -1).transpose(1, 0, 2)
        live = jnp.broadcast_to(live.reshape(-1, 1), (live_all.size, SEG)).astype(F32)
        (vec_grad, pos_grad, *cross_grads), grads_more, arrays = cross_whole(
            cross_info, both, live, cross_v, pos_table, wide,
            seg_v, arrays, (second, summed, slope), mid, down, seg_count,
        )
    else:
        weights = (matrix_of(wide[:3]), wide[3], matrix_of(wide[4:8]), wide[8:].reshape(-1, feat_dim), cross_v)
        heads_all, up_all = both[:, 0].reshape(-1, feat_dim), both[:, 1].reshape(-1, feat_dim)
        heads_in = heads_all.astype(F32).reshape(-1, seg_count, feat_dim) + pos_table[None]
        heads_in = heads_in.reshape(-1, feat_dim)
        cross_result, kept = encode(heads_in, heads_in.astype(LOW), weights, live_all)
        all_grad, pairs, vec_grad = encode_back(
            up_all.astype(F32), heads_in.astype(LOW), weights, live_all, kept
        )
        cross_grads = []
        for left, right in pairs:
            left = left.reshape(left.shape[0], -1, feat_dim)
            mine = lax.dynamic_slice_in_dim(left, me * width, width, 2)
            cross_grads.append(trans_left(mine.reshape(left.shape[0], -1), right))
        pos_grad = jnp.sum(all_grad.reshape(-1, seg_count, feat_dim), axis=0)
        own = seq_local * seg_count
        cross_own = lax.dynamic_slice_in_dim(cross_result, me * own, own)
        heads_grad = lax.dynamic_slice_in_dim(all_grad, me * own, own)
        first_half = back(after(cot_rows, heads_grad, *cross_grads), *args, half=0)
        *arrays, grads_two = back(cot_rows, *args, half=1, before=first_half[:5])
        arrays, grads_more = opening_backward(
            info, cross_own, heads_grad, seg_v, arrays, (second, summed, slope), mid, down, seg_count
        )
    layer_out, down_grad, hidden_grad, proj_grad, mixed_grad = arrays
    grads_two = grads_two + first_half[5] + grads_more
    down_sum = summing(links, *down_weight_grad(info, act, down_grad), 1)
    mid_parts = mid_weight_grad(info, mixed, proj_grad, low, after(hidden_grad, down_sum.keep if fast else down_sum.came))
    mid_sum = summing(links, *mid_parts, 5)
    half_grad, grads_one = attn_backward(
        info, packed, after(mixed_grad, mid_parts[1], down_sum.came), seg_count, 0
    )
    ready = after(mixed_grad, half_grad, *down_sum.far(), mid_sum.came)
    packed_grad, grads_more = attn_backward(info, packed, ready, seg_count, 1, half_grad)
    vec_parts = jnp.concatenate([grads_one + grads_more, grads_two[2:]]).reshape(seg_rows, devices, width)
    vec_parts = vec_parts.transpose(1, 0, 2).reshape(outer, inner, seg_rows * width).astype(LOW)
    if outer > 8:
        vec_parts = vec_parts.reshape(8, -1, seg_rows * width)
    vec_parts = jnp.pad(vec_parts, ((0, 0), (0, 16 - vec_parts.shape[1]), (0, feat_dim - seg_rows * width)))
    ready = after(packed_grad, *down_sum.near(), *mid_sum.far())
    keep, send = qkv_weight_grad(info, rows_in, ready, vec_parts)
    qkv_sum = summing(links, keep, after(send, *down_sum.turn(), *mid_sum.near()), 3)
    ready = after(packed_grad, qkv_sum.came)
    token_grad = token_gradient(info, ready, proj_grad, first)
    qkv_sum.direct()
    mid_sum.turn()
    qkv_sum.turn(token_grad)
    cross_grads[2] = unmix_columns(after(cross_grads[2], token_grad), devices)
    vec_grad = vec_grad.at[hidden_rows].set(
        unmix_columns(after(vec_grad[hidden_rows], token_grad).reshape(1, -1), devices).reshape(-1, feat_dim)
    )
    cross_vec_grad = lax.dynamic_slice_in_dim(vec_grad, me * width, width, 1)
    grad_positions = lax.dynamic_slice_in_dim(pos_grad, me * width, width, 1)
    grad_down = down_sum.total()
    grad_mid = mid_sum.total().reshape(5, -1, feat_dim)
    total = qkv_sum.total(cross_grads[2], cross_vec_grad)
    grad_qkv = matrix_of(total[: 3 * width].reshape(3, -1, feat_dim))
    grad_vec = total[3 * width, : seg_rows * width].reshape(seg_rows, width)
    return (
        layer_out.reshape(tokens.shape),
        token_grad.reshape(tokens.shape),
        grad_qkv,
        grad_mid[0],
        matrix_of(grad_mid[1:]),
        grad_down,
        grad_vec,
        *cross_grads,
        cross_vec_grad,
        grad_positions,
    )


def solution(mesh):
    in_specs = (
        P(("dp", "fsdp"), None, None),
        P(("dp", "fsdp"), None, None),
        P(),
        P(("dp", "fsdp"), None),
        P(("dp", "fsdp"), None),
        P(("dp", "fsdp"), None),
        P(("dp", "fsdp"), None),
        P(None, ("dp", "fsdp")),
        P(("dp", "fsdp"), None),
        P(("dp", "fsdp"), None),
        P(("dp", "fsdp"), None),
        P(("dp", "fsdp"), None),
        P(None, ("dp", "fsdp")),
        P(None, ("dp", "fsdp")),
    )
    out_specs = (
        P(("dp", "fsdp"), None, None),
        P(("dp", "fsdp"), None, None),
        P(("dp", "fsdp"), None),
        P(("dp", "fsdp"), None),
        P(("dp", "fsdp"), None),
        P(("dp", "fsdp"), None),
        P(None, ("dp", "fsdp")),
        P(("dp", "fsdp"), None),
        P(("dp", "fsdp"), None),
        P(("dp", "fsdp"), None),
        P(("dp", "fsdp"), None),
        P(None, ("dp", "fsdp")),
        P(None, ("dp", "fsdp")),
    )
    return jax.shard_map(
        functools.partial(shards, mesh.shape["dp"], mesh.shape["fsdp"]),
        mesh=mesh, in_specs=in_specs, out_specs=out_specs, check_vma=False)
```
